32 devices in a mesh: dom: 8 (over z, x), sub: 4 (over y, core).
Axes of the slice: x: 2, y: 2, z: 4, core: 2. Of those that a mesh axis runs over, the one named last changes fastest.
Arguments:
- solution: float32 [56, 9, 512], P(None, None, ('dom', 'sub')), may hold values from -1.5 to 1.5
- stiffness: float32 [3, 56, 56], replicated, may hold values from -0.75 to 0.75
- star_matrices: float32 [3, 9, 9, 512], P(None, None, None, ('dom', 'sub')), may hold values from -4.3 to 4.3
- face_restrict: float32 [4, 21, 56], replicated, may hold values from -0.75 to 0.75
- face_lift: float32 [4, 56, 21], replicated, may hold values from -1.25 to 1.25
- orient_maps: float32 [3, 21, 21], replicated, may hold values from -1.25 to 1.25
- flux_local: float32 [4, 9, 9, 512], P(None, None, None, ('dom', 'sub')), may hold values from -1 to 1
- flux_remote: float32 [4, 9, 9, 512], P(None, None, None, ('dom', 'sub')), may hold values from -1 to 1
- cluster_rate: int32 [512], P(('dom', 'sub')), may hold values from 1 to 2, as said below
- send_list: int32 [32, 4, 4], P(('dom', 'sub')), may hold values from 0 to 15, as said below
- neighbour_slot: int32 [4, 512], P(None, ('dom', 'sub')), may hold values from 0 to 31, as said below
- neighbour_face: int32 [4, 512], P(None, ('dom', 'sub')), may hold values from 0 to 3
- neighbour_turn: int32 [4, 512], P(None, ('dom', 'sub')), may hold values from 0 to 2
Outputs:
- new_solution: float32 [56, 9, 512], P(None, None, ('dom', 'sub'))
The draws below stay inside these ranges and needn't reach their ends.
Inputs may be any that keep to these rules, and one draw needn't show every extreme that they name: `cluster_rate`: 1 is the slow cluster, 2 the fast one. Among the 16 elements of one device at most 8 are fast, and some device has exactly 8. `send_list`: row p of a device's lists names elements of that device sent toward neighbour p (0: previous along dom, 1: next along dom, 2: previous along sub, 3: next along sub, cyclically); the four rows of a device hold each of its 16 elements exactly once. In every row the fast elements stand before the slow ones, at most 2 of them, and some row has exactly 2. `neighbour_slot`: A value below 16 names an element of the same device; the value 16 + p * 4 + k names the k-th element received from neighbour p, and each of these 16 values appears exactly once among one device's faces.
All inputs are finite; a program needn't handle non-finite values.
Results may differ from the reference program's by a relative error of at most 0.0001.
Values sent between devices are 32-bit elements; how exact they have to be, the bound alone decides.
No kernel may reach another device: no remote copies, remote signals or barrier semaphores. Data moves between devices by JAX's collectives and lax.ppermute only.
A program may use at most 64 MiB of HBM per device.

```python
import math
import jax
import jax.numpy as jnp
from jax import lax

MODES = 56
FACE_MODES = 21
FIELDS = 9
DERIVS = 6
E_DEV = 16
SEND = 4
FAST_MAX = 8
E_TOTAL = 512
N_DOM = 8
N_SUB = 4
DEVICES = 32


def cluster_layout(key):
    key_shift, key_pick, key_slots, key_order = jax.random.split(jax.random.fold_in(key, 11), 4)
    halvings = jax.random.randint(key_shift, (DEVICES,), 0, 4)
    busiest = jax.random.randint(key_pick, (), 0, DEVICES)
    halvings = jnp.where(jnp.arange(DEVICES) == busiest, 0, halvings)
    fast_count = jnp.right_shift(jnp.full((DEVICES,), FAST_MAX, jnp.int32), halvings.astype(jnp.int32))
    leading = SEND // 2
    slot_keys = jax.random.split(key_slots, DEVICES)
    capable = jax.vmap(lambda one_key: jax.random.permutation(one_key, 4 * leading))(slot_keys)
    chosen = (capable < fast_count[:, None]).reshape(DEVICES, 4, leading).astype(jnp.int32)
    row_fast = jnp.sum(chosen, axis=2).astype(jnp.int32)
    row_slow = (SEND - row_fast).astype(jnp.int32)
    fast_start = jnp.cumsum(row_fast, axis=1) - row_fast
    slow_start = jnp.cumsum(row_slow, axis=1) - row_slow
    position = jnp.arange(SEND, dtype=jnp.int32)[None, None, :]
    is_fast = position < row_fast[:, :, None]
    pick = jnp.where(is_fast, fast_start[:, :, None] + position, fast_count[:, None, None] + slow_start[:, :, None] + position - row_fast[:, :, None])
    order_keys = jax.random.split(key_order, DEVICES)
    elements = jax.vmap(lambda one_key: jax.random.permutation(one_key, E_DEV))(order_keys).astype(jnp.int32)
    send = jnp.take_along_axis(elements, pick.reshape(DEVICES, -1).astype(jnp.int32), axis=1)
    send = send.reshape(DEVICES, 4, SEND).astype(jnp.int32)
    inverse = jnp.argsort(elements, axis=1)
    cluster = jnp.where(inverse < fast_count[:, None], 2, 1)
    return (cluster.reshape(-1).astype(jnp.int32), send)


def draw_cluster_rate(key, part):
    cluster, send = cluster_layout(key)
    return cluster


def draw_send_list(key, part):
    cluster, send = cluster_layout(key)
    return send


def draw_neighbour_slot(key, part):
    key_place, key_local = jax.random.split(jax.random.fold_in(key, 37))
    place_keys = jax.random.split(key_place, DEVICES)
    placement = jax.vmap(lambda one_key: jax.random.permutation(one_key, 4 * E_DEV))(place_keys)
    local_pick = jax.random.randint(key_local, (DEVICES, 4 * E_DEV), 0, E_DEV)
    slots = jnp.where(placement < 4 * SEND, E_DEV + placement, local_pick)
    slots = slots.reshape(DEVICES, 4, E_DEV).transpose(1, 0, 2).reshape(4, DEVICES * E_DEV)
    return slots.astype(jnp.int32)


def plant(values, own_key, smallest, top_value):
    dims = values.shape
    spot = [jax.random.randint(jax.random.fold_in(own_key, axis), (), 0, dims[axis]) for axis in range(len(dims))]
    values = values.at[tuple(spot)].set(smallest)
    longest = dims.index(max(dims))
    spot[longest] = (spot[longest] + 1) % dims[longest]
    return values.at[tuple(spot)].set(top_value)


def steps_of(stream_key, shape, shards, low, top_value):
    def one(dim, blocks):
        draws = jax.random.uniform(jax.random.fold_in(jax.random.fold_in(stream_key, 6), dim), (blocks,), jnp.float32, low / len(shards), top_value / len(shards))
        return jnp.repeat(jnp.exp(draws), shape[dim] // blocks).reshape((-1,) + (1,) * (len(shape) - dim - 1))

    factor_of = one(*shards[0])
    for cut in shards[1:]:
        factor_of = factor_of * one(*cut)
    return factor_of


def centred(rng, extent, width, reach, cuts=(), kind=jnp.bfloat16):
    entries = jax.random.normal(rng, extent, jnp.float32) * width
    if len(cuts) > 0:
        entries = steps_of(rng, extent, cuts, -0.22, 0.18) * entries
    return jnp.clip(entries, min=-reach, max=reach).astype(kind)


def setup_inputs(seed: int = 0) -> dict:
    key_list = jax.random.split(jax.random.key(seed), 14)
    return {
        "solution": centred(key_list[0], (MODES, FIELDS, E_TOTAL), 0.25, 1.5, ((2, 32),), jnp.float32),
        "stiffness": centred(key_list[1], (3, MODES, MODES), MODES ** -0.5, 0.75, (), jnp.float32),
        "star_matrices": centred(key_list[2], (3, FIELDS, FIELDS, E_TOTAL), 0.72, 4.3, ((3, 32),), jnp.float32),
        "face_restrict": centred(key_list[3], (4, FACE_MODES, MODES), MODES ** -0.5, 0.75, (), jnp.float32),
        "face_lift": centred(key_list[4], (4, MODES, FACE_MODES), FACE_MODES ** -0.5, 1.25, (), jnp.float32),
        "orient_maps": centred(key_list[5], (3, FACE_MODES, FACE_MODES), FACE_MODES ** -0.5, 1.25, (), jnp.float32),
        "flux_local": centred(key_list[6], (4, FIELDS, FIELDS, E_TOTAL), (4 * FIELDS) ** -0.5, 1.0, ((3, 32),), jnp.float32),
        "flux_remote": centred(key_list[7], (4, FIELDS, FIELDS, E_TOTAL), (4 * FIELDS) ** -0.5, 1.0, ((3, 32),), jnp.float32),
        "cluster_rate": draw_cluster_rate(jax.random.fold_in(key_list[13], 71), 0),
        "send_list": draw_send_list(jax.random.fold_in(key_list[13], 71), 0),
        "neighbour_slot": draw_neighbour_slot(jax.random.fold_in(key_list[13], 71), 0),
        "neighbour_face": plant(jax.random.randint(key_list[11], (4, E_TOTAL), 0, 4), jax.random.fold_in(key_list[11], 1), 0, 3).astype(jnp.int32),
        "neighbour_turn": plant(jax.random.randint(key_list[12], (4, E_TOTAL), 0, 3), jax.random.fold_in(key_list[12], 1), 0, 2).astype(jnp.int32),
    }


highest = lax.Precision.HIGHEST


def matrix_apply(matrix, values):
    flattened = values.reshape(values.shape[0], -1)
    product = jnp.dot(matrix, flattened, precision=highest, preferred_element_type=jnp.float32)
    return product.reshape((matrix.shape[0],) + values.shape[1:])


def star_apply(values, coupling):
    result = values[:, 0:1, :] * coupling[0][None]
    for column in range(1, coupling.shape[0]):
        result = result + values[:, column:column + 1, :] * coupling[column][None]
    return result


def derive(values, stiffness, star_matrices):
    result = star_apply(matrix_apply(stiffness[0], values), star_matrices[0])
    for axis_dir in range(1, 3):
        result = result + star_apply(matrix_apply(stiffness[axis_dir], values), star_matrices[axis_dir])
    return -result


def taylor_weight(lower, upper, degree):
    return (upper ** (degree + 1) - lower ** (degree + 1)) / math.factorial(degree + 1)


def predict(values, stiffness, star_matrices):
    current = values
    early_part = taylor_weight(0.0, 0.5, 0) * current
    late_part = taylor_weight(0.5, 1.0, 0) * current
    for degree in range(1, DERIVS):
        current = derive(current, stiffness, star_matrices)
        early_part = early_part + taylor_weight(0.0, 0.5, degree) * current
        late_part = late_part + taylor_weight(0.5, 1.0, degree) * current
    return early_part, late_part


def trace_all(operators, values):
    stacked = operators.reshape(-1, operators.shape[2])
    product = matrix_apply(stacked, values)
    return product.reshape((operators.shape[0], operators.shape[1]) + values.shape[1:])


def pick_code(stacked, code, count):
    result = jnp.where((code == 0)[None, None, :], stacked[0], 0.0)
    for option_index in range(1, count):
        result = result + jnp.where((code == option_index)[None, None, :], stacked[option_index], 0.0)
    return result


def volume_term(values, stiffness, star_part):
    result = star_apply(matrix_apply(stiffness[0].T, values), star_part[0])
    for axis_dir in range(1, 3):
        result = result + star_apply(matrix_apply(stiffness[axis_dir].T, values), star_part[axis_dir])
    return result


def local_flux(own_traces, face_lift, local_part):
    result = matrix_apply(face_lift[0], star_apply(own_traces[0], local_part[0]))
    for face_index in range(1, 4):
        result = result + matrix_apply(face_lift[face_index], star_apply(own_traces[face_index], local_part[face_index]))
    return result


def oriented_flux(gathered, face_code, turn_code, face_index, face_lift, orient_maps, remote_part):
    chosen = pick_code(gathered, face_code, 4)
    turned = pick_code(trace_all(orient_maps, chosen), turn_code, 3)
    return matrix_apply(face_lift[face_index], star_apply(turned, remote_part[face_index]))


def remote_flux(integral, global_rows, neighbour_face, neighbour_turn, face_restrict, face_lift, orient_maps, flux_remote):
    result = None
    for face_index in range(4):
        gathered = trace_all(face_restrict, jnp.take(integral, global_rows[face_index], axis=2))
        contribution = oriented_flux(gathered, neighbour_face[face_index], neighbour_turn[face_index], face_index, face_lift, orient_maps, flux_remote)
        result = contribution if result is None else result + contribution
    return result


def advance(base, own, remote, stiffness, star_matrices, face_restrict, face_lift, flux_local):
    own_traces = trace_all(face_restrict, own)
    return base + volume_term(own, stiffness, star_matrices) - local_flux(own_traces, face_lift, flux_local) - remote


def global_neighbours(neighbour_slot, send_list, owner_device):
    ghost_index = neighbour_slot - E_DEV
    remote_flag = ghost_index >= 0
    ghost_index = jnp.maximum(ghost_index, 0)
    peer_side = ghost_index // SEND
    slot_index = ghost_index % SEND
    owners = jnp.broadcast_to(owner_device[None, :], neighbour_slot.shape)
    dom_place = owners // N_SUB
    sub_place = owners % N_SUB
    dom_peer = (dom_place + jnp.where(peer_side == 0, -1, jnp.where(peer_side == 1, 1, 0))) % N_DOM
    sub_peer = (sub_place + jnp.where(peer_side == 2, -1, jnp.where(peer_side == 3, 1, 0))) % N_SUB
    peer_device = (dom_peer * N_SUB + sub_peer).astype(jnp.int32)
    sent_element = send_list[peer_device, jnp.bitwise_xor(peer_side, 1), slot_index]
    local_rows = owners * E_DEV + neighbour_slot
    return jnp.where(remote_flag, peer_device * E_DEV + sent_element, local_rows).astype(jnp.int32)


def reference(solution, stiffness, star_matrices, face_restrict, face_lift, orient_maps, flux_local, flux_remote, cluster_rate, send_list, neighbour_slot, neighbour_face, neighbour_turn):
    owner_device = (jnp.arange(solution.shape[2], dtype=jnp.int32) // E_DEV).astype(jnp.int32)
    global_rows = global_neighbours(neighbour_slot, send_list, owner_device)
    fast_flag = (cluster_rate == 2)[None, None, :]
    early_part, late_part = predict(solution, stiffness, star_matrices)
    early_remote = remote_flux(early_part, global_rows, neighbour_face, neighbour_turn, face_restrict, face_lift, orient_maps, flux_remote)
    middle = advance(solution, early_part, early_remote, stiffness, star_matrices, face_restrict, face_lift, flux_local)
    restart, unused_part = predict(middle, stiffness, star_matrices)
    late_value = jnp.where(fast_flag, restart, late_part)
    late_remote = remote_flux(late_value, global_rows, neighbour_face, neighbour_turn, face_restrict, face_lift, orient_maps, flux_remote)
    fast_end = advance(middle, late_value, late_remote, stiffness, star_matrices, face_restrict, face_lift, flux_local)
    whole_part = early_part + late_value
    whole_remote = remote_flux(whole_part, global_rows, neighbour_face, neighbour_turn, face_restrict, face_lift, orient_maps, flux_remote)
    slow_end = advance(solution, whole_part, whole_remote, stiffness, star_matrices, face_restrict, face_lift, flux_local)
    return jnp.where(fast_flag, fast_end, slow_end)
```

```python
import math

import jax
import jax.numpy as jnp
from jax import lax
from jax.experimental import pallas as pl
from jax.experimental.pallas import tpu as pltpu
from jax.sharding import PartitionSpec as P

DERIVS = 6
LANES = 128
HALF = 64
ROWS = 8
F32 = jnp.float32
BF16 = jnp.bfloat16


def taylor_weight(lower, upper, degree):
    return (upper ** (degree + 1) - lower ** (degree + 1)) / math.factorial(degree + 1)


def weight_at(lower, upper, degree):
    result = jnp.float32(taylor_weight(lower, upper, 1))
    for option in range(2, DERIVS):
        result = jnp.where(degree == option, jnp.float32(taylor_weight(lower, upper, option)), result)
    return result


def split(values):
    high = values.astype(BF16)
    low = (values - high.astype(F32)).astype(BF16)
    return high, low


def stack_left(values):
    high, low = split(values)
    return jnp.concatenate([high, low, high], axis=1)


def stack_right(values):
    high, low = split(values)
    return jnp.concatenate([high, high, low], axis=0)


def product(left, right):
    return jnp.dot(left, right, preferred_element_type=F32)


def lane_index(shape):
    return lax.broadcasted_iota(jnp.int32, shape, len(shape) - 1)


def lower_half(shape):
    return lane_index(shape) < HALF


def swap_halves(values):
    return pltpu.roll(values, HALF, values.ndim - 1)


def pack(values_ref, packed_ref):
    modes = values_ref.shape[2]
    packed_ref[...] = jnp.zeros(packed_ref.shape, F32)
    packed_ref[:, :, 0:modes] = values_ref[:, 0:ROWS, :]
    packed_ref[:, :, HALF : HALF + modes] = values_ref[:, ROWS : 2 * ROWS, :]


def turn_matrices(source_ref, work_ref):
    fields, kinds, elements = source_ref.shape[0], source_ref.shape[2], source_ref.shape[3]
    tiles = []
    for pair in range((fields + 1) // 2):
        for row in range(2 * pair, min(2 * pair + 2, fields)):
            for col in range(fields):
                at = (row % 2) * HALF + col * 4
                work_ref[pair, at : at + kinds, 0:elements] = source_ref[row, col]
        tiles.append(work_ref[pair].T[0:elements, :])
    return tiles


def spread(tile, index):
    return jnp.take_along_axis(tile, index, axis=1, mode="promise_in_bounds")


def star_coefficients(star_ref, work_ref, star_out):
    fields, kinds = star_ref.shape[0], star_ref.shape[2]
    tiles = turn_matrices(star_ref, work_ref)
    lanes = lane_index((ROWS, LANES))
    base = (lanes // HALF) * HALF
    lower = lanes < HALF
    for row in range(fields):
        first, second = tiles[row // 2][0:ROWS], tiles[row // 2][ROWS : 2 * ROWS]
        if row % 2 == 0:
            both = jnp.where(lower, first, swap_halves(second))
        else:
            both = jnp.where(lower, swap_halves(first), second)
        for kind in range(kinds):
            for col in range(fields):
                star_out[(row * kinds + kind) * fields + col] = spread(both, base + (col * 4 + kind))


def star_mix(columns, star_ref, fields, kinds):
    sums = [None] * fields
    for row in range(fields):
        for kind in range(kinds):
            part = columns[row * ROWS : (row + 1) * ROWS, kind * LANES : (kind + 1) * LANES]
            for col in range(fields):
                term = star_ref[(row * kinds + kind) * fields + col] * part
                sums[col] = term if sums[col] is None else sums[col] + term
    return jnp.concatenate(sums, axis=0)


def stiffness_blocks(stiffness_ref, block_ref):
    kinds, modes = stiffness_ref.shape[0], stiffness_ref.shape[1]
    block_ref[...] = jnp.zeros(block_ref.shape, F32)
    for kind in range(kinds):
        block_ref[kind, 0:modes, 0:modes] = stiffness_ref[kind]
        block_ref[kind, HALF : HALF + modes, HALF : HALF + modes] = stiffness_ref[kind]


def derive_operator(block_ref):
    return jnp.concatenate([-block_ref[kind].T for kind in range(block_ref.shape[0])], axis=1)


def predict_kernel(
    solution_ref, stiffness_ref, star_ref, send_ref,
    early_out, late_out, to_before_dom, to_after_dom, to_before_sub, to_after_sub,
    packed_ref, work_ref, coef_ref, block_ref, derive_ref, early_rows, late_rows,
):
    fields, kinds = star_ref.shape[0], star_ref.shape[2]
    pairs = (fields + 1) // 2
    pack(solution_ref, packed_ref)
    stiffness_blocks(stiffness_ref, block_ref)
    derive_ref[...] = stack_right(derive_operator(block_ref))
    star_coefficients(star_ref, work_ref, coef_ref)
    start = packed_ref[...].reshape(fields * ROWS, LANES)

    def step(degree, carry):
        current, early, late = carry
        current = star_mix(product(stack_left(current), derive_ref[...]), coef_ref, fields, kinds)
        early = early + weight_at(0.0, 0.5, degree) * current
        late = late + weight_at(0.5, 1.0, degree) * current
        return current, early, late

    _, early, late = lax.fori_loop(
        1, DERIVS, step, (start, taylor_weight(0.0, 0.5, 0) * start, taylor_weight(0.5, 1.0, 0) * start)
    )
    early_out[...] = early.reshape(fields, ROWS, LANES)
    late_out[...] = late.reshape(fields, ROWS, LANES)
    rows_by_pair(early, early_rows, fields)
    rows_by_pair(late, late_rows, fields)
    sends = send_ref.shape[2]
    fast = sends // 2
    for side, out in enumerate((to_before_dom, to_after_dom, to_before_sub, to_after_sub)):
        out[...] = jnp.zeros(out.shape, F32)
        for place in range(sends):
            element = send_ref[0, side, place]
            for pair in range(pairs):
                row = pair * sends + place
                out[row : row + 1, :] = early_rows[pair, pl.ds(element, 1), :]
            if place >= fast:
                for pair in range(pairs):
                    row = pairs * sends + pair * fast + place - fast
                    out[row : row + 1, :] = late_rows[pair, pl.ds(element, 1), :]


def rows_by_pair(packed, out_ref, fields):
    lower = lower_half((ROWS, LANES))
    for pair in range((fields + 1) // 2):
        even = packed[2 * pair * ROWS : (2 * pair + 1) * ROWS]
        odd = jnp.zeros_like(even)
        if 2 * pair + 1 < fields:
            odd = packed[(2 * pair + 1) * ROWS : (2 * pair + 2) * ROWS]
        out_ref[pair, 0:ROWS, :] = jnp.where(lower, even, swap_halves(odd))
        out_ref[pair, ROWS : 2 * ROWS, :] = jnp.where(lower, swap_halves(even), odd)


def flux_local_coefficients(flux_ref, work_ref, out_ref):
    fields = flux_ref.shape[0]
    tiles = turn_matrices(flux_ref, work_ref)
    lanes = lane_index((ROWS, LANES))
    for row in range(fields):
        for col in range(fields):
            index = (row % 2) * HALF + col * 4 + lanes % 4
            for half in range(2):
                tile = tiles[row // 2][half * ROWS : (half + 1) * ROWS]
                out_ref[row * fields + col, half] = spread(tile, index)


def flux_remote_coefficients(flux_ref, work_ref, out_ref):
    fields, faces = flux_ref.shape[0], flux_ref.shape[2]
    pairs = (fields + 1) // 2
    tiles = turn_matrices(flux_ref, work_ref)
    lanes = lane_index((ROWS, LANES))
    base = (lanes // HALF) * HALF
    for pair in range(pairs):
        for face in range(faces):
            for col in range(fields):
                at = (face * pairs + pair) * fields + col
                for half in range(2):
                    tile = tiles[pair][half * ROWS : (half + 1) * ROWS]
                    out_ref[at, half * ROWS : (half + 1) * ROWS, :] = spread(tile, base + (col * 4 + face))


def local_terms(packed, star_ref, flux_ref, volume_ref, trace_ref, lift_ref, fields, kinds):
    left = stack_left(packed)
    volume = star_mix(product(left, volume_ref[...]), star_ref, fields, kinds)
    traces = product(left, trace_ref[...])
    sums = []
    for col in range(fields):
        halves = []
        for half in range(2):
            total = None
            for row in range(fields):
                part = traces[row * ROWS : (row + 1) * ROWS, half * LANES : (half + 1) * LANES]
                term = flux_ref[row * fields + col, half] * part
                total = term if total is None else total + term
            halves.append(total)
        sums.append(jnp.concatenate(halves, axis=1))
    return volume + product(stack_left(jnp.concatenate(sums, axis=0)), lift_ref[...])


def prepare_kernel(
    solution_ref, early_ref, stiffness_ref, star_ref, restrict_ref, lift_ref, orient_ref, flux_local_ref,
    flux_remote_ref, slot_ref, face_ref, turn_ref,
    base_out, star_out, local_out, remote_out, derive_out, volume_out, trace_out, local_lift_out, compose_out,
    remote_lift_out, choose_out, mask_out,
    packed_ref, work_ref, block_ref, wide_ref, face_work_ref, orient_work_ref, code_ref,
):
    fields, kinds = star_ref.shape[0], star_ref.shape[2]
    face_modes, faces, modes = restrict_ref.shape
    turns = orient_ref.shape[0]
    work_ref[...] = jnp.zeros(work_ref.shape, F32)
    star_coefficients(star_ref, work_ref, star_out)
    flux_local_coefficients(flux_local_ref, work_ref, local_out)
    flux_remote_coefficients(flux_remote_ref, work_ref, remote_out)

    stiffness_blocks(stiffness_ref, block_ref)
    derive_out[...] = stack_right(derive_operator(block_ref))
    volume_out[...] = stack_right(jnp.concatenate([block_ref[kind] for kind in range(kinds)], axis=1))

    wide_ref[...] = jnp.zeros(wide_ref.shape, F32)
    for mode in range(face_modes):
        at = mode * faces
        wide_ref[at : at + faces, 0:modes] = restrict_ref[mode]
        wide_ref[LANES + at : LANES + at + faces, HALF : HALF + modes] = restrict_ref[mode]
    trace_out[...] = stack_right(wide_ref[...].T)
    for mode in range(face_modes):
        at = mode * faces
        wide_ref[at : at + faces, 0:modes] = -lift_ref[mode]
        wide_ref[LANES + at : LANES + at + faces, HALF : HALF + modes] = -lift_ref[mode]
    local_lift_out[...] = stack_right(wide_ref[...])

    face_work_ref[...] = jnp.zeros(face_work_ref.shape, F32)
    orient_work_ref[...] = jnp.zeros(orient_work_ref.shape, F32)
    for turn in range(turns):
        orient_work_ref[turn * face_modes : (turn + 1) * face_modes, 0:face_modes] = orient_ref[turn]
    for face in range(faces):
        face_work_ref[0:face_modes, face * LANES : face * LANES + modes] = restrict_ref[:, face, :]
        face_work_ref[0:face_modes, face * LANES + HALF : face * LANES + HALF + modes] = restrict_ref[:, face, :]
    composed = jnp.dot(
        orient_work_ref[...], face_work_ref[...], precision=lax.Precision.HIGHEST, preferred_element_type=F32
    )
    stacked = jnp.concatenate([composed[:, face * LANES : (face + 1) * LANES] for face in range(faces)], axis=0)
    compose_out[...] = stack_right(stacked.T)
    for face in range(faces):
        orient_work_ref[...] = jnp.zeros(orient_work_ref.shape, F32)
        for turn in range(turns):
            rows = slice(turn * face_modes, (turn + 1) * face_modes)
            orient_work_ref[rows, 0:modes] = -lift_ref[:, face, :]
            orient_work_ref[rows, HALF : HALF + modes] = -lift_ref[:, face, :]
        high, low = split(orient_work_ref[...])
        remote_lift_out[face, 0] = high
        remote_lift_out[face, 1] = low

    elements = slot_ref.shape[1]
    code_ref[...] = jnp.zeros(code_ref.shape, F32)
    code_ref[0:faces, 0:elements] = slot_ref[...].astype(F32)
    code_ref[faces : 2 * faces, 0:elements] = (face_ref[...] * turns + turn_ref[...]).astype(F32)
    codes = code_ref[...].T[0:elements, :]
    sources = choose_out.shape[1] // 2
    source_lane = (lane_index((elements, 2 * sources)) % sources).astype(F32)
    lanes = lane_index((elements, mask_out.shape[1]))
    in_face = lanes % HALF
    lane_code = jnp.where(in_face < turns * face_modes, (lanes // HALF) * turns + in_face // face_modes, -1)
    lane_code = lane_code.astype(F32)
    picks, masks = [], []
    for face in range(faces):
        picks.append(jnp.where(codes[:, face : face + 1] == source_lane, 1.0, 0.0))
        masks.append(jnp.where(codes[:, faces + face : faces + face + 1] == lane_code, 1.0, 0.0))
    choose_out[...] = jnp.concatenate(picks, axis=0).astype(BF16)
    mask_out[...] = jnp.concatenate(masks, axis=0)

    pack(solution_ref, packed_ref)
    early = early_ref[...].reshape(fields * ROWS, LANES)
    terms = local_terms(early, star_out, local_out, volume_out, trace_out, local_lift_out, fields, kinds)
    base_out[...] = packed_ref[...] + terms.reshape(fields, ROWS, LANES)


def remote_terms(rows_ref, remote_ref, compose_ref, lift_ref, choose_ref, mask_ref, fields):
    pairs = rows_ref.shape[0]
    faces = lift_ref.shape[0]
    elements = choose_ref.shape[0] // faces
    sources = jnp.concatenate([rows_ref[pair] for pair in range(pairs)], axis=1)
    gathered = product(choose_ref[...], jnp.concatenate(split(sources), axis=0))
    result = None
    for face in range(faces):
        sums = []
        for col in range(fields):
            total = None
            for pair in range(pairs):
                part = gathered[face * elements : (face + 1) * elements, pair * LANES : (pair + 1) * LANES]
                term = remote_ref[(face * pairs + pair) * fields + col] * part
                total = term if total is None else total + term
            sums.append(total)
        turned = product(stack_left(jnp.concatenate(sums, axis=0)), compose_ref[...])
        mask = mask_ref[face * elements : (face + 1) * elements, :]
        chosen = turned.reshape(fields, elements, turned.shape[1]) * mask[None]
        left = stack_left(chosen.reshape(turned.shape))
        copies = turned.shape[1] // lift_ref.shape[2]
        high, low = lift_ref[face, 0], lift_ref[face, 1]
        right = jnp.concatenate([high] * (2 * copies) + [low] * copies, axis=0)
        lifted = product(left, right)
        result = lifted if result is None else result + lifted
    result = result.reshape(fields, 2, ROWS, LANES)
    return jnp.where(lower_half((ROWS, LANES))[None], result[:, 0], result[:, 1])


def middle_kernel(
    base_ref, early_ref, late_ref, star_ref, remote_ref, derive_ref, compose_ref, lift_ref, choose_ref, mask_ref,
    rate_ref, send_ref, from_before_dom, from_after_dom, from_before_sub, from_after_sub,
    middle_out, late_out, to_before_dom, to_after_dom, to_before_sub, to_after_sub,
    rows_ref, late_rows,
):
    fields = base_ref.shape[0]
    kinds = star_ref.shape[0] // (fields * fields)
    pairs = rows_ref.shape[0]
    sends = send_ref.shape[2]
    fast = sends // 2
    elements = 2 * ROWS
    rows_by_pair(early_ref[...].reshape(fields * ROWS, LANES), rows_ref, fields)
    for side, arrived in enumerate((from_before_dom, from_after_dom, from_before_sub, from_after_sub)):
        at = elements + side * sends
        for pair in range(pairs):
            rows_ref[pair, at : at + sends, :] = arrived[pair * sends : (pair + 1) * sends, :]
    middle = base_ref[...] + remote_terms(
        rows_ref, remote_ref, compose_ref, lift_ref, choose_ref, mask_ref, fields
    )
    middle_out[...] = middle
    start = middle.reshape(fields * ROWS, LANES)

    def step(degree, carry):
        current, early = carry
        current = star_mix(product(stack_left(current), derive_ref[...]), star_ref, fields, kinds)
        return current, early + weight_at(0.0, 0.5, degree) * current

    _, restart = lax.fori_loop(1, DERIVS, step, (start, taylor_weight(0.0, 0.5, 0) * start))
    sublane = lax.broadcasted_iota(jnp.int32, (ROWS, LANES), 0)
    lower = lower_half((ROWS, LANES))
    is_fast = jnp.zeros((ROWS, LANES), jnp.int32)
    for element in range(elements):
        here = (sublane == element % ROWS) & (lower if element < ROWS else jnp.logical_not(lower))
        is_fast = jnp.where(here, rate_ref[element], is_fast)
    late = jnp.where((is_fast == 2)[None], restart.reshape(fields, ROWS, LANES), late_ref[...])
    late_out[...] = late
    rows_by_pair(late.reshape(fields * ROWS, LANES), late_rows, fields)
    for side, out in enumerate((to_before_dom, to_after_dom, to_before_sub, to_after_sub)):
        out[...] = jnp.zeros(out.shape, F32)
        for place in range(fast):
            element = send_ref[0, side, place]
            for pair in range(pairs):
                row = pair * fast + place
                out[row : row + 1, :] = late_rows[pair, pl.ds(element, 1), :]


def local_kernel(middle_ref, late_ref, star_ref, flux_ref, volume_ref, trace_ref, lift_ref, base_out):
    fields = middle_ref.shape[0]
    kinds = star_ref.shape[0] // (fields * fields)
    late = late_ref[...].reshape(fields * ROWS, LANES)
    terms = local_terms(late, star_ref, flux_ref, volume_ref, trace_ref, lift_ref, fields, kinds)
    base_out[...] = middle_ref[...] + terms.reshape(fields, ROWS, LANES)


def final_kernel(
    base_ref, late_ref, remote_ref, compose_ref, lift_ref, choose_ref, mask_ref,
    first_before_dom, first_after_dom, first_before_sub, first_after_sub,
    second_before_dom, second_after_dom, second_before_sub, second_after_sub,
    result_out, rows_ref,
):
    fields = base_ref.shape[0]
    modes = result_out.shape[2]
    pairs = rows_ref.shape[0]
    elements = 2 * ROWS
    sends = (rows_ref.shape[1] - elements) // 4
    fast = sends // 2
    rows_by_pair(late_ref[...].reshape(fields * ROWS, LANES), rows_ref, fields)
    firsts = (first_before_dom, first_after_dom, first_before_sub, first_after_sub)
    seconds = (second_before_dom, second_after_dom, second_before_sub, second_after_sub)
    for side, (first, second) in enumerate(zip(firsts, seconds)):
        at = elements + side * sends
        for pair in range(pairs):
            rows_ref[pair, at : at + fast, :] = second[pair * fast : (pair + 1) * fast, :]
            row = pairs * sends + pair * fast
            rows_ref[pair, at + fast : at + sends, :] = first[row : row + fast, :]
    result = base_ref[...] + remote_terms(
        rows_ref, remote_ref, compose_ref, lift_ref, choose_ref, mask_ref, fields
    )
    result_out[:, 0:ROWS, :] = result[:, :, 0:modes]
    result_out[:, ROWS : 2 * ROWS, :] = result[:, :, HALF : HALF + modes]


VMEM = pl.BlockSpec(memory_space=pltpu.VMEM)
SMEM = pl.BlockSpec(memory_space=pltpu.SMEM)


def call(kernel, ins, outs, scratch, args, name, flops):
    shapes = [jax.ShapeDtypeStruct(shape, dtype) for shape, dtype in outs]
    return pl.pallas_call(
        kernel,
        out_shape=shapes,
        in_specs=ins,
        out_specs=[VMEM] * len(outs),
        scratch_shapes=[pltpu.VMEM(shape, dtype) for shape, dtype in scratch],
        compiler_params=pltpu.CompilerParams(vmem_limit_bytes=16 * 1024 * 1024),
        cost_estimate=pl.CostEstimate(flops=flops, bytes_accessed=4_000_000, transcendentals=0),
        name=name,
    )(*args)


def exchange(to_before_dom, to_after_dom, to_before_sub, to_after_sub):
    arrived = []
    for axis, to_before, to_after in (("dom", to_before_dom, to_after_dom), ("sub", to_before_sub, to_after_sub)):
        size = lax.axis_size(axis)
        up = [(i, (i + 1) % size) for i in range(size)]
        down = [(j, i) for i, j in up]
        arrived.append(lax.ppermute(to_after, axis, up))
        arrived.append(lax.ppermute(to_before, axis, down))
    return arrived


def up_to(count, multiple):
    return -(-count // multiple) * multiple


def local(
    solution, stiffness, star_matrices, face_restrict, face_lift, orient_maps, flux_local, flux_remote,
    cluster_rate, send_list, neighbour_slot, neighbour_face, neighbour_turn,
):
    fields, elements = solution.shape[1], solution.shape[2]
    kinds = stiffness.shape[0]
    faces = face_restrict.shape[0]
    sides, sends = send_list.shape[1], send_list.shape[2]
    fast = sends // 2
    pairs = (fields + 1) // 2
    assert elements == 2 * ROWS and solution.shape[0] <= HALF
    values = jnp.transpose(solution, (1, 2, 0))
    star = jnp.transpose(star_matrices, (1, 2, 0, 3))
    local_part = jnp.transpose(flux_local, (1, 2, 0, 3))
    remote_part = jnp.transpose(flux_remote, (1, 2, 0, 3))
    restrict = jnp.transpose(face_restrict, (1, 0, 2))
    lift = jnp.transpose(face_lift, (2, 0, 1))

    packed = (fields, ROWS, LANES)
    first_shape = (up_to(pairs * (sends + fast), ROWS), LANES)
    second_shape = (up_to(pairs * fast, ROWS), LANES)
    work = (pairs, LANES, LANES)
    star_shape = (fields * fields * kinds, ROWS, LANES)
    combos = faces * HALF
    sources = elements + sides * sends

    early, late, *outgoing = call(
        predict_kernel,
        [VMEM, VMEM, VMEM, SMEM],
        [(packed, F32)] * 2 + [(first_shape, F32)] * sides,
        [
            (packed, F32), (work, F32), (star_shape, F32), ((kinds, LANES, LANES), F32),
            ((3 * LANES, kinds * LANES), BF16), ((pairs, elements, LANES), F32), ((pairs, elements, LANES), F32),
        ],
        (values, stiffness, star, send_list),
        "predict", 100_000_000,
    )
    first = exchange(*outgoing)
    (
        base, star_coef, local_coef, remote_coef, derive_op, volume_op, trace_op, local_lift, compose_op, remote_lift,
        choose, mask,
    ) = call(
        prepare_kernel,
        [VMEM] * 12,
        [
            (packed, F32), (star_shape, F32), ((fields * fields, 2, ROWS, LANES), F32),
            ((faces * pairs * fields, elements, LANES), F32),
            ((3 * LANES, kinds * LANES), BF16), ((3 * LANES, kinds * LANES), BF16), ((3 * LANES, 2 * LANES), BF16),
            ((6 * LANES, LANES), BF16), ((3 * LANES, combos), BF16), ((faces, 2, HALF, LANES), BF16),
            ((faces * elements, 2 * sources), BF16), ((faces * elements, combos), F32),
        ],
        [
            (packed, F32), (work, F32), ((kinds, LANES, LANES), F32), ((2 * LANES, LANES), F32),
            ((LANES, faces * LANES), F32), ((HALF, LANES), F32), ((LANES, LANES), F32),
        ],
        (
            values, early, stiffness, star, restrict, lift, orient_maps, local_part, remote_part,
            neighbour_slot, neighbour_face, neighbour_turn,
        ),
        "prepare", 200_000_000,
    )
    middle, late_value, *outgoing = call(
        middle_kernel,
        [VMEM] * 10 + [SMEM] * 2 + [VMEM] * 4,
        [(packed, F32)] * 2 + [(second_shape, F32)] * sides,
        [((pairs, sources, LANES), F32), ((pairs, elements, LANES), F32)],
        (
            base, early, late, star_coef, remote_coef, derive_op, compose_op, remote_lift, choose, mask,
            cluster_rate, send_list, *first,
        ),
        "middle", 200_000_000,
    )
    second = exchange(*outgoing)
    (base,) = call(
        local_kernel,
        [VMEM] * 7,
        [(packed, F32)],
        [],
        (middle, late_value, star_coef, local_coef, volume_op, trace_op, local_lift),
        "local_late", 200_000_000,
    )
    (result,) = call(
        final_kernel,
        [VMEM] * 15,
        [(values.shape, F32)],
        [((pairs, sources, LANES), F32)],
        (base, late_value, remote_coef, compose_op, remote_lift, choose, mask, *first, *second),
        "final", 200_000_000,
    )
    return jnp.transpose(result, (2, 0, 1))


def solution(mesh):
    placed = (
        P(None, None, ("dom", "sub")),
        P(),
        P(None, None, None, ("dom", "sub")),
        P(),
        P(),
        P(),
        P(None, None, None, ("dom", "sub")),
        P(None, None, None, ("dom", "sub")),
        P(("dom", "sub")),
        P(("dom", "sub"), None, None),
        P(None, ("dom", "sub")),
        P(None, ("dom", "sub")),
        P(None, ("dom", "sub")),
    )
    return jax.shard_map(
        local, mesh=mesh, in_specs=placed, out_specs=P(None, None, ("dom", "sub")), check_vma=False
    )
```

```python
import math

import jax
import jax.numpy as jnp
from jax import lax
from jax.experimental import pallas as pl
from jax.experimental.pallas import tpu as pltpu
from jax.sharding import PartitionSpec as P

DERIVS = 6
LANES = 128
HALF = 64
ROWS = 8
F32 = jnp.float32
BF16 = jnp.bfloat16
LATER = ("flux_local", "flux_remote", "face_restrict", "face_lift", "orient_maps", "slot", "face", "turn")


def taylor_weight(lower, upper, degree):
    return (upper ** (degree + 1) - lower ** (degree + 1)) / math.factorial(degree + 1)


def weight_at(lower, upper, degree):
    result = jnp.float32(taylor_weight(lower, upper, 1))
    for option in range(2, DERIVS):
        result = jnp.where(degree == option, jnp.float32(taylor_weight(lower, upper, option)), result)
    return result


def split(values):
    high = values.astype(BF16)
    low = (values - high.astype(F32)).astype(BF16)
    return high, low


def stack_left(values):
    high, low = split(values)
    return jnp.concatenate([high, low, high], axis=1)


def stack_right(values):
    high, low = split(values)
    return jnp.concatenate([high, high, low], axis=0)


def product(left, right):
    return jnp.dot(left, right, preferred_element_type=F32)


def lane_index(shape):
    return lax.broadcasted_iota(jnp.int32, shape, len(shape) - 1)


def lower_half(shape):
    return lane_index(shape) < HALF


def swap_halves(values):
    return pltpu.roll(values, HALF, values.ndim - 1)


def pack(values_ref, packed_ref):
    modes = values_ref.shape[2]
    packed_ref[...] = jnp.zeros(packed_ref.shape, F32)
    packed_ref[:, :, 0:modes] = values_ref[:, 0:ROWS, :]
    packed_ref[:, :, HALF : HALF + modes] = values_ref[:, ROWS : 2 * ROWS, :]


def turn_matrices(source_ref, work_ref):
    fields, kinds, elements = source_ref.shape[0], source_ref.shape[2], source_ref.shape[3]
    tiles = []
    for pair in range((fields + 1) // 2):
        for row in range(2 * pair, min(2 * pair + 2, fields)):
            for col in range(fields):
                at = (row % 2) * HALF + col * 4
                work_ref[pair, at : at + kinds, 0:elements] = source_ref[row, col]
        tiles.append(work_ref[pair].T[0:elements, :])
    return tiles


def spread(tile, index):
    return jnp.take_along_axis(tile, index, axis=1, mode="promise_in_bounds")


def star_coefficients(star_ref, work_ref, star_out):
    fields, kinds = star_ref.shape[0], star_ref.shape[2]
    tiles = turn_matrices(star_ref, work_ref)
    lanes = lane_index((ROWS, LANES))
    base = (lanes // HALF) * HALF
    lower = lanes < HALF
    for row in range(fields):
        first, second = tiles[row // 2][0:ROWS], tiles[row // 2][ROWS : 2 * ROWS]
        if row % 2 == 0:
            both = jnp.where(lower, first, swap_halves(second))
        else:
            both = jnp.where(lower, swap_halves(first), second)
        for kind in range(kinds):
            for col in range(fields):
                star_out[(row * kinds + kind) * fields + col] = spread(both, base + (col * 4 + kind))


def star_mix(columns, star_ref, fields, kinds):
    sums = [None] * fields
    for row in range(fields):
        for kind in range(kinds):
            part = columns[row * ROWS : (row + 1) * ROWS, kind * LANES : (kind + 1) * LANES]
            for col in range(fields):
                term = star_ref[(row * kinds + kind) * fields + col] * part
                sums[col] = term if sums[col] is None else sums[col] + term
    return jnp.concatenate(sums, axis=0)


def stiffness_blocks(stiffness_ref, block_ref):
    kinds, modes = stiffness_ref.shape[0], stiffness_ref.shape[1]
    block_ref[...] = jnp.zeros(block_ref.shape, F32)
    for kind in range(kinds):
        block_ref[kind, 0:modes, 0:modes] = stiffness_ref[kind]
        block_ref[kind, HALF : HALF + modes, HALF : HALF + modes] = stiffness_ref[kind]


def derive_operator(block_ref):
    return jnp.concatenate([-block_ref[kind].T for kind in range(block_ref.shape[0])], axis=1)


def predict_kernel(*refs):
    later = len(LATER)
    solution_hbm, stiffness_hbm, star_hbm, send_hbm = refs[0:4]
    later_hbm, refs = refs[4 : 4 + later], refs[4 + later :]
    early_out, late_out, to_before_dom, to_after_dom, to_before_sub, to_after_sub = refs[0:6]
    packed_ref, coef_ref, derive_ref, block_ref = refs[6:10]
    later_out, refs = refs[10 : 10 + later], refs[10 + later :]
    work_ref, early_rows, late_rows, solution_ref, stiffness_ref, star_ref, send_ref, sems = refs

    sources = (stiffness_hbm, star_hbm, solution_hbm, send_hbm, *later_hbm)
    targets = (stiffness_ref, star_ref, solution_ref, send_ref, *later_out)
    copies = [
        pltpu.make_async_copy(source, target, sems.at[number])
        for number, (source, target) in enumerate(zip(sources, targets))
    ]
    for copy in copies:
        copy.start()
    fields, kinds = star_ref.shape[0], star_ref.shape[2]
    pairs = (fields + 1) // 2
    copies[0].wait()
    stiffness_blocks(stiffness_ref, block_ref)
    derive_ref[...] = stack_right(derive_operator(block_ref))
    copies[1].wait()
    star_coefficients(star_ref, work_ref, coef_ref)
    copies[2].wait()
    pack(solution_ref, packed_ref)
    start = packed_ref[...].reshape(fields * ROWS, LANES)

    def step(degree, carry):
        current, early, late = carry
        current = star_mix(product(stack_left(current), derive_ref[...]), coef_ref, fields, kinds)
        early = early + weight_at(0.0, 0.5, degree) * current
        late = late + weight_at(0.5, 1.0, degree) * current
        return current, early, late

    _, early, late = lax.fori_loop(
        1, DERIVS, step, (start, taylor_weight(0.0, 0.5, 0) * start, taylor_weight(0.5, 1.0, 0) * start)
    )
    early_out[...] = early.reshape(fields, ROWS, LANES)
    late_out[...] = late.reshape(fields, ROWS, LANES)
    rows_by_pair(early, early_rows, fields)
    rows_by_pair(late, late_rows, fields)
    copies[3].wait()
    sends = send_ref.shape[2]
    fast = sends // 2
    for side, out in enumerate((to_before_dom, to_after_dom, to_before_sub, to_after_sub)):
        out[...] = jnp.zeros(out.shape, F32)
        for place in range(sends):
            element = send_ref[0, side, place]
            for pair in range(pairs):
                row = pair * sends + place
                out[row : row + 1, :] = early_rows[pair, pl.ds(element, 1), :]
            if place >= fast:
                for pair in range(pairs):
                    row = pairs * sends + pair * fast + place - fast
                    out[row : row + 1, :] = late_rows[pair, pl.ds(element, 1), :]
    for copy in copies[4:]:
        copy.wait()


def rows_by_pair(packed, out_ref, fields):
    lower = lower_half((ROWS, LANES))
    for pair in range((fields + 1) // 2):
        even = packed[2 * pair * ROWS : (2 * pair + 1) * ROWS]
        odd = jnp.zeros_like(even)
        if 2 * pair + 1 < fields:
            odd = packed[(2 * pair + 1) * ROWS : (2 * pair + 2) * ROWS]
        out_ref[pair, 0:ROWS, :] = jnp.where(lower, even, swap_halves(odd))
        out_ref[pair, ROWS : 2 * ROWS, :] = jnp.where(lower, swap_halves(even), odd)


def flux_local_coefficients(flux_ref, work_ref, out_ref):
    fields = flux_ref.shape[0]
    tiles = turn_matrices(flux_ref, work_ref)
    lanes = lane_index((ROWS, LANES))
    for row in range(fields):
        for col in range(fields):
            index = (row % 2) * HALF + col * 4 + lanes % 4
            for half in range(2):
                tile = tiles[row // 2][half * ROWS : (half + 1) * ROWS]
                out_ref[row * fields + col, half] = spread(tile, index)


def flux_remote_coefficients(flux_ref, work_ref, out_ref):
    fields, faces = flux_ref.shape[0], flux_ref.shape[2]
    pairs = (fields + 1) // 2
    tiles = turn_matrices(flux_ref, work_ref)
    lanes = lane_index((ROWS, LANES))
    base = (lanes // HALF) * HALF
    for pair in range(pairs):
        for face in range(faces):
            for col in range(fields):
                at = (face * pairs + pair) * fields + col
                for half in range(2):
                    tile = tiles[pair][half * ROWS : (half + 1) * ROWS]
                    out_ref[at, half * ROWS : (half + 1) * ROWS, :] = spread(tile, base + (col * 4 + face))


def local_terms(packed, star_ref, flux_ref, volume_ref, trace_ref, lift_ref, fields, kinds):
    left = stack_left(packed)
    volume = star_mix(product(left, volume_ref[...]), star_ref, fields, kinds)
    traces = product(left, trace_ref[...])
    sums = []
    for col in range(fields):
        halves = []
        for half in range(2):
            total = None
            for row in range(fields):
                part = traces[row * ROWS : (row + 1) * ROWS, half * LANES : (half + 1) * LANES]
                term = flux_ref[row * fields + col, half] * part
                total = term if total is None else total + term
            halves.append(total)
        sums.append(jnp.concatenate(halves, axis=1))
    return volume + product(stack_left(jnp.concatenate(sums, axis=0)), lift_ref[...])


def prepare_kernel(
    packed_ref, early_ref, block_ref, star_ref, flux_local_ref, flux_remote_ref, restrict_ref, lift_ref, orient_ref,
    slot_ref, face_ref, turn_ref,
    base_out, local_out, remote_out, volume_out, trace_out, local_lift_out, compose_out,
    remote_lift_out, choose_out, mask_out,
    work_ref, wide_ref, face_work_ref, orient_work_ref, code_ref,
):
    fields, kinds = packed_ref.shape[0], block_ref.shape[0]
    face_modes, faces, modes = restrict_ref.shape
    turns = orient_ref.shape[0]
    work_ref[...] = jnp.zeros(work_ref.shape, F32)
    flux_local_coefficients(flux_local_ref, work_ref, local_out)
    flux_remote_coefficients(flux_remote_ref, work_ref, remote_out)

    volume_out[...] = stack_right(jnp.concatenate([block_ref[kind] for kind in range(kinds)], axis=1))

    wide_ref[...] = jnp.zeros(wide_ref.shape, F32)
    for mode in range(face_modes):
        at = mode * faces
        wide_ref[at : at + faces, 0:modes] = restrict_ref[mode]
        wide_ref[LANES + at : LANES + at + faces, HALF : HALF + modes] = restrict_ref[mode]
    trace_out[...] = stack_right(wide_ref[...].T)
    for mode in range(face_modes):
        at = mode * faces
        wide_ref[at : at + faces, 0:modes] = -lift_ref[mode]
        wide_ref[LANES + at : LANES + at + faces, HALF : HALF + modes] = -lift_ref[mode]
    local_lift_out[...] = stack_right(wide_ref[...])

    face_work_ref[...] = jnp.zeros(face_work_ref.shape, F32)
    orient_work_ref[...] = jnp.zeros(orient_work_ref.shape, F32)
    for turn in range(turns):
        orient_work_ref[turn * face_modes : (turn + 1) * face_modes, 0:face_modes] = orient_ref[turn]
    for face in range(faces):
        face_work_ref[0:face_modes, face * LANES : face * LANES + modes] = restrict_ref[:, face, :]
        face_work_ref[0:face_modes, face * LANES + HALF : face * LANES + HALF + modes] = restrict_ref[:, face, :]
    composed = jnp.dot(
        orient_work_ref[...], face_work_ref[...], precision=lax.Precision.HIGHEST, preferred_element_type=F32
    )
    stacked = jnp.concatenate([composed[:, face * LANES : (face + 1) * LANES] for face in range(faces)], axis=0)
    compose_out[...] = stack_right(stacked.T)
    for face in range(faces):
        orient_work_ref[...] = jnp.zeros(orient_work_ref.shape, F32)
        for turn in range(turns):
            rows = slice(turn * face_modes, (turn + 1) * face_modes)
            orient_work_ref[rows, 0:modes] = -lift_ref[:, face, :]
            orient_work_ref[rows, HALF : HALF + modes] = -lift_ref[:, face, :]
        high, low = split(orient_work_ref[...])
        remote_lift_out[face, 0] = high
        remote_lift_out[face, 1] = low

    elements = slot_ref.shape[1]
    code_ref[...] = jnp.zeros(code_ref.shape, F32)
    code_ref[0:faces, 0:elements] = slot_ref[...].astype(F32)
    code_ref[faces : 2 * faces, 0:elements] = (face_ref[...] * turns + turn_ref[...]).astype(F32)
    codes = code_ref[...].T[0:elements, :]
    sources = choose_out.shape[1] // 2
    source_lane = (lane_index((elements, 2 * sources)) % sources).astype(F32)
    lanes = lane_index((elements, mask_out.shape[1]))
    in_face = lanes % HALF
    lane_code = jnp.where(in_face < turns * face_modes, (lanes // HALF) * turns + in_face // face_modes, -1)
    lane_code = lane_code.astype(F32)
    picks, masks = [], []
    for face in range(faces):
        picks.append(jnp.where(codes[:, face : face + 1] == source_lane, 1.0, 0.0))
        masks.append(jnp.where(codes[:, faces + face : faces + face + 1] == lane_code, 1.0, 0.0))
    choose_out[...] = jnp.concatenate(picks, axis=0).astype(BF16)
    mask_out[...] = jnp.concatenate(masks, axis=0)

    early = early_ref[...].reshape(fields * ROWS, LANES)
    terms = local_terms(early, star_ref, local_out, volume_out, trace_out, local_lift_out, fields, kinds)
    base_out[...] = packed_ref[...] + terms.reshape(fields, ROWS, LANES)


def remote_terms(rows_ref, remote_ref, compose_ref, lift_ref, choose_ref, mask_ref, fields):
    pairs = rows_ref.shape[0]
    faces = lift_ref.shape[0]
    elements = choose_ref.shape[0] // faces
    sources = jnp.concatenate([rows_ref[pair] for pair in range(pairs)], axis=1)
    gathered = product(choose_ref[...], jnp.concatenate(split(sources), axis=0))
    result = None
    for face in range(faces):
        sums = []
        for col in range(fields):
            total = None
            for pair in range(pairs):
                part = gathered[face * elements : (face + 1) * elements, pair * LANES : (pair + 1) * LANES]
                term = remote_ref[(face * pairs + pair) * fields + col] * part
                total = term if total is None else total + term
            sums.append(total)
        turned = product(stack_left(jnp.concatenate(sums, axis=0)), compose_ref[...])
        mask = mask_ref[face * elements : (face + 1) * elements, :]
        chosen = turned.reshape(fields, elements, turned.shape[1]) * mask[None]
        left = stack_left(chosen.reshape(turned.shape))
        copies = turned.shape[1] // lift_ref.shape[2]
        high, low = lift_ref[face, 0], lift_ref[face, 1]
        right = jnp.concatenate([high] * (2 * copies) + [low] * copies, axis=0)
        lifted = product(left, right)
        result = lifted if result is None else result + lifted
    result = result.reshape(fields, 2, ROWS, LANES)
    return jnp.where(lower_half((ROWS, LANES))[None], result[:, 0], result[:, 1])


def middle_kernel(
    base_ref, early_ref, late_ref, star_ref, remote_ref, derive_ref, compose_ref, lift_ref, choose_ref, mask_ref,
    rate_hbm, send_hbm, from_before_dom, from_after_dom, from_before_sub, from_after_sub,
    middle_out, late_out, to_before_dom, to_after_dom, to_before_sub, to_after_sub,
    rows_ref, late_rows, rate_ref, send_ref, sems,
):
    copies = [
        pltpu.make_async_copy(rate_hbm, rate_ref, sems.at[0]),
        pltpu.make_async_copy(send_hbm, send_ref, sems.at[1]),
    ]
    for copy in copies:
        copy.start()
    fields = base_ref.shape[0]
    kinds = star_ref.shape[0] // (fields * fields)
    pairs = rows_ref.shape[0]
    sends = send_ref.shape[2]
    fast = sends // 2
    elements = 2 * ROWS
    rows_by_pair(early_ref[...].reshape(fields * ROWS, LANES), rows_ref, fields)
    for side, arrived in enumerate((from_before_dom, from_after_dom, from_before_sub, from_after_sub)):
        at = elements + side * sends
        for pair in range(pairs):
            rows_ref[pair, at : at + sends, :] = arrived[pair * sends : (pair + 1) * sends, :]
    middle = base_ref[...] + remote_terms(
        rows_ref, remote_ref, compose_ref, lift_ref, choose_ref, mask_ref, fields
    )
    middle_out[...] = middle
    start = middle.reshape(fields * ROWS, LANES)

    def step(degree, carry):
        current, early = carry
        current = star_mix(product(stack_left(current), derive_ref[...]), star_ref, fields, kinds)
        return current, early + weight_at(0.0, 0.5, degree) * current

    _, restart = lax.fori_loop(1, DERIVS, step, (start, taylor_weight(0.0, 0.5, 0) * start))
    for copy in copies:
        copy.wait()
    sublane = lax.broadcasted_iota(jnp.int32, (ROWS, LANES), 0)
    lower = lower_half((ROWS, LANES))
    is_fast = jnp.zeros((ROWS, LANES), jnp.int32)
    for element in range(elements):
        here = (sublane == element % ROWS) & (lower if element < ROWS else jnp.logical_not(lower))
        is_fast = jnp.where(here, rate_ref[element], is_fast)
    late = jnp.where((is_fast == 2)[None], restart.reshape(fields, ROWS, LANES), late_ref[...])
    late_out[...] = late
    rows_by_pair(late.reshape(fields * ROWS, LANES), late_rows, fields)
    for side, out in enumerate((to_before_dom, to_after_dom, to_before_sub, to_after_sub)):
        out[...] = jnp.zeros(out.shape, F32)
        for place in range(fast):
            element = send_ref[0, side, place]
            for pair in range(pairs):
                row = pair * fast + place
                out[row : row + 1, :] = late_rows[pair, pl.ds(element, 1), :]


def local_kernel(middle_ref, late_ref, star_ref, flux_ref, volume_ref, trace_ref, lift_ref, base_out):
    fields = middle_ref.shape[0]
    kinds = star_ref.shape[0] // (fields * fields)
    late = late_ref[...].reshape(fields * ROWS, LANES)
    terms = local_terms(late, star_ref, flux_ref, volume_ref, trace_ref, lift_ref, fields, kinds)
    base_out[...] = middle_ref[...] + terms.reshape(fields, ROWS, LANES)


def final_kernel(
    base_ref, late_ref, remote_ref, compose_ref, lift_ref, choose_ref, mask_ref,
    first_before_dom, first_after_dom, first_before_sub, first_after_sub,
    second_before_dom, second_after_dom, second_before_sub, second_after_sub,
    result_out, rows_ref,
):
    fields = base_ref.shape[0]
    modes = result_out.shape[2]
    pairs = rows_ref.shape[0]
    elements = 2 * ROWS
    sends = (rows_ref.shape[1] - elements) // 4
    fast = sends // 2
    rows_by_pair(late_ref[...].reshape(fields * ROWS, LANES), rows_ref, fields)
    firsts = (first_before_dom, first_after_dom, first_before_sub, first_after_sub)
    seconds = (second_before_dom, second_after_dom, second_before_sub, second_after_sub)
    for side, (first, second) in enumerate(zip(firsts, seconds)):
        at = elements + side * sends
        for pair in range(pairs):
            rows_ref[pair, at : at + fast, :] = second[pair * fast : (pair + 1) * fast, :]
            row = pairs * sends + pair * fast
            rows_ref[pair, at + fast : at + sends, :] = first[row : row + fast, :]
    result = base_ref[...] + remote_terms(
        rows_ref, remote_ref, compose_ref, lift_ref, choose_ref, mask_ref, fields
    )
    result_out[:, 0:ROWS, :] = result[:, :, 0:modes]
    result_out[:, ROWS : 2 * ROWS, :] = result[:, :, HALF : HALF + modes]


VMEM = pl.BlockSpec(memory_space=pltpu.VMEM)
HBM = pl.BlockSpec(memory_space=pltpu.HBM)


def call(kernel, ins, outs, scratch, args, name, flops):
    shapes = [jax.ShapeDtypeStruct(shape, dtype) for shape, dtype in outs]
    args = [
        pltpu.with_memory_space_constraint(arg, pltpu.HBM) if spec is HBM else arg for spec, arg in zip(ins, args)
    ]
    return pl.pallas_call(
        kernel,
        out_shape=shapes,
        in_specs=ins,
        out_specs=[VMEM] * len(outs),
        scratch_shapes=[pltpu.VMEM(*one) if isinstance(one, tuple) else one for one in scratch],
        compiler_params=pltpu.CompilerParams(vmem_limit_bytes=16 * 1024 * 1024),
        cost_estimate=pl.CostEstimate(flops=flops, bytes_accessed=4_000_000, transcendentals=0),
        name=name,
    )(*args)


def exchange(to_before_dom, to_after_dom, to_before_sub, to_after_sub):
    arrived = []
    for axis, to_before, to_after in (("dom", to_before_dom, to_after_dom), ("sub", to_before_sub, to_after_sub)):
        size = lax.axis_size(axis)
        up = [(i, (i + 1) % size) for i in range(size)]
        down = [(j, i) for i, j in up]
        arrived.append(lax.ppermute(to_after, axis, up))
        arrived.append(lax.ppermute(to_before, axis, down))
    return arrived


def up_to(count, multiple):
    return -(-count // multiple) * multiple


def local(
    solution, stiffness, star_matrices, face_restrict, face_lift, orient_maps, flux_local, flux_remote,
    cluster_rate, send_list, neighbour_slot, neighbour_face, neighbour_turn,
):
    fields, elements = solution.shape[1], solution.shape[2]
    kinds = stiffness.shape[0]
    faces = face_restrict.shape[0]
    sides, sends = send_list.shape[1], send_list.shape[2]
    fast = sends // 2
    pairs = (fields + 1) // 2
    assert elements == 2 * ROWS and solution.shape[0] <= HALF
    values = jnp.transpose(solution, (1, 2, 0))
    star = jnp.transpose(star_matrices, (1, 2, 0, 3))
    local_part = jnp.transpose(flux_local, (1, 2, 0, 3))
    remote_part = jnp.transpose(flux_remote, (1, 2, 0, 3))
    restrict = jnp.transpose(face_restrict, (1, 0, 2))
    lift = jnp.transpose(face_lift, (2, 0, 1))

    packed = (fields, ROWS, LANES)
    first_shape = (up_to(pairs * (sends + fast), ROWS), LANES)
    second_shape = (up_to(pairs * fast, ROWS), LANES)
    work = (pairs, LANES, LANES)
    star_shape = (fields * fields * kinds, ROWS, LANES)
    combos = faces * HALF
    sources = elements + sides * sends

    waiting = (local_part, remote_part, restrict, lift, orient_maps, neighbour_slot, neighbour_face, neighbour_turn)
    made = call(
        predict_kernel,
        [HBM] * (4 + len(LATER)),
        [(packed, F32)] * 2 + [(first_shape, F32)] * sides + [
            (packed, F32), (star_shape, F32), ((3 * LANES, kinds * LANES), BF16), ((kinds, LANES, LANES), F32),
        ] + [(array.shape, array.dtype) for array in waiting],
        [
            (work, F32), ((pairs, elements, LANES), F32), ((pairs, elements, LANES), F32),
            (values.shape, F32), (stiffness.shape, F32), (star.shape, F32),
            pltpu.SMEM(send_list.shape, jnp.int32), pltpu.SemaphoreType.DMA((4 + len(LATER),)),
        ],
        (values, stiffness, star, send_list, *waiting),
        "predict", 100_000_000,
    )
    early, late, outgoing = made[0], made[1], made[2 : 2 + sides]
    start, star_coef, derive_op, blocks = made[2 + sides : 6 + sides]
    waiting = made[6 + sides :]
    first = exchange(*outgoing)
    (
        base, local_coef, remote_coef, volume_op, trace_op, local_lift, compose_op, remote_lift, choose, mask,
    ) = call(
        prepare_kernel,
        [VMEM] * 12,
        [
            (packed, F32), ((fields * fields, 2, ROWS, LANES), F32),
            ((faces * pairs * fields, elements, LANES), F32),
            ((3 * LANES, kinds * LANES), BF16), ((3 * LANES, 2 * LANES), BF16),
            ((6 * LANES, LANES), BF16), ((3 * LANES, combos), BF16), ((faces, 2, HALF, LANES), BF16),
            ((faces * elements, 2 * sources), BF16), ((faces * elements, combos), F32),
        ],
        [
            (work, F32), ((2 * LANES, LANES), F32),
            ((LANES, faces * LANES), F32), ((HALF, LANES), F32), ((LANES, LANES), F32),
        ],
        (start, early, blocks, star_coef, *waiting),
        "prepare", 200_000_000,
    )
    middle, late_value, *outgoing = call(
        middle_kernel,
        [VMEM] * 10 + [HBM] * 2 + [VMEM] * 4,
        [(packed, F32)] * 2 + [(second_shape, F32)] * sides,
        [
            ((pairs, sources, LANES), F32), ((pairs, elements, LANES), F32),
            pltpu.SMEM(cluster_rate.shape, jnp.int32), pltpu.SMEM(send_list.shape, jnp.int32),
            pltpu.SemaphoreType.DMA((2,)),
        ],
        (
            base, early, late, star_coef, remote_coef, derive_op, compose_op, remote_lift, choose, mask,
            cluster_rate, send_list, *first,
        ),
        "middle", 200_000_000,
    )
    second = exchange(*outgoing)
    (base,) = call(
        local_kernel,
        [VMEM] * 7,
        [(packed, F32)],
        [],
        (middle, late_value, star_coef, local_coef, volume_op, trace_op, local_lift),
        "local_late", 200_000_000,
    )
    (result,) = call(
        final_kernel,
        [VMEM] * 15,
        [(values.shape, F32)],
        [((pairs, sources, LANES), F32)],
        (base, late_value, remote_coef, compose_op, remote_lift, choose, mask, *first, *second),
        "final", 200_000_000,
    )
    return jnp.transpose(result, (2, 0, 1))


def solution(mesh):
    placed = (
        P(None, None, ("dom", "sub")),
        P(),
        P(None, None, None, ("dom", "sub")),
        P(),
        P(),
        P(),
        P(None, None, None, ("dom", "sub")),
        P(None, None, None, ("dom", "sub")),
        P(("dom", "sub")),
        P(("dom", "sub"), None, None),
        P(None, ("dom", "sub")),
        P(None, ("dom", "sub")),
        P(None, ("dom", "sub")),
    )
    return jax.shard_map(
        local, mesh=mesh, in_specs=placed, out_specs=P(None, None, ("dom", "sub")), check_vma=False
    )
```

```python
import math

import jax
import jax.numpy as jnp
from jax import lax
from jax.experimental import pallas as pl
from jax.experimental.pallas import tpu as pltpu
from jax.sharding import PartitionSpec as P

DERIVS = 6
LANES = 128
HALF = 64
ROWS = 8
F32 = jnp.float32
BF16 = jnp.bfloat16
LATER = ("flux_local", "flux_remote", "face_restrict", "face_lift", "orient_maps", "slot", "face", "turn")


def taylor_weight(lower, upper, degree):
    return (upper ** (degree + 1) - lower ** (degree + 1)) / math.factorial(degree + 1)


def weight_at(lower, upper, degree):
    result = jnp.float32(taylor_weight(lower, upper, 1))
    for option in range(2, DERIVS):
        result = jnp.where(degree == option, jnp.float32(taylor_weight(lower, upper, option)), result)
    return result


def split(values):
    high = values.astype(BF16)
    low = (values - high.astype(F32)).astype(BF16)
    return high, low


def stack_left(values):
    high, low = split(values)
    return jnp.concatenate([high, low, high], axis=1)


def stack_right(values):
    high, low = split(values)
    return jnp.concatenate([high, high, low], axis=0)


def product(left, right):
    return jnp.dot(left, right, preferred_element_type=F32)


def odd_place(axis):
    return lax.rem(lax.axis_index(axis), 2)


def message_side(slot):
    odd = odd_place("dom" if slot < 2 else "sub")
    return slot + odd if slot % 2 == 0 else slot - odd


def lane_index(shape):
    return lax.broadcasted_iota(jnp.int32, shape, len(shape) - 1)


def lower_half(shape):
    return lane_index(shape) < HALF


def swap_halves(values):
    return pltpu.roll(values, HALF, values.ndim - 1)


def pack(values_ref, packed_ref):
    modes = values_ref.shape[2]
    packed_ref[...] = jnp.zeros(packed_ref.shape, F32)
    packed_ref[:, :, 0:modes] = values_ref[:, 0:ROWS, :]
    packed_ref[:, :, HALF : HALF + modes] = values_ref[:, ROWS : 2 * ROWS, :]


def turn_matrices(source_ref, work_ref):
    fields, kinds, elements = source_ref.shape[0], source_ref.shape[2], source_ref.shape[3]
    tiles = []
    for pair in range((fields + 1) // 2):
        for row in range(2 * pair, min(2 * pair + 2, fields)):
            for col in range(fields):
                at = (row % 2) * HALF + col * 4
                work_ref[pair, at : at + kinds, 0:elements] = source_ref[row, col]
        tiles.append(work_ref[pair].T[0:elements, :])
    return tiles


def spread(tile, index):
    return jnp.take_along_axis(tile, index, axis=1, mode="promise_in_bounds")


def star_coefficients(star_ref, work_ref, star_out):
    fields, kinds = star_ref.shape[0], star_ref.shape[2]
    tiles = turn_matrices(star_ref, work_ref)
    lanes = lane_index((ROWS, LANES))
    base = (lanes // HALF) * HALF
    lower = lanes < HALF
    for row in range(fields):
        first, second = tiles[row // 2][0:ROWS], tiles[row // 2][ROWS : 2 * ROWS]
        if row % 2 == 0:
            both = jnp.where(lower, first, swap_halves(second))
        else:
            both = jnp.where(lower, swap_halves(first), second)
        for kind in range(kinds):
            for col in range(fields):
                star_out[(row * kinds + kind) * fields + col] = spread(both, base + (col * 4 + kind))


def star_mix(columns, star_ref, fields, kinds):
    sums = [None] * fields
    for row in range(fields):
        for kind in range(kinds):
            part = columns[row * ROWS : (row + 1) * ROWS, kind * LANES : (kind + 1) * LANES]
            for col in range(fields):
                term = star_ref[(row * kinds + kind) * fields + col] * part
                sums[col] = term if sums[col] is None else sums[col] + term
    return jnp.concatenate(sums, axis=0)


def stiffness_blocks(stiffness_ref, block_ref):
    kinds, modes = stiffness_ref.shape[0], stiffness_ref.shape[1]
    block_ref[...] = jnp.zeros(block_ref.shape, F32)
    for kind in range(kinds):
        block_ref[kind, 0:modes, 0:modes] = stiffness_ref[kind]
        block_ref[kind, HALF : HALF + modes, HALF : HALF + modes] = stiffness_ref[kind]


def derive_operator(block_ref):
    return jnp.concatenate([-block_ref[kind].T for kind in range(block_ref.shape[0])], axis=1)


def predict_kernel(*refs):
    later = len(LATER)
    solution_hbm, stiffness_hbm, star_hbm, send_hbm = refs[0:4]
    later_hbm, refs = refs[4 : 4 + later], refs[4 + later :]
    early_out, late_out, far_dom_out, near_dom_out, far_sub_out, near_sub_out = refs[0:6]
    packed_ref, coef_ref, derive_ref, block_ref = refs[6:10]
    later_out, refs = refs[10 : 10 + later], refs[10 + later :]
    work_ref, early_rows, late_rows, solution_ref, stiffness_ref, star_ref, send_ref, sems = refs

    sources = (stiffness_hbm, star_hbm, solution_hbm, send_hbm, *later_hbm)
    targets = (stiffness_ref, star_ref, solution_ref, send_ref, *later_out)
    copies = [
        pltpu.make_async_copy(source, target, sems.at[number])
        for number, (source, target) in enumerate(zip(sources, targets))
    ]
    for copy in copies:
        copy.start()
    fields, kinds = star_ref.shape[0], star_ref.shape[2]
    pairs = (fields + 1) // 2
    copies[0].wait()
    stiffness_blocks(stiffness_ref, block_ref)
    derive_ref[...] = stack_right(derive_operator(block_ref))
    copies[1].wait()
    star_coefficients(star_ref, work_ref, coef_ref)
    copies[2].wait()
    pack(solution_ref, packed_ref)
    start = packed_ref[...].reshape(fields * ROWS, LANES)

    def step(degree, carry):
        current, early, late = carry
        current = star_mix(product(stack_left(current), derive_ref[...]), coef_ref, fields, kinds)
        early = early + weight_at(0.0, 0.5, degree) * current
        late = late + weight_at(0.5, 1.0, degree) * current
        return current, early, late

    _, early, late = lax.fori_loop(
        1, DERIVS, step, (start, taylor_weight(0.0, 0.5, 0) * start, taylor_weight(0.5, 1.0, 0) * start)
    )
    early_out[...] = early.reshape(fields, ROWS, LANES)
    late_out[...] = late.reshape(fields, ROWS, LANES)
    rows_by_pair(early, early_rows, fields)
    rows_by_pair(late, late_rows, fields)
    copies[3].wait()
    sends = send_ref.shape[2]
    fast = sends // 2
    for side, out in enumerate((far_dom_out, near_dom_out, far_sub_out, near_sub_out)):
        out[...] = jnp.zeros(out.shape, F32)
        for place in range(sends):
            element = send_ref[0, message_side(side), place]
            for pair in range(pairs):
                row = pair * sends + place
                out[row : row + 1, :] = early_rows[pair, pl.ds(element, 1), :]
            if place >= fast:
                for pair in range(pairs):
                    row = pairs * sends + pair * fast + place - fast
                    out[row : row + 1, :] = late_rows[pair, pl.ds(element, 1), :]
    for copy in copies[4:]:
        copy.wait()


def rows_by_pair(packed, out_ref, fields):
    lower = lower_half((ROWS, LANES))
    for pair in range((fields + 1) // 2):
        even = packed[2 * pair * ROWS : (2 * pair + 1) * ROWS]
        odd = jnp.zeros_like(even)
        if 2 * pair + 1 < fields:
            odd = packed[(2 * pair + 1) * ROWS : (2 * pair + 2) * ROWS]
        out_ref[pair, 0:ROWS, :] = jnp.where(lower, even, swap_halves(odd))
        out_ref[pair, ROWS : 2 * ROWS, :] = jnp.where(lower, swap_halves(even), odd)


def flux_local_coefficients(flux_ref, work_ref, out_ref):
    fields = flux_ref.shape[0]
    tiles = turn_matrices(flux_ref, work_ref)
    lanes = lane_index((ROWS, LANES))
    for row in range(fields):
        for col in range(fields):
            index = (row % 2) * HALF + col * 4 + lanes % 4
            for half in range(2):
                tile = tiles[row // 2][half * ROWS : (half + 1) * ROWS]
                out_ref[row * fields + col, half] = spread(tile, index)


def flux_remote_coefficients(flux_ref, work_ref, out_ref):
    fields, faces = flux_ref.shape[0], flux_ref.shape[2]
    pairs = (fields + 1) // 2
    tiles = turn_matrices(flux_ref, work_ref)
    lanes = lane_index((ROWS, LANES))
    base = (lanes // HALF) * HALF
    for pair in range(pairs):
        for face in range(faces):
            for col in range(fields):
                at = (face * pairs + pair) * fields + col
                for half in range(2):
                    tile = tiles[pair][half * ROWS : (half + 1) * ROWS]
                    out_ref[at, half * ROWS : (half + 1) * ROWS, :] = spread(tile, base + (col * 4 + face))


def local_terms(packed, star_ref, flux_ref, volume_ref, trace_ref, lift_ref, fields, kinds):
    left = stack_left(packed)
    volume = star_mix(product(left, volume_ref[...]), star_ref, fields, kinds)
    traces = product(left, trace_ref[...])
    sums = []
    for col in range(fields):
        halves = []
        for half in range(2):
            total = None
            for row in range(fields):
                part = traces[row * ROWS : (row + 1) * ROWS, half * LANES : (half + 1) * LANES]
                term = flux_ref[row * fields + col, half] * part
                total = term if total is None else total + term
            halves.append(total)
        sums.append(jnp.concatenate(halves, axis=1))
    return volume + product(stack_left(jnp.concatenate(sums, axis=0)), lift_ref[...])


def prepare_kernel(
    packed_ref, early_ref, block_ref, star_ref, flux_local_ref, flux_remote_ref, restrict_ref, lift_ref, orient_ref,
    slot_ref, face_ref, turn_ref,
    base_out, local_out, remote_out, volume_out, trace_out, local_lift_out, compose_out,
    remote_lift_out, choose_out, mask_out,
    work_ref, wide_ref, face_work_ref, orient_work_ref, code_ref,
):
    fields, kinds = packed_ref.shape[0], block_ref.shape[0]
    face_modes, faces, modes = restrict_ref.shape
    turns = orient_ref.shape[0]
    work_ref[...] = jnp.zeros(work_ref.shape, F32)
    flux_local_coefficients(flux_local_ref, work_ref, local_out)
    flux_remote_coefficients(flux_remote_ref, work_ref, remote_out)

    volume_out[...] = stack_right(jnp.concatenate([block_ref[kind] for kind in range(kinds)], axis=1))

    wide_ref[...] = jnp.zeros(wide_ref.shape, F32)
    for mode in range(face_modes):
        at = mode * faces
        wide_ref[at : at + faces, 0:modes] = restrict_ref[mode]
        wide_ref[LANES + at : LANES + at + faces, HALF : HALF + modes] = restrict_ref[mode]
    trace_out[...] = stack_right(wide_ref[...].T)
    for mode in range(face_modes):
        at = mode * faces
        wide_ref[at : at + faces, 0:modes] = -lift_ref[mode]
        wide_ref[LANES + at : LANES + at + faces, HALF : HALF + modes] = -lift_ref[mode]
    local_lift_out[...] = stack_right(wide_ref[...])

    face_work_ref[...] = jnp.zeros(face_work_ref.shape, F32)
    orient_work_ref[...] = jnp.zeros(orient_work_ref.shape, F32)
    for turn in range(turns):
        orient_work_ref[turn * face_modes : (turn + 1) * face_modes, 0:face_modes] = orient_ref[turn]
    for face in range(faces):
        face_work_ref[0:face_modes, face * LANES : face * LANES + modes] = restrict_ref[:, face, :]
        face_work_ref[0:face_modes, face * LANES + HALF : face * LANES + HALF + modes] = restrict_ref[:, face, :]
    composed = jnp.dot(
        orient_work_ref[...], face_work_ref[...], precision=lax.Precision.HIGHEST, preferred_element_type=F32
    )
    stacked = jnp.concatenate([composed[:, face * LANES : (face + 1) * LANES] for face in range(faces)], axis=0)
    compose_out[...] = stack_right(stacked.T)
    for face in range(faces):
        orient_work_ref[...] = jnp.zeros(orient_work_ref.shape, F32)
        for turn in range(turns):
            rows = slice(turn * face_modes, (turn + 1) * face_modes)
            orient_work_ref[rows, 0:modes] = -lift_ref[:, face, :]
            orient_work_ref[rows, HALF : HALF + modes] = -lift_ref[:, face, :]
        high, low = split(orient_work_ref[...])
        remote_lift_out[face, 0] = high
        remote_lift_out[face, 1] = low

    elements = slot_ref.shape[1]
    code_ref[...] = jnp.zeros(code_ref.shape, F32)
    slots = slot_ref[...]
    sends = (choose_out.shape[1] // 2 - elements) // 4
    group = (slots - elements) // sends
    odd = jnp.where(group < 2, odd_place("dom"), odd_place("sub"))
    moved = slots + jnp.where(group % 2 == 0, sends, -sends) * odd
    code_ref[0:faces, 0:elements] = jnp.where(slots < elements, slots, moved).astype(F32)
    code_ref[faces : 2 * faces, 0:elements] = (face_ref[...] * turns + turn_ref[...]).astype(F32)
    codes = code_ref[...].T[0:elements, :]
    sources = choose_out.shape[1] // 2
    source_lane = (lane_index((elements, 2 * sources)) % sources).astype(F32)
    lanes = lane_index((elements, mask_out.shape[1]))
    in_face = lanes % HALF
    lane_code = jnp.where(in_face < turns * face_modes, (lanes // HALF) * turns + in_face // face_modes, -1)
    lane_code = lane_code.astype(F32)
    picks, masks = [], []
    for face in range(faces):
        picks.append(jnp.where(codes[:, face : face + 1] == source_lane, 1.0, 0.0))
        masks.append(jnp.where(codes[:, faces + face : faces + face + 1] == lane_code, 1.0, 0.0))
    choose_out[...] = jnp.concatenate(picks, axis=0).astype(BF16)
    mask_out[...] = jnp.concatenate(masks, axis=0)

    early = early_ref[...].reshape(fields * ROWS, LANES)
    terms = local_terms(early, star_ref, local_out, volume_out, trace_out, local_lift_out, fields, kinds)
    base_out[...] = packed_ref[...] + terms.reshape(fields, ROWS, LANES)


def remote_terms(rows_ref, remote_ref, compose_ref, lift_ref, choose_ref, mask_ref, fields):
    pairs = rows_ref.shape[0]
    faces = lift_ref.shape[0]
    elements = choose_ref.shape[0] // faces
    sources = jnp.concatenate([rows_ref[pair] for pair in range(pairs)], axis=1)
    gathered = product(choose_ref[...], jnp.concatenate(split(sources), axis=0))
    result = None
    for face in range(faces):
        sums = []
        for col in range(fields):
            total = None
            for pair in range(pairs):
                part = gathered[face * elements : (face + 1) * elements, pair * LANES : (pair + 1) * LANES]
                term = remote_ref[(face * pairs + pair) * fields + col] * part
                total = term if total is None else total + term
            sums.append(total)
        turned = product(stack_left(jnp.concatenate(sums, axis=0)), compose_ref[...])
        mask = mask_ref[face * elements : (face + 1) * elements, :]
        chosen = turned.reshape(fields, elements, turned.shape[1]) * mask[None]
        left = stack_left(chosen.reshape(turned.shape))
        copies = turned.shape[1] // lift_ref.shape[2]
        high, low = lift_ref[face, 0], lift_ref[face, 1]
        right = jnp.concatenate([high] * (2 * copies) + [low] * copies, axis=0)
        lifted = product(left, right)
        result = lifted if result is None else result + lifted
    result = result.reshape(fields, 2, ROWS, LANES)
    return jnp.where(lower_half((ROWS, LANES))[None], result[:, 0], result[:, 1])


def middle_kernel(
    base_ref, early_ref, late_ref, star_ref, remote_ref, derive_ref, compose_ref, lift_ref, choose_ref, mask_ref,
    rate_hbm, send_hbm, far_dom, near_dom, far_sub, near_sub,
    middle_out, late_out, far_dom_out, near_dom_out, far_sub_out, near_sub_out,
    rows_ref, late_rows, rate_ref, send_ref, sems,
):
    copies = [
        pltpu.make_async_copy(rate_hbm, rate_ref, sems.at[0]),
        pltpu.make_async_copy(send_hbm, send_ref, sems.at[1]),
    ]
    for copy in copies:
        copy.start()
    fields = base_ref.shape[0]
    kinds = star_ref.shape[0] // (fields * fields)
    pairs = rows_ref.shape[0]
    sends = send_ref.shape[2]
    fast = sends // 2
    elements = 2 * ROWS
    rows_by_pair(early_ref[...].reshape(fields * ROWS, LANES), rows_ref, fields)
    for side, arrived in enumerate((far_dom, near_dom, far_sub, near_sub)):
        at = elements + side * sends
        for pair in range(pairs):
            rows_ref[pair, at : at + sends, :] = arrived[pair * sends : (pair + 1) * sends, :]
    middle = base_ref[...] + remote_terms(
        rows_ref, remote_ref, compose_ref, lift_ref, choose_ref, mask_ref, fields
    )
    middle_out[...] = middle
    start = middle.reshape(fields * ROWS, LANES)

    def step(degree, carry):
        current, early = carry
        current = star_mix(product(stack_left(current), derive_ref[...]), star_ref, fields, kinds)
        return current, early + weight_at(0.0, 0.5, degree) * current

    _, restart = lax.fori_loop(1, DERIVS, step, (start, taylor_weight(0.0, 0.5, 0) * start))
    for copy in copies:
        copy.wait()
    sublane = lax.broadcasted_iota(jnp.int32, (ROWS, LANES), 0)
    lower = lower_half((ROWS, LANES))
    is_fast = jnp.zeros((ROWS, LANES), jnp.int32)
    for element in range(elements):
        here = (sublane == element % ROWS) & (lower if element < ROWS else jnp.logical_not(lower))
        is_fast = jnp.where(here, rate_ref[element], is_fast)
    late = jnp.where((is_fast == 2)[None], restart.reshape(fields, ROWS, LANES), late_ref[...])
    late_out[...] = late
    rows_by_pair(late.reshape(fields * ROWS, LANES), late_rows, fields)
    for side, out in enumerate((far_dom_out, near_dom_out, far_sub_out, near_sub_out)):
        out[...] = jnp.zeros(out.shape, F32)
        for place in range(fast):
            element = send_ref[0, message_side(side), place]
            for pair in range(pairs):
                row = pair * fast + place
                out[row : row + 1, :] = late_rows[pair, pl.ds(element, 1), :]


def local_kernel(middle_ref, late_ref, star_ref, flux_ref, volume_ref, trace_ref, lift_ref, base_out):
    fields = middle_ref.shape[0]
    kinds = star_ref.shape[0] // (fields * fields)
    late = late_ref[...].reshape(fields * ROWS, LANES)
    terms = local_terms(late, star_ref, flux_ref, volume_ref, trace_ref, lift_ref, fields, kinds)
    base_out[...] = middle_ref[...] + terms.reshape(fields, ROWS, LANES)


def final_kernel(
    base_ref, late_ref, remote_ref, compose_ref, lift_ref, choose_ref, mask_ref,
    first_far_dom, first_near_dom, first_far_sub, first_near_sub,
    second_far_dom, second_near_dom, second_far_sub, second_near_sub,
    result_out, rows_ref,
):
    fields = base_ref.shape[0]
    modes = result_out.shape[2]
    pairs = rows_ref.shape[0]
    elements = 2 * ROWS
    sends = (rows_ref.shape[1] - elements) // 4
    fast = sends // 2
    rows_by_pair(late_ref[...].reshape(fields * ROWS, LANES), rows_ref, fields)
    firsts = (first_far_dom, first_near_dom, first_far_sub, first_near_sub)
    seconds = (second_far_dom, second_near_dom, second_far_sub, second_near_sub)
    for side, (first, second) in enumerate(zip(firsts, seconds)):
        at = elements + side * sends
        for pair in range(pairs):
            rows_ref[pair, at : at + fast, :] = second[pair * fast : (pair + 1) * fast, :]
            row = pairs * sends + pair * fast
            rows_ref[pair, at + fast : at + sends, :] = first[row : row + fast, :]
    result = base_ref[...] + remote_terms(
        rows_ref, remote_ref, compose_ref, lift_ref, choose_ref, mask_ref, fields
    )
    result_out[:, 0:ROWS, :] = result[:, :, 0:modes]
    result_out[:, ROWS : 2 * ROWS, :] = result[:, :, HALF : HALF + modes]


VMEM = pl.BlockSpec(memory_space=pltpu.VMEM)
HBM = pl.BlockSpec(memory_space=pltpu.HBM)


def call(kernel, ins, outs, scratch, args, name, flops):
    shapes = [jax.ShapeDtypeStruct(shape, dtype) for shape, dtype in outs]
    args = [
        pltpu.with_memory_space_constraint(arg, pltpu.HBM) if spec is HBM else arg for spec, arg in zip(ins, args)
    ]
    return pl.pallas_call(
        kernel,
        out_shape=shapes,
        in_specs=ins,
        out_specs=[VMEM] * len(outs),
        scratch_shapes=[pltpu.VMEM(*one) if isinstance(one, tuple) else one for one in scratch],
        compiler_params=pltpu.CompilerParams(vmem_limit_bytes=16 * 1024 * 1024),
        cost_estimate=pl.CostEstimate(flops=flops, bytes_accessed=4_000_000, transcendentals=0),
        name=name,
    )(*args)


def exchange(outgoing):
    arrived = [None] * 4
    for slot, axis, first in ((0, "dom", 1), (2, "sub", 1), (1, "dom", 0), (3, "sub", 0)):
        size = lax.axis_size(axis)
        assert size % 2 == 0
        pairs = []
        for even in range(first, size, 2):
            odd = (even + 1) % size
            pairs += [(even, odd), (odd, even)]
        arrived[slot] = lax.ppermute(outgoing[slot], axis, pairs)
    return arrived


def up_to(count, multiple):
    return -(-count // multiple) * multiple


def local(
    solution, stiffness, star_matrices, face_restrict, face_lift, orient_maps, flux_local, flux_remote,
    cluster_rate, send_list, neighbour_slot, neighbour_face, neighbour_turn,
):
    fields, elements = solution.shape[1], solution.shape[2]
    kinds = stiffness.shape[0]
    faces = face_restrict.shape[0]
    sides, sends = send_list.shape[1], send_list.shape[2]
    fast = sends // 2
    pairs = (fields + 1) // 2
    assert elements == 2 * ROWS and solution.shape[0] <= HALF
    values = jnp.transpose(solution, (1, 2, 0))
    star = jnp.transpose(star_matrices, (1, 2, 0, 3))
    local_part = jnp.transpose(flux_local, (1, 2, 0, 3))
    remote_part = jnp.transpose(flux_remote, (1, 2, 0, 3))
    restrict = jnp.transpose(face_restrict, (1, 0, 2))
    lift = jnp.transpose(face_lift, (2, 0, 1))

    packed = (fields, ROWS, LANES)
    first_shape = (up_to(pairs * (sends + fast), ROWS), LANES)
    second_shape = (up_to(pairs * fast, ROWS), LANES)
    work = (pairs, LANES, LANES)
    star_shape = (fields * fields * kinds, ROWS, LANES)
    combos = faces * HALF
    sources = elements + sides * sends

    waiting = (local_part, remote_part, restrict, lift, orient_maps, neighbour_slot, neighbour_face, neighbour_turn)
    made = call(
        predict_kernel,
        [HBM] * (4 + len(LATER)),
        [(packed, F32)] * 2 + [(first_shape, F32)] * sides + [
            (packed, F32), (star_shape, F32), ((3 * LANES, kinds * LANES), BF16), ((kinds, LANES, LANES), F32),
        ] + [(array.shape, array.dtype) for array in waiting],
        [
            (work, F32), ((pairs, elements, LANES), F32), ((pairs, elements, LANES), F32),
            (values.shape, F32), (stiffness.shape, F32), (star.shape, F32),
            pltpu.SMEM(send_list.shape, jnp.int32), pltpu.SemaphoreType.DMA((4 + len(LATER),)),
        ],
        (values, stiffness, star, send_list, *waiting),
        "predict", 100_000_000,
    )
    early, late, outgoing = made[0], made[1], made[2 : 2 + sides]
    start, star_coef, derive_op, blocks = made[2 + sides : 6 + sides]
    waiting = made[6 + sides :]
    first = exchange(outgoing)
    (
        base, local_coef, remote_coef, volume_op, trace_op, local_lift, compose_op, remote_lift, choose, mask,
    ) = call(
        prepare_kernel,
        [VMEM] * 12,
        [
            (packed, F32), ((fields * fields, 2, ROWS, LANES), F32),
            ((faces * pairs * fields, elements, LANES), F32),
            ((3 * LANES, kinds * LANES), BF16), ((3 * LANES, 2 * LANES), BF16),
            ((6 * LANES, LANES), BF16), ((3 * LANES, combos), BF16), ((faces, 2, HALF, LANES), BF16),
            ((faces * elements, 2 * sources), BF16), ((faces * elements, combos), F32),
        ],
        [
            (work, F32), ((2 * LANES, LANES), F32),
            ((LANES, faces * LANES), F32), ((HALF, LANES), F32), ((LANES, LANES), F32),
        ],
        (start, early, blocks, star_coef, *waiting),
        "prepare", 200_000_000,
    )
    middle, late_value, *outgoing = call(
        middle_kernel,
        [VMEM] * 10 + [HBM] * 2 + [VMEM] * 4,
        [(packed, F32)] * 2 + [(second_shape, F32)] * sides,
        [
            ((pairs, sources, LANES), F32), ((pairs, elements, LANES), F32),
            pltpu.SMEM(cluster_rate.shape, jnp.int32), pltpu.SMEM(send_list.shape, jnp.int32),
            pltpu.SemaphoreType.DMA((2,)),
        ],
        (
            base, early, late, star_coef, remote_coef, derive_op, compose_op, remote_lift, choose, mask,
            cluster_rate, send_list, *first,
        ),
        "middle", 200_000_000,
    )
    second = exchange(outgoing)
    (base,) = call(
        local_kernel,
        [VMEM] * 7,
        [(packed, F32)],
        [],
        (middle, late_value, star_coef, local_coef, volume_op, trace_op, local_lift),
        "local_late", 200_000_000,
    )
    (result,) = call(
        final_kernel,
        [VMEM] * 15,
        [(values.shape, F32)],
        [((pairs, sources, LANES), F32)],
        (base, late_value, remote_coef, compose_op, remote_lift, choose, mask, *first, *second),
        "final", 200_000_000,
    )
    return jnp.transpose(result, (2, 0, 1))


def solution(mesh):
    placed = (
        P(None, None, ("dom", "sub")),
        P(),
        P(None, None, None, ("dom", "sub")),
        P(),
        P(),
        P(),
        P(None, None, None, ("dom", "sub")),
        P(None, None, None, ("dom", "sub")),
        P(("dom", "sub")),
        P(("dom", "sub"), None, None),
        P(None, ("dom", "sub")),
        P(None, ("dom", "sub")),
        P(None, ("dom", "sub")),
    )
    return jax.shard_map(
        local, mesh=mesh, in_specs=placed, out_specs=P(None, None, ("dom", "sub")), check_vma=False
    )
```

```python
import math

import jax
import jax.numpy as jnp
from jax import lax
from jax.experimental import pallas as pl
from jax.experimental.pallas import tpu as pltpu
from jax.sharding import PartitionSpec as P

DERIVS = 6
LANES = 128
HALF = 64
ROWS = 8
F32 = jnp.float32
BF16 = jnp.bfloat16
LATER = ("flux_local", "flux_remote", "face_restrict", "face_lift", "orient_maps", "slot", "face", "turn")


def taylor_weight(lower, upper, degree):
    return (upper ** (degree + 1) - lower ** (degree + 1)) / math.factorial(degree + 1)


def weight_at(lower, upper, degree):
    result = jnp.float32(taylor_weight(lower, upper, 1))
    for option in range(2, DERIVS):
        result = jnp.where(degree == option, jnp.float32(taylor_weight(lower, upper, option)), result)
    return result


def split(values):
    high = values.astype(BF16)
    low = (values - high.astype(F32)).astype(BF16)
    return high, low


def stack_left(values):
    high, low = split(values)
    return jnp.concatenate([high, low, high], axis=1)


def stack_right(values):
    high, low = split(values)
    return jnp.concatenate([high, high, low], axis=0)


def product(left, right):
    return jnp.dot(left, right, preferred_element_type=F32)


def odd_place(axis):
    return lax.rem(lax.axis_index(axis), 2)


def message_side(slot):
    odd = odd_place("dom" if slot < 2 else "sub")
    return slot + odd if slot % 2 == 0 else slot - odd


def lane_index(shape):
    return lax.broadcasted_iota(jnp.int32, shape, len(shape) - 1)


def lower_half(shape):
    return lane_index(shape) < HALF


def swap_halves(values):
    return pltpu.roll(values, HALF, values.ndim - 1)


def pack(values_ref, packed_ref):
    modes = values_ref.shape[2]
    packed_ref[...] = jnp.zeros(packed_ref.shape, F32)
    packed_ref[:, :, 0:modes] = values_ref[:, 0:ROWS, :]
    packed_ref[:, :, HALF : HALF + modes] = values_ref[:, ROWS : 2 * ROWS, :]


def turn_matrices(source_ref, work_ref):
    fields, kinds, elements = source_ref.shape[0], source_ref.shape[2], source_ref.shape[3]
    tiles = []
    for pair in range((fields + 1) // 2):
        for row in range(2 * pair, min(2 * pair + 2, fields)):
            for col in range(fields):
                at = (row % 2) * HALF + col * 4
                work_ref[pair, at : at + kinds, 0:elements] = source_ref[row, col]
        tiles.append(work_ref[pair].T[0:elements, :])
    return tiles


def spread(tile, index):
    return jnp.take_along_axis(tile, index, axis=1, mode="promise_in_bounds")


def star_coefficients(star_ref, stage_ref, star_out):
    fields, kinds, elements = star_ref.shape[0], star_ref.shape[2], star_ref.shape[3]
    lanes = lane_index((ROWS, LANES))
    sublanes = lax.broadcasted_iota(jnp.int32, (ROWS, LANES), 0)
    pick = jnp.where((lanes % ROWS == sublanes) & (lanes < 2 * elements), 1.0, 0.0)
    to_lane = lane_index((LANES, LANES))
    from_lane = lax.broadcasted_iota(jnp.int32, (LANES, LANES), 0)
    same_half = (from_lane % elements) // ROWS == to_lane // HALF
    right = jnp.where(same_half & (from_lane < 2 * elements), 1.0, 0.0).astype(BF16)
    filled = lane_index(stage_ref.shape[1:]) < elements
    for row in range(fields):
        for col in range(fields):
            stage_ref[row, col * 4 : col * 4 + kinds, 0:elements] = star_ref[row, col]
        values = jnp.where(filled, stage_ref[row], 0.0)
        high = values.astype(BF16).astype(F32)
        stage_ref[row] = high + pltpu.roll(values - high, elements, 1)
        spreads = []
        for kind in range(kinds):
            for col in range(fields):
                at = col * 4 + kind
                spreads.append(stage_ref[row, at : at + 1, :] * pick)
        spread_out = product(jnp.concatenate(spreads, axis=0).astype(BF16), right)
        count = kinds * fields
        star_out[row * count : (row + 1) * count] = spread_out.reshape(count, ROWS, LANES)


def star_mix(columns, star_ref, fields, kinds):
    sums = [None] * fields
    for row in range(fields):
        for kind in range(kinds):
            part = columns[row * ROWS : (row + 1) * ROWS, kind * LANES : (kind + 1) * LANES]
            for col in range(fields):
                term = star_ref[(row * kinds + kind) * fields + col] * part
                sums[col] = term if sums[col] is None else sums[col] + term
    return jnp.concatenate(sums, axis=0)


def stiffness_blocks(stiffness_ref, block_ref):
    kinds, modes = stiffness_ref.shape[0], stiffness_ref.shape[1]
    block_ref[...] = jnp.zeros(block_ref.shape, F32)
    for kind in range(kinds):
        block_ref[kind, 0:modes, 0:modes] = stiffness_ref[kind]
        block_ref[kind, HALF : HALF + modes, HALF : HALF + modes] = stiffness_ref[kind]


def derive_operator(block_ref):
    return jnp.concatenate([-block_ref[kind].T for kind in range(block_ref.shape[0])], axis=1)


def predict_kernel(*refs):
    later = len(LATER)
    solution_hbm, stiffness_hbm, star_hbm, send_hbm = refs[0:4]
    later_hbm, refs = refs[4 : 4 + later], refs[4 + later :]
    early_out, late_out, far_dom_out, near_dom_out, far_sub_out, near_sub_out = refs[0:6]
    packed_ref, coef_ref, derive_ref, block_ref = refs[6:10]
    later_out, refs = refs[10 : 10 + later], refs[10 + later :]
    work_ref, early_rows, late_rows, solution_ref, stiffness_ref, star_ref, send_ref, sems = refs

    sources = (stiffness_hbm, star_hbm, solution_hbm, send_hbm, *later_hbm)
    targets = (stiffness_ref, star_ref, solution_ref, send_ref, *later_out)
    copies = [
        pltpu.make_async_copy(source, target, sems.at[number])
        for number, (source, target) in enumerate(zip(sources, targets))
    ]
    for copy in copies:
        copy.start()
    fields, kinds = star_ref.shape[0], star_ref.shape[2]
    pairs = (fields + 1) // 2
    copies[0].wait()
    stiffness_blocks(stiffness_ref, block_ref)
    derive_ref[...] = stack_right(derive_operator(block_ref))
    copies[1].wait()
    star_coefficients(star_ref, work_ref, coef_ref)
    copies[2].wait()
    pack(solution_ref, packed_ref)
    start = packed_ref[...].reshape(fields * ROWS, LANES)

    def step(degree, carry):
        current, early, late = carry
        current = star_mix(product(stack_left(current), derive_ref[...]), coef_ref, fields, kinds)
        early = early + weight_at(0.0, 0.5, degree) * current
        late = late + weight_at(0.5, 1.0, degree) * current
        return current, early, late

    _, early, late = lax.fori_loop(
        1, DERIVS, step, (start, taylor_weight(0.0, 0.5, 0) * start, taylor_weight(0.5, 1.0, 0) * start)
    )
    early_out[...] = early.reshape(fields, ROWS, LANES)
    late_out[...] = late.reshape(fields, ROWS, LANES)
    rows_by_pair(early, early_rows, fields)
    rows_by_pair(late, late_rows, fields)
    copies[3].wait()
    sends = send_ref.shape[2]
    fast = sends // 2
    for side, out in enumerate((far_dom_out, near_dom_out, far_sub_out, near_sub_out)):
        out[...] = jnp.zeros(out.shape, F32)
        for place in range(sends):
            element = send_ref[0, message_side(side), place]
            for pair in range(pairs):
                row = pair * sends + place
                out[row : row + 1, :] = early_rows[pair, pl.ds(element, 1), :]
            if place >= fast:
                for pair in range(pairs):
                    row = pairs * sends + pair * fast + place - fast
                    out[row : row + 1, :] = late_rows[pair, pl.ds(element, 1), :]
    for copy in copies[4:]:
        copy.wait()


def rows_by_pair(packed, out_ref, fields):
    lower = lower_half((ROWS, LANES))
    for pair in range((fields + 1) // 2):
        even = packed[2 * pair * ROWS : (2 * pair + 1) * ROWS]
        odd = jnp.zeros_like(even)
        if 2 * pair + 1 < fields:
            odd = packed[(2 * pair + 1) * ROWS : (2 * pair + 2) * ROWS]
        out_ref[pair, 0:ROWS, :] = jnp.where(lower, even, swap_halves(odd))
        out_ref[pair, ROWS : 2 * ROWS, :] = jnp.where(lower, swap_halves(even), odd)


def flux_local_coefficients(flux_ref, work_ref, out_ref):
    fields = flux_ref.shape[0]
    tiles = turn_matrices(flux_ref, work_ref)
    lanes = lane_index((ROWS, LANES))
    for row in range(fields):
        for col in range(fields):
            index = (row % 2) * HALF + col * 4 + lanes % 4
            for half in range(2):
                tile = tiles[row // 2][half * ROWS : (half + 1) * ROWS]
                out_ref[row * fields + col, half] = spread(tile, index)


def flux_remote_coefficients(flux_ref, work_ref, out_ref):
    fields, faces = flux_ref.shape[0], flux_ref.shape[2]
    pairs = (fields + 1) // 2
    tiles = turn_matrices(flux_ref, work_ref)
    lanes = lane_index((ROWS, LANES))
    base = (lanes // HALF) * HALF
    for pair in range(pairs):
        for face in range(faces):
            for col in range(fields):
                at = (face * pairs + pair) * fields + col
                for half in range(2):
                    tile = tiles[pair][half * ROWS : (half + 1) * ROWS]
                    out_ref[at, half * ROWS : (half + 1) * ROWS, :] = spread(tile, base + (col * 4 + face))


def local_terms(packed, star_ref, flux_ref, volume_ref, trace_ref, lift_ref, fields, kinds):
    left = stack_left(packed)
    volume = star_mix(product(left, volume_ref[...]), star_ref, fields, kinds)
    traces = product(left, trace_ref[...])
    sums = []
    for col in range(fields):
        halves = []
        for half in range(2):
            total = None
            for row in range(fields):
                part = traces[row * ROWS : (row + 1) * ROWS, half * LANES : (half + 1) * LANES]
                term = flux_ref[row * fields + col, half] * part
                total = term if total is None else total + term
            halves.append(total)
        sums.append(jnp.concatenate(halves, axis=1))
    return volume + product(stack_left(jnp.concatenate(sums, axis=0)), lift_ref[...])


def prepare_kernel(
    packed_ref, early_ref, block_ref, star_ref, flux_local_ref, flux_remote_ref, restrict_ref, lift_ref, orient_ref,
    slot_ref, face_ref, turn_ref,
    base_out, local_out, remote_out, volume_out, trace_out, local_lift_out, compose_out,
    remote_lift_out, choose_out, mask_out,
    work_ref, wide_ref, face_work_ref, orient_work_ref, code_ref,
):
    fields, kinds = packed_ref.shape[0], block_ref.shape[0]
    face_modes, faces, modes = restrict_ref.shape
    turns = orient_ref.shape[0]
    work_ref[...] = jnp.zeros(work_ref.shape, F32)
    flux_local_coefficients(flux_local_ref, work_ref, local_out)
    flux_remote_coefficients(flux_remote_ref, work_ref, remote_out)

    volume_out[...] = stack_right(jnp.concatenate([block_ref[kind] for kind in range(kinds)], axis=1))

    wide_ref[...] = jnp.zeros(wide_ref.shape, F32)
    for mode in range(face_modes):
        at = mode * faces
        wide_ref[at : at + faces, 0:modes] = restrict_ref[mode]
        wide_ref[LANES + at : LANES + at + faces, HALF : HALF + modes] = restrict_ref[mode]
    trace_out[...] = stack_right(wide_ref[...].T)
    for mode in range(face_modes):
        at = mode * faces
        wide_ref[at : at + faces, 0:modes] = -lift_ref[mode]
        wide_ref[LANES + at : LANES + at + faces, HALF : HALF + modes] = -lift_ref[mode]
    local_lift_out[...] = stack_right(wide_ref[...])

    face_work_ref[...] = jnp.zeros(face_work_ref.shape, F32)
    orient_work_ref[...] = jnp.zeros(orient_work_ref.shape, F32)
    for turn in range(turns):
        orient_work_ref[turn * face_modes : (turn + 1) * face_modes, 0:face_modes] = orient_ref[turn]
    for face in range(faces):
        face_work_ref[0:face_modes, face * LANES : face * LANES + modes] = restrict_ref[:, face, :]
        face_work_ref[0:face_modes, face * LANES + HALF : face * LANES + HALF + modes] = restrict_ref[:, face, :]
    composed = jnp.dot(
        orient_work_ref[...], face_work_ref[...], precision=lax.Precision.HIGHEST, preferred_element_type=F32
    )
    stacked = jnp.concatenate([composed[:, face * LANES : (face + 1) * LANES] for face in range(faces)], axis=0)
    compose_out[...] = stack_right(stacked.T)
    wide_ref[...] = jnp.zeros(wide_ref.shape, F32)
    for face in range(faces):
        for turn in range(turns):
            rows = slice(face * HALF + turn * face_modes, face * HALF + (turn + 1) * face_modes)
            wide_ref[rows, 0:modes] = -lift_ref[:, face, :]
            wide_ref[rows, HALF : HALF + modes] = -lift_ref[:, face, :]
    remote_lift_out[...] = stack_right(wide_ref[...])

    elements = slot_ref.shape[1]
    code_ref[...] = jnp.zeros(code_ref.shape, F32)
    slots = slot_ref[...]
    sends = (choose_out.shape[1] // 2 - elements) // 4
    group = (slots - elements) // sends
    odd = jnp.where(group < 2, odd_place("dom"), odd_place("sub"))
    moved = slots + jnp.where(group % 2 == 0, sends, -sends) * odd
    code_ref[0:faces, 0:elements] = jnp.where(slots < elements, slots, moved).astype(F32)
    code_ref[faces : 2 * faces, 0:elements] = (face_ref[...] * turns + turn_ref[...]).astype(F32)
    codes = code_ref[...].T[0:elements, :]
    sources = choose_out.shape[1] // 2
    source_lane = (lane_index((elements, 2 * sources)) % sources).astype(F32)
    lanes = lane_index((elements, mask_out.shape[1]))
    in_face = lanes % HALF
    lane_code = jnp.where(in_face < turns * face_modes, (lanes // HALF) * turns + in_face // face_modes, -1)
    lane_code = lane_code.astype(F32)
    picks, masks = [], []
    for face in range(faces):
        picks.append(jnp.where(codes[:, face : face + 1] == source_lane, 1.0, 0.0))
        masks.append(jnp.where(codes[:, faces + face : faces + face + 1] == lane_code, 1.0, 0.0))
    choose_out[...] = jnp.concatenate(picks, axis=0).astype(BF16)
    mask_out[...] = jnp.concatenate(masks, axis=0)

    early = early_ref[...].reshape(fields * ROWS, LANES)
    terms = local_terms(early, star_ref, local_out, volume_out, trace_out, local_lift_out, fields, kinds)
    base_out[...] = packed_ref[...] + terms.reshape(fields, ROWS, LANES)


def remote_terms(rows_ref, remote_ref, compose_ref, lift_ref, choose_ref, mask_ref, fields):
    pairs = rows_ref.shape[0]
    faces = lift_ref.shape[0] // (3 * HALF)
    elements = choose_ref.shape[0] // faces
    sources = jnp.concatenate([rows_ref[pair] for pair in range(pairs)], axis=1)
    gathered = product(choose_ref[...], jnp.concatenate(split(sources), axis=0))
    folded = []
    for face in range(faces):
        sums = []
        for col in range(fields):
            total = None
            for pair in range(pairs):
                part = gathered[face * elements : (face + 1) * elements, pair * LANES : (pair + 1) * LANES]
                term = remote_ref[(face * pairs + pair) * fields + col] * part
                total = term if total is None else total + term
            sums.append(total)
        turned = product(stack_left(jnp.concatenate(sums, axis=0)), compose_ref[...])
        mask = mask_ref[face * elements : (face + 1) * elements, :]
        chosen = (turned.reshape(fields, elements, turned.shape[1]) * mask[None]).reshape(turned.shape)
        both = chosen[:, 0:LANES] + chosen[:, LANES : 2 * LANES]
        folded.append(both + swap_halves(both))
    lower = lower_half(folded[0].shape)
    left = [jnp.where(lower, folded[face], folded[face + 1]) for face in range(0, faces, 2)]
    result = product(stack_left(jnp.concatenate(left, axis=1)), lift_ref[...])
    result = result.reshape(fields, 2, ROWS, LANES)
    return jnp.where(lower_half((ROWS, LANES))[None], result[:, 0], result[:, 1])


def middle_kernel(
    base_ref, early_ref, late_ref, star_ref, remote_ref, derive_ref, compose_ref, lift_ref, choose_ref, mask_ref,
    rate_hbm, send_hbm, far_dom, near_dom, far_sub, near_sub,
    middle_out, late_out, far_dom_out, near_dom_out, far_sub_out, near_sub_out,
    rows_ref, late_rows, rate_ref, send_ref, sems,
):
    copies = [
        pltpu.make_async_copy(rate_hbm, rate_ref, sems.at[0]),
        pltpu.make_async_copy(send_hbm, send_ref, sems.at[1]),
    ]
    for copy in copies:
        copy.start()
    fields = base_ref.shape[0]
    kinds = star_ref.shape[0] // (fields * fields)
    pairs = rows_ref.shape[0]
    sends = send_ref.shape[2]
    fast = sends // 2
    elements = 2 * ROWS
    rows_by_pair(early_ref[...].reshape(fields * ROWS, LANES), rows_ref, fields)
    for side, arrived in enumerate((far_dom, near_dom, far_sub, near_sub)):
        at = elements + side * sends
        for pair in range(pairs):
            rows_ref[pair, at : at + sends, :] = arrived[pair * sends : (pair + 1) * sends, :]
    middle = base_ref[...] + remote_terms(
        rows_ref, remote_ref, compose_ref, lift_ref, choose_ref, mask_ref, fields
    )
    middle_out[...] = middle
    start = middle.reshape(fields * ROWS, LANES)

    def step(degree, carry):
        current, early = carry
        current = star_mix(product(stack_left(current), derive_ref[...]), star_ref, fields, kinds)
        return current, early + weight_at(0.0, 0.5, degree) * current

    _, restart = lax.fori_loop(1, DERIVS, step, (start, taylor_weight(0.0, 0.5, 0) * start))
    for copy in copies:
        copy.wait()
    sublane = lax.broadcasted_iota(jnp.int32, (ROWS, LANES), 0)
    lower = lower_half((ROWS, LANES))
    is_fast = jnp.zeros((ROWS, LANES), jnp.int32)
    for element in range(elements):
        here = (sublane == element % ROWS) & (lower if element < ROWS else jnp.logical_not(lower))
        is_fast = jnp.where(here, rate_ref[element], is_fast)
    late = jnp.where((is_fast == 2)[None], restart.reshape(fields, ROWS, LANES), late_ref[...])
    late_out[...] = late
    rows_by_pair(late.reshape(fields * ROWS, LANES), late_rows, fields)
    for side, out in enumerate((far_dom_out, near_dom_out, far_sub_out, near_sub_out)):
        out[...] = jnp.zeros(out.shape, F32)
        for place in range(fast):
            element = send_ref[0, message_side(side), place]
            for pair in range(pairs):
                row = pair * fast + place
                out[row : row + 1, :] = late_rows[pair, pl.ds(element, 1), :]


def local_kernel(middle_ref, late_ref, star_ref, flux_ref, volume_ref, trace_ref, lift_ref, base_out):
    fields = middle_ref.shape[0]
    kinds = star_ref.shape[0] // (fields * fields)
    late = late_ref[...].reshape(fields * ROWS, LANES)
    terms = local_terms(late, star_ref, flux_ref, volume_ref, trace_ref, lift_ref, fields, kinds)
    base_out[...] = middle_ref[...] + terms.reshape(fields, ROWS, LANES)


def final_kernel(
    base_ref, late_ref, remote_ref, compose_ref, lift_ref, choose_ref, mask_ref,
    first_far_dom, first_near_dom, first_far_sub, first_near_sub,
    second_far_dom, second_near_dom, second_far_sub, second_near_sub,
    result_out, rows_ref,
):
    fields = base_ref.shape[0]
    modes = result_out.shape[2]
    pairs = rows_ref.shape[0]
    elements = 2 * ROWS
    sends = (rows_ref.shape[1] - elements) // 4
    fast = sends // 2
    rows_by_pair(late_ref[...].reshape(fields * ROWS, LANES), rows_ref, fields)
    firsts = (first_far_dom, first_near_dom, first_far_sub, first_near_sub)
    seconds = (second_far_dom, second_near_dom, second_far_sub, second_near_sub)
    for side, (first, second) in enumerate(zip(firsts, seconds)):
        at = elements + side * sends
        for pair in range(pairs):
            rows_ref[pair, at : at + fast, :] = second[pair * fast : (pair + 1) * fast, :]
            row = pairs * sends + pair * fast
            rows_ref[pair, at + fast : at + sends, :] = first[row : row + fast, :]
    result = base_ref[...] + remote_terms(
        rows_ref, remote_ref, compose_ref, lift_ref, choose_ref, mask_ref, fields
    )
    result_out[:, 0:ROWS, :] = result[:, :, 0:modes]
    result_out[:, ROWS : 2 * ROWS, :] = result[:, :, HALF : HALF + modes]


VMEM = pl.BlockSpec(memory_space=pltpu.VMEM)
HBM = pl.BlockSpec(memory_space=pltpu.HBM)


def call(kernel, ins, outs, scratch, args, name, flops):
    shapes = [jax.ShapeDtypeStruct(shape, dtype) for shape, dtype in outs]
    args = [
        pltpu.with_memory_space_constraint(arg, pltpu.HBM) if spec is HBM else arg for spec, arg in zip(ins, args)
    ]
    return pl.pallas_call(
        kernel,
        out_shape=shapes,
        in_specs=ins,
        out_specs=[VMEM] * len(outs),
        scratch_shapes=[pltpu.VMEM(*one) if isinstance(one, tuple) else one for one in scratch],
        compiler_params=pltpu.CompilerParams(vmem_limit_bytes=16 * 1024 * 1024),
        cost_estimate=pl.CostEstimate(flops=flops, bytes_accessed=4_000_000, transcendentals=0),
        name=name,
    )(*args)


def exchange(outgoing):
    arrived = [None] * 4
    for slot, axis, first in ((0, "dom", 1), (2, "sub", 1), (1, "dom", 0), (3, "sub", 0)):
        size = lax.axis_size(axis)
        assert size % 2 == 0
        pairs = []
        for even in range(first, size, 2):
            odd = (even + 1) % size
            pairs += [(even, odd), (odd, even)]
        arrived[slot] = lax.ppermute(outgoing[slot], axis, pairs)
    return arrived


def up_to(count, multiple):
    return -(-count // multiple) * multiple


def local(
    solution, stiffness, star_matrices, face_restrict, face_lift, orient_maps, flux_local, flux_remote,
    cluster_rate, send_list, neighbour_slot, neighbour_face, neighbour_turn,
):
    fields, elements = solution.shape[1], solution.shape[2]
    kinds = stiffness.shape[0]
    faces = face_restrict.shape[0]
    sides, sends = send_list.shape[1], send_list.shape[2]
    fast = sends // 2
    pairs = (fields + 1) // 2
    assert elements == 2 * ROWS and solution.shape[0] <= HALF
    values = jnp.transpose(solution, (1, 2, 0))
    star = jnp.transpose(star_matrices, (1, 2, 0, 3))
    local_part = jnp.transpose(flux_local, (1, 2, 0, 3))
    remote_part = jnp.transpose(flux_remote, (1, 2, 0, 3))
    restrict = jnp.transpose(face_restrict, (1, 0, 2))
    lift = jnp.transpose(face_lift, (2, 0, 1))

    packed = (fields, ROWS, LANES)
    first_shape = (up_to(pairs * (sends + fast), ROWS), LANES)
    second_shape = (up_to(pairs * fast, ROWS), LANES)
    work = (pairs, LANES, LANES)
    star_shape = (fields * fields * kinds, ROWS, LANES)
    combos = faces * HALF
    sources = elements + sides * sends

    waiting = (local_part, remote_part, restrict, lift, orient_maps, neighbour_slot, neighbour_face, neighbour_turn)
    made = call(
        predict_kernel,
        [HBM] * (4 + len(LATER)),
        [(packed, F32)] * 2 + [(first_shape, F32)] * sides + [
            (packed, F32), (star_shape, F32), ((3 * LANES, kinds * LANES), BF16), ((kinds, LANES, LANES), F32),
        ] + [(array.shape, array.dtype) for array in waiting],
        [
            ((fields, up_to(4 * fields, ROWS), LANES), F32),
            ((pairs, elements, LANES), F32), ((pairs, elements, LANES), F32),
            (values.shape, F32), (stiffness.shape, F32), (star.shape, F32),
            pltpu.SMEM(send_list.shape, jnp.int32), pltpu.SemaphoreType.DMA((4 + len(LATER),)),
        ],
        (values, stiffness, star, send_list, *waiting),
        "predict", 100_000_000,
    )
    early, late, outgoing = made[0], made[1], made[2 : 2 + sides]
    start, star_coef, derive_op, blocks = made[2 + sides : 6 + sides]
    waiting = made[6 + sides :]
    first = exchange(outgoing)
    (
        base, local_coef, remote_coef, volume_op, trace_op, local_lift, compose_op, remote_lift, choose, mask,
    ) = call(
        prepare_kernel,
        [VMEM] * 12,
        [
            (packed, F32), ((fields * fields, 2, ROWS, LANES), F32),
            ((faces * pairs * fields, elements, LANES), F32),
            ((3 * LANES, kinds * LANES), BF16), ((3 * LANES, 2 * LANES), BF16),
            ((6 * LANES, LANES), BF16), ((3 * LANES, combos), BF16), ((3 * faces * HALF, LANES), BF16),
            ((faces * elements, 2 * sources), BF16), ((faces * elements, combos), F32),
        ],
        [
            (work, F32), ((2 * LANES, LANES), F32),
            ((LANES, faces * LANES), F32), ((HALF, LANES), F32), ((LANES, LANES), F32),
        ],
        (start, early, blocks, star_coef, *waiting),
        "prepare", 200_000_000,
    )
    middle, late_value, *outgoing = call(
        middle_kernel,
        [VMEM] * 10 + [HBM] * 2 + [VMEM] * 4,
        [(packed, F32)] * 2 + [(second_shape, F32)] * sides,
        [
            ((pairs, sources, LANES), F32), ((pairs, elements, LANES), F32),
            pltpu.SMEM(cluster_rate.shape, jnp.int32), pltpu.SMEM(send_list.shape, jnp.int32),
            pltpu.SemaphoreType.DMA((2,)),
        ],
        (
            base, early, late, star_coef, remote_coef, derive_op, compose_op, remote_lift, choose, mask,
            cluster_rate, send_list, *first,
        ),
        "middle", 200_000_000,
    )
    second = exchange(outgoing)
    (base,) = call(
        local_kernel,
        [VMEM] * 7,
        [(packed, F32)],
        [],
        (middle, late_value, star_coef, local_coef, volume_op, trace_op, local_lift),
        "local_late", 200_000_000,
    )
    (result,) = call(
        final_kernel,
        [VMEM] * 15,
        [(values.shape, F32)],
        [((pairs, sources, LANES), F32)],
        (base, late_value, remote_coef, compose_op, remote_lift, choose, mask, *first, *second),
        "final", 200_000_000,
    )
    return jnp.transpose(result, (2, 0, 1))


def solution(mesh):
    placed = (
        P(None, None, ("dom", "sub")),
        P(),
        P(None, None, None, ("dom", "sub")),
        P(),
        P(),
        P(),
        P(None, None, None, ("dom", "sub")),
        P(None, None, None, ("dom", "sub")),
        P(("dom", "sub")),
        P(("dom", "sub"), None, None),
        P(None, ("dom", "sub")),
        P(None, ("dom", "sub")),
        P(None, ("dom", "sub")),
    )
    return jax.shard_map(
        local, mesh=mesh, in_specs=placed, out_specs=P(None, None, ("dom", "sub")), check_vma=False
    )
```

```python
import math

import jax
import jax.numpy as jnp
from jax import lax
from jax.experimental import pallas as pl
from jax.experimental.pallas import tpu as pltpu
from jax.sharding import PartitionSpec as P

DERIVS = 6
LANES = 128
HALF = 64
ROWS = 8
F32 = jnp.float32
BF16 = jnp.bfloat16
LATER = ("flux_local", "flux_remote", "face_restrict", "face_lift", "orient_maps", "slot", "face", "turn")


def taylor_weight(lower, upper, degree):
    return (upper ** (degree + 1) - lower ** (degree + 1)) / math.factorial(degree + 1)


def weight_at(lower, upper, degree):
    result = jnp.float32(taylor_weight(lower, upper, 1))
    for option in range(2, DERIVS):
        result = jnp.where(degree == option, jnp.float32(taylor_weight(lower, upper, option)), result)
    return result


def split(values):
    high = values.astype(BF16)
    low = (values - high.astype(F32)).astype(BF16)
    return high, low


def stack_left(values):
    high, low = split(values)
    return jnp.concatenate([high, low, high], axis=1)


def stack_right(values):
    high, low = split(values)
    return jnp.concatenate([high, high, low], axis=0)


def product(left, right):
    return jnp.dot(left, right, preferred_element_type=F32)


def odd_place(axis):
    return lax.rem(lax.axis_index(axis), 2)


def message_side(slot):
    odd = odd_place("dom" if slot < 2 else "sub")
    return slot + odd if slot % 2 == 0 else slot - odd


def partner_place(slot):
    odd = odd_place("dom" if slot < 2 else "sub")
    return odd if slot % 2 == 0 else 1 - odd


def lane_index(shape):
    return lax.broadcasted_iota(jnp.int32, shape, len(shape) - 1)


def lower_half(shape):
    return lane_index(shape) < HALF


def swap_halves(values):
    return pltpu.roll(values, HALF, values.ndim - 1)


def pack(values_ref, packed_ref):
    modes = values_ref.shape[2]
    packed_ref[...] = jnp.zeros(packed_ref.shape, F32)
    packed_ref[:, :, 0:modes] = values_ref[:, 0:ROWS, :]
    packed_ref[:, :, HALF : HALF + modes] = values_ref[:, ROWS : 2 * ROWS, :]


def turn_matrices(source_ref, work_ref):
    fields, kinds, elements = source_ref.shape[0], source_ref.shape[2], source_ref.shape[3]
    tiles = []
    for pair in range((fields + 1) // 2):
        for row in range(2 * pair, min(2 * pair + 2, fields)):
            for col in range(fields):
                at = (row % 2) * HALF + col * 4
                work_ref[pair, at : at + kinds, 0:elements] = source_ref[row, col]
        tiles.append(work_ref[pair].T[0:elements, :])
    return tiles


def spread(tile, index):
    return jnp.take_along_axis(tile, index, axis=1, mode="promise_in_bounds")


def star_coefficients(star_ref, stage_ref, star_out):
    fields, kinds, elements = star_ref.shape[0], star_ref.shape[2], star_ref.shape[3]
    lanes = lane_index((ROWS, LANES))
    sublanes = lax.broadcasted_iota(jnp.int32, (ROWS, LANES), 0)
    pick = jnp.where((lanes % ROWS == sublanes) & (lanes < 2 * elements), 1.0, 0.0)
    to_lane = lane_index((LANES, LANES))
    from_lane = lax.broadcasted_iota(jnp.int32, (LANES, LANES), 0)
    same_half = (from_lane % elements) // ROWS == to_lane // HALF
    right = jnp.where(same_half & (from_lane < 2 * elements), 1.0, 0.0).astype(BF16)
    filled = lane_index(stage_ref.shape[1:]) < elements
    for row in range(fields):
        for col in range(fields):
            stage_ref[row, col * 4 : col * 4 + kinds, 0:elements] = star_ref[row, col]
        values = jnp.where(filled, stage_ref[row], 0.0)
        high = values.astype(BF16).astype(F32)
        stage_ref[row] = high + pltpu.roll(values - high, elements, 1)
        spreads = []
        for kind in range(kinds):
            for col in range(fields):
                at = col * 4 + kind
                spreads.append(stage_ref[row, at : at + 1, :] * pick)
        spread_out = product(jnp.concatenate(spreads, axis=0).astype(BF16), right)
        count = kinds * fields
        star_out[row * count : (row + 1) * count] = spread_out.reshape(count, ROWS, LANES)


def star_mix(columns, star_ref, fields, kinds):
    sums = [None] * fields
    for row in range(fields):
        for kind in range(kinds):
            part = columns[row * ROWS : (row + 1) * ROWS, kind * LANES : (kind + 1) * LANES]
            for col in range(fields):
                term = star_ref[(row * kinds + kind) * fields + col] * part
                sums[col] = term if sums[col] is None else sums[col] + term
    return jnp.concatenate(sums, axis=0)


def stiffness_blocks(stiffness_ref, block_ref):
    kinds, modes = stiffness_ref.shape[0], stiffness_ref.shape[1]
    block_ref[...] = jnp.zeros(block_ref.shape, F32)
    for kind in range(kinds):
        block_ref[kind, 0:modes, 0:modes] = stiffness_ref[kind]
        block_ref[kind, HALF : HALF + modes, HALF : HALF + modes] = stiffness_ref[kind]


def derive_operator(block_ref):
    return jnp.concatenate([-block_ref[kind].T for kind in range(block_ref.shape[0])], axis=1)


def predict_kernel(*refs):
    later = len(LATER)
    solution_hbm, stiffness_hbm, star_hbm, send_hbm = refs[0:4]
    later_hbm, refs = refs[4 : 4 + later], refs[4 + later :]
    early_out, late_out, far_dom_out, near_dom_out, far_sub_out, near_sub_out = refs[0:6]
    packed_ref, coef_ref, derive_ref, block_ref = refs[6:10]
    later_out, refs = refs[10 : 10 + later], refs[10 + later :]
    work_ref, early_rows, late_rows, solution_ref, stiffness_ref, star_ref, send_ref, sems = refs

    sources = (stiffness_hbm, star_hbm, solution_hbm, send_hbm, *later_hbm)
    targets = (stiffness_ref, star_ref, solution_ref, send_ref, *later_out)
    copies = [
        pltpu.make_async_copy(source, target, sems.at[number])
        for number, (source, target) in enumerate(zip(sources, targets))
    ]
    for copy in copies:
        copy.start()
    fields, kinds = star_ref.shape[0], star_ref.shape[2]
    pairs = (fields + 1) // 2
    copies[0].wait()
    stiffness_blocks(stiffness_ref, block_ref)
    derive_ref[...] = stack_right(derive_operator(block_ref))
    copies[1].wait()
    star_coefficients(star_ref, work_ref, coef_ref)
    copies[2].wait()
    pack(solution_ref, packed_ref)
    start = packed_ref[...].reshape(fields * ROWS, LANES)

    def step(degree, carry):
        current, early, late = carry
        current = star_mix(product(stack_left(current), derive_ref[...]), coef_ref, fields, kinds)
        early = early + weight_at(0.0, 0.5, degree) * current
        late = late + weight_at(0.5, 1.0, degree) * current
        return current, early, late

    _, early, late = lax.fori_loop(
        1, DERIVS, step, (start, taylor_weight(0.0, 0.5, 0) * start, taylor_weight(0.5, 1.0, 0) * start)
    )
    early_out[...] = early.reshape(fields, ROWS, LANES)
    late_out[...] = late.reshape(fields, ROWS, LANES)
    rows_by_pair(early, early_rows, fields)
    rows_by_pair(late, late_rows, fields)
    copies[3].wait()
    sends = send_ref.shape[2]
    fast = sends // 2
    for side, out in enumerate((far_dom_out, near_dom_out, far_sub_out, near_sub_out)):
        out[...] = jnp.zeros(out.shape, F32)
        for place in range(sends):
            element = send_ref[0, message_side(side), place]
            for pair in range(pairs):
                row = pair * sends + place
                out[row : row + 1, :] = early_rows[pair, pl.ds(element, 1), :]
            if place >= fast:
                for pair in range(pairs):
                    row = pairs * sends + pair * fast + place - fast
                    out[row : row + 1, :] = late_rows[pair, pl.ds(element, 1), :]
    for copy in copies[4:]:
        copy.wait()


def rows_by_pair(packed, out_ref, fields):
    lower = lower_half((ROWS, LANES))
    for pair in range((fields + 1) // 2):
        even = packed[2 * pair * ROWS : (2 * pair + 1) * ROWS]
        odd = jnp.zeros_like(even)
        if 2 * pair + 1 < fields:
            odd = packed[(2 * pair + 1) * ROWS : (2 * pair + 2) * ROWS]
        out_ref[pair, 0:ROWS, :] = jnp.where(lower, even, swap_halves(odd))
        out_ref[pair, ROWS : 2 * ROWS, :] = jnp.where(lower, swap_halves(even), odd)


def flux_local_coefficients(flux_ref, work_ref, out_ref):
    fields = flux_ref.shape[0]
    tiles = turn_matrices(flux_ref, work_ref)
    lanes = lane_index((ROWS, LANES))
    for row in range(fields):
        for col in range(fields):
            index = (row % 2) * HALF + col * 4 + lanes % 4
            for half in range(2):
                tile = tiles[row // 2][half * ROWS : (half + 1) * ROWS]
                out_ref[row * fields + col, half] = spread(tile, index)


def flux_remote_coefficients(flux_ref, work_ref, out_ref):
    fields, faces = flux_ref.shape[0], flux_ref.shape[2]
    pairs = (fields + 1) // 2
    tiles = turn_matrices(flux_ref, work_ref)
    lanes = lane_index((ROWS, LANES))
    base = (lanes // HALF) * HALF
    for pair in range(pairs):
        for face in range(faces):
            for col in range(fields):
                at = (face * pairs + pair) * fields + col
                for half in range(2):
                    tile = tiles[pair][half * ROWS : (half + 1) * ROWS]
                    out_ref[at, half * ROWS : (half + 1) * ROWS, :] = spread(tile, base + (col * 4 + face))


def local_terms(packed, star_ref, flux_ref, volume_ref, trace_ref, lift_ref, fields, kinds):
    left = stack_left(packed)
    volume = star_mix(product(left, volume_ref[...]), star_ref, fields, kinds)
    traces = product(left, trace_ref[...])
    sums = []
    for col in range(fields):
        halves = []
        for half in range(2):
            total = None
            for row in range(fields):
                part = traces[row * ROWS : (row + 1) * ROWS, half * LANES : (half + 1) * LANES]
                term = flux_ref[row * fields + col, half] * part
                total = term if total is None else total + term
            halves.append(total)
        sums.append(jnp.concatenate(halves, axis=1))
    return volume + product(stack_left(jnp.concatenate(sums, axis=0)), lift_ref[...])


def prepare_kernel(
    packed_ref, early_ref, block_ref, star_ref, flux_local_ref, flux_remote_ref, restrict_ref, lift_ref, orient_ref,
    slot_ref, face_ref, turn_ref,
    base_out, local_out, remote_out, volume_out, trace_out, local_lift_out, compose_out,
    remote_lift_out, choose_out, mask_out,
    work_ref, wide_ref, face_work_ref, orient_work_ref, code_ref,
):
    fields, kinds = packed_ref.shape[0], block_ref.shape[0]
    face_modes, faces, modes = restrict_ref.shape
    turns = orient_ref.shape[0]
    work_ref[...] = jnp.zeros(work_ref.shape, F32)
    flux_local_coefficients(flux_local_ref, work_ref, local_out)
    flux_remote_coefficients(flux_remote_ref, work_ref, remote_out)

    volume_out[...] = stack_right(jnp.concatenate([block_ref[kind] for kind in range(kinds)], axis=1))

    wide_ref[...] = jnp.zeros(wide_ref.shape, F32)
    for mode in range(face_modes):
        at = mode * faces
        wide_ref[at : at + faces, 0:modes] = restrict_ref[mode]
        wide_ref[LANES + at : LANES + at + faces, HALF : HALF + modes] = restrict_ref[mode]
    trace_out[...] = stack_right(wide_ref[...].T)
    for mode in range(face_modes):
        at = mode * faces
        wide_ref[at : at + faces, 0:modes] = -lift_ref[mode]
        wide_ref[LANES + at : LANES + at + faces, HALF : HALF + modes] = -lift_ref[mode]
    local_lift_out[...] = stack_right(wide_ref[...])

    face_work_ref[...] = jnp.zeros(face_work_ref.shape, F32)
    orient_work_ref[...] = jnp.zeros(orient_work_ref.shape, F32)
    for turn in range(turns):
        orient_work_ref[turn * face_modes : (turn + 1) * face_modes, 0:face_modes] = orient_ref[turn]
    for face in range(faces):
        face_work_ref[0:face_modes, face * LANES : face * LANES + modes] = restrict_ref[:, face, :]
        face_work_ref[0:face_modes, face * LANES + HALF : face * LANES + HALF + modes] = restrict_ref[:, face, :]
    composed = jnp.dot(
        orient_work_ref[...], face_work_ref[...], precision=lax.Precision.HIGHEST, preferred_element_type=F32
    )
    stacked = jnp.concatenate([composed[:, face * LANES : (face + 1) * LANES] for face in range(faces)], axis=0)
    compose_out[...] = stack_right(stacked.T)
    wide_ref[...] = jnp.zeros(wide_ref.shape, F32)
    for face in range(faces):
        for turn in range(turns):
            rows = slice(face * HALF + turn * face_modes, face * HALF + (turn + 1) * face_modes)
            wide_ref[rows, 0:modes] = -lift_ref[:, face, :]
            wide_ref[rows, HALF : HALF + modes] = -lift_ref[:, face, :]
    remote_lift_out[...] = stack_right(wide_ref[...])

    elements = slot_ref.shape[1]
    code_ref[...] = jnp.zeros(code_ref.shape, F32)
    slots = slot_ref[...]
    sends = (choose_out.shape[1] // 2 - elements) // 4
    group = (slots - elements) // sends
    odd = jnp.where(group < 2, odd_place("dom"), odd_place("sub"))
    moved = slots + jnp.where(group % 2 == 0, sends, -sends) * odd
    code_ref[0:faces, 0:elements] = jnp.where(slots < elements, slots, moved).astype(F32)
    code_ref[faces : 2 * faces, 0:elements] = (face_ref[...] * turns + turn_ref[...]).astype(F32)
    codes = code_ref[...].T[0:elements, :]
    sources = choose_out.shape[1] // 2
    source_lane = (lane_index((elements, 2 * sources)) % sources).astype(F32)
    lanes = lane_index((elements, mask_out.shape[1]))
    in_face = lanes % HALF
    lane_code = jnp.where(in_face < turns * face_modes, (lanes // HALF) * turns + in_face // face_modes, -1)
    lane_code = lane_code.astype(F32)
    picks, masks = [], []
    for face in range(faces):
        picks.append(jnp.where(codes[:, face : face + 1] == source_lane, 1.0, 0.0))
        masks.append(jnp.where(codes[:, faces + face : faces + face + 1] == lane_code, 1.0, 0.0))
    choose_out[...] = jnp.concatenate(picks, axis=0).astype(BF16)
    mask_out[...] = jnp.concatenate(masks, axis=0)

    early = early_ref[...].reshape(fields * ROWS, LANES)
    terms = local_terms(early, star_ref, local_out, volume_out, trace_out, local_lift_out, fields, kinds)
    base_out[...] = packed_ref[...] + terms.reshape(fields, ROWS, LANES)


def remote_terms(rows_ref, remote_ref, compose_ref, lift_ref, choose_ref, mask_ref, fields):
    pairs = rows_ref.shape[0]
    faces = lift_ref.shape[0] // (3 * HALF)
    elements = choose_ref.shape[0] // faces
    sources = jnp.concatenate([rows_ref[pair] for pair in range(pairs)], axis=1)
    gathered = product(choose_ref[...], jnp.concatenate(split(sources), axis=0))
    folded = []
    for face in range(faces):
        sums = []
        for col in range(fields):
            total = None
            for pair in range(pairs):
                part = gathered[face * elements : (face + 1) * elements, pair * LANES : (pair + 1) * LANES]
                term = remote_ref[(face * pairs + pair) * fields + col] * part
                total = term if total is None else total + term
            sums.append(total)
        turned = product(stack_left(jnp.concatenate(sums, axis=0)), compose_ref[...])
        mask = mask_ref[face * elements : (face + 1) * elements, :]
        chosen = (turned.reshape(fields, elements, turned.shape[1]) * mask[None]).reshape(turned.shape)
        both = chosen[:, 0:LANES] + chosen[:, LANES : 2 * LANES]
        folded.append(both + swap_halves(both))
    lower = lower_half(folded[0].shape)
    left = [jnp.where(lower, folded[face], folded[face + 1]) for face in range(0, faces, 2)]
    result = product(stack_left(jnp.concatenate(left, axis=1)), lift_ref[...])
    result = result.reshape(fields, 2, ROWS, LANES)
    return jnp.where(lower_half((ROWS, LANES))[None], result[:, 0], result[:, 1])


def middle_kernel(
    base_ref, early_ref, late_ref, star_ref, remote_ref, derive_ref, compose_ref, lift_ref, choose_ref, mask_ref,
    rate_hbm, send_hbm, far_dom, near_dom, far_sub, near_sub,
    middle_out, late_out, far_dom_out, near_dom_out, far_sub_out, near_sub_out,
    rows_ref, late_rows, rate_ref, send_ref, arrived_ref, sems,
):
    copies = [
        pltpu.make_async_copy(gathered.at[partner_place(side)], arrived_ref.at[side], sems.at[2 + side])
        for side, gathered in enumerate((far_dom, near_dom, far_sub, near_sub))
    ]
    copies += [
        pltpu.make_async_copy(rate_hbm, rate_ref, sems.at[0]),
        pltpu.make_async_copy(send_hbm, send_ref, sems.at[1]),
    ]
    for copy in copies:
        copy.start()
    fields = base_ref.shape[0]
    kinds = star_ref.shape[0] // (fields * fields)
    pairs = rows_ref.shape[0]
    sends = send_ref.shape[2]
    fast = sends // 2
    elements = 2 * ROWS
    rows_by_pair(early_ref[...].reshape(fields * ROWS, LANES), rows_ref, fields)
    for side in range(4):
        at = elements + side * sends
        copies[side].wait()
        for pair in range(pairs):
            rows_ref[pair, at : at + sends, :] = arrived_ref[side, pair * sends : (pair + 1) * sends, :]
    middle = base_ref[...] + remote_terms(
        rows_ref, remote_ref, compose_ref, lift_ref, choose_ref, mask_ref, fields
    )
    middle_out[...] = middle
    start = middle.reshape(fields * ROWS, LANES)

    def step(degree, carry):
        current, early = carry
        current = star_mix(product(stack_left(current), derive_ref[...]), star_ref, fields, kinds)
        return current, early + weight_at(0.0, 0.5, degree) * current

    _, restart = lax.fori_loop(1, DERIVS, step, (start, taylor_weight(0.0, 0.5, 0) * start))
    for copy in copies[4:]:
        copy.wait()
    sublane = lax.broadcasted_iota(jnp.int32, (ROWS, LANES), 0)
    lower = lower_half((ROWS, LANES))
    is_fast = jnp.zeros((ROWS, LANES), jnp.int32)
    for element in range(elements):
        here = (sublane == element % ROWS) & (lower if element < ROWS else jnp.logical_not(lower))
        is_fast = jnp.where(here, rate_ref[element], is_fast)
    late = jnp.where((is_fast == 2)[None], restart.reshape(fields, ROWS, LANES), late_ref[...])
    late_out[...] = late
    rows_by_pair(late.reshape(fields * ROWS, LANES), late_rows, fields)
    for side, out in enumerate((far_dom_out, near_dom_out, far_sub_out, near_sub_out)):
        out[...] = jnp.zeros(out.shape, F32)
        for place in range(fast):
            element = send_ref[0, message_side(side), place]
            for pair in range(pairs):
                row = pair * fast + place
                out[row : row + 1, :] = late_rows[pair, pl.ds(element, 1), :]


def local_kernel(middle_ref, late_ref, star_ref, flux_ref, volume_ref, trace_ref, lift_ref, base_out):
    fields = middle_ref.shape[0]
    kinds = star_ref.shape[0] // (fields * fields)
    late = late_ref[...].reshape(fields * ROWS, LANES)
    terms = local_terms(late, star_ref, flux_ref, volume_ref, trace_ref, lift_ref, fields, kinds)
    base_out[...] = middle_ref[...] + terms.reshape(fields, ROWS, LANES)


def final_kernel(
    base_ref, late_ref, remote_ref, compose_ref, lift_ref, choose_ref, mask_ref,
    first_far_dom, first_near_dom, first_far_sub, first_near_sub,
    second_far_dom, second_near_dom, second_far_sub, second_near_sub,
    result_out, rows_ref, first_ref, second_ref, sems,
):
    fields = base_ref.shape[0]
    modes = result_out.shape[2]
    pairs = rows_ref.shape[0]
    elements = 2 * ROWS
    sends = (rows_ref.shape[1] - elements) // 4
    fast = sends // 2
    firsts = (first_far_dom, first_near_dom, first_far_sub, first_near_sub)
    seconds = (second_far_dom, second_near_dom, second_far_sub, second_near_sub)
    copies = []
    for side, (first, second) in enumerate(zip(firsts, seconds)):
        place = partner_place(side)
        copies.append(pltpu.make_async_copy(first.at[place], first_ref.at[side], sems.at[2 * side]))
        copies.append(pltpu.make_async_copy(second.at[place], second_ref.at[side], sems.at[2 * side + 1]))
    for copy in copies:
        copy.start()
    rows_by_pair(late_ref[...].reshape(fields * ROWS, LANES), rows_ref, fields)
    for copy in copies:
        copy.wait()
    for side in range(4):
        at = elements + side * sends
        for pair in range(pairs):
            rows_ref[pair, at : at + fast, :] = second_ref[side, pair * fast : (pair + 1) * fast, :]
            row = pairs * sends + pair * fast
            rows_ref[pair, at + fast : at + sends, :] = first_ref[side, row : row + fast, :]
    result = base_ref[...] + remote_terms(
        rows_ref, remote_ref, compose_ref, lift_ref, choose_ref, mask_ref, fields
    )
    result_out[:, 0:ROWS, :] = result[:, :, 0:modes]
    result_out[:, ROWS : 2 * ROWS, :] = result[:, :, HALF : HALF + modes]


VMEM = pl.BlockSpec(memory_space=pltpu.VMEM)
HBM = pl.BlockSpec(memory_space=pltpu.HBM)


def call(kernel, ins, outs, scratch, args, name, flops):
    shapes = [jax.ShapeDtypeStruct(shape, dtype) for shape, dtype in outs]
    args = [
        pltpu.with_memory_space_constraint(arg, pltpu.HBM) if spec is HBM else arg for spec, arg in zip(ins, args)
    ]
    return pl.pallas_call(
        kernel,
        out_shape=shapes,
        in_specs=ins,
        out_specs=[VMEM] * len(outs),
        scratch_shapes=[pltpu.VMEM(*one) if isinstance(one, tuple) else one for one in scratch],
        compiler_params=pltpu.CompilerParams(vmem_limit_bytes=16 * 1024 * 1024),
        cost_estimate=pl.CostEstimate(flops=flops, bytes_accessed=4_000_000, transcendentals=0),
        name=name,
    )(*args)


def exchange(outgoing):
    arrived = [None] * 4
    for slot, axis, first in ((0, "dom", 1), (2, "sub", 1), (1, "dom", 0), (3, "sub", 0)):
        size = lax.axis_size(axis)
        assert size % 2 == 0
        pairs = []
        for even in range(first, size, 2):
            odd = (even + 1) % size
            pairs += [[even, odd]]
        arrived[slot] = lax.all_gather(outgoing[slot], axis, axis_index_groups=pairs)
    return arrived


def up_to(count, multiple):
    return -(-count // multiple) * multiple


def local(
    solution, stiffness, star_matrices, face_restrict, face_lift, orient_maps, flux_local, flux_remote,
    cluster_rate, send_list, neighbour_slot, neighbour_face, neighbour_turn,
):
    fields, elements = solution.shape[1], solution.shape[2]
    kinds = stiffness.shape[0]
    faces = face_restrict.shape[0]
    sides, sends = send_list.shape[1], send_list.shape[2]
    fast = sends // 2
    pairs = (fields + 1) // 2
    assert elements == 2 * ROWS and solution.shape[0] <= HALF
    values = jnp.transpose(solution, (1, 2, 0))
    star = jnp.transpose(star_matrices, (1, 2, 0, 3))
    local_part = jnp.transpose(flux_local, (1, 2, 0, 3))
    remote_part = jnp.transpose(flux_remote, (1, 2, 0, 3))
    restrict = jnp.transpose(face_restrict, (1, 0, 2))
    lift = jnp.transpose(face_lift, (2, 0, 1))

    packed = (fields, ROWS, LANES)
    first_shape = (up_to(pairs * (sends + fast), ROWS), LANES)
    second_shape = (up_to(pairs * fast, ROWS), LANES)
    work = (pairs, LANES, LANES)
    star_shape = (fields * fields * kinds, ROWS, LANES)
    combos = faces * HALF
    sources = elements + sides * sends

    waiting = (local_part, remote_part, restrict, lift, orient_maps, neighbour_slot, neighbour_face, neighbour_turn)
    made = call(
        predict_kernel,
        [HBM] * (4 + len(LATER)),
        [(packed, F32)] * 2 + [(first_shape, F32)] * sides + [
            (packed, F32), (star_shape, F32), ((3 * LANES, kinds * LANES), BF16), ((kinds, LANES, LANES), F32),
        ] + [(array.shape, array.dtype) for array in waiting],
        [
            ((fields, up_to(4 * fields, ROWS), LANES), F32),
            ((pairs, elements, LANES), F32), ((pairs, elements, LANES), F32),
            (values.shape, F32), (stiffness.shape, F32), (star.shape, F32),
            pltpu.SMEM(send_list.shape, jnp.int32), pltpu.SemaphoreType.DMA((4 + len(LATER),)),
        ],
        (values, stiffness, star, send_list, *waiting),
        "predict", 100_000_000,
    )
    early, late, outgoing = made[0], made[1], made[2 : 2 + sides]
    start, star_coef, derive_op, blocks = made[2 + sides : 6 + sides]
    waiting = made[6 + sides :]
    first = exchange(outgoing)
    (
        base, local_coef, remote_coef, volume_op, trace_op, local_lift, compose_op, remote_lift, choose, mask,
    ) = call(
        prepare_kernel,
        [VMEM] * 12,
        [
            (packed, F32), ((fields * fields, 2, ROWS, LANES), F32),
            ((faces * pairs * fields, elements, LANES), F32),
            ((3 * LANES, kinds * LANES), BF16), ((3 * LANES, 2 * LANES), BF16),
            ((6 * LANES, LANES), BF16), ((3 * LANES, combos), BF16), ((3 * faces * HALF, LANES), BF16),
            ((faces * elements, 2 * sources), BF16), ((faces * elements, combos), F32),
        ],
        [
            (work, F32), ((2 * LANES, LANES), F32),
            ((LANES, faces * LANES), F32), ((HALF, LANES), F32), ((LANES, LANES), F32),
        ],
        (start, early, blocks, star_coef, *waiting),
        "prepare", 200_000_000,
    )
    middle, late_value, *outgoing = call(
        middle_kernel,
        [VMEM] * 10 + [HBM] * 6,
        [(packed, F32)] * 2 + [(second_shape, F32)] * sides,
        [
            ((pairs, sources, LANES), F32), ((pairs, elements, LANES), F32),
            pltpu.SMEM(cluster_rate.shape, jnp.int32), pltpu.SMEM(send_list.shape, jnp.int32),
            ((sides, *first_shape), F32), pltpu.SemaphoreType.DMA((2 + sides,)),
        ],
        (
            base, early, late, star_coef, remote_coef, derive_op, compose_op, remote_lift, choose, mask,
            cluster_rate, send_list, *first,
        ),
        "middle", 200_000_000,
    )
    second = exchange(outgoing)
    (base,) = call(
        local_kernel,
        [VMEM] * 7,
        [(packed, F32)],
        [],
        (middle, late_value, star_coef, local_coef, volume_op, trace_op, local_lift),
        "local_late", 200_000_000,
    )
    (result,) = call(
        final_kernel,
        [VMEM] * 7 + [HBM] * 8,
        [(values.shape, F32)],
        [
            ((pairs, sources, LANES), F32), ((sides, *first_shape), F32), ((sides, *second_shape), F32),
            pltpu.SemaphoreType.DMA((2 * sides,)),
        ],
        (base, late_value, remote_coef, compose_op, remote_lift, choose, mask, *first, *second),
        "final", 200_000_000,
    )
    return jnp.transpose(result, (2, 0, 1))


def solution(mesh):
    placed = (
        P(None, None, ("dom", "sub")),
        P(),
        P(None, None, None, ("dom", "sub")),
        P(),
        P(),
        P(),
        P(None, None, None, ("dom", "sub")),
        P(None, None, None, ("dom", "sub")),
        P(("dom", "sub")),
        P(("dom", "sub"), None, None),
        P(None, ("dom", "sub")),
        P(None, ("dom", "sub")),
        P(None, ("dom", "sub")),
    )
    return jax.shard_map(
        local, mesh=mesh, in_specs=placed, out_specs=P(None, None, ("dom", "sub")), check_vma=False
    )
```

```python
import math

import jax
import jax.numpy as jnp
from jax import lax
from jax.experimental import pallas as pl
from jax.experimental.pallas import tpu as pltpu
from jax.sharding import PartitionSpec as P

DERIVS = 6
LANES = 128
HALF = 64
ROWS = 8
F32 = jnp.float32
BF16 = jnp.bfloat16
LATER = ("flux_local", "flux_remote", "face_restrict", "face_lift", "orient_maps", "slot", "face", "turn")
AXES = ("dom", "sub")
SWAPS = (("dom", False), ("sub", False), ("sub", True), ("dom", True))


def taylor_weight(lower, upper, degree):
    return (upper ** (degree + 1) - lower ** (degree + 1)) / math.factorial(degree + 1)


def weight_at(lower, upper, degree):
    result = jnp.float32(taylor_weight(lower, upper, 1))
    for option in range(2, DERIVS):
        result = jnp.where(degree == option, jnp.float32(taylor_weight(lower, upper, option)), result)
    return result


def split(values):
    high = values.astype(BF16)
    low = (values - high.astype(F32)).astype(BF16)
    return high, low


def stack_left(values):
    high, low = split(values)
    return jnp.concatenate([high, low, high], axis=1)


def stack_right(values):
    high, low = split(values)
    return jnp.concatenate([high, high, low], axis=0)


def product(left, right):
    return jnp.dot(left, right, preferred_element_type=F32)


def odd_place(axis):
    return lax.rem(lax.axis_index(axis), 2)


def message_side(slot):
    axis, far = SWAPS[slot]
    odd = odd_place(axis)
    return 2 * AXES.index(axis) + (odd if far else 1 - odd)


def ghost_slot(side):
    axis = AXES[side // 2]
    even_far = side % 2 == 0
    return jnp.where(odd_place(axis) == 0, SWAPS.index((axis, even_far)), SWAPS.index((axis, not even_far)))


def lane_index(shape):
    return lax.broadcasted_iota(jnp.int32, shape, len(shape) - 1)


def lower_half(shape):
    return lane_index(shape) < HALF


def swap_halves(values):
    return pltpu.roll(values, HALF, values.ndim - 1)


def pack(values_ref, packed_ref):
    modes = values_ref.shape[2]
    packed_ref[...] = jnp.zeros(packed_ref.shape, F32)
    packed_ref[:, :, 0:modes] = values_ref[:, 0:ROWS, :]
    packed_ref[:, :, HALF : HALF + modes] = values_ref[:, ROWS : 2 * ROWS, :]


def turn_matrices(source_ref, work_ref):
    fields, kinds, elements = source_ref.shape[0], source_ref.shape[2], source_ref.shape[3]
    tiles = []
    for pair in range((fields + 1) // 2):
        for row in range(2 * pair, min(2 * pair + 2, fields)):
            for col in range(fields):
                at = (row % 2) * HALF + col * 4
                work_ref[pair, at : at + kinds, 0:elements] = source_ref[row, col]
        tiles.append(work_ref[pair].T[0:elements, :])
    return tiles


def spread(tile, index):
    return jnp.take_along_axis(tile, index, axis=1, mode="promise_in_bounds")


def star_coefficients(star_ref, stage_ref, star_out):
    fields, kinds, elements = star_ref.shape[0], star_ref.shape[2], star_ref.shape[3]
    lanes = lane_index((ROWS, LANES))
    sublanes = lax.broadcasted_iota(jnp.int32, (ROWS, LANES), 0)
    pick = jnp.where((lanes % ROWS == sublanes) & (lanes < 2 * elements), 1.0, 0.0)
    to_lane = lane_index((LANES, LANES))
    from_lane = lax.broadcasted_iota(jnp.int32, (LANES, LANES), 0)
    same_half = (from_lane % elements) // ROWS == to_lane // HALF
    right = jnp.where(same_half & (from_lane < 2 * elements), 1.0, 0.0).astype(BF16)
    filled = lane_index(stage_ref.shape[1:]) < elements
    for row in range(fields):
        for col in range(fields):
            stage_ref[row, col * 4 : col * 4 + kinds, 0:elements] = star_ref[row, col]
        values = jnp.where(filled, stage_ref[row], 0.0)
        high = values.astype(BF16).astype(F32)
        stage_ref[row] = high + pltpu.roll(values - high, elements, 1)
        spreads = []
        for kind in range(kinds):
            for col in range(fields):
                at = col * 4 + kind
                spreads.append(stage_ref[row, at : at + 1, :] * pick)
        spread_out = product(jnp.concatenate(spreads, axis=0).astype(BF16), right)
        count = kinds * fields
        star_out[row * count : (row + 1) * count] = spread_out.reshape(count, ROWS, LANES)


def star_mix(columns, star_ref, fields, kinds):
    sums = [None] * fields
    for row in range(fields):
        for kind in range(kinds):
            part = columns[row * ROWS : (row + 1) * ROWS, kind * LANES : (kind + 1) * LANES]
            for col in range(fields):
                term = star_ref[(row * kinds + kind) * fields + col] * part
                sums[col] = term if sums[col] is None else sums[col] + term
    return jnp.concatenate(sums, axis=0)


def stiffness_blocks(stiffness_ref, block_ref, turned):
    kinds, modes = stiffness_ref.shape[0], stiffness_ref.shape[1]
    block_ref[...] = jnp.zeros(block_ref.shape, F32)
    for kind in range(kinds):
        matrix = -stiffness_ref[kind].T if turned else stiffness_ref[kind]
        block_ref[kind, 0:modes, 0:modes] = matrix
        block_ref[kind, HALF : HALF + modes, HALF : HALF + modes] = matrix
    return jnp.concatenate([block_ref[kind] for kind in range(kinds)], axis=1)


def predict_kernel(*refs):
    later = len(LATER)
    solution_hbm, stiffness_hbm, star_hbm, send_hbm = refs[0:4]
    later_hbm, refs = refs[4 : 4 + later], refs[4 + later :]
    early_out, late_out, near_dom_out, near_sub_out, far_sub_out, far_dom_out = refs[0:6]
    packed_ref, coef_ref, derive_ref, stiffness_ref = refs[6:10]
    later_out, refs = refs[10 : 10 + later], refs[10 + later :]
    work_ref, early_rows, late_rows, solution_ref, block_ref, star_ref, send_ref, sems = refs

    sources = (star_hbm, stiffness_hbm, solution_hbm, send_hbm, *later_hbm)
    targets = (star_ref, stiffness_ref, solution_ref, send_ref, *later_out)
    copies = [
        pltpu.make_async_copy(source, target, sems.at[number])
        for number, (source, target) in enumerate(zip(sources, targets))
    ]
    for copy in copies:
        copy.start()
    fields, kinds = star_ref.shape[0], star_ref.shape[2]
    pairs = (fields + 1) // 2
    for copy in copies[0:3]:
        copy.wait()
    derive_ref[...] = stack_right(stiffness_blocks(stiffness_ref, block_ref, True))
    star_coefficients(star_ref, work_ref, coef_ref)
    pack(solution_ref, packed_ref)
    start = packed_ref[...].reshape(fields * ROWS, LANES)

    def step(degree, carry):
        current, early, late = carry
        current = star_mix(product(stack_left(current), derive_ref[...]), coef_ref, fields, kinds)
        early = early + weight_at(0.0, 0.5, degree) * current
        late = late + weight_at(0.5, 1.0, degree) * current
        return current, early, late

    _, early, late = lax.fori_loop(
        1, DERIVS, step, (start, taylor_weight(0.0, 0.5, 0) * start, taylor_weight(0.5, 1.0, 0) * start)
    )
    early_out[...] = early.reshape(fields, ROWS, LANES)
    late_out[...] = late.reshape(fields, ROWS, LANES)
    rows_by_pair(early, early_rows, fields)
    rows_by_pair(late, late_rows, fields)
    copies[3].wait()
    sends = send_ref.shape[2]
    fast = sends // 2
    for side, out in enumerate((near_dom_out, near_sub_out, far_sub_out, far_dom_out)):
        out[...] = jnp.zeros(out.shape, F32)
        for place in range(sends):
            element = send_ref[0, message_side(side), place]
            for pair in range(pairs):
                row = pair * sends + place
                out[row : row + 1, :] = early_rows[pair, pl.ds(element, 1), :]
            if place >= fast:
                for pair in range(pairs):
                    row = pairs * sends + pair * fast + place - fast
                    out[row : row + 1, :] = late_rows[pair, pl.ds(element, 1), :]
    for copy in copies[4:]:
        copy.wait()


def rows_by_pair(packed, out_ref, fields):
    lower = lower_half((ROWS, LANES))
    for pair in range((fields + 1) // 2):
        even = packed[2 * pair * ROWS : (2 * pair + 1) * ROWS]
        odd = jnp.zeros_like(even)
        if 2 * pair + 1 < fields:
            odd = packed[(2 * pair + 1) * ROWS : (2 * pair + 2) * ROWS]
        out_ref[pair, 0:ROWS, :] = jnp.where(lower, even, swap_halves(odd))
        out_ref[pair, ROWS : 2 * ROWS, :] = jnp.where(lower, swap_halves(even), odd)


def flux_local_coefficients(flux_ref, work_ref, out_ref):
    fields = flux_ref.shape[0]
    tiles = turn_matrices(flux_ref, work_ref)
    lanes = lane_index((ROWS, LANES))
    for row in range(fields):
        for col in range(fields):
            index = (row % 2) * HALF + col * 4 + lanes % 4
            for half in range(2):
                tile = tiles[row // 2][half * ROWS : (half + 1) * ROWS]
                out_ref[row * fields + col, half] = spread(tile, index)


def flux_remote_coefficients(flux_ref, work_ref, out_ref):
    fields, faces = flux_ref.shape[0], flux_ref.shape[2]
    pairs = (fields + 1) // 2
    tiles = turn_matrices(flux_ref, work_ref)
    lanes = lane_index((ROWS, LANES))
    base = (lanes // HALF) * HALF
    for pair in range(pairs):
        for face in range(faces):
            for col in range(fields):
                at = (face * pairs + pair) * fields + col
                for half in range(2):
                    tile = tiles[pair][half * ROWS : (half + 1) * ROWS]
                    out_ref[at, half * ROWS : (half + 1) * ROWS, :] = spread(tile, base + (col * 4 + face))


def local_terms(packed, star_ref, flux_ref, volume_ref, trace_ref, lift_ref, fields, kinds):
    left = stack_left(packed)
    volume = star_mix(product(left, volume_ref[...]), star_ref, fields, kinds)
    traces = product(left, trace_ref[...])
    sums = []
    for col in range(fields):
        halves = []
        for half in range(2):
            total = None
            for row in range(fields):
                part = traces[row * ROWS : (row + 1) * ROWS, half * LANES : (half + 1) * LANES]
                term = flux_ref[row * fields + col, half] * part
                total = term if total is None else total + term
            halves.append(total)
        sums.append(jnp.concatenate(halves, axis=1))
    return volume + product(stack_left(jnp.concatenate(sums, axis=0)), lift_ref[...])


def prepare_kernel(
    packed_ref, early_ref, stiffness_ref, star_ref, flux_local_ref, flux_remote_ref, restrict_ref, lift_ref, orient_ref,
    slot_ref, face_ref, turn_ref,
    base_out, local_out, remote_out, volume_out, trace_out, local_lift_out, compose_out,
    remote_lift_out, choose_out, mask_out,
    work_ref, block_ref, wide_ref, face_work_ref, orient_work_ref, code_ref,
):
    fields, kinds = packed_ref.shape[0], stiffness_ref.shape[0]
    face_modes, faces, modes = restrict_ref.shape
    turns = orient_ref.shape[0]
    work_ref[...] = jnp.zeros(work_ref.shape, F32)
    flux_local_coefficients(flux_local_ref, work_ref, local_out)
    flux_remote_coefficients(flux_remote_ref, work_ref, remote_out)

    volume_out[...] = stack_right(stiffness_blocks(stiffness_ref, block_ref, False))

    wide_ref[...] = jnp.zeros(wide_ref.shape, F32)
    for mode in range(face_modes):
        at = mode * faces
        wide_ref[at : at + faces, 0:modes] = restrict_ref[mode]
        wide_ref[LANES + at : LANES + at + faces, HALF : HALF + modes] = restrict_ref[mode]
    trace_out[...] = stack_right(wide_ref[...].T)
    for mode in range(face_modes):
        at = mode * faces
        wide_ref[at : at + faces, 0:modes] = -lift_ref[mode]
        wide_ref[LANES + at : LANES + at + faces, HALF : HALF + modes] = -lift_ref[mode]
    local_lift_out[...] = stack_right(wide_ref[...])

    face_work_ref[...] = jnp.zeros(face_work_ref.shape, F32)
    orient_work_ref[...] = jnp.zeros(orient_work_ref.shape, F32)
    for turn in range(turns):
        orient_work_ref[turn * face_modes : (turn + 1) * face_modes, 0:face_modes] = orient_ref[turn]
    for face in range(faces):
        face_work_ref[0:face_modes, face * LANES : face * LANES + modes] = restrict_ref[:, face, :]
        face_work_ref[0:face_modes, face * LANES + HALF : face * LANES + HALF + modes] = restrict_ref[:, face, :]
    composed = jnp.dot(
        orient_work_ref[...], face_work_ref[...], precision=lax.Precision.HIGHEST, preferred_element_type=F32
    )
    stacked = jnp.concatenate([composed[:, face * LANES : (face + 1) * LANES] for face in range(faces)], axis=0)
    high, low = split(stacked.T[0:HALF])
    compose_out[...] = jnp.concatenate([high, high, low, jnp.zeros_like(low)], axis=0)
    wide_ref[...] = jnp.zeros(wide_ref.shape, F32)
    for face in range(faces):
        for turn in range(turns):
            rows = slice(face * HALF + turn * face_modes, face * HALF + (turn + 1) * face_modes)
            wide_ref[rows, 0:modes] = -lift_ref[:, face, :]
            wide_ref[rows, HALF : HALF + modes] = -lift_ref[:, face, :]
    remote_lift_out[...] = stack_right(wide_ref[...])

    elements = slot_ref.shape[1]
    code_ref[...] = jnp.zeros(code_ref.shape, F32)
    slots = slot_ref[...]
    sends = (choose_out.shape[1] // 2 - elements) // 4
    group = (slots - elements) // sends
    moved = slots
    for side in range(4):
        moved = jnp.where(group == side, slots + (ghost_slot(side) - side) * sends, moved)
    code_ref[0:faces, 0:elements] = jnp.where(slots < elements, slots, moved).astype(F32)
    code_ref[faces : 2 * faces, 0:elements] = (face_ref[...] * turns + turn_ref[...]).astype(F32)
    codes = code_ref[...].T[0:elements, :]
    sources = choose_out.shape[1] // 2
    source_lane = (lane_index((elements, 2 * sources)) % sources).astype(F32)
    lanes = lane_index((elements, mask_out.shape[1]))
    in_face = lanes % HALF
    lane_code = jnp.where(in_face < turns * face_modes, (lanes // HALF) * turns + in_face // face_modes, -1)
    lane_code = lane_code.astype(F32)
    picks, masks = [], []
    for face in range(faces):
        picks.append(jnp.where(codes[:, face : face + 1] == source_lane, 1.0, 0.0))
        masks.append(jnp.where(codes[:, faces + face : faces + face + 1] == lane_code, 1.0, 0.0))
    choose_out[...] = jnp.concatenate(picks, axis=0).astype(BF16)
    mask_out[...] = jnp.concatenate(masks, axis=0)

    early = early_ref[...].reshape(fields * ROWS, LANES)
    terms = local_terms(early, star_ref, local_out, volume_out, trace_out, local_lift_out, fields, kinds)
    base_out[...] = packed_ref[...] + terms.reshape(fields, ROWS, LANES)


def remote_terms(rows_ref, remote_ref, compose_ref, lift_ref, choose_ref, mask_ref, fields):
    pairs = rows_ref.shape[0]
    faces = lift_ref.shape[0] // (3 * HALF)
    elements = choose_ref.shape[0] // faces
    sources = jnp.concatenate([rows_ref[pair] for pair in range(pairs)], axis=1)
    gathered = product(choose_ref[...], jnp.concatenate(split(sources), axis=0))
    folded = []
    for face in range(faces):
        sums = []
        for col in range(fields):
            total = None
            for pair in range(pairs):
                part = gathered[face * elements : (face + 1) * elements, pair * LANES : (pair + 1) * LANES]
                term = remote_ref[(face * pairs + pair) * fields + col] * part
                total = term if total is None else total + term
            sums.append(total)
        mixed = jnp.concatenate(sums, axis=0)
        high, low = split(mixed + swap_halves(mixed))
        first = jnp.where(lower_half(high.shape), high, low)
        turned = product(jnp.concatenate([first, high], axis=1), compose_ref[...])
        mask = mask_ref[face * elements : (face + 1) * elements, :]
        chosen = (turned.reshape(fields, elements, turned.shape[1]) * mask[None]).reshape(turned.shape)
        both = chosen[:, 0:LANES] + chosen[:, LANES : 2 * LANES]
        folded.append(both + swap_halves(both))
    lower = lower_half(folded[0].shape)
    left = [jnp.where(lower, folded[face], folded[face + 1]) for face in range(0, faces, 2)]
    result = product(stack_left(jnp.concatenate(left, axis=1)), lift_ref[...])
    result = result.reshape(fields, 2, ROWS, LANES)
    return jnp.where(lower_half((ROWS, LANES))[None], result[:, 0], result[:, 1])


def middle_kernel(
    base_ref, early_ref, late_ref, star_ref, remote_ref, derive_ref, compose_ref, lift_ref, choose_ref, mask_ref,
    rate_hbm, send_hbm, near_dom, near_sub, far_sub, far_dom,
    middle_out, late_out, near_dom_out, near_sub_out, far_sub_out, far_dom_out,
    rows_ref, late_rows, rate_ref, send_ref, sems,
):
    copies = [
        pltpu.make_async_copy(rate_hbm, rate_ref, sems.at[0]),
        pltpu.make_async_copy(send_hbm, send_ref, sems.at[1]),
    ]
    for copy in copies:
        copy.start()
    fields = base_ref.shape[0]
    kinds = star_ref.shape[0] // (fields * fields)
    pairs = rows_ref.shape[0]
    sends = send_ref.shape[2]
    fast = sends // 2
    elements = 2 * ROWS
    rows_by_pair(early_ref[...].reshape(fields * ROWS, LANES), rows_ref, fields)
    for side, arrived in enumerate((near_dom, near_sub, far_sub, far_dom)):
        at = elements + side * sends
        for pair in range(pairs):
            rows_ref[pair, at : at + sends, :] = arrived[pair * sends : (pair + 1) * sends, :]
    middle = base_ref[...] + remote_terms(
        rows_ref, remote_ref, compose_ref, lift_ref, choose_ref, mask_ref, fields
    )
    middle_out[...] = middle
    start = middle.reshape(fields * ROWS, LANES)

    def step(degree, carry):
        current, early = carry
        current = star_mix(product(stack_left(current), derive_ref[...]), star_ref, fields, kinds)
        return current, early + weight_at(0.0, 0.5, degree) * current

    _, restart = lax.fori_loop(1, DERIVS, step, (start, taylor_weight(0.0, 0.5, 0) * start))
    for copy in copies:
        copy.wait()
    sublane = lax.broadcasted_iota(jnp.int32, (ROWS, LANES), 0)
    lower = lower_half((ROWS, LANES))
    is_fast = jnp.zeros((ROWS, LANES), jnp.int32)
    for element in range(elements):
        here = (sublane == element % ROWS) & (lower if element < ROWS else jnp.logical_not(lower))
        is_fast = jnp.where(here, rate_ref[element], is_fast)
    late = jnp.where((is_fast == 2)[None], restart.reshape(fields, ROWS, LANES), late_ref[...])
    late_out[...] = late
    rows_by_pair(late.reshape(fields * ROWS, LANES), late_rows, fields)
    for side, out in enumerate((near_dom_out, near_sub_out, far_sub_out, far_dom_out)):
        out[...] = jnp.zeros(out.shape, F32)
        for place in range(fast):
            element = send_ref[0, message_side(side), place]
            for pair in range(pairs):
                row = pair * fast + place
                out[row : row + 1, :] = late_rows[pair, pl.ds(element, 1), :]


def local_kernel(middle_ref, late_ref, star_ref, flux_ref, volume_ref, trace_ref, lift_ref, base_out):
    fields = middle_ref.shape[0]
    kinds = star_ref.shape[0] // (fields * fields)
    late = late_ref[...].reshape(fields * ROWS, LANES)
    terms = local_terms(late, star_ref, flux_ref, volume_ref, trace_ref, lift_ref, fields, kinds)
    base_out[...] = middle_ref[...] + terms.reshape(fields, ROWS, LANES)


def final_kernel(
    base_ref, late_ref, remote_ref, compose_ref, lift_ref, choose_ref, mask_ref,
    first_near_dom, first_near_sub, first_far_sub, first_far_dom,
    second_near_dom, second_near_sub, second_far_sub, second_far_dom,
    result_out, rows_ref,
):
    fields = base_ref.shape[0]
    modes = result_out.shape[2]
    pairs = rows_ref.shape[0]
    elements = 2 * ROWS
    sends = (rows_ref.shape[1] - elements) // 4
    fast = sends // 2
    rows_by_pair(late_ref[...].reshape(fields * ROWS, LANES), rows_ref, fields)
    firsts = (first_near_dom, first_near_sub, first_far_sub, first_far_dom)
    seconds = (second_near_dom, second_near_sub, second_far_sub, second_far_dom)
    for side, (first, second) in enumerate(zip(firsts, seconds)):
        at = elements + side * sends
        for pair in range(pairs):
            rows_ref[pair, at : at + fast, :] = second[pair * fast : (pair + 1) * fast, :]
            row = pairs * sends + pair * fast
            rows_ref[pair, at + fast : at + sends, :] = first[row : row + fast, :]
    result = base_ref[...] + remote_terms(
        rows_ref, remote_ref, compose_ref, lift_ref, choose_ref, mask_ref, fields
    )
    result_out[:, 0:ROWS, :] = result[:, :, 0:modes]
    result_out[:, ROWS : 2 * ROWS, :] = result[:, :, HALF : HALF + modes]


VMEM = pl.BlockSpec(memory_space=pltpu.VMEM)
HBM = pl.BlockSpec(memory_space=pltpu.HBM)


def call(kernel, ins, outs, scratch, args, name, flops):
    shapes = [jax.ShapeDtypeStruct(shape, dtype) for shape, dtype in outs]
    args = [
        pltpu.with_memory_space_constraint(arg, pltpu.HBM) if spec is HBM else arg for spec, arg in zip(ins, args)
    ]
    return pl.pallas_call(
        kernel,
        out_shape=shapes,
        in_specs=ins,
        out_specs=[VMEM] * len(outs),
        scratch_shapes=[pltpu.VMEM(*one) if isinstance(one, tuple) else one for one in scratch],
        compiler_params=pltpu.CompilerParams(vmem_limit_bytes=16 * 1024 * 1024),
        cost_estimate=pl.CostEstimate(flops=flops, bytes_accessed=4_000_000, transcendentals=0),
        name=name,
    )(*args)


def exchange(outgoing):
    arrived = []
    for (axis, far), message in zip(SWAPS, outgoing):
        size = lax.axis_size(axis)
        assert size % 2 == 0
        pairs = []
        for first in range(1 if far else 0, size, 2):
            second = (first + 1) % size
            pairs += [(first, second), (second, first)]
        arrived.append(lax.ppermute(message, axis, pairs))
    return arrived


def up_to(count, multiple):
    return -(-count // multiple) * multiple


def local(
    solution, stiffness, star_matrices, face_restrict, face_lift, orient_maps, flux_local, flux_remote,
    cluster_rate, send_list, neighbour_slot, neighbour_face, neighbour_turn,
):
    fields, elements = solution.shape[1], solution.shape[2]
    kinds = stiffness.shape[0]
    faces = face_restrict.shape[0]
    sides, sends = send_list.shape[1], send_list.shape[2]
    fast = sends // 2
    pairs = (fields + 1) // 2
    assert elements == 2 * ROWS and solution.shape[0] <= HALF
    values = jnp.transpose(solution, (1, 2, 0))
    star = jnp.transpose(star_matrices, (1, 2, 0, 3))
    local_part = jnp.transpose(flux_local, (1, 2, 0, 3))
    remote_part = jnp.transpose(flux_remote, (1, 2, 0, 3))
    restrict = jnp.transpose(face_restrict, (1, 0, 2))
    lift = jnp.transpose(face_lift, (2, 0, 1))

    packed = (fields, ROWS, LANES)
    first_shape = (up_to(pairs * (sends + fast), ROWS), LANES)
    second_shape = (up_to(pairs * fast, ROWS), LANES)
    work = (pairs, LANES, LANES)
    star_shape = (fields * fields * kinds, ROWS, LANES)
    combos = faces * HALF
    sources = elements + sides * sends

    waiting = (local_part, remote_part, restrict, lift, orient_maps, neighbour_slot, neighbour_face, neighbour_turn)
    made = call(
        predict_kernel,
        [HBM] * (4 + len(LATER)),
        [(packed, F32)] * 2 + [(first_shape, F32)] * sides + [
            (packed, F32), (star_shape, F32), ((3 * LANES, kinds * LANES), BF16), (stiffness.shape, F32),
        ] + [(array.shape, array.dtype) for array in waiting],
        [
            ((fields, up_to(4 * fields, ROWS), LANES), F32),
            ((pairs, elements, LANES), F32), ((pairs, elements, LANES), F32),
            (values.shape, F32), ((kinds, LANES, LANES), F32), (star.shape, F32),
            pltpu.SMEM(send_list.shape, jnp.int32), pltpu.SemaphoreType.DMA((4 + len(LATER),)),
        ],
        (values, stiffness, star, send_list, *waiting),
        "predict", 100_000_000,
    )
    early, late, outgoing = made[0], made[1], made[2 : 2 + sides]
    start, star_coef, derive_op, stiffness_kept = made[2 + sides : 6 + sides]
    waiting = made[6 + sides :]
    first = exchange(outgoing)
    (
        base, local_coef, remote_coef, volume_op, trace_op, local_lift, compose_op, remote_lift, choose, mask,
    ) = call(
        prepare_kernel,
        [VMEM] * 12,
        [
            (packed, F32), ((fields * fields, 2, ROWS, LANES), F32),
            ((faces * pairs * fields, elements, LANES), F32),
            ((3 * LANES, kinds * LANES), BF16), ((3 * LANES, 2 * LANES), BF16),
            ((6 * LANES, LANES), BF16), ((2 * LANES, combos), BF16), ((3 * faces * HALF, LANES), BF16),
            ((faces * elements, 2 * sources), BF16), ((faces * elements, combos), F32),
        ],
        [
            (work, F32), ((kinds, LANES, LANES), F32), ((2 * LANES, LANES), F32),
            ((LANES, faces * LANES), F32), ((HALF, LANES), F32), ((LANES, LANES), F32),
        ],
        (start, early, stiffness_kept, star_coef, *waiting),
        "prepare", 200_000_000,
    )
    middle, late_value, *outgoing = call(
        middle_kernel,
        [VMEM] * 10 + [HBM] * 2 + [VMEM] * 4,
        [(packed, F32)] * 2 + [(second_shape, F32)] * sides,
        [
            ((pairs, sources, LANES), F32), ((pairs, elements, LANES), F32),
            pltpu.SMEM(cluster_rate.shape, jnp.int32), pltpu.SMEM(send_list.shape, jnp.int32),
            pltpu.SemaphoreType.DMA((2,)),
        ],
        (
            base, early, late, star_coef, remote_coef, derive_op, compose_op, remote_lift, choose, mask,
            cluster_rate, send_list, *first,
        ),
        "middle", 200_000_000,
    )
    second = exchange(outgoing)
    (base,) = call(
        local_kernel,
        [VMEM] * 7,
        [(packed, F32)],
        [],
        (middle, late_value, star_coef, local_coef, volume_op, trace_op, local_lift),
        "local_late", 200_000_000,
    )
    (result,) = call(
        final_kernel,
        [VMEM] * 15,
        [(values.shape, F32)],
        [((pairs, sources, LANES), F32)],
        (base, late_value, remote_coef, compose_op, remote_lift, choose, mask, *first, *second),
        "final", 200_000_000,
    )
    return jnp.transpose(result, (2, 0, 1))


def solution(mesh):
    placed = (
        P(None, None, ("dom", "sub")),
        P(),
        P(None, None, None, ("dom", "sub")),
        P(),
        P(),
        P(),
        P(None, None, None, ("dom", "sub")),
        P(None, None, None, ("dom", "sub")),
        P(("dom", "sub")),
        P(("dom", "sub"), None, None),
        P(None, ("dom", "sub")),
        P(None, ("dom", "sub")),
        P(None, ("dom", "sub")),
    )
    return jax.shard_map(
        local, mesh=mesh, in_specs=placed, out_specs=P(None, None, ("dom", "sub")), check_vma=False
    )
```

```python
import math

import jax
import jax.numpy as jnp
from jax import lax
from jax.experimental import pallas as pl
from jax.experimental.pallas import tpu as pltpu
from jax.sharding import PartitionSpec as P

DERIVS = 6
LANES = 128
HALF = 64
ROWS = 8
F32 = jnp.float32
BF16 = jnp.bfloat16
LATER = ("flux_local", "flux_remote", "face_restrict", "face_lift", "orient_maps", "slot", "face", "turn")
AXES = ("dom", "sub")
SWAPS = (("dom", True), ("sub", True), ("sub", False), ("dom", False))


def taylor_weight(lower, upper, degree):
    return (upper ** (degree + 1) - lower ** (degree + 1)) / math.factorial(degree + 1)


def weight_at(lower, upper, degree):
    result = jnp.float32(taylor_weight(lower, upper, 1))
    for option in range(2, DERIVS):
        result = jnp.where(degree == option, jnp.float32(taylor_weight(lower, upper, option)), result)
    return result


def split(values):
    high = values.astype(BF16)
    low = (values - high.astype(F32)).astype(BF16)
    return high, low


def stack_left(values):
    high, low = split(values)
    return jnp.concatenate([high, low, high], axis=1)


def stack_right(values):
    high, low = split(values)
    return jnp.concatenate([high, high, low], axis=0)


def product(left, right):
    return jnp.dot(left, right, preferred_element_type=F32)


def odd_place(axis):
    return lax.rem(lax.axis_index(axis), 2)


def message_side(slot):
    axis, far = SWAPS[slot]
    odd = odd_place(axis)
    return 2 * AXES.index(axis) + (odd if far else 1 - odd)


def ghost_slot(side):
    axis = AXES[side // 2]
    even_far = side % 2 == 0
    return jnp.where(odd_place(axis) == 0, SWAPS.index((axis, even_far)), SWAPS.index((axis, not even_far)))


def lane_index(shape):
    return lax.broadcasted_iota(jnp.int32, shape, len(shape) - 1)


def lower_half(shape):
    return lane_index(shape) < HALF


def swap_halves(values):
    return pltpu.roll(values, HALF, values.ndim - 1)


def pack(values_ref, packed_ref):
    modes = values_ref.shape[2]
    packed_ref[...] = jnp.zeros(packed_ref.shape, F32)
    packed_ref[:, :, 0:modes] = values_ref[:, 0:ROWS, :]
    packed_ref[:, :, HALF : HALF + modes] = values_ref[:, ROWS : 2 * ROWS, :]


def high_and_low(values, shift):
    high = values.astype(BF16).astype(F32)
    return high + pltpu.roll(values - high, shift, 1)


def row_index(shape):
    return lax.broadcasted_iota(jnp.int32, shape, len(shape) - 2)


def one_where(condition):
    return jnp.where(condition, 1.0, 0.0)


def star_coefficients(star_ref, stage_ref, star_out):
    fields, kinds, elements = star_ref.shape[0], star_ref.shape[2], star_ref.shape[3]
    lanes = lane_index((ROWS, LANES))
    pick = one_where((lanes % ROWS == row_index((ROWS, LANES))) & (lanes < 2 * elements))
    from_lane = row_index((LANES, LANES))
    same_half = (from_lane % elements) // ROWS == lane_index((LANES, LANES)) // HALF
    right = one_where(same_half & (from_lane < 2 * elements)).astype(BF16)
    filled = lane_index(stage_ref.shape[1:]) < elements
    for row in range(fields):
        for col in range(fields):
            stage_ref[row, col * 4 : col * 4 + kinds, 0:elements] = star_ref[row, col]
        values = jnp.where(filled, stage_ref[row], 0.0)
        stage_ref[row] = high_and_low(values, elements)
        spreads = []
        for kind in range(kinds):
            for col in range(fields):
                at = col * 4 + kind
                spreads.append(stage_ref[row, at : at + 1, :] * pick)
        spread_out = product(jnp.concatenate(spreads, axis=0).astype(BF16), right)
        count = kinds * fields
        star_out[row * count : (row + 1) * count] = spread_out.reshape(count, ROWS, LANES)


def star_mix(columns, star_ref, fields, kinds):
    sums = [None] * fields
    for row in range(fields):
        for kind in range(kinds):
            part = columns[row * ROWS : (row + 1) * ROWS, kind * LANES : (kind + 1) * LANES]
            for col in range(fields):
                term = star_ref[(row * kinds + kind) * fields + col] * part
                sums[col] = term if sums[col] is None else sums[col] + term
    return jnp.concatenate(sums, axis=0)


def stiffness_blocks(stiffness_ref, block_ref, turned):
    kinds, modes = stiffness_ref.shape[0], stiffness_ref.shape[1]
    block_ref[...] = jnp.zeros(block_ref.shape, F32)
    for kind in range(kinds):
        matrix = -stiffness_ref[kind].T if turned else stiffness_ref[kind]
        block_ref[kind, 0:modes, 0:modes] = matrix
        block_ref[kind, HALF : HALF + modes, HALF : HALF + modes] = matrix
    return jnp.concatenate([block_ref[kind] for kind in range(kinds)], axis=1)


def predict_kernel(*refs):
    later = len(LATER)
    solution_hbm, stiffness_hbm, star_hbm, send_hbm = refs[0:4]
    later_hbm, refs = refs[4 : 4 + later], refs[4 + later :]
    early_out, late_out, send_0, send_1, send_2, send_3 = refs[0:6]
    packed_ref, coef_ref, derive_ref, stiffness_ref = refs[6:10]
    later_out, refs = refs[10 : 10 + later], refs[10 + later :]
    work_ref, early_rows, late_rows, solution_ref, block_ref, star_ref, send_ref, sems = refs

    sources = (star_hbm, stiffness_hbm, solution_hbm, send_hbm, *later_hbm)
    targets = (star_ref, stiffness_ref, solution_ref, send_ref, *later_out)
    copies = [
        pltpu.make_async_copy(source, target, sems.at[number])
        for number, (source, target) in enumerate(zip(sources, targets))
    ]
    for copy in copies:
        copy.start()
    fields, kinds = star_ref.shape[0], star_ref.shape[2]
    pairs = (fields + 1) // 2
    for copy in copies[0:3]:
        copy.wait()
    derive_ref[...] = stack_right(stiffness_blocks(stiffness_ref, block_ref, True))
    star_coefficients(star_ref, work_ref, coef_ref)
    pack(solution_ref, packed_ref)
    start = packed_ref[...].reshape(fields * ROWS, LANES)

    def step(degree, carry):
        current, early, late = carry
        current = star_mix(product(stack_left(current), derive_ref[...]), coef_ref, fields, kinds)
        early = early + weight_at(0.0, 0.5, degree) * current
        late = late + weight_at(0.5, 1.0, degree) * current
        return current, early, late

    _, early, late = lax.fori_loop(
        1, DERIVS, step, (start, taylor_weight(0.0, 0.5, 0) * start, taylor_weight(0.5, 1.0, 0) * start)
    )
    early_out[...] = early.reshape(fields, ROWS, LANES)
    late_out[...] = late.reshape(fields, ROWS, LANES)
    rows_by_pair(early, early_rows, fields)
    rows_by_pair(late, late_rows, fields)
    copies[3].wait()
    sends = send_ref.shape[2]
    fast = sends // 2
    for side, out in enumerate((send_0, send_1, send_2, send_3)):
        out[...] = jnp.zeros(out.shape, F32)
        for place in range(sends):
            element = send_ref[0, message_side(side), place]
            for pair in range(pairs):
                row = pair * sends + place
                out[row : row + 1, :] = early_rows[pair, pl.ds(element, 1), :]
            if place >= fast:
                for pair in range(pairs):
                    row = pairs * sends + pair * fast + place - fast
                    out[row : row + 1, :] = late_rows[pair, pl.ds(element, 1), :]
    for copy in copies[4:]:
        copy.wait()


def rows_by_pair(packed, out_ref, fields):
    lower = lower_half((ROWS, LANES))
    for pair in range((fields + 1) // 2):
        even = packed[2 * pair * ROWS : (2 * pair + 1) * ROWS]
        odd = jnp.zeros_like(even)
        if 2 * pair + 1 < fields:
            odd = packed[(2 * pair + 1) * ROWS : (2 * pair + 2) * ROWS]
        out_ref[pair, 0:ROWS, :] = jnp.where(lower, even, swap_halves(odd))
        out_ref[pair, ROWS : 2 * ROWS, :] = jnp.where(lower, swap_halves(even), odd)


def flux_local_coefficients(flux_ref, stage_ref, out_ref):
    fields, faces, elements = flux_ref.shape[0], flux_ref.shape[2], flux_ref.shape[3]
    rows = 2 * ROWS
    filled = lane_index((rows, LANES)) < elements
    lanes, sublanes = lane_index((ROWS, LANES)), row_index((ROWS, LANES))
    picks = [one_where(lanes % elements == half * ROWS + sublanes) for half in range(2)]
    square = (LANES, LANES)
    right = one_where(row_index(square) // (2 * elements) == lane_index(square) % faces).astype(BF16)
    for row in range(fields):
        values = None
        for face in range(faces):
            stage_ref[row, face * rows : face * rows + fields, 0:elements] = flux_ref[row, :, face, :]
            part = jnp.where(filled, stage_ref[row, face * rows : (face + 1) * rows, :], 0.0)
            values = part if values is None else values + pltpu.roll(part, face * 2 * elements, 1)
        stage_ref[row, 0:rows, :] = high_and_low(values, elements)
        left = [stage_ref[row, col : col + 1, :] * pick for col in range(fields) for pick in picks]
        spread = product(jnp.concatenate(left, axis=0).astype(BF16), right)
        out_ref[row * fields : (row + 1) * fields] = spread.reshape(fields, 2, ROWS, LANES)


def flux_remote_coefficients(flux_ref, stage_ref, out_ref):
    fields, faces, elements = flux_ref.shape[0], flux_ref.shape[2], flux_ref.shape[3]
    pairs = (fields + 1) // 2
    rows = stage_ref.shape[1] // 2
    filled = lane_index((rows, LANES)) < elements
    lanes, sublanes = lane_index((elements, LANES)), row_index((elements, LANES))
    pick = one_where((lanes % elements == sublanes) & (lanes < 4 * elements))
    square = (LANES, LANES)
    from_lane = row_index(square)
    same_parity = (from_lane // elements) % 2 == lane_index(square) // HALF
    right = one_where(same_parity & (from_lane < 4 * elements)).astype(BF16)
    for pair in range(pairs):
        values = None
        for row in range(2 * pair, min(2 * pair + 2, fields)):
            start = (row % 2) * rows
            for col in range(fields):
                at = start + col * faces
                stage_ref[pair, at : at + faces, 0:elements] = flux_ref[row, col]
            part = jnp.where(filled, stage_ref[pair, start : start + rows, :], 0.0)
            values = part if values is None else values + pltpu.roll(part, elements, 1)
        stage_ref[pair, 0:rows, :] = high_and_low(values, 2 * elements)
        for face in range(faces):
            left = []
            for col in range(fields):
                at = col * faces + face
                left.append(stage_ref[pair, at : at + 1, :] * pick)
            spread = product(jnp.concatenate(left, axis=0).astype(BF16), right)
            at = (face * pairs + pair) * fields
            out_ref[at : at + fields] = spread.reshape(fields, elements, LANES)


def local_terms(packed, star_ref, flux_ref, volume_ref, trace_ref, lift_ref, fields, kinds):
    left = stack_left(packed)
    volume = star_mix(product(left, volume_ref[...]), star_ref, fields, kinds)
    traces = product(left, trace_ref[...])
    sums = []
    for col in range(fields):
        halves = []
        for half in range(2):
            total = None
            for row in range(fields):
                part = traces[row * ROWS : (row + 1) * ROWS, half * LANES : (half + 1) * LANES]
                term = flux_ref[row * fields + col, half] * part
                total = term if total is None else total + term
            halves.append(total)
        sums.append(jnp.concatenate(halves, axis=1))
    return volume + product(stack_left(jnp.concatenate(sums, axis=0)), lift_ref[...])


def prepare_kernel(
    packed_ref, early_ref, stiffness_ref, star_ref, flux_local_ref, flux_remote_ref, restrict_ref, lift_ref, orient_ref,
    slot_ref, face_ref, turn_ref,
    base_out, local_out, remote_out, volume_out, trace_out, local_lift_out, compose_out,
    remote_lift_out, choose_out, mask_out,
    local_work_ref, remote_work_ref, block_ref, wide_ref, face_work_ref, orient_work_ref, code_ref,
):
    fields, kinds = packed_ref.shape[0], stiffness_ref.shape[0]
    face_modes, faces, modes = restrict_ref.shape
    turns = orient_ref.shape[0]
    flux_local_coefficients(flux_local_ref, local_work_ref, local_out)
    flux_remote_coefficients(flux_remote_ref, remote_work_ref, remote_out)

    volume_out[...] = stack_right(stiffness_blocks(stiffness_ref, block_ref, False))

    wide_ref[...] = jnp.zeros(wide_ref.shape, F32)
    for mode in range(face_modes):
        at = mode * faces
        wide_ref[at : at + faces, 0:modes] = restrict_ref[mode]
        wide_ref[LANES + at : LANES + at + faces, HALF : HALF + modes] = restrict_ref[mode]
    trace_out[...] = stack_right(wide_ref[...].T)
    for mode in range(face_modes):
        at = mode * faces
        wide_ref[at : at + faces, 0:modes] = -lift_ref[mode]
        wide_ref[LANES + at : LANES + at + faces, HALF : HALF + modes] = -lift_ref[mode]
    local_lift_out[...] = stack_right(wide_ref[...])

    face_work_ref[...] = jnp.zeros(face_work_ref.shape, F32)
    orient_work_ref[...] = jnp.zeros(orient_work_ref.shape, F32)
    for turn in range(turns):
        orient_work_ref[turn * face_modes : (turn + 1) * face_modes, 0:face_modes] = orient_ref[turn]
    for face in range(faces):
        face_work_ref[0:face_modes, face * LANES : face * LANES + modes] = restrict_ref[:, face, :]
        face_work_ref[0:face_modes, face * LANES + HALF : face * LANES + HALF + modes] = restrict_ref[:, face, :]
    composed = jnp.dot(
        orient_work_ref[...], face_work_ref[...], precision=lax.Precision.HIGHEST, preferred_element_type=F32
    )
    stacked = jnp.concatenate([composed[:, face * LANES : (face + 1) * LANES] for face in range(faces)], axis=0)
    high, low = split(stacked.T[0:HALF])
    compose_out[...] = jnp.concatenate([high, high, low, jnp.zeros_like(low)], axis=0)
    wide_ref[...] = jnp.zeros(wide_ref.shape, F32)
    for face in range(faces):
        for turn in range(turns):
            rows = slice(face * HALF + turn * face_modes, face * HALF + (turn + 1) * face_modes)
            wide_ref[rows, 0:modes] = -lift_ref[:, face, :]
            wide_ref[rows, HALF : HALF + modes] = -lift_ref[:, face, :]
    remote_lift_out[...] = stack_right(wide_ref[...])

    elements = slot_ref.shape[1]
    code_ref[...] = jnp.zeros(code_ref.shape, F32)
    slots = slot_ref[...]
    sends = (choose_out.shape[1] // 2 - elements) // 4
    group = (slots - elements) // sends
    moved = slots
    for side in range(4):
        moved = jnp.where(group == side, slots + (ghost_slot(side) - side) * sends, moved)
    code_ref[0:faces, 0:elements] = jnp.where(slots < elements, slots, moved).astype(F32)
    code_ref[faces : 2 * faces, 0:elements] = (face_ref[...] * turns + turn_ref[...]).astype(F32)
    codes = code_ref[...].T[0:elements, :]
    sources = choose_out.shape[1] // 2
    source_lane = (lane_index((elements, 2 * sources)) % sources).astype(F32)
    lanes = lane_index((elements, mask_out.shape[1]))
    in_face = lanes % HALF
    lane_code = jnp.where(in_face < turns * face_modes, (lanes // HALF) * turns + in_face // face_modes, -1)
    lane_code = lane_code.astype(F32)
    picks, masks = [], []
    for face in range(faces):
        picks.append(jnp.where(codes[:, face : face + 1] == source_lane, 1.0, 0.0))
        masks.append(jnp.where(codes[:, faces + face : faces + face + 1] == lane_code, 1.0, 0.0))
    choose_out[...] = jnp.concatenate(picks, axis=0).astype(BF16)
    mask_out[...] = jnp.concatenate(masks, axis=0)

    early = early_ref[...].reshape(fields * ROWS, LANES)
    terms = local_terms(early, star_ref, local_out, volume_out, trace_out, local_lift_out, fields, kinds)
    base_out[...] = packed_ref[...] + terms.reshape(fields, ROWS, LANES)


def remote_terms(rows_ref, remote_ref, compose_ref, lift_ref, choose_ref, mask_ref, fields):
    pairs = rows_ref.shape[0]
    faces = lift_ref.shape[0] // (3 * HALF)
    elements = choose_ref.shape[0] // faces
    sources = jnp.concatenate([rows_ref[pair] for pair in range(pairs)], axis=1)
    gathered = product(choose_ref[...], jnp.concatenate(split(sources), axis=0))
    folded = []
    for face in range(faces):
        sums = []
        for col in range(fields):
            total = None
            for pair in range(pairs):
                part = gathered[face * elements : (face + 1) * elements, pair * LANES : (pair + 1) * LANES]
                term = remote_ref[(face * pairs + pair) * fields + col] * part
                total = term if total is None else total + term
            sums.append(total)
        mixed = jnp.concatenate(sums, axis=0)
        high, low = split(mixed + swap_halves(mixed))
        first = jnp.where(lower_half(high.shape), high, low)
        turned = product(jnp.concatenate([first, high], axis=1), compose_ref[...])
        mask = mask_ref[face * elements : (face + 1) * elements, :]
        chosen = (turned.reshape(fields, elements, turned.shape[1]) * mask[None]).reshape(turned.shape)
        both = chosen[:, 0:LANES] + chosen[:, LANES : 2 * LANES]
        folded.append(both + swap_halves(both))
    lower = lower_half(folded[0].shape)
    left = [jnp.where(lower, folded[face], folded[face + 1]) for face in range(0, faces, 2)]
    result = product(stack_left(jnp.concatenate(left, axis=1)), lift_ref[...])
    result = result.reshape(fields, 2, ROWS, LANES)
    return jnp.where(lower_half((ROWS, LANES))[None], result[:, 0], result[:, 1])


def middle_kernel(
    base_ref, early_ref, late_ref, star_ref, remote_ref, derive_ref, compose_ref, lift_ref, choose_ref, mask_ref,
    rate_hbm, send_hbm, from_0, from_1, from_2, from_3,
    middle_out, late_out, send_0, send_1, send_2, send_3,
    rows_ref, late_rows, rate_ref, send_ref, sems,
):
    copies = [
        pltpu.make_async_copy(rate_hbm, rate_ref, sems.at[0]),
        pltpu.make_async_copy(send_hbm, send_ref, sems.at[1]),
    ]
    for copy in copies:
        copy.start()
    fields = base_ref.shape[0]
    kinds = star_ref.shape[0] // (fields * fields)
    pairs = rows_ref.shape[0]
    sends = send_ref.shape[2]
    fast = sends // 2
    elements = 2 * ROWS
    rows_by_pair(early_ref[...].reshape(fields * ROWS, LANES), rows_ref, fields)
    for side, arrived in enumerate((from_0, from_1, from_2, from_3)):
        at = elements + side * sends
        for pair in range(pairs):
            rows_ref[pair, at : at + sends, :] = arrived[pair * sends : (pair + 1) * sends, :]
    middle = base_ref[...] + remote_terms(
        rows_ref, remote_ref, compose_ref, lift_ref, choose_ref, mask_ref, fields
    )
    middle_out[...] = middle
    start = middle.reshape(fields * ROWS, LANES)

    def step(degree, carry):
        current, early = carry
        current = star_mix(product(stack_left(current), derive_ref[...]), star_ref, fields, kinds)
        return current, early + weight_at(0.0, 0.5, degree) * current

    _, restart = lax.fori_loop(1, DERIVS, step, (start, taylor_weight(0.0, 0.5, 0) * start))
    for copy in copies:
        copy.wait()
    sublane = lax.broadcasted_iota(jnp.int32, (ROWS, LANES), 0)
    lower = lower_half((ROWS, LANES))
    is_fast = jnp.zeros((ROWS, LANES), jnp.int32)
    for element in range(elements):
        here = (sublane == element % ROWS) & (lower if element < ROWS else jnp.logical_not(lower))
        is_fast = jnp.where(here, rate_ref[element], is_fast)
    late = jnp.where((is_fast == 2)[None], restart.reshape(fields, ROWS, LANES), late_ref[...])
    late_out[...] = late
    rows_by_pair(late.reshape(fields * ROWS, LANES), late_rows, fields)
    for side, out in enumerate((send_0, send_1, send_2, send_3)):
        out[...] = jnp.zeros(out.shape, F32)
        for place in range(fast):
            element = send_ref[0, message_side(side), place]
            for pair in range(pairs):
                row = pair * fast + place
                out[row : row + 1, :] = late_rows[pair, pl.ds(element, 1), :]


def local_kernel(middle_ref, late_ref, star_ref, flux_ref, volume_ref, trace_ref, lift_ref, base_out):
    fields = middle_ref.shape[0]
    kinds = star_ref.shape[0] // (fields * fields)
    late = late_ref[...].reshape(fields * ROWS, LANES)
    terms = local_terms(late, star_ref, flux_ref, volume_ref, trace_ref, lift_ref, fields, kinds)
    base_out[...] = middle_ref[...] + terms.reshape(fields, ROWS, LANES)


def final_kernel(
    base_ref, late_ref, remote_ref, compose_ref, lift_ref, choose_ref, mask_ref,
    first_0, first_1, first_2, first_3,
    second_0, second_1, second_2, second_3,
    result_out, rows_ref,
):
    fields = base_ref.shape[0]
    modes = result_out.shape[2]
    pairs = rows_ref.shape[0]
    elements = 2 * ROWS
    sends = (rows_ref.shape[1] - elements) // 4
    fast = sends // 2
    rows_by_pair(late_ref[...].reshape(fields * ROWS, LANES), rows_ref, fields)
    firsts = (first_0, first_1, first_2, first_3)
    seconds = (second_0, second_1, second_2, second_3)
    for side, (first, second) in enumerate(zip(firsts, seconds)):
        at = elements + side * sends
        for pair in range(pairs):
            rows_ref[pair, at : at + fast, :] = second[pair * fast : (pair + 1) * fast, :]
            row = pairs * sends + pair * fast
            rows_ref[pair, at + fast : at + sends, :] = first[row : row + fast, :]
    result = base_ref[...] + remote_terms(
        rows_ref, remote_ref, compose_ref, lift_ref, choose_ref, mask_ref, fields
    )
    result_out[:, 0:ROWS, :] = result[:, :, 0:modes]
    result_out[:, ROWS : 2 * ROWS, :] = result[:, :, HALF : HALF + modes]


VMEM = pl.BlockSpec(memory_space=pltpu.VMEM)
HBM = pl.BlockSpec(memory_space=pltpu.HBM)


def call(kernel, ins, outs, scratch, args, name, flops):
    shapes = [jax.ShapeDtypeStruct(shape, dtype) for shape, dtype in outs]
    args = [
        pltpu.with_memory_space_constraint(arg, pltpu.HBM) if spec is HBM else arg for spec, arg in zip(ins, args)
    ]
    return pl.pallas_call(
        kernel,
        out_shape=shapes,
        in_specs=ins,
        out_specs=[VMEM] * len(outs),
        scratch_shapes=[pltpu.VMEM(*one) if isinstance(one, tuple) else one for one in scratch],
        compiler_params=pltpu.CompilerParams(vmem_limit_bytes=16 * 1024 * 1024),
        cost_estimate=pl.CostEstimate(flops=flops, bytes_accessed=4_000_000, transcendentals=0),
        name=name,
    )(*args)


def exchange(outgoing):
    arrived = []
    for (axis, far), message in zip(SWAPS, outgoing):
        size = lax.axis_size(axis)
        assert size % 2 == 0
        pairs = []
        for first in range(1 if far else 0, size, 2):
            second = (first + 1) % size
            pairs += [(first, second), (second, first)]
        arrived.append(lax.ppermute(message, axis, pairs))
    return arrived


def up_to(count, multiple):
    return -(-count // multiple) * multiple


def local(
    solution, stiffness, star_matrices, face_restrict, face_lift, orient_maps, flux_local, flux_remote,
    cluster_rate, send_list, neighbour_slot, neighbour_face, neighbour_turn,
):
    fields, elements = solution.shape[1], solution.shape[2]
    kinds = stiffness.shape[0]
    faces = face_restrict.shape[0]
    sides, sends = send_list.shape[1], send_list.shape[2]
    fast = sends // 2
    pairs = (fields + 1) // 2
    assert elements == 2 * ROWS and solution.shape[0] <= HALF
    values = jnp.transpose(solution, (1, 2, 0))
    star = jnp.transpose(star_matrices, (1, 2, 0, 3))
    local_part = jnp.transpose(flux_local, (1, 2, 0, 3))
    remote_part = jnp.transpose(flux_remote, (1, 2, 0, 3))
    restrict = jnp.transpose(face_restrict, (1, 0, 2))
    lift = jnp.transpose(face_lift, (2, 0, 1))

    packed = (fields, ROWS, LANES)
    first_shape = (up_to(pairs * (sends + fast), ROWS), LANES)
    second_shape = (up_to(pairs * fast, ROWS), LANES)
    star_shape = (fields * fields * kinds, ROWS, LANES)
    combos = faces * HALF
    sources = elements + sides * sends

    waiting = (local_part, remote_part, restrict, lift, orient_maps, neighbour_slot, neighbour_face, neighbour_turn)
    made = call(
        predict_kernel,
        [HBM] * (4 + len(LATER)),
        [(packed, F32)] * 2 + [(first_shape, F32)] * sides + [
            (packed, F32), (star_shape, F32), ((3 * LANES, kinds * LANES), BF16), (stiffness.shape, F32),
        ] + [(array.shape, array.dtype) for array in waiting],
        [
            ((fields, up_to(4 * fields, ROWS), LANES), F32),
            ((pairs, elements, LANES), F32), ((pairs, elements, LANES), F32),
            (values.shape, F32), ((kinds, LANES, LANES), F32), (star.shape, F32),
            pltpu.SMEM(send_list.shape, jnp.int32), pltpu.SemaphoreType.DMA((4 + len(LATER),)),
        ],
        (values, stiffness, star, send_list, *waiting),
        "predict", 100_000_000,
    )
    early, late, outgoing = made[0], made[1], made[2 : 2 + sides]
    start, star_coef, derive_op, stiffness_kept = made[2 + sides : 6 + sides]
    waiting = made[6 + sides :]
    first = exchange(outgoing)
    (
        base, local_coef, remote_coef, volume_op, trace_op, local_lift, compose_op, remote_lift, choose, mask,
    ) = call(
        prepare_kernel,
        [VMEM] * 12,
        [
            (packed, F32), ((fields * fields, 2, ROWS, LANES), F32),
            ((faces * pairs * fields, elements, LANES), F32),
            ((3 * LANES, kinds * LANES), BF16), ((3 * LANES, 2 * LANES), BF16),
            ((6 * LANES, LANES), BF16), ((2 * LANES, combos), BF16), ((3 * faces * HALF, LANES), BF16),
            ((faces * elements, 2 * sources), BF16), ((faces * elements, combos), F32),
        ],
        [
            ((fields, 2 * ROWS * faces, LANES), F32), ((pairs, 2 * up_to(4 * fields, ROWS), LANES), F32),
            ((kinds, LANES, LANES), F32), ((2 * LANES, LANES), F32),
            ((LANES, faces * LANES), F32), ((HALF, LANES), F32), ((LANES, LANES), F32),
        ],
        (start, early, stiffness_kept, star_coef, *waiting),
        "prepare", 200_000_000,
    )
    middle, late_value, *outgoing = call(
        middle_kernel,
        [VMEM] * 10 + [HBM] * 2 + [VMEM] * 4,
        [(packed, F32)] * 2 + [(second_shape, F32)] * sides,
        [
            ((pairs, sources, LANES), F32), ((pairs, elements, LANES), F32),
            pltpu.SMEM(cluster_rate.shape, jnp.int32), pltpu.SMEM(send_list.shape, jnp.int32),
            pltpu.SemaphoreType.DMA((2,)),
        ],
        (
            base, early, late, star_coef, remote_coef, derive_op, compose_op, remote_lift, choose, mask,
            cluster_rate, send_list, *first,
        ),
        "middle", 200_000_000,
    )
    second = exchange(outgoing)
    (base,) = call(
        local_kernel,
        [VMEM] * 7,
        [(packed, F32)],
        [],
        (middle, late_value, star_coef, local_coef, volume_op, trace_op, local_lift),
        "local_late", 200_000_000,
    )
    (result,) = call(
        final_kernel,
        [VMEM] * 15,
        [(values.shape, F32)],
        [((pairs, sources, LANES), F32)],
        (base, late_value, remote_coef, compose_op, remote_lift, choose, mask, *first, *second),
        "final", 200_000_000,
    )
    return jnp.transpose(result, (2, 0, 1))


def solution(mesh):
    placed = (
        P(None, None, ("dom", "sub")),
        P(),
        P(None, None, None, ("dom", "sub")),
        P(),
        P(),
        P(),
        P(None, None, None, ("dom", "sub")),
        P(None, None, None, ("dom", "sub")),
        P(("dom", "sub")),
        P(("dom", "sub"), None, None),
        P(None, ("dom", "sub")),
        P(None, ("dom", "sub")),
        P(None, ("dom", "sub")),
    )
    return jax.shard_map(
        local, mesh=mesh, in_specs=placed, out_specs=P(None, None, ("dom", "sub")), check_vma=False
    )
```

```python
import math

import jax
import jax.numpy as jnp
from jax import lax
from jax.experimental import pallas as pl
from jax.experimental.pallas import tpu as pltpu
from jax.sharding import PartitionSpec as P

DERIVS = 6
LANES = 128
HALF = 64
ROWS = 8
F32 = jnp.float32
BF16 = jnp.bfloat16
LATER = ("flux_local", "flux_remote", "face_restrict", "face_lift", "orient_maps", "slot", "face", "turn")
AXES = ("dom", "sub")
SWAPS = (("dom", True), ("dom", False), ("sub", True), ("sub", False))


def taylor_weight(lower, upper, degree):
    return (upper ** (degree + 1) - lower ** (degree + 1)) / math.factorial(degree + 1)


def weight_at(lower, upper, degree):
    result = jnp.float32(taylor_weight(lower, upper, 1))
    for option in range(2, DERIVS):
        result = jnp.where(degree == option, jnp.float32(taylor_weight(lower, upper, option)), result)
    return result


def split(values):
    high = values.astype(BF16)
    low = (values - high.astype(F32)).astype(BF16)
    return high, low


def stack_left(values):
    high, low = split(values)
    return jnp.concatenate([high, low, high], axis=1)


def stack_right(values):
    high, low = split(values)
    return jnp.concatenate([high, high, low], axis=0)


def product(left, right):
    return jnp.dot(left, right, preferred_element_type=F32)


def odd_place(axis):
    return lax.rem(lax.axis_index(axis), 2)


def message_side(slot):
    axis, far = SWAPS[slot]
    odd = odd_place(axis)
    return 2 * AXES.index(axis) + (odd if far else 1 - odd)


def ghost_slot(side):
    axis = AXES[side // 2]
    even_far = side % 2 == 0
    return jnp.where(odd_place(axis) == 0, SWAPS.index((axis, even_far)), SWAPS.index((axis, not even_far)))


def lane_index(shape):
    return lax.broadcasted_iota(jnp.int32, shape, len(shape) - 1)


def lower_half(shape):
    return lane_index(shape) < HALF


def swap_halves(values):
    return pltpu.roll(values, HALF, values.ndim - 1)


def pack(values_ref, packed_ref):
    modes = values_ref.shape[2]
    packed_ref[...] = jnp.zeros(packed_ref.shape, F32)
    packed_ref[:, :, 0:modes] = values_ref[:, 0:ROWS, :]
    packed_ref[:, :, HALF : HALF + modes] = values_ref[:, ROWS : 2 * ROWS, :]


def high_and_low(values, shift):
    high = values.astype(BF16).astype(F32)
    return high + pltpu.roll(values - high, shift, 1)


def row_index(shape):
    return lax.broadcasted_iota(jnp.int32, shape, len(shape) - 2)


def one_where(condition):
    return jnp.where(condition, 1.0, 0.0)


def star_coefficients(star_ref, stage_ref, star_out):
    fields, kinds, elements = star_ref.shape[0], star_ref.shape[2], star_ref.shape[3]
    lanes = lane_index((ROWS, LANES))
    pick = one_where((lanes % ROWS == row_index((ROWS, LANES))) & (lanes < 2 * elements))
    from_lane = row_index((LANES, LANES))
    same_half = (from_lane % elements) // ROWS == lane_index((LANES, LANES)) // HALF
    right = one_where(same_half & (from_lane < 2 * elements)).astype(BF16)
    filled = lane_index(stage_ref.shape[1:]) < elements
    for row in range(fields):
        for col in range(fields):
            stage_ref[row, col * 4 : col * 4 + kinds, 0:elements] = star_ref[row, col]
        values = jnp.where(filled, stage_ref[row], 0.0)
        stage_ref[row] = high_and_low(values, elements)
        spreads = []
        for kind in range(kinds):
            for col in range(fields):
                at = col * 4 + kind
                spreads.append(stage_ref[row, at : at + 1, :] * pick)
        spread_out = product(jnp.concatenate(spreads, axis=0).astype(BF16), right)
        count = kinds * fields
        star_out[row * count : (row + 1) * count] = spread_out.reshape(count, ROWS, LANES)


def star_mix(columns, star_ref, fields, kinds):
    sums = [None] * fields
    for row in range(fields):
        for kind in range(kinds):
            part = columns[row * ROWS : (row + 1) * ROWS, kind * LANES : (kind + 1) * LANES]
            for col in range(fields):
                term = star_ref[(row * kinds + kind) * fields + col] * part
                sums[col] = term if sums[col] is None else sums[col] + term
    return jnp.concatenate(sums, axis=0)


def stiffness_blocks(stiffness_ref, block_ref, turned):
    kinds, modes = stiffness_ref.shape[0], stiffness_ref.shape[1]
    block_ref[...] = jnp.zeros(block_ref.shape, F32)
    for kind in range(kinds):
        matrix = -stiffness_ref[kind].T if turned else stiffness_ref[kind]
        block_ref[kind, 0:modes, 0:modes] = matrix
        block_ref[kind, HALF : HALF + modes, HALF : HALF + modes] = matrix
    return jnp.concatenate([block_ref[kind] for kind in range(kinds)], axis=1)


def predict_kernel(*refs):
    later = len(LATER)
    solution_hbm, stiffness_hbm, star_hbm, send_hbm = refs[0:4]
    later_hbm, refs = refs[4 : 4 + later], refs[4 + later :]
    early_out, late_out, send_0, send_1, send_2, send_3 = refs[0:6]
    packed_ref, coef_ref, derive_ref, stiffness_ref = refs[6:10]
    later_out, refs = refs[10 : 10 + later], refs[10 + later :]
    work_ref, early_rows, late_rows, solution_ref, block_ref, star_ref, send_ref, sems = refs

    sources = (star_hbm, stiffness_hbm, solution_hbm, send_hbm, *later_hbm)
    targets = (star_ref, stiffness_ref, solution_ref, send_ref, *later_out)
    copies = [
        pltpu.make_async_copy(source, target, sems.at[number])
        for number, (source, target) in enumerate(zip(sources, targets))
    ]
    for copy in copies:
        copy.start()
    fields, kinds = star_ref.shape[0], star_ref.shape[2]
    pairs = (fields + 1) // 2
    for copy in copies[0:3]:
        copy.wait()
    derive_ref[...] = stack_right(stiffness_blocks(stiffness_ref, block_ref, True))
    star_coefficients(star_ref, work_ref, coef_ref)
    pack(solution_ref, packed_ref)
    start = packed_ref[...].reshape(fields * ROWS, LANES)

    def step(degree, carry):
        current, early, late = carry
        current = star_mix(product(stack_left(current), derive_ref[...]), coef_ref, fields, kinds)
        early = early + weight_at(0.0, 0.5, degree) * current
        late = late + weight_at(0.5, 1.0, degree) * current
        return current, early, late

    _, early, late = lax.fori_loop(
        1, DERIVS, step, (start, taylor_weight(0.0, 0.5, 0) * start, taylor_weight(0.5, 1.0, 0) * start)
    )
    early_out[...] = early.reshape(fields, ROWS, LANES)
    late_out[...] = late.reshape(fields, ROWS, LANES)
    rows_by_pair(early, early_rows, fields)
    rows_by_pair(late, late_rows, fields)
    copies[3].wait()
    sends = send_ref.shape[2]
    fast = sends // 2
    for side, out in enumerate((send_0, send_1, send_2, send_3)):
        out[...] = jnp.zeros(out.shape, F32)
        for place in range(sends):
            element = send_ref[0, message_side(side), place]
            for pair in range(pairs):
                row = pair * sends + place
                out[row : row + 1, :] = early_rows[pair, pl.ds(element, 1), :]
            if place >= fast:
                for pair in range(pairs):
                    row = pairs * sends + pair * fast + place - fast
                    out[row : row + 1, :] = late_rows[pair, pl.ds(element, 1), :]
    for copy in copies[4:]:
        copy.wait()


def rows_by_pair(packed, out_ref, fields):
    lower = lower_half((ROWS, LANES))
    for pair in range((fields + 1) // 2):
        even = packed[2 * pair * ROWS : (2 * pair + 1) * ROWS]
        odd = jnp.zeros_like(even)
        if 2 * pair + 1 < fields:
            odd = packed[(2 * pair + 1) * ROWS : (2 * pair + 2) * ROWS]
        out_ref[pair, 0:ROWS, :] = jnp.where(lower, even, swap_halves(odd))
        out_ref[pair, ROWS : 2 * ROWS, :] = jnp.where(lower, swap_halves(even), odd)


def flux_local_coefficients(flux_ref, stage_ref, out_ref):
    fields, faces, elements = flux_ref.shape[0], flux_ref.shape[2], flux_ref.shape[3]
    rows = 2 * ROWS
    filled = lane_index((rows, LANES)) < elements
    lanes, sublanes = lane_index((ROWS, LANES)), row_index((ROWS, LANES))
    picks = [one_where(lanes % elements == half * ROWS + sublanes) for half in range(2)]
    square = (LANES, LANES)
    right = one_where(row_index(square) // (2 * elements) == lane_index(square) % faces).astype(BF16)
    for row in range(fields):
        values = None
        for face in range(faces):
            stage_ref[row, face * rows : face * rows + fields, 0:elements] = flux_ref[row, :, face, :]
            part = jnp.where(filled, stage_ref[row, face * rows : (face + 1) * rows, :], 0.0)
            values = part if values is None else values + pltpu.roll(part, face * 2 * elements, 1)
        stage_ref[row, 0:rows, :] = high_and_low(values, elements)
        left = [stage_ref[row, col : col + 1, :] * pick for col in range(fields) for pick in picks]
        spread = product(jnp.concatenate(left, axis=0).astype(BF16), right)
        out_ref[row * fields : (row + 1) * fields] = spread.reshape(fields, 2, ROWS, LANES)


def flux_remote_coefficients(flux_ref, stage_ref, out_ref):
    fields, faces, elements = flux_ref.shape[0], flux_ref.shape[2], flux_ref.shape[3]
    pairs = (fields + 1) // 2
    rows = stage_ref.shape[1] // 2
    filled = lane_index((rows, LANES)) < elements
    lanes, sublanes = lane_index((elements, LANES)), row_index((elements, LANES))
    pick = one_where((lanes % elements == sublanes) & (lanes < 4 * elements))
    square = (LANES, LANES)
    from_lane = row_index(square)
    same_parity = (from_lane // elements) % 2 == lane_index(square) // HALF
    right = one_where(same_parity & (from_lane < 4 * elements)).astype(BF16)
    for pair in range(pairs):
        values = None
        for row in range(2 * pair, min(2 * pair + 2, fields)):
            start = (row % 2) * rows
            for col in range(fields):
                at = start + col * faces
                stage_ref[pair, at : at + faces, 0:elements] = flux_ref[row, col]
            part = jnp.where(filled, stage_ref[pair, start : start + rows, :], 0.0)
            values = part if values is None else values + pltpu.roll(part, elements, 1)
        stage_ref[pair, 0:rows, :] = high_and_low(values, 2 * elements)
        for face in range(faces):
            left = []
            for col in range(fields):
                at = col * faces + face
                left.append(stage_ref[pair, at : at + 1, :] * pick)
            spread = product(jnp.concatenate(left, axis=0).astype(BF16), right)
            at = (face * pairs + pair) * fields
            out_ref[at : at + fields] = spread.reshape(fields, elements, LANES)


def local_terms(packed, star_ref, flux_ref, volume_ref, trace_ref, lift_ref, fields, kinds):
    left = stack_left(packed)
    volume = star_mix(product(left, volume_ref[...]), star_ref, fields, kinds)
    traces = product(left, trace_ref[...])
    sums = []
    for col in range(fields):
        halves = []
        for half in range(2):
            total = None
            for row in range(fields):
                part = traces[row * ROWS : (row + 1) * ROWS, half * LANES : (half + 1) * LANES]
                term = flux_ref[row * fields + col, half] * part
                total = term if total is None else total + term
            halves.append(total)
        sums.append(jnp.concatenate(halves, axis=1))
    return volume + product(stack_left(jnp.concatenate(sums, axis=0)), lift_ref[...])


def prepare_kernel(
    packed_ref, early_ref, stiffness_ref, star_ref, flux_local_ref, flux_remote_ref, restrict_ref, lift_ref, orient_ref,
    slot_ref, face_ref, turn_ref,
    base_out, local_out, remote_out, volume_out, trace_out, local_lift_out, compose_out,
    remote_lift_out, choose_out, mask_out,
    local_work_ref, remote_work_ref, block_ref, wide_ref, face_work_ref, orient_work_ref, code_ref,
):
    fields, kinds = packed_ref.shape[0], stiffness_ref.shape[0]
    face_modes, faces, modes = restrict_ref.shape
    turns = orient_ref.shape[0]
    flux_local_coefficients(flux_local_ref, local_work_ref, local_out)
    flux_remote_coefficients(flux_remote_ref, remote_work_ref, remote_out)

    volume_out[...] = stack_right(stiffness_blocks(stiffness_ref, block_ref, False))

    wide_ref[...] = jnp.zeros(wide_ref.shape, F32)
    for mode in range(face_modes):
        at = mode * faces
        wide_ref[at : at + faces, 0:modes] = restrict_ref[mode]
        wide_ref[LANES + at : LANES + at + faces, HALF : HALF + modes] = restrict_ref[mode]
    trace_out[...] = stack_right(wide_ref[...].T)
    for mode in range(face_modes):
        at = mode * faces
        wide_ref[at : at + faces, 0:modes] = -lift_ref[mode]
        wide_ref[LANES + at : LANES + at + faces, HALF : HALF + modes] = -lift_ref[mode]
    local_lift_out[...] = stack_right(wide_ref[...])

    face_work_ref[...] = jnp.zeros(face_work_ref.shape, F32)
    orient_work_ref[...] = jnp.zeros(orient_work_ref.shape, F32)
    for turn in range(turns):
        orient_work_ref[turn * face_modes : (turn + 1) * face_modes, 0:face_modes] = orient_ref[turn]
    for face in range(faces):
        face_work_ref[0:face_modes, face * LANES : face * LANES + modes] = restrict_ref[:, face, :]
        face_work_ref[0:face_modes, face * LANES + HALF : face * LANES + HALF + modes] = restrict_ref[:, face, :]
    composed = jnp.dot(
        orient_work_ref[...], face_work_ref[...], precision=lax.Precision.HIGHEST, preferred_element_type=F32
    )
    stacked = jnp.concatenate([composed[:, face * LANES : (face + 1) * LANES] for face in range(faces)], axis=0)
    high, low = split(stacked.T[0:HALF])
    compose_out[...] = jnp.concatenate([high, high, low, jnp.zeros_like(low)], axis=0)
    wide_ref[...] = jnp.zeros(wide_ref.shape, F32)
    for face in range(faces):
        for turn in range(turns):
            rows = slice(face * HALF + turn * face_modes, face * HALF + (turn + 1) * face_modes)
            wide_ref[rows, 0:modes] = -lift_ref[:, face, :]
            wide_ref[rows, HALF : HALF + modes] = -lift_ref[:, face, :]
    remote_lift_out[...] = stack_right(wide_ref[...])

    elements = slot_ref.shape[1]
    code_ref[...] = jnp.zeros(code_ref.shape, F32)
    slots = slot_ref[...]
    sends = (choose_out.shape[1] // 2 - elements) // 4
    group = (slots - elements) // sends
    moved = slots
    for side in range(4):
        moved = jnp.where(group == side, slots + (ghost_slot(side) - side) * sends, moved)
    code_ref[0:faces, 0:elements] = jnp.where(slots < elements, slots, moved).astype(F32)
    code_ref[faces : 2 * faces, 0:elements] = (face_ref[...] * turns + turn_ref[...]).astype(F32)
    codes = code_ref[...].T[0:elements, :]
    sources = choose_out.shape[1] // 2
    source_lane = (lane_index((elements, 2 * sources)) % sources).astype(F32)
    lanes = lane_index((elements, mask_out.shape[1]))
    in_face = lanes % HALF
    lane_code = jnp.where(in_face < turns * face_modes, (lanes // HALF) * turns + in_face // face_modes, -1)
    lane_code = lane_code.astype(F32)
    picks, masks = [], []
    for face in range(faces):
        picks.append(jnp.where(codes[:, face : face + 1] == source_lane, 1.0, 0.0))
        masks.append(jnp.where(codes[:, faces + face : faces + face + 1] == lane_code, 1.0, 0.0))
    choose_out[...] = jnp.concatenate(picks, axis=0).astype(BF16)
    mask_out[...] = jnp.concatenate(masks, axis=0)

    early = early_ref[...].reshape(fields * ROWS, LANES)
    terms = local_terms(early, star_ref, local_out, volume_out, trace_out, local_lift_out, fields, kinds)
    base_out[...] = packed_ref[...] + terms.reshape(fields, ROWS, LANES)


def remote_terms(rows_ref, remote_ref, compose_ref, lift_ref, choose_ref, mask_ref, fields):
    pairs = rows_ref.shape[0]
    faces = lift_ref.shape[0] // (3 * HALF)
    elements = choose_ref.shape[0] // faces
    sources = jnp.concatenate([rows_ref[pair] for pair in range(pairs)], axis=1)
    gathered = product(choose_ref[...], jnp.concatenate(split(sources), axis=0))
    folded = []
    for face in range(faces):
        sums = []
        for col in range(fields):
            total = None
            for pair in range(pairs):
                part = gathered[face * elements : (face + 1) * elements, pair * LANES : (pair + 1) * LANES]
                term = remote_ref[(face * pairs + pair) * fields + col] * part
                total = term if total is None else total + term
            sums.append(total)
        mixed = jnp.concatenate(sums, axis=0)
        high, low = split(mixed + swap_halves(mixed))
        first = jnp.where(lower_half(high.shape), high, low)
        turned = product(jnp.concatenate([first, high], axis=1), compose_ref[...])
        mask = mask_ref[face * elements : (face + 1) * elements, :]
        chosen = (turned.reshape(fields, elements, turned.shape[1]) * mask[None]).reshape(turned.shape)
        both = chosen[:, 0:LANES] + chosen[:, LANES : 2 * LANES]
        folded.append(both + swap_halves(both))
    lower = lower_half(folded[0].shape)
    left = [jnp.where(lower, folded[face], folded[face + 1]) for face in range(0, faces, 2)]
    result = product(stack_left(jnp.concatenate(left, axis=1)), lift_ref[...])
    result = result.reshape(fields, 2, ROWS, LANES)
    return jnp.where(lower_half((ROWS, LANES))[None], result[:, 0], result[:, 1])


def middle_kernel(
    base_ref, early_ref, late_ref, star_ref, remote_ref, derive_ref, compose_ref, lift_ref, choose_ref, mask_ref,
    rate_hbm, send_hbm, from_0, from_1, from_2, from_3,
    middle_out, late_out, send_0, send_1, send_2, send_3,
    rows_ref, late_rows, rate_ref, send_ref, sems,
):
    copies = [
        pltpu.make_async_copy(rate_hbm, rate_ref, sems.at[0]),
        pltpu.make_async_copy(send_hbm, send_ref, sems.at[1]),
    ]
    for copy in copies:
        copy.start()
    fields = base_ref.shape[0]
    kinds = star_ref.shape[0] // (fields * fields)
    pairs = rows_ref.shape[0]
    sends = send_ref.shape[2]
    fast = sends // 2
    elements = 2 * ROWS
    rows_by_pair(early_ref[...].reshape(fields * ROWS, LANES), rows_ref, fields)
    for side, arrived in enumerate((from_0, from_1, from_2, from_3)):
        at = elements + side * sends
        for pair in range(pairs):
            rows_ref[pair, at : at + sends, :] = arrived[pair * sends : (pair + 1) * sends, :]
    middle = base_ref[...] + remote_terms(
        rows_ref, remote_ref, compose_ref, lift_ref, choose_ref, mask_ref, fields
    )
    middle_out[...] = middle
    start = middle.reshape(fields * ROWS, LANES)

    def step(degree, carry):
        current, early = carry
        current = star_mix(product(stack_left(current), derive_ref[...]), star_ref, fields, kinds)
        return current, early + weight_at(0.0, 0.5, degree) * current

    _, restart = lax.fori_loop(1, DERIVS, step, (start, taylor_weight(0.0, 0.5, 0) * start))
    for copy in copies:
        copy.wait()
    sublane = lax.broadcasted_iota(jnp.int32, (ROWS, LANES), 0)
    lower = lower_half((ROWS, LANES))
    is_fast = jnp.zeros((ROWS, LANES), jnp.int32)
    for element in range(elements):
        here = (sublane == element % ROWS) & (lower if element < ROWS else jnp.logical_not(lower))
        is_fast = jnp.where(here, rate_ref[element], is_fast)
    late = jnp.where((is_fast == 2)[None], restart.reshape(fields, ROWS, LANES), late_ref[...])
    late_out[...] = late
    rows_by_pair(late.reshape(fields * ROWS, LANES), late_rows, fields)
    for side, out in enumerate((send_0, send_1, send_2, send_3)):
        out[...] = jnp.zeros(out.shape, F32)
        for place in range(fast):
            element = send_ref[0, message_side(side), place]
            for pair in range(pairs):
                row = pair * fast + place
                out[row : row + 1, :] = late_rows[pair, pl.ds(element, 1), :]


def local_kernel(middle_ref, late_ref, star_ref, flux_ref, volume_ref, trace_ref, lift_ref, base_out):
    fields = middle_ref.shape[0]
    kinds = star_ref.shape[0] // (fields * fields)
    late = late_ref[...].reshape(fields * ROWS, LANES)
    terms = local_terms(late, star_ref, flux_ref, volume_ref, trace_ref, lift_ref, fields, kinds)
    base_out[...] = middle_ref[...] + terms.reshape(fields, ROWS, LANES)


def final_kernel(
    base_ref, late_ref, remote_ref, compose_ref, lift_ref, choose_ref, mask_ref,
    first_0, first_1, first_2, first_3,
    second_0, second_1, second_2, second_3,
    result_out, rows_ref,
):
    fields = base_ref.shape[0]
    modes = result_out.shape[2]
    pairs = rows_ref.shape[0]
    elements = 2 * ROWS
    sends = (rows_ref.shape[1] - elements) // 4
    fast = sends // 2
    rows_by_pair(late_ref[...].reshape(fields * ROWS, LANES), rows_ref, fields)
    firsts = (first_0, first_1, first_2, first_3)
    seconds = (second_0, second_1, second_2, second_3)
    for side, (first, second) in enumerate(zip(firsts, seconds)):
        at = elements + side * sends
        for pair in range(pairs):
            rows_ref[pair, at : at + fast, :] = second[pair * fast : (pair + 1) * fast, :]
            row = pairs * sends + pair * fast
            rows_ref[pair, at + fast : at + sends, :] = first[row : row + fast, :]
    result = base_ref[...] + remote_terms(
        rows_ref, remote_ref, compose_ref, lift_ref, choose_ref, mask_ref, fields
    )
    result_out[:, 0:ROWS, :] = result[:, :, 0:modes]
    result_out[:, ROWS : 2 * ROWS, :] = result[:, :, HALF : HALF + modes]


VMEM = pl.BlockSpec(memory_space=pltpu.VMEM)
HBM = pl.BlockSpec(memory_space=pltpu.HBM)


def call(kernel, ins, outs, scratch, args, name, flops):
    shapes = [jax.ShapeDtypeStruct(shape, dtype) for shape, dtype in outs]
    args = [
        pltpu.with_memory_space_constraint(arg, pltpu.HBM) if spec is HBM else arg for spec, arg in zip(ins, args)
    ]
    return pl.pallas_call(
        kernel,
        out_shape=shapes,
        in_specs=ins,
        out_specs=[VMEM] * len(outs),
        scratch_shapes=[pltpu.VMEM(*one) if isinstance(one, tuple) else one for one in scratch],
        compiler_params=pltpu.CompilerParams(vmem_limit_bytes=16 * 1024 * 1024),
        cost_estimate=pl.CostEstimate(flops=flops, bytes_accessed=4_000_000, transcendentals=0),
        name=name,
    )(*args)


def exchange(outgoing):
    arrived = []
    for (axis, far), message in zip(SWAPS, outgoing):
        size = lax.axis_size(axis)
        assert size % 2 == 0
        pairs = []
        for first in range(1 if far else 0, size, 2):
            second = (first + 1) % size
            pairs += [(first, second), (second, first)]
        arrived.append(lax.ppermute(message, axis, pairs))
    return arrived


def up_to(count, multiple):
    return -(-count // multiple) * multiple


def local(
    solution, stiffness, star_matrices, face_restrict, face_lift, orient_maps, flux_local, flux_remote,
    cluster_rate, send_list, neighbour_slot, neighbour_face, neighbour_turn,
):
    fields, elements = solution.shape[1], solution.shape[2]
    kinds = stiffness.shape[0]
    faces = face_restrict.shape[0]
    sides, sends = send_list.shape[1], send_list.shape[2]
    fast = sends // 2
    pairs = (fields + 1) // 2
    assert elements == 2 * ROWS and solution.shape[0] <= HALF
    values = jnp.transpose(solution, (1, 2, 0))
    star = jnp.transpose(star_matrices, (1, 2, 0, 3))
    local_part = jnp.transpose(flux_local, (1, 2, 0, 3))
    remote_part = jnp.transpose(flux_remote, (1, 2, 0, 3))
    restrict = jnp.transpose(face_restrict, (1, 0, 2))
    lift = jnp.transpose(face_lift, (2, 0, 1))

    packed = (fields, ROWS, LANES)
    first_shape = (up_to(pairs * (sends + fast), ROWS), LANES)
    second_shape = (up_to(pairs * fast, ROWS), LANES)
    star_shape = (fields * fields * kinds, ROWS, LANES)
    combos = faces * HALF
    sources = elements + sides * sends

    waiting = (local_part, remote_part, restrict, lift, orient_maps, neighbour_slot, neighbour_face, neighbour_turn)
    made = call(
        predict_kernel,
        [HBM] * (4 + len(LATER)),
        [(packed, F32)] * 2 + [(first_shape, F32)] * sides + [
            (packed, F32), (star_shape, F32), ((3 * LANES, kinds * LANES), BF16), (stiffness.shape, F32),
        ] + [(array.shape, array.dtype) for array in waiting],
        [
            ((fields, up_to(4 * fields, ROWS), LANES), F32),
            ((pairs, elements, LANES), F32), ((pairs, elements, LANES), F32),
            (values.shape, F32), ((kinds, LANES, LANES), F32), (star.shape, F32),
            pltpu.SMEM(send_list.shape, jnp.int32), pltpu.SemaphoreType.DMA((4 + len(LATER),)),
        ],
        (values, stiffness, star, send_list, *waiting),
        "predict", 100_000_000,
    )
    early, late, outgoing = made[0], made[1], made[2 : 2 + sides]
    start, star_coef, derive_op, stiffness_kept = made[2 + sides : 6 + sides]
    waiting = made[6 + sides :]
    first = exchange(outgoing)
    (
        base, local_coef, remote_coef, volume_op, trace_op, local_lift, compose_op, remote_lift, choose, mask,
    ) = call(
        prepare_kernel,
        [VMEM] * 12,
        [
            (packed, F32), ((fields * fields, 2, ROWS, LANES), F32),
            ((faces * pairs * fields, elements, LANES), F32),
            ((3 * LANES, kinds * LANES), BF16), ((3 * LANES, 2 * LANES), BF16),
            ((6 * LANES, LANES), BF16), ((2 * LANES, combos), BF16), ((3 * faces * HALF, LANES), BF16),
            ((faces * elements, 2 * sources), BF16), ((faces * elements, combos), F32),
        ],
        [
            ((fields, 2 * ROWS * faces, LANES), F32), ((pairs, 2 * up_to(4 * fields, ROWS), LANES), F32),
            ((kinds, LANES, LANES), F32), ((2 * LANES, LANES), F32),
            ((LANES, faces * LANES), F32), ((HALF, LANES), F32), ((LANES, LANES), F32),
        ],
        (start, early, stiffness_kept, star_coef, *waiting),
        "prepare", 200_000_000,
    )
    middle, late_value, *outgoing = call(
        middle_kernel,
        [VMEM] * 10 + [HBM] * 2 + [VMEM] * 4,
        [(packed, F32)] * 2 + [(second_shape, F32)] * sides,
        [
            ((pairs, sources, LANES), F32), ((pairs, elements, LANES), F32),
            pltpu.SMEM(cluster_rate.shape, jnp.int32), pltpu.SMEM(send_list.shape, jnp.int32),
            pltpu.SemaphoreType.DMA((2,)),
        ],
        (
            base, early, late, star_coef, remote_coef, derive_op, compose_op, remote_lift, choose, mask,
            cluster_rate, send_list, *first,
        ),
        "middle", 200_000_000,
    )
    second = exchange(outgoing)
    (base,) = call(
        local_kernel,
        [VMEM] * 7,
        [(packed, F32)],
        [],
        (middle, late_value, star_coef, local_coef, volume_op, trace_op, local_lift),
        "local_late", 200_000_000,
    )
    (result,) = call(
        final_kernel,
        [VMEM] * 15,
        [(values.shape, F32)],
        [((pairs, sources, LANES), F32)],
        (base, late_value, remote_coef, compose_op, remote_lift, choose, mask, *first, *second),
        "final", 200_000_000,
    )
    return jnp.transpose(result, (2, 0, 1))


def solution(mesh):
    placed = (
        P(None, None, ("dom", "sub")),
        P(),
        P(None, None, None, ("dom", "sub")),
        P(),
        P(),
        P(),
        P(None, None, None, ("dom", "sub")),
        P(None, None, None, ("dom", "sub")),
        P(("dom", "sub")),
        P(("dom", "sub"), None, None),
        P(None, ("dom", "sub")),
        P(None, ("dom", "sub")),
        P(None, ("dom", "sub")),
    )
    return jax.shard_map(
        local, mesh=mesh, in_specs=placed, out_specs=P(None, None, ("dom", "sub")), check_vma=False
    )
```

```python
import math

import jax
import jax.numpy as jnp
from jax import lax
from jax.experimental import pallas as pl
from jax.experimental.pallas import tpu as pltpu
from jax.sharding import PartitionSpec as P

DERIVS = 6
LANES = 128
HALF = 64
ROWS = 8
F32 = jnp.float32
BF16 = jnp.bfloat16
LATER = ("flux_local", "flux_remote", "face_restrict", "face_lift", "orient_maps", "slot", "face", "turn")
AXES = ("dom", "sub")
SWAPS = (("dom", True), ("dom", False), ("sub", True), ("sub", False))


def taylor_weight(lower, upper, degree):
    return (upper ** (degree + 1) - lower ** (degree + 1)) / math.factorial(degree + 1)


def weight_at(lower, upper, degree):
    result = jnp.float32(taylor_weight(lower, upper, 1))
    for option in range(2, DERIVS):
        result = jnp.where(degree == option, jnp.float32(taylor_weight(lower, upper, option)), result)
    return result


def split(values):
    high = values.astype(BF16)
    low = (values - high.astype(F32)).astype(BF16)
    return high, low


def stack_left(values):
    high, low = split(values)
    return jnp.concatenate([high, low, high], axis=1)


def stack_right(values):
    high, low = split(values)
    return jnp.concatenate([high, high, low], axis=0)


def product(left, right):
    return jnp.dot(left, right, preferred_element_type=F32)


def odd_place(axis):
    return lax.rem(lax.axis_index(axis), 2)


def message_side(slot):
    axis, far = SWAPS[slot]
    odd = odd_place(axis)
    return 2 * AXES.index(axis) + (odd if far else 1 - odd)


def ghost_slot(side):
    axis = AXES[side // 2]
    even_far = side % 2 == 0
    return jnp.where(odd_place(axis) == 0, SWAPS.index((axis, even_far)), SWAPS.index((axis, not even_far)))


def lane_index(shape):
    return lax.broadcasted_iota(jnp.int32, shape, len(shape) - 1)


def lower_half(shape):
    return lane_index(shape) < HALF


def swap_halves(values):
    return pltpu.roll(values, HALF, values.ndim - 1)


def pack(values_ref, packed_ref):
    modes = values_ref.shape[2]
    packed_ref[...] = jnp.zeros(packed_ref.shape, F32)
    packed_ref[:, :, 0:modes] = values_ref[:, 0:ROWS, :]
    packed_ref[:, :, HALF : HALF + modes] = values_ref[:, ROWS : 2 * ROWS, :]


def high_and_low(values, shift):
    high = values.astype(BF16).astype(F32)
    return high + pltpu.roll(values - high, shift, 1)


def row_index(shape):
    return lax.broadcasted_iota(jnp.int32, shape, len(shape) - 2)


def one_where(condition):
    return jnp.where(condition, 1.0, 0.0)


def star_coefficients(star_ref, stage_ref, star_out):
    fields, kinds, elements = star_ref.shape[0], star_ref.shape[2], star_ref.shape[3]
    lanes = lane_index((ROWS, LANES))
    pick = one_where((lanes % ROWS == row_index((ROWS, LANES))) & (lanes < 2 * elements))
    from_lane = row_index((LANES, LANES))
    same_half = (from_lane % elements) // ROWS == lane_index((LANES, LANES)) // HALF
    right = one_where(same_half & (from_lane < 2 * elements)).astype(BF16)
    filled = lane_index(stage_ref.shape[1:]) < elements
    for row in range(fields):
        for col in range(fields):
            stage_ref[row, col * 4 : col * 4 + kinds, 0:elements] = star_ref[row, col]
        values = jnp.where(filled, stage_ref[row], 0.0)
        stage_ref[row] = high_and_low(values, elements)
        spreads = []
        for kind in range(kinds):
            for col in range(fields):
                at = col * 4 + kind
                spreads.append(stage_ref[row, at : at + 1, :] * pick)
        spread_out = product(jnp.concatenate(spreads, axis=0).astype(BF16), right)
        count = kinds * fields
        star_out[row * count : (row + 1) * count] = spread_out.reshape(count, ROWS, LANES)


def star_mix(columns, star_ref, fields, kinds):
    sums = [None] * fields
    for row in range(fields):
        for kind in range(kinds):
            part = columns[row * ROWS : (row + 1) * ROWS, kind * LANES : (kind + 1) * LANES]
            for col in range(fields):
                term = star_ref[(row * kinds + kind) * fields + col] * part
                sums[col] = term if sums[col] is None else sums[col] + term
    return jnp.concatenate(sums, axis=0)


def stiffness_blocks(stiffness_ref, block_ref, turned):
    kinds, modes = stiffness_ref.shape[0], stiffness_ref.shape[1]
    block_ref[...] = jnp.zeros(block_ref.shape, F32)
    for kind in range(kinds):
        matrix = -stiffness_ref[kind].T if turned else stiffness_ref[kind]
        block_ref[kind, 0:modes, 0:modes] = matrix
        block_ref[kind, HALF : HALF + modes, HALF : HALF + modes] = matrix
    return jnp.concatenate([block_ref[kind] for kind in range(kinds)], axis=1)


def predict_kernel(*refs):
    later = len(LATER)
    solution_hbm, stiffness_hbm, star_hbm, send_hbm = refs[0:4]
    later_hbm, refs = refs[4 : 4 + later], refs[4 + later :]
    early_out, late_out, send_0, send_1, send_2, send_3 = refs[0:6]
    packed_ref, coef_ref, derive_ref, stiffness_ref = refs[6:10]
    later_out, refs = refs[10 : 10 + later], refs[10 + later :]
    work_ref, early_rows, late_rows, solution_ref, block_ref, star_ref, send_ref, sems = refs

    sources = (star_hbm, stiffness_hbm, solution_hbm, send_hbm, *later_hbm)
    targets = (star_ref, stiffness_ref, solution_ref, send_ref, *later_out)
    copies = [
        pltpu.make_async_copy(source, target, sems.at[number])
        for number, (source, target) in enumerate(zip(sources, targets))
    ]
    for copy in copies:
        copy.start()
    fields, kinds = star_ref.shape[0], star_ref.shape[2]
    pairs = (fields + 1) // 2
    for copy in copies[0:3]:
        copy.wait()
    derive_ref[...] = stack_right(stiffness_blocks(stiffness_ref, block_ref, True))
    star_coefficients(star_ref, work_ref, coef_ref)
    pack(solution_ref, packed_ref)
    start = packed_ref[...].reshape(fields * ROWS, LANES)

    def step(degree, carry):
        current, early, late = carry
        current = star_mix(product(stack_left(current), derive_ref[...]), coef_ref, fields, kinds)
        early = early + weight_at(0.0, 0.5, degree) * current
        late = late + weight_at(0.5, 1.0, degree) * current
        return current, early, late

    _, early, late = lax.fori_loop(
        1, DERIVS, step, (start, taylor_weight(0.0, 0.5, 0) * start, taylor_weight(0.5, 1.0, 0) * start)
    )
    early_out[...] = early.reshape(fields, ROWS, LANES)
    late_out[...] = late.reshape(fields, ROWS, LANES)
    rows_by_pair(early, early_rows, fields)
    rows_by_pair(late, late_rows, fields)
    copies[3].wait()
    sends = send_ref.shape[2]
    fast = sends // 2
    for side, out in enumerate((send_0, send_1, send_2, send_3)):
        out[...] = jnp.zeros(out.shape, F32)
        for place in range(sends):
            element = send_ref[0, message_side(side), place]
            for pair in range(pairs):
                row = pair * sends + place
                out[row : row + 1, :] = early_rows[pair, pl.ds(element, 1), :]
            if place >= fast:
                for pair in range(pairs):
                    row = pairs * sends + pair * fast + place - fast
                    out[row : row + 1, :] = late_rows[pair, pl.ds(element, 1), :]
    for copy in copies[4:]:
        copy.wait()


def rows_by_pair(packed, out_ref, fields):
    lower = lower_half((ROWS, LANES))
    for pair in range((fields + 1) // 2):
        even = packed[2 * pair * ROWS : (2 * pair + 1) * ROWS]
        odd = jnp.zeros_like(even)
        if 2 * pair + 1 < fields:
            odd = packed[(2 * pair + 1) * ROWS : (2 * pair + 2) * ROWS]
        out_ref[pair, 0:ROWS, :] = jnp.where(lower, even, swap_halves(odd))
        out_ref[pair, ROWS : 2 * ROWS, :] = jnp.where(lower, swap_halves(even), odd)


def flux_local_coefficients(flux_ref, stage_ref, out_ref):
    fields, faces, elements = flux_ref.shape[0], flux_ref.shape[2], flux_ref.shape[3]
    rows = 2 * ROWS
    filled = lane_index((rows, LANES)) < elements
    lanes, sublanes = lane_index((ROWS, LANES)), row_index((ROWS, LANES))
    picks = [one_where(lanes % elements == half * ROWS + sublanes) for half in range(2)]
    square = (LANES, LANES)
    right = one_where(row_index(square) // (2 * elements) == lane_index(square) % faces).astype(BF16)
    for row in range(fields):
        values = None
        for face in range(faces):
            stage_ref[row, face * rows : face * rows + fields, 0:elements] = flux_ref[row, :, face, :]
            part = jnp.where(filled, stage_ref[row, face * rows : (face + 1) * rows, :], 0.0)
            values = part if values is None else values + pltpu.roll(part, face * 2 * elements, 1)
        stage_ref[row, 0:rows, :] = high_and_low(values, elements)
        left = [stage_ref[row, col : col + 1, :] * pick for col in range(fields) for pick in picks]
        spread = product(jnp.concatenate(left, axis=0).astype(BF16), right)
        out_ref[row * fields : (row + 1) * fields] = spread.reshape(fields, 2, ROWS, LANES)


def flux_remote_coefficients(flux_ref, stage_ref, out_ref):
    fields, faces, elements = flux_ref.shape[0], flux_ref.shape[2], flux_ref.shape[3]
    pairs = (fields + 1) // 2
    rows = stage_ref.shape[1] // 2
    filled = lane_index((rows, LANES)) < elements
    lanes, sublanes = lane_index((elements, LANES)), row_index((elements, LANES))
    pick = one_where((lanes % elements == sublanes) & (lanes < 4 * elements))
    square = (LANES, LANES)
    from_lane = row_index(square)
    same_parity = (from_lane // elements) % 2 == lane_index(square) // HALF
    right = one_where(same_parity & (from_lane < 4 * elements)).astype(BF16)
    for pair in range(pairs):
        values = None
        for row in range(2 * pair, min(2 * pair + 2, fields)):
            start = (row % 2) * rows
            for col in range(fields):
                at = start + col * faces
                stage_ref[pair, at : at + faces, 0:elements] = flux_ref[row, col]
            part = jnp.where(filled, stage_ref[pair, start : start + rows, :], 0.0)
            values = part if values is None else values + pltpu.roll(part, elements, 1)
        stage_ref[pair, 0:rows, :] = high_and_low(values, 2 * elements)
        for face in range(faces):
            left = []
            for col in range(fields):
                at = col * faces + face
                left.append(stage_ref[pair, at : at + 1, :] * pick)
            spread = product(jnp.concatenate(left, axis=0).astype(BF16), right)
            at = (face * pairs + pair) * fields
            out_ref[at : at + fields] = spread.reshape(fields, elements, LANES)


def local_terms(packed, star_ref, flux_ref, volume_ref, trace_ref, lift_ref, fields, kinds):
    left = stack_left(packed)
    volume = star_mix(product(left, volume_ref[...]), star_ref, fields, kinds)
    traces = product(left, trace_ref[...])
    sums = []
    for col in range(fields):
        halves = []
        for half in range(2):
            total = None
            for row in range(fields):
                part = traces[row * ROWS : (row + 1) * ROWS, half * LANES : (half + 1) * LANES]
                term = flux_ref[row * fields + col, half] * part
                total = term if total is None else total + term
            halves.append(total)
        sums.append(jnp.concatenate(halves, axis=1))
    return volume + product(stack_left(jnp.concatenate(sums, axis=0)), lift_ref[...])


def ghost_terms(
    flux_ref, stage_ref, code_ref, composed, lift_sides, lane_code, flux_out, operator_out, scatter_out, sends, fields
):
    faces, elements = flux_ref.shape[2], flux_ref.shape[3]
    rows = 2 * ROWS
    shape = (rows, LANES)
    lanes = lane_index(shape)

    def along_lanes(start):
        row = code_ref[start : start + 1, :]
        for face in range(1, faces):
            row = row + pltpu.roll(code_ref[start + face : start + face + 1, :], face * elements, 1)
        return row + swap_halves(row)

    slots, codes = along_lanes(0), along_lanes(faces)
    ghosts = elements + row_index(shape)
    found = one_where(jnp.broadcast_to(slots, shape) == ghosts.astype(F32))
    first = jnp.where(lanes < HALF, found, 0.0)
    code = jnp.sum(first * codes, axis=1, keepdims=True)
    face_of = jnp.sum(first * (lanes // elements).astype(F32), axis=1, keepdims=True)
    element_of = jnp.sum(first * (lanes % elements).astype(F32), axis=1, keepdims=True)
    numbers = [slot * sends + place for slot in range(4) for place in range(sends // 2)]

    filled = lanes < elements
    values = []
    for field in range(fields):
        total = None
        for face in range(faces):
            stage_ref[field, face * rows : face * rows + fields, 0:elements] = flux_ref[field, :, face, :]
            part = jnp.where(filled, stage_ref[field, face * rows : (face + 1) * rows, :], 0.0)
            total = part if total is None else total + pltpu.roll(part, face * elements, 1)
        total = jnp.where(row_index(shape) < fields, total, 0.0)
        values.append(high_and_low(total, HALF))
    picked = jnp.concatenate([jnp.broadcast_to(found[number : number + 1], (HALF, LANES)) for number in numbers], axis=0)
    flux_out[...] = lax.dot_general(
        jnp.concatenate(values, axis=0).astype(BF16), picked.astype(BF16), (((1,), (1,)), ((), ())),
        preferred_element_type=F32,
    )

    left = []
    for number in numbers:
        chosen = composed * one_where(lane_code == code[number : number + 1])
        both = chosen[:, 0:LANES] + chosen[:, LANES : 2 * LANES]
        high, low = split(both + swap_halves(both))
        left.append(jnp.concatenate([jnp.where(lower_half(high.shape), high, low), high], axis=1))
    high, low = split(lift_sides)
    lifts = product(jnp.concatenate(left, axis=0), jnp.concatenate([high, high, low, jnp.zeros_like(low)], axis=0))
    side_lane = (lane_index((1, faces * HALF)) // HALF).astype(F32)
    place_of = jnp.zeros((1, LANES), F32)
    for at, number in enumerate(numbers):
        chosen = lifts[at * HALF : (at + 1) * HALF] * one_where(side_lane == face_of[number : number + 1])
        both = chosen[:, 0:LANES] + chosen[:, LANES : 2 * LANES]
        high, low = split(both + swap_halves(both))
        operator_out[at] = jnp.concatenate([high, high, low, jnp.zeros_like(low)], axis=0)
        place_of = jnp.where(lane_index((1, LANES)) // rows == at, element_of[number : number + 1], place_of)
    square = (fields * elements, LANES)
    here = (row_index(square) // elements == lane_index(square) % rows) & (
        (row_index(square) % elements).astype(F32) == place_of
    )
    one = one_where(here).astype(BF16)
    scatter_out[...] = jnp.concatenate([one, one], axis=1)


def prepare_kernel(
    packed_ref, early_ref, stiffness_ref, star_ref, flux_local_ref, flux_remote_ref, restrict_ref, lift_ref, orient_ref,
    slot_ref, face_ref, turn_ref,
    base_out, local_out, remote_out, volume_out, trace_out, local_lift_out, compose_out,
    remote_lift_out, choose_out, mask_out, ghost_flux_out, ghost_operator_out, scatter_out,
    sides_ref, local_work_ref, remote_work_ref, block_ref, wide_ref, face_work_ref, orient_work_ref, code_ref,
):
    fields, kinds = packed_ref.shape[0], stiffness_ref.shape[0]
    face_modes, faces, modes = restrict_ref.shape
    turns = orient_ref.shape[0]
    flux_local_coefficients(flux_local_ref, local_work_ref, local_out)
    flux_remote_coefficients(flux_remote_ref, remote_work_ref, remote_out)

    volume_out[...] = stack_right(stiffness_blocks(stiffness_ref, block_ref, False))

    wide_ref[...] = jnp.zeros(wide_ref.shape, F32)
    for mode in range(face_modes):
        at = mode * faces
        wide_ref[at : at + faces, 0:modes] = restrict_ref[mode]
        wide_ref[LANES + at : LANES + at + faces, HALF : HALF + modes] = restrict_ref[mode]
    trace_out[...] = stack_right(wide_ref[...].T)
    for mode in range(face_modes):
        at = mode * faces
        wide_ref[at : at + faces, 0:modes] = -lift_ref[mode]
        wide_ref[LANES + at : LANES + at + faces, HALF : HALF + modes] = -lift_ref[mode]
    local_lift_out[...] = stack_right(wide_ref[...])

    face_work_ref[...] = jnp.zeros(face_work_ref.shape, F32)
    orient_work_ref[...] = jnp.zeros(orient_work_ref.shape, F32)
    for turn in range(turns):
        orient_work_ref[turn * face_modes : (turn + 1) * face_modes, 0:face_modes] = orient_ref[turn]
    for face in range(faces):
        face_work_ref[0:face_modes, face * LANES : face * LANES + modes] = restrict_ref[:, face, :]
        face_work_ref[0:face_modes, face * LANES + HALF : face * LANES + HALF + modes] = restrict_ref[:, face, :]
    composed = jnp.dot(
        orient_work_ref[...], face_work_ref[...], precision=lax.Precision.HIGHEST, preferred_element_type=F32
    )
    stacked = jnp.concatenate([composed[:, face * LANES : (face + 1) * LANES] for face in range(faces)], axis=0)
    high, low = split(stacked.T[0:HALF])
    compose_out[...] = jnp.concatenate([high, high, low, jnp.zeros_like(low)], axis=0)
    wide_ref[...] = jnp.zeros(wide_ref.shape, F32)
    for face in range(faces):
        for turn in range(turns):
            rows = slice(face * HALF + turn * face_modes, face * HALF + (turn + 1) * face_modes)
            wide_ref[rows, 0:modes] = -lift_ref[:, face, :]
            wide_ref[rows, HALF : HALF + modes] = -lift_ref[:, face, :]
    remote_lift_out[...] = stack_right(wide_ref[...])

    elements = slot_ref.shape[1]
    code_ref[...] = jnp.zeros(code_ref.shape, F32)
    slots = slot_ref[...]
    sends = (choose_out.shape[1] // 2 - elements) // 4
    group = (slots - elements) // sends
    moved = slots
    for side in range(4):
        moved = jnp.where(group == side, slots + (ghost_slot(side) - side) * sends, moved)
    code_ref[0:faces, 0:elements] = jnp.where(slots < elements, slots, moved).astype(F32)
    code_ref[faces : 2 * faces, 0:elements] = (face_ref[...] * turns + turn_ref[...]).astype(F32)
    codes = code_ref[...].T[0:elements, :]
    sources = choose_out.shape[1] // 2
    source_lane = (lane_index((elements, 2 * sources)) % sources).astype(F32)
    lanes = lane_index((elements, mask_out.shape[1]))
    in_face = lanes % HALF
    lane_code = jnp.where(in_face < turns * face_modes, (lanes // HALF) * turns + in_face // face_modes, -1)
    lane_code = lane_code.astype(F32)
    picks, masks = [], []
    for face in range(faces):
        picks.append(jnp.where(codes[:, face : face + 1] == source_lane, 1.0, 0.0))
        masks.append(jnp.where(codes[:, faces + face : faces + face + 1] == lane_code, 1.0, 0.0))
    choose_out[...] = jnp.concatenate(picks, axis=0).astype(BF16)
    mask_out[...] = jnp.concatenate(masks, axis=0)

    sides_ref[...] = jnp.zeros(sides_ref.shape, F32)
    for face in range(faces):
        for turn in range(turns):
            rows = slice(turn * face_modes, (turn + 1) * face_modes)
            sides_ref[rows, face * HALF : face * HALF + modes] = -lift_ref[:, face, :]
    ghost_terms(
        flux_remote_ref, local_work_ref, code_ref, stacked.T[0:HALF], sides_ref[...], lane_code[0:1],
        ghost_flux_out, ghost_operator_out, scatter_out, sends, fields,
    )

    early = early_ref[...].reshape(fields * ROWS, LANES)
    terms = local_terms(early, star_ref, local_out, volume_out, trace_out, local_lift_out, fields, kinds)
    base_out[...] = packed_ref[...] + terms.reshape(fields, ROWS, LANES)


def remote_terms(rows_ref, remote_ref, compose_ref, lift_ref, choose_ref, mask_ref, fields):
    pairs = rows_ref.shape[0]
    faces = lift_ref.shape[0] // (3 * HALF)
    elements = choose_ref.shape[0] // faces
    sources = jnp.concatenate([rows_ref[pair] for pair in range(pairs)], axis=1)
    gathered = product(choose_ref[...], jnp.concatenate(split(sources), axis=0))
    folded = []
    for face in range(faces):
        sums = []
        for col in range(fields):
            total = None
            for pair in range(pairs):
                part = gathered[face * elements : (face + 1) * elements, pair * LANES : (pair + 1) * LANES]
                term = remote_ref[(face * pairs + pair) * fields + col] * part
                total = term if total is None else total + term
            sums.append(total)
        mixed = jnp.concatenate(sums, axis=0)
        high, low = split(mixed + swap_halves(mixed))
        first = jnp.where(lower_half(high.shape), high, low)
        turned = product(jnp.concatenate([first, high], axis=1), compose_ref[...])
        mask = mask_ref[face * elements : (face + 1) * elements, :]
        chosen = (turned.reshape(fields, elements, turned.shape[1]) * mask[None]).reshape(turned.shape)
        both = chosen[:, 0:LANES] + chosen[:, LANES : 2 * LANES]
        folded.append(both + swap_halves(both))
    lower = lower_half(folded[0].shape)
    left = [jnp.where(lower, folded[face], folded[face + 1]) for face in range(0, faces, 2)]
    result = product(stack_left(jnp.concatenate(left, axis=1)), lift_ref[...])
    result = result.reshape(fields, 2, ROWS, LANES)
    return jnp.where(lower_half((ROWS, LANES))[None], result[:, 0], result[:, 1])


def middle_kernel(
    base_ref, early_ref, late_ref, star_ref, remote_ref, derive_ref, compose_ref, lift_ref, choose_ref, mask_ref,
    rate_hbm, send_hbm, from_0, from_1, from_2, from_3,
    middle_out, late_out, send_0, send_1, send_2, send_3,
    rows_ref, late_rows, rate_ref, send_ref, sems,
):
    copies = [
        pltpu.make_async_copy(rate_hbm, rate_ref, sems.at[0]),
        pltpu.make_async_copy(send_hbm, send_ref, sems.at[1]),
    ]
    for copy in copies:
        copy.start()
    fields = base_ref.shape[0]
    kinds = star_ref.shape[0] // (fields * fields)
    pairs = rows_ref.shape[0]
    sends = send_ref.shape[2]
    fast = sends // 2
    elements = 2 * ROWS
    rows_by_pair(early_ref[...].reshape(fields * ROWS, LANES), rows_ref, fields)
    for side, arrived in enumerate((from_0, from_1, from_2, from_3)):
        at = elements + side * sends
        for pair in range(pairs):
            rows_ref[pair, at : at + sends, :] = arrived[pair * sends : (pair + 1) * sends, :]
    middle = base_ref[...] + remote_terms(
        rows_ref, remote_ref, compose_ref, lift_ref, choose_ref, mask_ref, fields
    )
    middle_out[...] = middle
    start = middle.reshape(fields * ROWS, LANES)

    def step(degree, carry):
        current, early = carry
        current = star_mix(product(stack_left(current), derive_ref[...]), star_ref, fields, kinds)
        return current, early + weight_at(0.0, 0.5, degree) * current

    _, restart = lax.fori_loop(1, DERIVS, step, (start, taylor_weight(0.0, 0.5, 0) * start))
    for copy in copies:
        copy.wait()
    sublane = lax.broadcasted_iota(jnp.int32, (ROWS, LANES), 0)
    lower = lower_half((ROWS, LANES))
    is_fast = jnp.zeros((ROWS, LANES), jnp.int32)
    for element in range(elements):
        here = (sublane == element % ROWS) & (lower if element < ROWS else jnp.logical_not(lower))
        is_fast = jnp.where(here, rate_ref[element], is_fast)
    late = jnp.where((is_fast == 2)[None], restart.reshape(fields, ROWS, LANES), late_ref[...])
    late_out[...] = late
    both = late.reshape(fields * ROWS, LANES)
    swapped = swap_halves(both)
    wide = lower_half(both.shape)
    late_rows[:, 0:ROWS, :] = jnp.where(wide, both, swapped).reshape(late.shape)
    late_rows[:, ROWS : 2 * ROWS, :] = jnp.where(wide, swapped, both).reshape(late.shape)
    first_half = lower_half((1, LANES))
    for slot, out in enumerate((send_0, send_1, send_2, send_3)):
        out[...] = jnp.zeros(out.shape, F32)
        side = message_side(slot)
        places = [send_ref[0, side, place] for place in range(fast)]
        for field in range(fields):
            halves = [late_rows[field, pl.ds(element, 1), :] for element in places]
            out[field : field + 1, :] = jnp.where(first_half, *halves)


def local_kernel(
    middle_ref, late_ref, star_ref, flux_ref, volume_ref, trace_ref, lift_ref,
    remote_ref, compose_ref, remote_lift_ref, choose_ref, mask_ref, first_0, first_1, first_2, first_3,
    base_out, rows_ref,
):
    fields = middle_ref.shape[0]
    kinds = star_ref.shape[0] // (fields * fields)
    pairs = rows_ref.shape[0]
    elements = 2 * ROWS
    sends = (rows_ref.shape[1] - elements) // 4
    fast = sends // 2
    late = late_ref[...].reshape(fields * ROWS, LANES)
    rows_by_pair(late, rows_ref, fields)
    for slot, first in enumerate((first_0, first_1, first_2, first_3)):
        at = elements + slot * sends
        for pair in range(pairs):
            rows_ref[pair, at : at + fast, :] = jnp.zeros((fast, LANES), F32)
            row = pairs * sends + pair * fast
            rows_ref[pair, at + fast : at + sends, :] = first[row : row + fast, :]
    terms = local_terms(late, star_ref, flux_ref, volume_ref, trace_ref, lift_ref, fields, kinds)
    remote = remote_terms(rows_ref, remote_ref, compose_ref, remote_lift_ref, choose_ref, mask_ref, fields)
    base_out[...] = middle_ref[...] + terms.reshape(fields, ROWS, LANES) + remote


def final_kernel(
    base_ref, ghost_flux_ref, ghost_operator_ref, scatter_ref, second_0, second_1, second_2, second_3, result_out,
):
    fields = base_ref.shape[0]
    modes = result_out.shape[2]
    rows = second_0.shape[0]
    lower = lower_half((rows, LANES))
    added = []
    for slot, second in enumerate((second_0, second_1, second_2, second_3)):
        mixed = None
        for field in range(fields):
            coefficient = ghost_flux_ref[field * rows : (field + 1) * rows, slot * LANES : (slot + 1) * LANES]
            term = coefficient * second[field : field + 1, :]
            mixed = term if mixed is None else mixed + term
        high, low = split(mixed)
        high_swapped, low_swapped = split(swap_halves(mixed))
        for place, parts in enumerate(((high, low_swapped, high), (high_swapped, low, high_swapped))):
            left = jnp.concatenate([jnp.where(lower, parts[0], parts[1]), parts[2]], axis=1)
            added.append(product(left, ghost_operator_ref[2 * slot + place]))
    right = jnp.concatenate(split(jnp.concatenate(added, axis=0)), axis=0)
    scattered = product(scatter_ref[...], right).reshape(fields, 2, ROWS, LANES)
    result = base_ref[...] + jnp.where(lower_half((ROWS, LANES))[None], scattered[:, 0], scattered[:, 1])
    result_out[:, 0:ROWS, :] = result[:, :, 0:modes]
    result_out[:, ROWS : 2 * ROWS, :] = result[:, :, HALF : HALF + modes]


VMEM = pl.BlockSpec(memory_space=pltpu.VMEM)
HBM = pl.BlockSpec(memory_space=pltpu.HBM)


def call(kernel, ins, outs, scratch, args, name, flops):
    shapes = [jax.ShapeDtypeStruct(shape, dtype) for shape, dtype in outs]
    args = [
        pltpu.with_memory_space_constraint(arg, pltpu.HBM) if spec is HBM else arg for spec, arg in zip(ins, args)
    ]
    return pl.pallas_call(
        kernel,
        out_shape=shapes,
        in_specs=ins,
        out_specs=[VMEM] * len(outs),
        scratch_shapes=[pltpu.VMEM(*one) if isinstance(one, tuple) else one for one in scratch],
        compiler_params=pltpu.CompilerParams(vmem_limit_bytes=16 * 1024 * 1024),
        cost_estimate=pl.CostEstimate(flops=flops, bytes_accessed=4_000_000, transcendentals=0),
        name=name,
    )(*args)


def exchange(outgoing):
    arrived = []
    for (axis, far), message in zip(SWAPS, outgoing):
        size = lax.axis_size(axis)
        assert size % 2 == 0
        pairs = []
        for first in range(1 if far else 0, size, 2):
            second = (first + 1) % size
            pairs += [(first, second), (second, first)]
        arrived.append(lax.ppermute(message, axis, pairs))
    return arrived


def up_to(count, multiple):
    return -(-count // multiple) * multiple


def local(
    solution, stiffness, star_matrices, face_restrict, face_lift, orient_maps, flux_local, flux_remote,
    cluster_rate, send_list, neighbour_slot, neighbour_face, neighbour_turn,
):
    fields, elements = solution.shape[1], solution.shape[2]
    kinds = stiffness.shape[0]
    faces = face_restrict.shape[0]
    sides, sends = send_list.shape[1], send_list.shape[2]
    fast = sends // 2
    pairs = (fields + 1) // 2
    assert elements == 2 * ROWS and solution.shape[0] <= HALF and fast == 2
    values = jnp.transpose(solution, (1, 2, 0))
    star = jnp.transpose(star_matrices, (1, 2, 0, 3))
    local_part = jnp.transpose(flux_local, (1, 2, 0, 3))
    remote_part = jnp.transpose(flux_remote, (1, 2, 0, 3))
    restrict = jnp.transpose(face_restrict, (1, 0, 2))
    lift = jnp.transpose(face_lift, (2, 0, 1))

    packed = (fields, ROWS, LANES)
    first_shape = (up_to(pairs * (sends + fast), ROWS), LANES)
    second_shape = (up_to(fields, 2 * ROWS), LANES)
    star_shape = (fields * fields * kinds, ROWS, LANES)
    combos = faces * HALF
    sources = elements + sides * sends

    waiting = (local_part, remote_part, restrict, lift, orient_maps, neighbour_slot, neighbour_face, neighbour_turn)
    made = call(
        predict_kernel,
        [HBM] * (4 + len(LATER)),
        [(packed, F32)] * 2 + [(first_shape, F32)] * sides + [
            (packed, F32), (star_shape, F32), ((3 * LANES, kinds * LANES), BF16), (stiffness.shape, F32),
        ] + [(array.shape, array.dtype) for array in waiting],
        [
            ((fields, up_to(4 * fields, ROWS), LANES), F32),
            ((pairs, elements, LANES), F32), ((pairs, elements, LANES), F32),
            (values.shape, F32), ((kinds, LANES, LANES), F32), (star.shape, F32),
            pltpu.SMEM(send_list.shape, jnp.int32), pltpu.SemaphoreType.DMA((4 + len(LATER),)),
        ],
        (values, stiffness, star, send_list, *waiting),
        "predict", 100_000_000,
    )
    early, late, outgoing = made[0], made[1], made[2 : 2 + sides]
    start, star_coef, derive_op, stiffness_kept = made[2 + sides : 6 + sides]
    waiting = made[6 + sides :]
    first = exchange(outgoing)
    (
        base, local_coef, remote_coef, volume_op, trace_op, local_lift, compose_op, remote_lift, choose, mask,
        ghost_flux, ghost_op, scatter,
    ) = call(
        prepare_kernel,
        [VMEM] * 12,
        [
            (packed, F32), ((fields * fields, 2, ROWS, LANES), F32),
            ((faces * pairs * fields, elements, LANES), F32),
            ((3 * LANES, kinds * LANES), BF16), ((3 * LANES, 2 * LANES), BF16),
            ((6 * LANES, LANES), BF16), ((2 * LANES, combos), BF16), ((3 * faces * HALF, LANES), BF16),
            ((faces * elements, 2 * sources), BF16), ((faces * elements, combos), F32),
            ((fields * second_shape[0], sides * LANES), F32), ((sides * fast, 2 * LANES, LANES), BF16),
            ((fields * elements, 2 * LANES), BF16),
        ],
        [
            ((HALF, faces * HALF), F32), ((fields, 2 * ROWS * faces, LANES), F32), ((pairs, 2 * up_to(4 * fields, ROWS), LANES), F32),
            ((kinds, LANES, LANES), F32), ((2 * LANES, LANES), F32),
            ((LANES, faces * LANES), F32), ((HALF, LANES), F32), ((LANES, LANES), F32),
        ],
        (start, early, stiffness_kept, star_coef, *waiting),
        "prepare", 200_000_000,
    )
    middle, late_value, *outgoing = call(
        middle_kernel,
        [VMEM] * 10 + [HBM] * 2 + [VMEM] * 4,
        [(packed, F32)] * 2 + [(second_shape, F32)] * sides,
        [
            ((pairs, sources, LANES), F32), ((fields, elements, LANES), F32),
            pltpu.SMEM(cluster_rate.shape, jnp.int32), pltpu.SMEM(send_list.shape, jnp.int32),
            pltpu.SemaphoreType.DMA((2,)),
        ],
        (
            base, early, late, star_coef, remote_coef, derive_op, compose_op, remote_lift, choose, mask,
            cluster_rate, send_list, *first,
        ),
        "middle", 200_000_000,
    )
    second = exchange(outgoing)
    (base,) = call(
        local_kernel,
        [VMEM] * 16,
        [(packed, F32)],
        [((pairs, sources, LANES), F32)],
        (
            middle, late_value, star_coef, local_coef, volume_op, trace_op, local_lift,
            remote_coef, compose_op, remote_lift, choose, mask, *first,
        ),
        "local_late", 200_000_000,
    )
    (result,) = call(
        final_kernel,
        [VMEM] * 8,
        [(values.shape, F32)],
        [],
        (base, ghost_flux, ghost_op, scatter, *second),
        "final", 200_000_000,
    )
    return jnp.transpose(result, (2, 0, 1))


def solution(mesh):
    placed = (
        P(None, None, ("dom", "sub")),
        P(),
        P(None, None, None, ("dom", "sub")),
        P(),
        P(),
        P(),
        P(None, None, None, ("dom", "sub")),
        P(None, None, None, ("dom", "sub")),
        P(("dom", "sub")),
        P(("dom", "sub"), None, None),
        P(None, ("dom", "sub")),
        P(None, ("dom", "sub")),
        P(None, ("dom", "sub")),
    )
    return jax.shard_map(
        local, mesh=mesh, in_specs=placed, out_specs=P(None, None, ("dom", "sub")), check_vma=False
    )
```

```python
import math

import jax
import jax.numpy as jnp
from jax import lax
from jax.experimental import pallas as pl
from jax.experimental.pallas import tpu as pltpu
from jax.sharding import PartitionSpec as P

DERIVS = 6
LANES = 128
HALF = 64
ROWS = 8
F32 = jnp.float32
BF16 = jnp.bfloat16
LATER = ("flux_local", "flux_remote", "face_restrict", "face_lift", "orient_maps", "slot", "face", "turn")
AXES = ("dom", "sub")
AHEAD = 1
SWAPS = (("dom", True), ("dom", False), ("sub", True), ("sub", False))


def taylor_weight(lower, upper, degree):
    return (upper ** (degree + 1) - lower ** (degree + 1)) / math.factorial(degree + 1)


def weight_at(lower, upper, degree):
    result = jnp.float32(taylor_weight(lower, upper, 1))
    for option in range(2, DERIVS):
        result = jnp.where(degree == option, jnp.float32(taylor_weight(lower, upper, option)), result)
    return result


def split(values):
    high = values.astype(BF16)
    low = (values - high.astype(F32)).astype(BF16)
    return high, low


def stack_left(values):
    high, low = split(values)
    return jnp.concatenate([high, low, high], axis=1)


def stack_right(values):
    high, low = split(values)
    return jnp.concatenate([high, high, low], axis=0)


def product(left, right):
    return jnp.dot(left, right, preferred_element_type=F32)


def odd_place(axis):
    return lax.rem(lax.axis_index(axis), 2)


def message_side(slot):
    axis, far = SWAPS[slot]
    odd = odd_place(axis)
    return 2 * AXES.index(axis) + (odd if far else 1 - odd)


def ghost_slot(side):
    axis = AXES[side // 2]
    even_far = side % 2 == 0
    return jnp.where(odd_place(axis) == 0, SWAPS.index((axis, even_far)), SWAPS.index((axis, not even_far)))


def lane_index(shape):
    return lax.broadcasted_iota(jnp.int32, shape, len(shape) - 1)


def lower_half(shape):
    return lane_index(shape) < HALF


def swap_halves(values):
    return pltpu.roll(values, HALF, values.ndim - 1)


def pack(values_ref, packed_ref):
    modes = values_ref.shape[2]
    packed_ref[:, :, 0:modes] = values_ref[:, 0:ROWS, :]
    packed_ref[:, :, HALF : HALF + modes] = values_ref[:, ROWS : 2 * ROWS, :]


def high_and_low(values, shift):
    high = values.astype(BF16).astype(F32)
    return high + pltpu.roll(values - high, shift, 1)


def row_index(shape):
    return lax.broadcasted_iota(jnp.int32, shape, len(shape) - 2)


def one_where(condition):
    return jnp.where(condition, 1.0, 0.0)


def star_coefficients(star_ref, stage_ref, star_out):
    fields, kinds, elements = star_ref.shape[0], star_ref.shape[2], star_ref.shape[3]
    rows = 2 * ROWS
    lanes = lane_index((ROWS, LANES))
    pick = one_where((lanes % ROWS == row_index((ROWS, LANES))) & (lanes < 2 * kinds * elements))
    shape = (LANES, kinds * LANES)
    from_lane, to_lane = row_index(shape), lane_index(shape)
    same_kind = from_lane // (2 * elements) == to_lane // LANES
    same_half = (from_lane % elements) // ROWS == (to_lane % LANES) // HALF
    right = one_where(same_kind & same_half).astype(BF16)
    filled = lane_index((rows, LANES)) < elements
    for row in range(fields):
        values = None
        for kind in range(kinds):
            stage_ref[row, kind * rows : kind * rows + fields, 0:elements] = star_ref[row, :, kind, :]
            part = jnp.where(filled, stage_ref[row, kind * rows : (kind + 1) * rows, :], 0.0)
            values = part if values is None else values + pltpu.roll(part, kind * 2 * elements, 1)
        stage_ref[row, 0:rows, :] = high_and_low(values, elements)
        left = [stage_ref[row, col : col + 1, :] * pick for col in range(fields)]
        spread = product(jnp.concatenate(left, axis=0).astype(BF16), right)
        for kind in range(kinds):
            at = (row * kinds + kind) * fields
            part = spread[:, kind * LANES : (kind + 1) * LANES]
            star_out[at : at + fields] = part.reshape(fields, ROWS, LANES)


def star_mix(columns, star_ref, fields, kinds):
    sums = [None] * fields
    for row in range(fields):
        for kind in range(kinds):
            part = columns[row * ROWS : (row + 1) * ROWS, kind * LANES : (kind + 1) * LANES]
            for col in range(fields):
                term = star_ref[(row * kinds + kind) * fields + col] * part
                sums[col] = term if sums[col] is None else sums[col] + term
    return jnp.concatenate(sums, axis=0)


def stiffness_blocks(stiffness_ref, block_ref, turned):
    kinds, modes = stiffness_ref.shape[0], stiffness_ref.shape[1]
    for kind in range(kinds):
        matrix = -stiffness_ref[kind].T if turned else stiffness_ref[kind]
        block_ref[kind, 0:modes, 0:modes] = matrix
        block_ref[kind, HALF : HALF + modes, HALF : HALF + modes] = matrix
    return jnp.concatenate([block_ref[kind] for kind in range(kinds)], axis=1)


def predict_kernel(*refs):
    later = len(LATER)
    solution_hbm, stiffness_hbm, star_hbm, send_hbm = refs[0:4]
    later_hbm, refs = refs[4 : 4 + later], refs[4 + later :]
    early_out, late_out, ahead_out, send_0, send_1, send_2, send_3 = refs[0:7]
    packed_ref, coef_ref, derive_ref, stiffness_ref = refs[7:11]
    later_out, refs = refs[11 : 11 + later], refs[11 + later :]
    work_ref, early_rows, late_rows, solution_ref, block_ref, star_ref, send_ref, sems = refs

    sources = (star_hbm, stiffness_hbm, solution_hbm, send_hbm, *later_hbm)
    targets = (star_ref, stiffness_ref, solution_ref, send_ref, *later_out)
    copies = [
        pltpu.make_async_copy(source, target, sems.at[number])
        for number, (source, target) in enumerate(zip(sources, targets))
    ]
    for copy in copies[0:4]:
        copy.start()
    fields, kinds = star_ref.shape[0], star_ref.shape[2]
    pairs = (fields + 1) // 2
    for cleared in (packed_ref, block_ref, send_0, send_1, send_2, send_3):
        cleared[...] = jnp.zeros(cleared.shape, F32)
    for copy in copies[4:]:
        copy.start()
    for copy in copies[0:3]:
        copy.wait()
    derive_ref[...] = stack_right(stiffness_blocks(stiffness_ref, block_ref, True))
    star_coefficients(star_ref, work_ref, coef_ref)
    pack(solution_ref, packed_ref)
    start = packed_ref[...].reshape(fields * ROWS, LANES)

    def step(degree, carry):
        current, early, late = carry
        current = star_mix(product(stack_left(current), derive_ref[...]), coef_ref, fields, kinds)
        early = early + weight_at(0.0, 0.5, degree) * current
        late = late + weight_at(0.5, 1.0, degree) * current
        return current, early, late

    _, early, late = lax.fori_loop(
        1, DERIVS, step, (start, taylor_weight(0.0, 0.5, 0) * start, taylor_weight(0.5, 1.0, 0) * start)
    )
    early_out[...] = early.reshape(fields, ROWS, LANES)
    late_out[...] = late.reshape(fields, ROWS, LANES)
    rows_by_pair(early, early_rows, fields)
    rows_by_pair(late, late_rows, fields)
    copies[3].wait()
    sends = send_ref.shape[2]
    fast = sends // 2
    for side, out in enumerate((send_0, send_1, send_2, send_3)):
        for place in range(sends):
            element = send_ref[0, message_side(side), place]
            for pair in range(pairs):
                row = pair * sends + place
                out[row : row + 1, :] = early_rows[pair, pl.ds(element, 1), :]
            if place >= fast:
                for pair in range(pairs):
                    row = pairs * sends + pair * fast + place - fast
                    out[row : row + 1, :] = late_rows[pair, pl.ds(element, 1), :]
    ahead_out[...] = (send_0, send_1, send_2, send_3)[AHEAD][...]
    for copy in copies[4:]:
        copy.wait()


def rows_by_pair(packed, out_ref, fields):
    lower = lower_half((ROWS, LANES))
    for pair in range((fields + 1) // 2):
        even = packed[2 * pair * ROWS : (2 * pair + 1) * ROWS]
        odd = jnp.zeros_like(even)
        if 2 * pair + 1 < fields:
            odd = packed[(2 * pair + 1) * ROWS : (2 * pair + 2) * ROWS]
        out_ref[pair, 0:ROWS, :] = jnp.where(lower, even, swap_halves(odd))
        out_ref[pair, ROWS : 2 * ROWS, :] = jnp.where(lower, swap_halves(even), odd)


def flux_local_coefficients(flux_ref, stage_ref, out_ref):
    fields, faces, elements = flux_ref.shape[0], flux_ref.shape[2], flux_ref.shape[3]
    rows = 2 * ROWS
    filled = lane_index((rows, LANES)) < elements
    lanes, sublanes = lane_index((ROWS, LANES)), row_index((ROWS, LANES))
    picks = [one_where(lanes % elements == half * ROWS + sublanes) for half in range(2)]
    square = (LANES, LANES)
    right = one_where(row_index(square) // (2 * elements) == lane_index(square) % faces).astype(BF16)
    for row in range(fields):
        values = None
        for face in range(faces):
            stage_ref[row, face * rows : face * rows + fields, 0:elements] = flux_ref[row, :, face, :]
            part = jnp.where(filled, stage_ref[row, face * rows : (face + 1) * rows, :], 0.0)
            values = part if values is None else values + pltpu.roll(part, face * 2 * elements, 1)
        stage_ref[row, 0:rows, :] = high_and_low(values, elements)
        left = [stage_ref[row, col : col + 1, :] * pick for col in range(fields) for pick in picks]
        spread = product(jnp.concatenate(left, axis=0).astype(BF16), right)
        out_ref[row * fields : (row + 1) * fields] = spread.reshape(fields, 2, ROWS, LANES)


def flux_remote_coefficients(flux_ref, stage_ref, out_ref):
    fields, faces, elements = flux_ref.shape[0], flux_ref.shape[2], flux_ref.shape[3]
    pairs = (fields + 1) // 2
    rows = stage_ref.shape[1] // 2
    filled = lane_index((rows, LANES)) < elements
    lanes, sublanes = lane_index((elements, LANES)), row_index((elements, LANES))
    pick = one_where((lanes % elements == sublanes) & (lanes < 4 * elements))
    square = (LANES, LANES)
    from_lane = row_index(square)
    same_parity = (from_lane // elements) % 2 == lane_index(square) // HALF
    right = one_where(same_parity & (from_lane < 4 * elements)).astype(BF16)
    for pair in range(pairs):
        values = None
        for row in range(2 * pair, min(2 * pair + 2, fields)):
            start = (row % 2) * rows
            for col in range(fields):
                at = start + col * faces
                stage_ref[pair, at : at + faces, 0:elements] = flux_ref[row, col]
            part = jnp.where(filled, stage_ref[pair, start : start + rows, :], 0.0)
            values = part if values is None else values + pltpu.roll(part, elements, 1)
        stage_ref[pair, 0:rows, :] = high_and_low(values, 2 * elements)
        for face in range(faces):
            left = []
            for col in range(fields):
                at = col * faces + face
                left.append(stage_ref[pair, at : at + 1, :] * pick)
            spread = product(jnp.concatenate(left, axis=0).astype(BF16), right)
            at = (face * pairs + pair) * fields
            out_ref[at : at + fields] = spread.reshape(fields, elements, LANES)


def local_terms(packed, star_ref, flux_ref, volume_ref, trace_ref, lift_ref, fields, kinds):
    left = stack_left(packed)
    volume = star_mix(product(left, volume_ref[...]), star_ref, fields, kinds)
    traces = product(left, trace_ref[...])
    sums = []
    for col in range(fields):
        halves = []
        for half in range(2):
            total = None
            for row in range(fields):
                part = traces[row * ROWS : (row + 1) * ROWS, half * LANES : (half + 1) * LANES]
                term = flux_ref[row * fields + col, half] * part
                total = term if total is None else total + term
            halves.append(total)
        sums.append(jnp.concatenate(halves, axis=1))
    return volume + product(stack_left(jnp.concatenate(sums, axis=0)), lift_ref[...])


def combo_code(lanes, turns, face_modes):
    in_face = lanes % HALF
    code = jnp.where(in_face < turns * face_modes, (lanes // HALF) * turns + in_face // face_modes, -1)
    return code.astype(F32)


def ghost_terms(
    flux_ref, stage_ref, code_ref, composed, lift_sides, lane_code, flux_out, operator_out, scatter_out, sends, fields
):
    faces, elements = flux_ref.shape[2], flux_ref.shape[3]
    rows = 2 * ROWS
    shape = (rows, LANES)
    lanes = lane_index(shape)

    def along_lanes(start):
        row = code_ref[start : start + 1, :]
        for face in range(1, faces):
            row = row + pltpu.roll(code_ref[start + face : start + face + 1, :], face * elements, 1)
        return row + swap_halves(row)

    slots, codes = along_lanes(0), along_lanes(faces)
    ghosts = elements + row_index(shape)
    found = one_where(jnp.broadcast_to(slots, shape) == ghosts.astype(F32))
    first = jnp.where(lanes < HALF, found, 0.0)
    code = jnp.sum(first * codes, axis=1, keepdims=True)
    face_of = jnp.sum(first * (lanes // elements).astype(F32), axis=1, keepdims=True)
    element_of = jnp.sum(first * (lanes % elements).astype(F32), axis=1, keepdims=True)
    numbers = [slot * sends + place for slot in range(4) for place in range(sends // 2)]

    filled = lanes < elements
    values = []
    for field in range(fields):
        total = None
        for face in range(faces):
            stage_ref[field, face * rows : face * rows + fields, 0:elements] = flux_ref[field, :, face, :]
            part = jnp.where(filled, stage_ref[field, face * rows : (face + 1) * rows, :], 0.0)
            total = part if total is None else total + pltpu.roll(part, face * elements, 1)
        total = jnp.where(row_index(shape) < fields, total, 0.0)
        values.append(high_and_low(total, HALF))
    picked = jnp.concatenate([jnp.broadcast_to(found[number : number + 1], (HALF, LANES)) for number in numbers], axis=0)
    flux_out[...] = lax.dot_general(
        jnp.concatenate(values, axis=0).astype(BF16), picked.astype(BF16), (((1,), (1,)), ((), ())),
        preferred_element_type=F32,
    )

    left = []
    for number in numbers:
        chosen = composed * one_where(lane_code == code[number : number + 1])
        both = chosen[:, 0:LANES] + chosen[:, LANES : 2 * LANES]
        high, low = split(both + swap_halves(both))
        left.append(jnp.concatenate([jnp.where(lower_half(high.shape), high, low), high], axis=1))
    high, low = split(lift_sides)
    lifts = product(jnp.concatenate(left, axis=0), jnp.concatenate([high, high, low, jnp.zeros_like(low)], axis=0))
    side_lane = (lane_index((1, faces * HALF)) // HALF).astype(F32)
    place_of = jnp.zeros((1, LANES), F32)
    for at, number in enumerate(numbers):
        chosen = lifts[at * HALF : (at + 1) * HALF] * one_where(side_lane == face_of[number : number + 1])
        both = chosen[:, 0:LANES] + chosen[:, LANES : 2 * LANES]
        high, low = split(both + swap_halves(both))
        operator_out[at] = jnp.concatenate([high, high, low, jnp.zeros_like(low)], axis=0)
        place_of = jnp.where(lane_index((1, LANES)) // rows == at, element_of[number : number + 1], place_of)
    square = (fields * elements, LANES)
    here = (row_index(square) // elements == lane_index(square) % rows) & (
        (row_index(square) % elements).astype(F32) == place_of
    )
    one = one_where(here).astype(BF16)
    scatter_out[...] = jnp.concatenate([one, one], axis=1)


def prepare_kernel(
    packed_ref, early_ref, stiffness_ref, star_ref, flux_local_ref, flux_remote_ref, restrict_ref, lift_ref, orient_ref,
    slot_ref, face_ref, turn_ref,
    base_out, local_out, remote_out, volume_out, trace_out, local_lift_out, compose_out,
    remote_lift_out, choose_out, mask_out, code_ref, composed_out, sides_ref,
    local_work_ref, remote_work_ref, block_ref, wide_ref, face_work_ref, orient_work_ref, code_work_ref,
):
    fields, kinds = packed_ref.shape[0], stiffness_ref.shape[0]
    face_modes, faces, modes = restrict_ref.shape
    turns = orient_ref.shape[0]
    flux_local_coefficients(flux_local_ref, local_work_ref, local_out)
    flux_remote_coefficients(flux_remote_ref, remote_work_ref, remote_out)

    block_ref[...] = jnp.zeros(block_ref.shape, F32)
    volume_out[...] = stack_right(stiffness_blocks(stiffness_ref, block_ref, False))

    wide_ref[...] = jnp.zeros(wide_ref.shape, F32)
    for mode in range(face_modes):
        at = mode * faces
        wide_ref[at : at + faces, 0:modes] = restrict_ref[mode]
        wide_ref[LANES + at : LANES + at + faces, HALF : HALF + modes] = restrict_ref[mode]
    trace_out[...] = stack_right(wide_ref[...].T)
    for mode in range(face_modes):
        at = mode * faces
        wide_ref[at : at + faces, 0:modes] = -lift_ref[mode]
        wide_ref[LANES + at : LANES + at + faces, HALF : HALF + modes] = -lift_ref[mode]
    local_lift_out[...] = stack_right(wide_ref[...])

    face_work_ref[...] = jnp.zeros(face_work_ref.shape, F32)
    orient_work_ref[...] = jnp.zeros(orient_work_ref.shape, F32)
    for turn in range(turns):
        orient_work_ref[turn * face_modes : (turn + 1) * face_modes, 0:face_modes] = orient_ref[turn]
    for face in range(faces):
        face_work_ref[0:face_modes, face * LANES : face * LANES + modes] = restrict_ref[:, face, :]
        face_work_ref[0:face_modes, face * LANES + HALF : face * LANES + HALF + modes] = restrict_ref[:, face, :]
    composed = jnp.dot(
        orient_work_ref[...], face_work_ref[...], precision=lax.Precision.HIGHEST, preferred_element_type=F32
    )
    stacked = jnp.concatenate([composed[:, face * LANES : (face + 1) * LANES] for face in range(faces)], axis=0)
    high, low = split(stacked.T[0:HALF])
    compose_out[...] = jnp.concatenate([high, high, low, jnp.zeros_like(low)], axis=0)
    wide_ref[...] = jnp.zeros(wide_ref.shape, F32)
    for face in range(faces):
        for turn in range(turns):
            rows = slice(face * HALF + turn * face_modes, face * HALF + (turn + 1) * face_modes)
            wide_ref[rows, 0:modes] = -lift_ref[:, face, :]
            wide_ref[rows, HALF : HALF + modes] = -lift_ref[:, face, :]
    remote_lift_out[...] = stack_right(wide_ref[...])

    elements = slot_ref.shape[1]
    code_work_ref[...] = jnp.zeros(code_work_ref.shape, F32)
    slots = slot_ref[...]
    sends = (choose_out.shape[1] // 2 - elements) // 4
    group = (slots - elements) // sends
    moved = slots
    for side in range(4):
        moved = jnp.where(group == side, slots + (ghost_slot(side) - side) * sends, moved)
    code_work_ref[0:faces, 0:elements] = jnp.where(slots < elements, slots, moved).astype(F32)
    code_work_ref[faces : 2 * faces, 0:elements] = (face_ref[...] * turns + turn_ref[...]).astype(F32)
    code_ref[...] = code_work_ref[0 : 2 * faces, :]
    codes = code_work_ref[...].T[0:elements, :]
    sources = choose_out.shape[1] // 2
    source_lane = (lane_index((elements, 2 * sources)) % sources).astype(F32)
    lanes = lane_index((elements, mask_out.shape[1]))
    lane_code = combo_code(lanes, turns, face_modes)
    picks, masks = [], []
    for face in range(faces):
        picks.append(jnp.where(codes[:, face : face + 1] == source_lane, 1.0, 0.0))
        masks.append(jnp.where(codes[:, faces + face : faces + face + 1] == lane_code, 1.0, 0.0))
    choose_out[...] = jnp.concatenate(picks, axis=0).astype(BF16)
    mask_out[...] = jnp.concatenate(masks, axis=0)

    sides_ref[...] = jnp.zeros(sides_ref.shape, F32)
    for face in range(faces):
        for turn in range(turns):
            rows = slice(turn * face_modes, (turn + 1) * face_modes)
            sides_ref[rows, face * HALF : face * HALF + modes] = -lift_ref[:, face, :]
    composed_out[...] = stacked.T[0:HALF]

    early = early_ref[...].reshape(fields * ROWS, LANES)
    terms = local_terms(early, star_ref, local_out, volume_out, trace_out, local_lift_out, fields, kinds)
    base_out[...] = packed_ref[...] + terms.reshape(fields, ROWS, LANES)


def remote_terms(rows_ref, remote_ref, compose_ref, lift_ref, choose_ref, mask_ref, fields):
    pairs = rows_ref.shape[0]
    faces = lift_ref.shape[0] // (3 * HALF)
    elements = choose_ref.shape[0] // faces
    sources = jnp.concatenate([rows_ref[pair] for pair in range(pairs)], axis=1)
    gathered = product(choose_ref[...], jnp.concatenate(split(sources), axis=0))
    folded = []
    for face in range(faces):
        sums = []
        for col in range(fields):
            total = None
            for pair in range(pairs):
                part = gathered[face * elements : (face + 1) * elements, pair * LANES : (pair + 1) * LANES]
                term = remote_ref[(face * pairs + pair) * fields + col] * part
                total = term if total is None else total + term
            sums.append(total)
        mixed = jnp.concatenate(sums, axis=0)
        high, low = split(mixed + swap_halves(mixed))
        first = jnp.where(lower_half(high.shape), high, low)
        turned = product(jnp.concatenate([first, high], axis=1), compose_ref[...])
        mask = mask_ref[face * elements : (face + 1) * elements, :]
        chosen = (turned.reshape(fields, elements, turned.shape[1]) * mask[None]).reshape(turned.shape)
        both = chosen[:, 0:LANES] + chosen[:, LANES : 2 * LANES]
        folded.append(both + swap_halves(both))
    lower = lower_half(folded[0].shape)
    left = [jnp.where(lower, folded[face], folded[face + 1]) for face in range(0, faces, 2)]
    result = product(stack_left(jnp.concatenate(left, axis=1)), lift_ref[...])
    result = result.reshape(fields, 2, ROWS, LANES)
    return jnp.where(lower_half((ROWS, LANES))[None], result[:, 0], result[:, 1])


def middle_kernel(
    base_ref, early_ref, late_ref, star_ref, remote_ref, derive_ref, compose_ref, lift_ref, choose_ref, mask_ref,
    rate_hbm, send_hbm, ahead_1, from_0, from_1, from_2, from_3,
    middle_out, late_out, send_0, send_1, send_2, send_3,
    rows_ref, late_rows, rate_ref, send_ref, sems,
):
    copies = [
        pltpu.make_async_copy(rate_hbm, rate_ref, sems.at[0]),
        pltpu.make_async_copy(send_hbm, send_ref, sems.at[1]),
    ]
    for copy in copies:
        copy.start()
    fields = base_ref.shape[0]
    kinds = star_ref.shape[0] // (fields * fields)
    pairs = rows_ref.shape[0]
    sends = send_ref.shape[2]
    fast = sends // 2
    elements = 2 * ROWS
    rows_by_pair(early_ref[...].reshape(fields * ROWS, LANES), rows_ref, fields)
    for side, arrived in enumerate((from_0, from_1, from_2, from_3)):
        at = elements + side * sends
        for pair in range(pairs):
            rows = slice(pair * sends, (pair + 1) * sends)
            got = arrived[rows, :]
            rows_ref[pair, at : at + sends, :] = got + ahead_1[rows, :] if side == AHEAD else got
    middle = base_ref[...] + remote_terms(
        rows_ref, remote_ref, compose_ref, lift_ref, choose_ref, mask_ref, fields
    )
    middle_out[...] = middle
    start = middle.reshape(fields * ROWS, LANES)

    def step(degree, carry):
        current, early = carry
        current = star_mix(product(stack_left(current), derive_ref[...]), star_ref, fields, kinds)
        return current, early + weight_at(0.0, 0.5, degree) * current

    _, restart = lax.fori_loop(1, DERIVS, step, (start, taylor_weight(0.0, 0.5, 0) * start))
    for copy in copies:
        copy.wait()
    sublane = lax.broadcasted_iota(jnp.int32, (ROWS, LANES), 0)
    lower = lower_half((ROWS, LANES))
    is_fast = jnp.zeros((ROWS, LANES), jnp.int32)
    for element in range(elements):
        here = (sublane == element % ROWS) & (lower if element < ROWS else jnp.logical_not(lower))
        is_fast = jnp.where(here, rate_ref[element], is_fast)
    late = jnp.where((is_fast == 2)[None], restart.reshape(fields, ROWS, LANES), late_ref[...])
    late_out[...] = late
    both = late.reshape(fields * ROWS, LANES)
    swapped = swap_halves(both)
    wide = lower_half(both.shape)
    late_rows[:, 0:ROWS, :] = jnp.where(wide, both, swapped).reshape(late.shape)
    late_rows[:, ROWS : 2 * ROWS, :] = jnp.where(wide, swapped, both).reshape(late.shape)
    first_half = lower_half((1, LANES))
    for slot, out in enumerate((send_0, send_1, send_2, send_3)):
        out[...] = jnp.zeros(out.shape, F32)
        side = message_side(slot)
        places = [send_ref[0, side, place] for place in range(fast)]
        for field in range(fields):
            halves = [late_rows[field, pl.ds(element, 1), :] for element in places]
            out[field : field + 1, :] = jnp.where(first_half, *halves)


def local_kernel(
    middle_ref, late_ref, star_ref, flux_ref, volume_ref, trace_ref, lift_ref,
    remote_ref, compose_ref, remote_lift_ref, choose_ref, mask_ref, flux_remote_ref, code_ref, composed_ref, sides_ref,
    orient_ref, ahead_1, first_0, first_1, first_2, first_3,
    base_out, ghost_flux_out, ghost_operator_out, scatter_out, rows_ref, stage_ref,
):
    fields = middle_ref.shape[0]
    kinds = star_ref.shape[0] // (fields * fields)
    pairs = rows_ref.shape[0]
    elements = 2 * ROWS
    sends = (rows_ref.shape[1] - elements) // 4
    fast = sends // 2
    late = late_ref[...].reshape(fields * ROWS, LANES)
    rows_by_pair(late, rows_ref, fields)
    for slot, first in enumerate((first_0, first_1, first_2, first_3)):
        at = elements + slot * sends
        for pair in range(pairs):
            rows_ref[pair, at : at + fast, :] = jnp.zeros((fast, LANES), F32)
            row = pairs * sends + pair * fast
            got = first[row : row + fast, :]
            rows_ref[pair, at + fast : at + sends, :] = got + ahead_1[row : row + fast, :] if slot == AHEAD else got
    terms = local_terms(late, star_ref, flux_ref, volume_ref, trace_ref, lift_ref, fields, kinds)
    remote = remote_terms(rows_ref, remote_ref, compose_ref, remote_lift_ref, choose_ref, mask_ref, fields)
    base_out[...] = middle_ref[...] + terms.reshape(fields, ROWS, LANES) + remote
    lane_code = combo_code(lane_index((1, composed_ref.shape[1])), orient_ref.shape[0], orient_ref.shape[1])
    ghost_terms(
        flux_remote_ref, stage_ref, code_ref, composed_ref[...], sides_ref[...], lane_code,
        ghost_flux_out, ghost_operator_out, scatter_out, sends, fields,
    )


def final_kernel(
    base_ref, ghost_flux_ref, ghost_operator_ref, scatter_ref, second_0, second_1, second_2, second_3, result_out,
):
    fields = base_ref.shape[0]
    modes = result_out.shape[2]
    rows = second_0.shape[0]
    lower = lower_half((rows, LANES))
    added = []
    for slot, second in enumerate((second_0, second_1, second_2, second_3)):
        mixed = None
        for field in range(fields):
            coefficient = ghost_flux_ref[field * rows : (field + 1) * rows, slot * LANES : (slot + 1) * LANES]
            term = coefficient * second[field : field + 1, :]
            mixed = term if mixed is None else mixed + term
        high, low = split(mixed)
        high_swapped, low_swapped = split(swap_halves(mixed))
        for place, parts in enumerate(((high, low_swapped, high), (high_swapped, low, high_swapped))):
            left = jnp.concatenate([jnp.where(lower, parts[0], parts[1]), parts[2]], axis=1)
            added.append(product(left, ghost_operator_ref[2 * slot + place]))
    right = jnp.concatenate(split(jnp.concatenate(added, axis=0)), axis=0)
    scattered = product(scatter_ref[...], right).reshape(fields, 2, ROWS, LANES)
    result = base_ref[...] + jnp.where(lower_half((ROWS, LANES))[None], scattered[:, 0], scattered[:, 1])
    result_out[:, 0:ROWS, :] = result[:, :, 0:modes]
    result_out[:, ROWS : 2 * ROWS, :] = result[:, :, HALF : HALF + modes]


VMEM = pl.BlockSpec(memory_space=pltpu.VMEM)
HBM = pl.BlockSpec(memory_space=pltpu.HBM)


def call(kernel, ins, outs, scratch, args, name, flops):
    shapes = [jax.ShapeDtypeStruct(shape, dtype) for shape, dtype in outs]
    args = [
        pltpu.with_memory_space_constraint(arg, pltpu.HBM) if spec is HBM else arg for spec, arg in zip(ins, args)
    ]
    return pl.pallas_call(
        kernel,
        out_shape=shapes,
        in_specs=ins,
        out_specs=[VMEM] * len(outs),
        scratch_shapes=[pltpu.VMEM(*one) if isinstance(one, tuple) else one for one in scratch],
        compiler_params=pltpu.CompilerParams(vmem_limit_bytes=16 * 1024 * 1024),
        cost_estimate=pl.CostEstimate(flops=flops, bytes_accessed=4_000_000, transcendentals=0),
        name=name,
    )(*args)


def exchange(outgoing, ahead=None):
    arrived, early = [], []
    for slot, ((axis, far), message) in enumerate(zip(SWAPS, outgoing)):
        size = lax.axis_size(axis)
        assert size % 2 == 0
        pairs = []
        for first in range(1 if far else 0, size, 2):
            second = (first + 1) % size
            pairs += [(first, second), (second, first)]
        if ahead is not None and slot == AHEAD:
            early.append(lax.ppermute(ahead, axis, pairs[0:2]))
            pairs = pairs[2:]
        arrived.append(lax.ppermute(message, axis, pairs))
    return early + arrived


def up_to(count, multiple):
    return -(-count // multiple) * multiple


def local(
    solution, stiffness, star_matrices, face_restrict, face_lift, orient_maps, flux_local, flux_remote,
    cluster_rate, send_list, neighbour_slot, neighbour_face, neighbour_turn,
):
    fields, elements = solution.shape[1], solution.shape[2]
    kinds = stiffness.shape[0]
    faces = face_restrict.shape[0]
    sides, sends = send_list.shape[1], send_list.shape[2]
    fast = sends // 2
    pairs = (fields + 1) // 2
    assert elements == 2 * ROWS and solution.shape[0] <= HALF and fast == 2
    values = jnp.transpose(solution, (1, 2, 0))
    star = jnp.transpose(star_matrices, (1, 2, 0, 3))
    local_part = jnp.transpose(flux_local, (1, 2, 0, 3))
    remote_part = jnp.transpose(flux_remote, (1, 2, 0, 3))
    restrict = jnp.transpose(face_restrict, (1, 0, 2))
    lift = jnp.transpose(face_lift, (2, 0, 1))

    packed = (fields, ROWS, LANES)
    first_shape = (up_to(pairs * (sends + fast), ROWS), LANES)
    second_shape = (up_to(fields, 2 * ROWS), LANES)
    star_shape = (fields * fields * kinds, ROWS, LANES)
    combos = faces * HALF
    sources = elements + sides * sends

    waiting = (local_part, remote_part, restrict, lift, orient_maps, neighbour_slot, neighbour_face, neighbour_turn)
    made = call(
        predict_kernel,
        [HBM] * (4 + len(LATER)),
        [(packed, F32)] * 2 + [(first_shape, F32)] * (1 + sides) + [
            (packed, F32), (star_shape, F32), ((3 * LANES, kinds * LANES), BF16), (stiffness.shape, F32),
        ] + [(array.shape, array.dtype) for array in waiting],
        [
            ((fields, kinds * up_to(fields, 2 * ROWS), LANES), F32),
            ((pairs, elements, LANES), F32), ((pairs, elements, LANES), F32),
            (values.shape, F32), ((kinds, LANES, LANES), F32), (star.shape, F32),
            pltpu.SMEM(send_list.shape, jnp.int32), pltpu.SemaphoreType.DMA((4 + len(LATER),)),
        ],
        (values, stiffness, star, send_list, *waiting),
        "predict", 100_000_000,
    )
    early, late, ahead, outgoing = made[0], made[1], made[2], made[3 : 3 + sides]
    start, star_coef, derive_op, stiffness_kept = made[3 + sides : 7 + sides]
    waiting = made[7 + sides :]
    first = exchange(outgoing, ahead)
    (
        base, local_coef, remote_coef, volume_op, trace_op, local_lift, compose_op, remote_lift, choose, mask,
        codes, composed, lift_sides,
    ) = call(
        prepare_kernel,
        [VMEM] * 12,
        [
            (packed, F32), ((fields * fields, 2, ROWS, LANES), F32),
            ((faces * pairs * fields, elements, LANES), F32),
            ((3 * LANES, kinds * LANES), BF16), ((3 * LANES, 2 * LANES), BF16),
            ((6 * LANES, LANES), BF16), ((2 * LANES, combos), BF16), ((3 * faces * HALF, LANES), BF16),
            ((faces * elements, 2 * sources), BF16), ((faces * elements, combos), F32),
            ((2 * faces, LANES), F32), ((HALF, combos), F32), ((HALF, faces * HALF), F32),
        ],
        [
            ((fields, 2 * ROWS * faces, LANES), F32), ((pairs, 2 * up_to(4 * fields, ROWS), LANES), F32),
            ((kinds, LANES, LANES), F32), ((2 * LANES, LANES), F32),
            ((LANES, faces * LANES), F32), ((HALF, LANES), F32), ((LANES, LANES), F32),
        ],
        (start, early, stiffness_kept, star_coef, *waiting),
        "prepare", 200_000_000,
    )
    middle, late_value, *outgoing = call(
        middle_kernel,
        [VMEM] * 10 + [HBM] * 2 + [VMEM] * len(first),
        [(packed, F32)] * 2 + [(second_shape, F32)] * sides,
        [
            ((pairs, sources, LANES), F32), ((fields, elements, LANES), F32),
            pltpu.SMEM(cluster_rate.shape, jnp.int32), pltpu.SMEM(send_list.shape, jnp.int32),
            pltpu.SemaphoreType.DMA((2,)),
        ],
        (
            base, early, late, star_coef, remote_coef, derive_op, compose_op, remote_lift, choose, mask,
            cluster_rate, send_list, *first,
        ),
        "middle", 200_000_000,
    )
    second = exchange(outgoing)
    base, ghost_flux, ghost_op, scatter = call(
        local_kernel,
        [VMEM] * (17 + len(first)),
        [
            (packed, F32), ((fields * second_shape[0], sides * LANES), F32),
            ((sides * fast, 2 * LANES, LANES), BF16), ((fields * elements, 2 * LANES), BF16),
        ],
        [((pairs, sources, LANES), F32), ((fields, 2 * ROWS * faces, LANES), F32)],
        (
            middle, late_value, star_coef, local_coef, volume_op, trace_op, local_lift,
            remote_coef, compose_op, remote_lift, choose, mask, waiting[1], codes, composed, lift_sides, waiting[4],
            *first,
        ),
        "local_late", 200_000_000,
    )
    (result,) = call(
        final_kernel,
        [VMEM] * 8,
        [(values.shape, F32)],
        [],
        (base, ghost_flux, ghost_op, scatter, *second),
        "final", 200_000_000,
    )
    return jnp.transpose(result, (2, 0, 1))


def solution(mesh):
    placed = (
        P(None, None, ("dom", "sub")),
        P(),
        P(None, None, None, ("dom", "sub")),
        P(),
        P(),
        P(),
        P(None, None, None, ("dom", "sub")),
        P(None, None, None, ("dom", "sub")),
        P(("dom", "sub")),
        P(("dom", "sub"), None, None),
        P(None, ("dom", "sub")),
        P(None, ("dom", "sub")),
        P(None, ("dom", "sub")),
    )
    return jax.shard_map(
        local, mesh=mesh, in_specs=placed, out_specs=P(None, None, ("dom", "sub")), check_vma=False
    )
```

```python
import math

import jax
import jax.numpy as jnp
from jax import lax
from jax.experimental import pallas as pl
from jax.experimental.pallas import tpu as pltpu
from jax.sharding import PartitionSpec as P

DERIVS = 6
LANES = 128
HALF = 64
ROWS = 8
F32 = jnp.float32
BF16 = jnp.bfloat16
LATER = ("flux_local", "flux_remote", "face_restrict", "face_lift", "orient_maps", "slot", "face", "turn")
AXES = ("dom", "sub")
SWAPS = (("dom", True), ("dom", False), ("sub", True), ("sub", False))


def taylor_weight(lower, upper, degree):
    return (upper ** (degree + 1) - lower ** (degree + 1)) / math.factorial(degree + 1)


def weight_at(lower, upper, degree):
    result = jnp.float32(taylor_weight(lower, upper, 1))
    for option in range(2, DERIVS):
        result = jnp.where(degree == option, jnp.float32(taylor_weight(lower, upper, option)), result)
    return result


def split(values):
    high = values.astype(BF16)
    low = (values - high.astype(F32)).astype(BF16)
    return high, low


def stack_left(values):
    high, low = split(values)
    return jnp.concatenate([high, low, high], axis=1)


def stack_right(values):
    high, low = split(values)
    return jnp.concatenate([high, high, low], axis=0)


def product(left, right):
    return jnp.dot(left, right, preferred_element_type=F32)


def odd_place(axis):
    return lax.rem(lax.axis_index(axis), 2)


def message_side(slot):
    axis, far = SWAPS[slot]
    odd = odd_place(axis)
    return 2 * AXES.index(axis) + (odd if far else 1 - odd)


def ghost_slot(side):
    axis = AXES[side // 2]
    even_far = side % 2 == 0
    return jnp.where(odd_place(axis) == 0, SWAPS.index((axis, even_far)), SWAPS.index((axis, not even_far)))


def lane_index(shape):
    return lax.broadcasted_iota(jnp.int32, shape, len(shape) - 1)


def lower_half(shape):
    return lane_index(shape) < HALF


def swap_halves(values):
    return pltpu.roll(values, HALF, values.ndim - 1)


def pack(values_ref, packed_ref):
    modes = values_ref.shape[2]
    packed_ref[...] = jnp.zeros(packed_ref.shape, F32)
    packed_ref[:, :, 0:modes] = values_ref[:, 0:ROWS, :]
    packed_ref[:, :, HALF : HALF + modes] = values_ref[:, ROWS : 2 * ROWS, :]


def high_and_low(values, shift):
    high = values.astype(BF16).astype(F32)
    return high + pltpu.roll(values - high, shift, 1)


def row_index(shape):
    return lax.broadcasted_iota(jnp.int32, shape, len(shape) - 2)


def one_where(condition):
    return jnp.where(condition, 1.0, 0.0)


def star_coefficients(star_ref, stage_ref, star_out):
    fields, kinds, elements = star_ref.shape[0], star_ref.shape[2], star_ref.shape[3]
    lanes = lane_index((ROWS, LANES))
    pick = one_where((lanes % ROWS == row_index((ROWS, LANES))) & (lanes < 2 * elements))
    from_lane = row_index((LANES, LANES))
    same_half = (from_lane % elements) // ROWS == lane_index((LANES, LANES)) // HALF
    right = one_where(same_half & (from_lane < 2 * elements)).astype(BF16)
    filled = lane_index(stage_ref.shape[1:]) < elements
    for row in range(fields):
        for col in range(fields):
            stage_ref[row, col * 4 : col * 4 + kinds, 0:elements] = star_ref[row, col]
        values = jnp.where(filled, stage_ref[row], 0.0)
        stage_ref[row] = high_and_low(values, elements)
        spreads = []
        for kind in range(kinds):
            for col in range(fields):
                at = col * 4 + kind
                spreads.append(stage_ref[row, at : at + 1, :] * pick)
        spread_out = product(jnp.concatenate(spreads, axis=0).astype(BF16), right)
        count = kinds * fields
        star_out[row * count : (row + 1) * count] = spread_out.reshape(count, ROWS, LANES)


def star_mix(columns, star_ref, fields, kinds):
    sums = []
    for col in range(fields):
        parts = []
        for kind in range(kinds):
            total = None
            for row in range(fields):
                part = columns[row * ROWS : (row + 1) * ROWS, kind * LANES : (kind + 1) * LANES]
                term = star_ref[(row * kinds + kind) * fields + col] * part
                total = term if total is None else total + term
            parts.append(total)
        sums.append(sum(parts[1:], parts[0]))
    return jnp.concatenate(sums, axis=0)


def stiffness_blocks(stiffness_ref, block_ref, turned):
    kinds, modes = stiffness_ref.shape[0], stiffness_ref.shape[1]
    block_ref[...] = jnp.zeros(block_ref.shape, F32)
    for kind in range(kinds):
        matrix = -stiffness_ref[kind].T if turned else stiffness_ref[kind]
        block_ref[kind, 0:modes, 0:modes] = matrix
        block_ref[kind, HALF : HALF + modes, HALF : HALF + modes] = matrix
    return jnp.concatenate([block_ref[kind] for kind in range(kinds)], axis=1)


def predict_kernel(*refs):
    later = len(LATER)
    solution_hbm, stiffness_hbm, star_hbm, send_hbm = refs[0:4]
    later_hbm, refs = refs[4 : 4 + later], refs[4 + later :]
    early_out, late_out, send_0, send_1, send_2, send_3 = refs[0:6]
    packed_ref, coef_ref, derive_ref, stiffness_ref = refs[6:10]
    later_out, refs = refs[10 : 10 + later], refs[10 + later :]
    work_ref, early_rows, late_rows, solution_ref, block_ref, star_ref, send_ref, sems = refs

    sources = (star_hbm, stiffness_hbm, solution_hbm, send_hbm, *later_hbm)
    targets = (star_ref, stiffness_ref, solution_ref, send_ref, *later_out)
    copies = [
        pltpu.make_async_copy(source, target, sems.at[number])
        for number, (source, target) in enumerate(zip(sources, targets))
    ]
    for copy in copies:
        copy.start()
    fields, kinds = star_ref.shape[0], star_ref.shape[2]
    pairs = (fields + 1) // 2
    for copy in copies[0:3]:
        copy.wait()
    derive_ref[...] = stack_right(stiffness_blocks(stiffness_ref, block_ref, True))
    star_coefficients(star_ref, work_ref, coef_ref)
    pack(solution_ref, packed_ref)
    start = packed_ref[...].reshape(fields * ROWS, LANES)

    def step(degree, carry):
        current, early, late = carry
        current = star_mix(product(stack_left(current), derive_ref[...]), coef_ref, fields, kinds)
        early = early + weight_at(0.0, 0.5, degree) * current
        late = late + weight_at(0.5, 1.0, degree) * current
        return current, early, late

    _, early, late = lax.fori_loop(
        1, DERIVS, step, (start, taylor_weight(0.0, 0.5, 0) * start, taylor_weight(0.5, 1.0, 0) * start)
    )
    early_out[...] = early.reshape(fields, ROWS, LANES)
    late_out[...] = late.reshape(fields, ROWS, LANES)
    rows_by_pair(early, early_rows, fields)
    rows_by_pair(late, late_rows, fields)
    copies[3].wait()
    sends = send_ref.shape[2]
    fast = sends // 2
    for side, out in enumerate((send_0, send_1, send_2, send_3)):
        out[...] = jnp.zeros(out.shape, F32)
        for place in range(sends):
            element = send_ref[0, message_side(side), place]
            for pair in range(pairs):
                row = pair * sends + place
                out[row : row + 1, :] = early_rows[pair, pl.ds(element, 1), :]
            if place >= fast:
                for pair in range(pairs):
                    row = pairs * sends + pair * fast + place - fast
                    out[row : row + 1, :] = late_rows[pair, pl.ds(element, 1), :]
    for copy in copies[4:]:
        copy.wait()


def rows_by_pair(packed, out_ref, fields):
    lower = lower_half((ROWS, LANES))
    for pair in range((fields + 1) // 2):
        even = packed[2 * pair * ROWS : (2 * pair + 1) * ROWS]
        odd = jnp.zeros_like(even)
        if 2 * pair + 1 < fields:
            odd = packed[(2 * pair + 1) * ROWS : (2 * pair + 2) * ROWS]
        out_ref[pair, 0:ROWS, :] = jnp.where(lower, even, swap_halves(odd))
        out_ref[pair, ROWS : 2 * ROWS, :] = jnp.where(lower, swap_halves(even), odd)


def flux_local_coefficients(flux_ref, stage_ref, out_ref):
    fields, faces, elements = flux_ref.shape[0], flux_ref.shape[2], flux_ref.shape[3]
    rows = 2 * ROWS
    filled = lane_index((rows, LANES)) < elements
    lanes, sublanes = lane_index((ROWS, LANES)), row_index((ROWS, LANES))
    picks = [one_where(lanes % elements == half * ROWS + sublanes) for half in range(2)]
    square = (LANES, LANES)
    right = one_where(row_index(square) // (2 * elements) == lane_index(square) % faces).astype(BF16)
    for row in range(fields):
        values = None
        for face in range(faces):
            stage_ref[row, face * rows : face * rows + fields, 0:elements] = flux_ref[row, :, face, :]
            part = jnp.where(filled, stage_ref[row, face * rows : (face + 1) * rows, :], 0.0)
            values = part if values is None else values + pltpu.roll(part, face * 2 * elements, 1)
        stage_ref[row, 0:rows, :] = high_and_low(values, elements)
        left = [stage_ref[row, col : col + 1, :] * pick for col in range(fields) for pick in picks]
        spread = product(jnp.concatenate(left, axis=0).astype(BF16), right)
        out_ref[row * fields : (row + 1) * fields] = spread.reshape(fields, 2, ROWS, LANES)


def flux_remote_coefficients(flux_ref, stage_ref, out_ref):
    fields, faces, elements = flux_ref.shape[0], flux_ref.shape[2], flux_ref.shape[3]
    pairs = (fields + 1) // 2
    rows = stage_ref.shape[1] // 2
    filled = lane_index((rows, LANES)) < elements
    lanes, sublanes = lane_index((elements, LANES)), row_index((elements, LANES))
    pick = one_where((lanes % elements == sublanes) & (lanes < 4 * elements))
    square = (LANES, LANES)
    from_lane = row_index(square)
    same_parity = (from_lane // elements) % 2 == lane_index(square) // HALF
    right = one_where(same_parity & (from_lane < 4 * elements)).astype(BF16)
    for pair in range(pairs):
        values = None
        for row in range(2 * pair, min(2 * pair + 2, fields)):
            start = (row % 2) * rows
            for col in range(fields):
                at = start + col * faces
                stage_ref[pair, at : at + faces, 0:elements] = flux_ref[row, col]
            part = jnp.where(filled, stage_ref[pair, start : start + rows, :], 0.0)
            values = part if values is None else values + pltpu.roll(part, elements, 1)
        stage_ref[pair, 0:rows, :] = high_and_low(values, 2 * elements)
        for face in range(faces):
            left = []
            for col in range(fields):
                at = col * faces + face
                left.append(stage_ref[pair, at : at + 1, :] * pick)
            spread = product(jnp.concatenate(left, axis=0).astype(BF16), right)
            at = (face * pairs + pair) * fields
            out_ref[at : at + fields] = spread.reshape(fields, elements, LANES)


def local_terms(packed, star_ref, flux_ref, volume_ref, trace_ref, lift_ref, fields, kinds):
    left = stack_left(packed)
    volume = star_mix(product(left, volume_ref[...]), star_ref, fields, kinds)
    traces = product(left, trace_ref[...])
    sums = []
    for col in range(fields):
        halves = []
        for half in range(2):
            total = None
            for row in range(fields):
                part = traces[row * ROWS : (row + 1) * ROWS, half * LANES : (half + 1) * LANES]
                term = flux_ref[row * fields + col, half] * part
                total = term if total is None else total + term
            halves.append(total)
        sums.append(jnp.concatenate(halves, axis=1))
    return volume + product(stack_left(jnp.concatenate(sums, axis=0)), lift_ref[...])


def combo_code(lanes, turns, face_modes):
    in_face = lanes % HALF
    code = jnp.where(in_face < turns * face_modes, (lanes // HALF) * turns + in_face // face_modes, -1)
    return code.astype(F32)


def ghost_terms(
    flux_ref, stage_ref, code_ref, composed, lift_sides, lane_code, flux_out, operator_out, scatter_out, sends, fields
):
    faces, elements = flux_ref.shape[2], flux_ref.shape[3]
    rows = 2 * ROWS
    shape = (rows, LANES)
    lanes = lane_index(shape)

    def along_lanes(start):
        row = code_ref[start : start + 1, :]
        for face in range(1, faces):
            row = row + pltpu.roll(code_ref[start + face : start + face + 1, :], face * elements, 1)
        return row + swap_halves(row)

    slots, codes = along_lanes(0), along_lanes(faces)
    ghosts = elements + row_index(shape)
    found = one_where(jnp.broadcast_to(slots, shape) == ghosts.astype(F32))
    first = jnp.where(lanes < HALF, found, 0.0)
    code = jnp.sum(first * codes, axis=1, keepdims=True)
    face_of = jnp.sum(first * (lanes // elements).astype(F32), axis=1, keepdims=True)
    element_of = jnp.sum(first * (lanes % elements).astype(F32), axis=1, keepdims=True)
    numbers = [slot * sends + place for slot in range(4) for place in range(sends // 2)]

    filled = lanes < elements
    values = []
    for field in range(fields):
        total = None
        for face in range(faces):
            stage_ref[field, face * rows : face * rows + fields, 0:elements] = flux_ref[field, :, face, :]
            part = jnp.where(filled, stage_ref[field, face * rows : (face + 1) * rows, :], 0.0)
            total = part if total is None else total + pltpu.roll(part, face * elements, 1)
        total = jnp.where(row_index(shape) < fields, total, 0.0)
        values.append(high_and_low(total, HALF))
    picked = jnp.concatenate([jnp.broadcast_to(found[number : number + 1], (HALF, LANES)) for number in numbers], axis=0)
    flux_out[...] = lax.dot_general(
        jnp.concatenate(values, axis=0).astype(BF16), picked.astype(BF16), (((1,), (1,)), ((), ())),
        preferred_element_type=F32,
    )

    left = []
    for number in numbers:
        chosen = composed * one_where(lane_code == code[number : number + 1])
        both = chosen[:, 0:LANES] + chosen[:, LANES : 2 * LANES]
        high, low = split(both + swap_halves(both))
        left.append(jnp.concatenate([jnp.where(lower_half(high.shape), high, low), high], axis=1))
    high, low = split(lift_sides)
    lifts = product(jnp.concatenate(left, axis=0), jnp.concatenate([high, high, low, jnp.zeros_like(low)], axis=0))
    side_lane = (lane_index((1, faces * HALF)) // HALF).astype(F32)
    place_of = jnp.zeros((1, LANES), F32)
    for at, number in enumerate(numbers):
        chosen = lifts[at * HALF : (at + 1) * HALF] * one_where(side_lane == face_of[number : number + 1])
        both = chosen[:, 0:LANES] + chosen[:, LANES : 2 * LANES]
        high, low = split(both + swap_halves(both))
        operator_out[at] = jnp.concatenate([high, high, low, jnp.zeros_like(low)], axis=0)
        place_of = jnp.where(lane_index((1, LANES)) // rows == at, element_of[number : number + 1], place_of)
    square = (fields * elements, LANES)
    here = (row_index(square) // elements == lane_index(square) % rows) & (
        (row_index(square) % elements).astype(F32) == place_of
    )
    one = one_where(here).astype(BF16)
    scatter_out[...] = jnp.concatenate([one, one], axis=1)


def prepare_kernel(
    packed_ref, early_ref, stiffness_ref, star_ref, flux_local_ref, flux_remote_ref, restrict_ref, lift_ref, orient_ref,
    slot_ref, face_ref, turn_ref,
    base_out, local_out, remote_out, volume_out, trace_out, local_lift_out, compose_out,
    remote_lift_out, choose_out, mask_out, code_ref, composed_out, sides_ref,
    local_work_ref, remote_work_ref, block_ref, wide_ref, face_work_ref, orient_work_ref, code_work_ref,
):
    fields, kinds = packed_ref.shape[0], stiffness_ref.shape[0]
    face_modes, faces, modes = restrict_ref.shape
    turns = orient_ref.shape[0]
    flux_local_coefficients(flux_local_ref, local_work_ref, local_out)
    flux_remote_coefficients(flux_remote_ref, remote_work_ref, remote_out)

    volume_out[...] = stack_right(stiffness_blocks(stiffness_ref, block_ref, False))

    wide_ref[...] = jnp.zeros(wide_ref.shape, F32)
    for mode in range(face_modes):
        at = mode * faces
        wide_ref[at : at + faces, 0:modes] = restrict_ref[mode]
        wide_ref[LANES + at : LANES + at + faces, HALF : HALF + modes] = restrict_ref[mode]
    trace_out[...] = stack_right(wide_ref[...].T)
    for mode in range(face_modes):
        at = mode * faces
        wide_ref[at : at + faces, 0:modes] = -lift_ref[mode]
        wide_ref[LANES + at : LANES + at + faces, HALF : HALF + modes] = -lift_ref[mode]
    local_lift_out[...] = stack_right(wide_ref[...])

    face_work_ref[...] = jnp.zeros(face_work_ref.shape, F32)
    orient_work_ref[...] = jnp.zeros(orient_work_ref.shape, F32)
    for turn in range(turns):
        orient_work_ref[turn * face_modes : (turn + 1) * face_modes, 0:face_modes] = orient_ref[turn]
    for face in range(faces):
        face_work_ref[0:face_modes, face * LANES : face * LANES + modes] = restrict_ref[:, face, :]
        face_work_ref[0:face_modes, face * LANES + HALF : face * LANES + HALF + modes] = restrict_ref[:, face, :]
    composed = jnp.dot(
        orient_work_ref[...], face_work_ref[...], precision=lax.Precision.HIGHEST, preferred_element_type=F32
    )
    stacked = jnp.concatenate([composed[:, face * LANES : (face + 1) * LANES] for face in range(faces)], axis=0)
    high, low = split(stacked.T[0:HALF])
    compose_out[...] = jnp.concatenate([high, high, low, jnp.zeros_like(low)], axis=0)
    wide_ref[...] = jnp.zeros(wide_ref.shape, F32)
    for face in range(faces):
        for turn in range(turns):
            rows = slice(face * HALF + turn * face_modes, face * HALF + (turn + 1) * face_modes)
            wide_ref[rows, 0:modes] = -lift_ref[:, face, :]
            wide_ref[rows, HALF : HALF + modes] = -lift_ref[:, face, :]
    remote_lift_out[...] = stack_right(wide_ref[...])

    elements = slot_ref.shape[1]
    code_work_ref[...] = jnp.zeros(code_work_ref.shape, F32)
    slots = slot_ref[...]
    sends = (choose_out.shape[1] // 2 - elements) // 4
    group = (slots - elements) // sends
    moved = slots
    for side in range(4):
        moved = jnp.where(group == side, slots + (ghost_slot(side) - side) * sends, moved)
    code_work_ref[0:faces, 0:elements] = jnp.where(slots < elements, slots, moved).astype(F32)
    code_work_ref[faces : 2 * faces, 0:elements] = (face_ref[...] * turns + turn_ref[...]).astype(F32)
    code_ref[...] = code_work_ref[0 : 2 * faces, :]
    codes = code_work_ref[...].T[0:elements, :]
    sources = choose_out.shape[1] // 2
    source_lane = (lane_index((elements, 2 * sources)) % sources).astype(F32)
    lanes = lane_index((elements, mask_out.shape[1]))
    lane_code = combo_code(lanes, turns, face_modes)
    picks, masks = [], []
    for face in range(faces):
        picks.append(jnp.where(codes[:, face : face + 1] == source_lane, 1.0, 0.0))
        masks.append(jnp.where(codes[:, faces + face : faces + face + 1] == lane_code, 1.0, 0.0))
    choose_out[...] = jnp.concatenate(picks, axis=0).astype(BF16)
    mask_out[...] = jnp.concatenate(masks, axis=0)

    sides_ref[...] = jnp.zeros(sides_ref.shape, F32)
    for face in range(faces):
        for turn in range(turns):
            rows = slice(turn * face_modes, (turn + 1) * face_modes)
            sides_ref[rows, face * HALF : face * HALF + modes] = -lift_ref[:, face, :]
    composed_out[...] = stacked.T[0:HALF]

    early = early_ref[...].reshape(fields * ROWS, LANES)
    terms = local_terms(early, star_ref, local_out, volume_out, trace_out, local_lift_out, fields, kinds)
    base_out[...] = packed_ref[...] + terms.reshape(fields, ROWS, LANES)


def remote_terms(rows_ref, remote_ref, compose_ref, lift_ref, choose_ref, mask_ref, fields):
    pairs = rows_ref.shape[0]
    faces = lift_ref.shape[0] // (3 * HALF)
    elements = choose_ref.shape[0] // faces
    sources = jnp.concatenate([rows_ref[pair] for pair in range(pairs)], axis=1)
    gathered = product(choose_ref[...], jnp.concatenate(split(sources), axis=0))
    folded = []
    for face in range(faces):
        sums = []
        for col in range(fields):
            total = None
            for pair in range(pairs):
                part = gathered[face * elements : (face + 1) * elements, pair * LANES : (pair + 1) * LANES]
                term = remote_ref[(face * pairs + pair) * fields + col] * part
                total = term if total is None else total + term
            sums.append(total)
        mixed = jnp.concatenate(sums, axis=0)
        high, low = split(mixed + swap_halves(mixed))
        first = jnp.where(lower_half(high.shape), high, low)
        turned = product(jnp.concatenate([first, high], axis=1), compose_ref[...])
        mask = mask_ref[face * elements : (face + 1) * elements, :]
        chosen = (turned.reshape(fields, elements, turned.shape[1]) * mask[None]).reshape(turned.shape)
        both = chosen[:, 0:LANES] + chosen[:, LANES : 2 * LANES]
        folded.append(both + swap_halves(both))
    lower = lower_half(folded[0].shape)
    left = [jnp.where(lower, folded[face], folded[face + 1]) for face in range(0, faces, 2)]
    result = product(stack_left(jnp.concatenate(left, axis=1)), lift_ref[...])
    result = result.reshape(fields, 2, ROWS, LANES)
    return jnp.where(lower_half((ROWS, LANES))[None], result[:, 0], result[:, 1])


def middle_kernel(
    base_ref, early_ref, late_ref, star_ref, remote_ref, derive_ref, compose_ref, lift_ref, choose_ref, mask_ref,
    rate_hbm, send_hbm, from_0, from_1, from_2, from_3,
    middle_out, late_out, send_0, send_1, send_2, send_3,
    rows_ref, late_rows, rate_ref, send_ref, sems,
):
    copies = [
        pltpu.make_async_copy(rate_hbm, rate_ref, sems.at[0]),
        pltpu.make_async_copy(send_hbm, send_ref, sems.at[1]),
    ]
    for copy in copies:
        copy.start()
    fields = base_ref.shape[0]
    kinds = star_ref.shape[0] // (fields * fields)
    pairs = rows_ref.shape[0]
    sends = send_ref.shape[2]
    fast = sends // 2
    elements = 2 * ROWS
    rows_by_pair(early_ref[...].reshape(fields * ROWS, LANES), rows_ref, fields)
    for side, arrived in enumerate((from_0, from_1, from_2, from_3)):
        at = elements + side * sends
        for pair in range(pairs):
            rows_ref[pair, at : at + sends, :] = arrived[pair * sends : (pair + 1) * sends, :]
    middle = base_ref[...] + remote_terms(
        rows_ref, remote_ref, compose_ref, lift_ref, choose_ref, mask_ref, fields
    )
    middle_out[...] = middle
    start = middle.reshape(fields * ROWS, LANES)

    def step(degree, carry):
        current, early = carry
        current = star_mix(product(stack_left(current), derive_ref[...]), star_ref, fields, kinds)
        return current, early + weight_at(0.0, 0.5, degree) * current

    _, restart = lax.fori_loop(1, DERIVS, step, (start, taylor_weight(0.0, 0.5, 0) * start))
    for copy in copies:
        copy.wait()
    sublane = lax.broadcasted_iota(jnp.int32, (ROWS, LANES), 0)
    lower = lower_half((ROWS, LANES))
    is_fast = jnp.zeros((ROWS, LANES), jnp.int32)
    for element in range(elements):
        here = (sublane == element % ROWS) & (lower if element < ROWS else jnp.logical_not(lower))
        is_fast = jnp.where(here, rate_ref[element], is_fast)
    late = jnp.where((is_fast == 2)[None], restart.reshape(fields, ROWS, LANES), late_ref[...])
    late_out[...] = late
    both = late.reshape(fields * ROWS, LANES)
    swapped = swap_halves(both)
    wide = lower_half(both.shape)
    late_rows[:, 0:ROWS, :] = jnp.where(wide, both, swapped).reshape(late.shape)
    late_rows[:, ROWS : 2 * ROWS, :] = jnp.where(wide, swapped, both).reshape(late.shape)
    first_half = lower_half((1, LANES))
    for slot, out in enumerate((send_0, send_1, send_2, send_3)):
        out[...] = jnp.zeros(out.shape, F32)
        side = message_side(slot)
        places = [send_ref[0, side, place] for place in range(fast)]
        for field in range(fields):
            halves = [late_rows[field, pl.ds(element, 1), :] for element in places]
            out[field : field + 1, :] = jnp.where(first_half, *halves)


def local_kernel(
    middle_ref, late_ref, star_ref, flux_ref, volume_ref, trace_ref, lift_ref,
    remote_ref, compose_ref, remote_lift_ref, choose_ref, mask_ref, flux_remote_ref, code_ref, composed_ref, sides_ref,
    orient_ref, first_0, first_1, first_2, first_3,
    base_out, ghost_flux_out, ghost_operator_out, scatter_out, rows_ref, stage_ref,
):
    fields = middle_ref.shape[0]
    kinds = star_ref.shape[0] // (fields * fields)
    pairs = rows_ref.shape[0]
    elements = 2 * ROWS
    sends = (rows_ref.shape[1] - elements) // 4
    fast = sends // 2
    late = late_ref[...].reshape(fields * ROWS, LANES)
    rows_by_pair(late, rows_ref, fields)
    for slot, first in enumerate((first_0, first_1, first_2, first_3)):
        at = elements + slot * sends
        for pair in range(pairs):
            rows_ref[pair, at : at + fast, :] = jnp.zeros((fast, LANES), F32)
            row = pairs * sends + pair * fast
            rows_ref[pair, at + fast : at + sends, :] = first[row : row + fast, :]
    terms = local_terms(late, star_ref, flux_ref, volume_ref, trace_ref, lift_ref, fields, kinds)
    remote = remote_terms(rows_ref, remote_ref, compose_ref, remote_lift_ref, choose_ref, mask_ref, fields)
    base_out[...] = middle_ref[...] + terms.reshape(fields, ROWS, LANES) + remote
    lane_code = combo_code(lane_index((1, composed_ref.shape[1])), orient_ref.shape[0], orient_ref.shape[1])
    ghost_terms(
        flux_remote_ref, stage_ref, code_ref, composed_ref[...], sides_ref[...], lane_code,
        ghost_flux_out, ghost_operator_out, scatter_out, sends, fields,
    )


def final_kernel(
    base_ref, ghost_flux_ref, ghost_operator_ref, scatter_ref, second_0, second_1, second_2, second_3, result_out,
):
    fields = base_ref.shape[0]
    modes = result_out.shape[2]
    rows = second_0.shape[0]
    lower = lower_half((rows, LANES))
    added = []
    for slot, second in enumerate((second_0, second_1, second_2, second_3)):
        mixed = None
        for field in range(fields):
            coefficient = ghost_flux_ref[field * rows : (field + 1) * rows, slot * LANES : (slot + 1) * LANES]
            term = coefficient * second[field : field + 1, :]
            mixed = term if mixed is None else mixed + term
        high, low = split(mixed)
        high_swapped, low_swapped = split(swap_halves(mixed))
        for place, parts in enumerate(((high, low_swapped, high), (high_swapped, low, high_swapped))):
            left = jnp.concatenate([jnp.where(lower, parts[0], parts[1]), parts[2]], axis=1)
            added.append(product(left, ghost_operator_ref[2 * slot + place]))
    right = jnp.concatenate(split(jnp.concatenate(added, axis=0)), axis=0)
    scattered = product(scatter_ref[...], right).reshape(fields, 2, ROWS, LANES)
    result = base_ref[...] + jnp.where(lower_half((ROWS, LANES))[None], scattered[:, 0], scattered[:, 1])
    result_out[:, 0:ROWS, :] = result[:, :, 0:modes]
    result_out[:, ROWS : 2 * ROWS, :] = result[:, :, HALF : HALF + modes]


VMEM = pl.BlockSpec(memory_space=pltpu.VMEM)
HBM = pl.BlockSpec(memory_space=pltpu.HBM)


def call(kernel, ins, outs, scratch, args, name, flops):
    shapes = [jax.ShapeDtypeStruct(shape, dtype) for shape, dtype in outs]
    args = [
        pltpu.with_memory_space_constraint(arg, pltpu.HBM) if spec is HBM else arg for spec, arg in zip(ins, args)
    ]
    return pl.pallas_call(
        kernel,
        out_shape=shapes,
        in_specs=ins,
        out_specs=[VMEM] * len(outs),
        scratch_shapes=[pltpu.VMEM(*one) if isinstance(one, tuple) else one for one in scratch],
        compiler_params=pltpu.CompilerParams(vmem_limit_bytes=16 * 1024 * 1024),
        cost_estimate=pl.CostEstimate(flops=flops, bytes_accessed=4_000_000, transcendentals=0),
        name=name,
    )(*args)


def exchange(outgoing):
    arrived = []
    for (axis, far), message in zip(SWAPS, outgoing):
        size = lax.axis_size(axis)
        assert size % 2 == 0
        pairs = []
        for first in range(1 if far else 0, size, 2):
            second = (first + 1) % size
            pairs += [(first, second), (second, first)]
        arrived.append(lax.ppermute(message, axis, pairs))
    return arrived


def up_to(count, multiple):
    return -(-count // multiple) * multiple


def local(
    solution, stiffness, star_matrices, face_restrict, face_lift, orient_maps, flux_local, flux_remote,
    cluster_rate, send_list, neighbour_slot, neighbour_face, neighbour_turn,
):
    fields, elements = solution.shape[1], solution.shape[2]
    kinds = stiffness.shape[0]
    faces = face_restrict.shape[0]
    sides, sends = send_list.shape[1], send_list.shape[2]
    fast = sends // 2
    pairs = (fields + 1) // 2
    assert elements == 2 * ROWS and solution.shape[0] <= HALF and fast == 2
    values = jnp.transpose(solution, (1, 2, 0))
    star = jnp.transpose(star_matrices, (1, 2, 0, 3))
    local_part = jnp.transpose(flux_local, (1, 2, 0, 3))
    remote_part = jnp.transpose(flux_remote, (1, 2, 0, 3))
    restrict = jnp.transpose(face_restrict, (1, 0, 2))
    lift = jnp.transpose(face_lift, (2, 0, 1))

    packed = (fields, ROWS, LANES)
    first_shape = (up_to(pairs * (sends + fast), ROWS), LANES)
    second_shape = (up_to(fields, 2 * ROWS), LANES)
    star_shape = (fields * fields * kinds, ROWS, LANES)
    combos = faces * HALF
    sources = elements + sides * sends

    waiting = (local_part, remote_part, restrict, lift, orient_maps, neighbour_slot, neighbour_face, neighbour_turn)
    made = call(
        predict_kernel,
        [HBM] * (4 + len(LATER)),
        [(packed, F32)] * 2 + [(first_shape, F32)] * sides + [
            (packed, F32), (star_shape, F32), ((3 * LANES, kinds * LANES), BF16), (stiffness.shape, F32),
        ] + [(array.shape, array.dtype) for array in waiting],
        [
            ((fields, up_to(4 * fields, ROWS), LANES), F32),
            ((pairs, elements, LANES), F32), ((pairs, elements, LANES), F32),
            (values.shape, F32), ((kinds, LANES, LANES), F32), (star.shape, F32),
            pltpu.SMEM(send_list.shape, jnp.int32), pltpu.SemaphoreType.DMA((4 + len(LATER),)),
        ],
        (values, stiffness, star, send_list, *waiting),
        "predict", 100_000_000,
    )
    early, late, outgoing = made[0], made[1], made[2 : 2 + sides]
    start, star_coef, derive_op, stiffness_kept = made[2 + sides : 6 + sides]
    waiting = made[6 + sides :]
    first = exchange(outgoing)
    (
        base, local_coef, remote_coef, volume_op, trace_op, local_lift, compose_op, remote_lift, choose, mask,
        codes, composed, lift_sides,
    ) = call(
        prepare_kernel,
        [VMEM] * 12,
        [
            (packed, F32), ((fields * fields, 2, ROWS, LANES), F32),
            ((faces * pairs * fields, elements, LANES), F32),
            ((3 * LANES, kinds * LANES), BF16), ((3 * LANES, 2 * LANES), BF16),
            ((6 * LANES, LANES), BF16), ((2 * LANES, combos), BF16), ((3 * faces * HALF, LANES), BF16),
            ((faces * elements, 2 * sources), BF16), ((faces * elements, combos), F32),
            ((2 * faces, LANES), F32), ((HALF, combos), F32), ((HALF, faces * HALF), F32),
        ],
        [
            ((fields, 2 * ROWS * faces, LANES), F32), ((pairs, 2 * up_to(4 * fields, ROWS), LANES), F32),
            ((kinds, LANES, LANES), F32), ((2 * LANES, LANES), F32),
            ((LANES, faces * LANES), F32), ((HALF, LANES), F32), ((LANES, LANES), F32),
        ],
        (start, early, stiffness_kept, star_coef, *waiting),
        "prepare", 200_000_000,
    )
    middle, late_value, *outgoing = call(
        middle_kernel,
        [VMEM] * 10 + [HBM] * 2 + [VMEM] * 4,
        [(packed, F32)] * 2 + [(second_shape, F32)] * sides,
        [
            ((pairs, sources, LANES), F32), ((fields, elements, LANES), F32),
            pltpu.SMEM(cluster_rate.shape, jnp.int32), pltpu.SMEM(send_list.shape, jnp.int32),
            pltpu.SemaphoreType.DMA((2,)),
        ],
        (
            base, early, late, star_coef, remote_coef, derive_op, compose_op, remote_lift, choose, mask,
            cluster_rate, send_list, *first,
        ),
        "middle", 200_000_000,
    )
    second = exchange(outgoing)
    base, ghost_flux, ghost_op, scatter = call(
        local_kernel,
        [VMEM] * (17 + len(first)),
        [
            (packed, F32), ((fields * second_shape[0], sides * LANES), F32),
            ((sides * fast, 2 * LANES, LANES), BF16), ((fields * elements, 2 * LANES), BF16),
        ],
        [((pairs, sources, LANES), F32), ((fields, 2 * ROWS * faces, LANES), F32)],
        (
            middle, late_value, star_coef, local_coef, volume_op, trace_op, local_lift,
            remote_coef, compose_op, remote_lift, choose, mask, waiting[1], codes, composed, lift_sides, waiting[4],
            *first,
        ),
        "local_late", 200_000_000,
    )
    (result,) = call(
        final_kernel,
        [VMEM] * 8,
        [(values.shape, F32)],
        [],
        (base, ghost_flux, ghost_op, scatter, *second),
        "final", 200_000_000,
    )
    return jnp.transpose(result, (2, 0, 1))


def solution(mesh):
    placed = (
        P(None, None, ("dom", "sub")),
        P(),
        P(None, None, None, ("dom", "sub")),
        P(),
        P(),
        P(),
        P(None, None, None, ("dom", "sub")),
        P(None, None, None, ("dom", "sub")),
        P(("dom", "sub")),
        P(("dom", "sub"), None, None),
        P(None, ("dom", "sub")),
        P(None, ("dom", "sub")),
        P(None, ("dom", "sub")),
    )
    return jax.shard_map(
        local, mesh=mesh, in_specs=placed, out_specs=P(None, None, ("dom", "sub")), check_vma=False
    )
```

```python
import math

import jax
import jax.numpy as jnp
from jax import lax
from jax.experimental import pallas as pl
from jax.experimental.pallas import tpu as pltpu
from jax.sharding import PartitionSpec as P

DERIVS = 6
LANES = 128
HALF = 64
ROWS = 8
F32 = jnp.float32
BF16 = jnp.bfloat16
LATER = ("flux_local", "flux_remote", "face_restrict", "face_lift", "orient_maps", "slot", "face", "turn", "rate")
AXES = ("dom", "sub")
SWAPS = (("dom", True), ("dom", False), ("sub", False), ("sub", True))


def taylor_weight(lower, upper, degree):
    return (upper ** (degree + 1) - lower ** (degree + 1)) / math.factorial(degree + 1)


def weight_at(lower, upper, degree):
    result = jnp.float32(taylor_weight(lower, upper, 1))
    for option in range(2, DERIVS):
        result = jnp.where(degree == option, jnp.float32(taylor_weight(lower, upper, option)), result)
    return result


def split(values):
    high = values.astype(BF16)
    low = (values - high.astype(F32)).astype(BF16)
    return high, low


def stack_left(values):
    high, low = split(values)
    return jnp.concatenate([high, low, high], axis=1)


def stack_right(values):
    high, low = split(values)
    return jnp.concatenate([high, high, low], axis=0)


def product(left, right):
    return jnp.dot(left, right, preferred_element_type=F32)


def odd_place(axis):
    return lax.rem(lax.axis_index(axis), 2)


def message_side(slot):
    axis, far = SWAPS[slot]
    odd = odd_place(axis)
    return 2 * AXES.index(axis) + (odd if far else 1 - odd)


def ghost_slot(side):
    axis = AXES[side // 2]
    even_far = side % 2 == 0
    return jnp.where(odd_place(axis) == 0, SWAPS.index((axis, even_far)), SWAPS.index((axis, not even_far)))


def lane_index(shape):
    return lax.broadcasted_iota(jnp.int32, shape, len(shape) - 1)


def lower_half(shape):
    return lane_index(shape) < HALF


def swap_halves(values):
    return pltpu.roll(values, HALF, values.ndim - 1)


def pack(values_ref, packed_ref):
    modes = values_ref.shape[2]
    packed_ref[...] = jnp.zeros(packed_ref.shape, F32)
    packed_ref[:, :, 0:modes] = values_ref[:, 0:ROWS, :]
    packed_ref[:, :, HALF : HALF + modes] = values_ref[:, ROWS : 2 * ROWS, :]


def high_and_low(values, shift):
    high = values.astype(BF16).astype(F32)
    return high + pltpu.roll(values - high, shift, 1)


def row_index(shape):
    return lax.broadcasted_iota(jnp.int32, shape, len(shape) - 2)


def one_where(condition):
    return jnp.where(condition, 1.0, 0.0)


def star_coefficients(star_ref, stage_ref, star_out):
    fields, kinds, elements = star_ref.shape[0], star_ref.shape[2], star_ref.shape[3]
    lanes = lane_index((ROWS, LANES))
    pick = one_where((lanes % ROWS == row_index((ROWS, LANES))) & (lanes < 2 * elements))
    from_lane = row_index((LANES, LANES))
    same_half = (from_lane % elements) // ROWS == lane_index((LANES, LANES)) // HALF
    right = one_where(same_half & (from_lane < 2 * elements)).astype(BF16)
    filled = lane_index(stage_ref.shape[1:]) < elements
    for row in range(fields):
        for col in range(fields):
            stage_ref[row, col * 4 : col * 4 + kinds, 0:elements] = star_ref[row, col]
        values = jnp.where(filled, stage_ref[row], 0.0)
        stage_ref[row] = high_and_low(values, elements)
        spreads = []
        for kind in range(kinds):
            for col in range(fields):
                at = col * 4 + kind
                spreads.append(stage_ref[row, at : at + 1, :] * pick)
        spread_out = product(jnp.concatenate(spreads, axis=0).astype(BF16), right)
        count = kinds * fields
        star_out[row * count : (row + 1) * count] = spread_out.reshape(count, ROWS, LANES)


def star_mix(columns, star_ref, fields, kinds):
    sums = []
    for col in range(fields):
        parts = []
        for kind in range(kinds):
            total = None
            for row in range(fields):
                part = columns[row * ROWS : (row + 1) * ROWS, kind * LANES : (kind + 1) * LANES]
                term = star_ref[(row * kinds + kind) * fields + col] * part
                total = term if total is None else total + term
            parts.append(total)
        sums.append(sum(parts[1:], parts[0]))
    return jnp.concatenate(sums, axis=0)


def stiffness_blocks(stiffness_ref, block_ref, turned):
    kinds, modes = stiffness_ref.shape[0], stiffness_ref.shape[1]
    block_ref[...] = jnp.zeros(block_ref.shape, F32)
    for kind in range(kinds):
        matrix = -stiffness_ref[kind].T if turned else stiffness_ref[kind]
        block_ref[kind, 0:modes, 0:modes] = matrix
        block_ref[kind, HALF : HALF + modes, HALF : HALF + modes] = matrix
    return jnp.concatenate([block_ref[kind] for kind in range(kinds)], axis=1)


def predict_kernel(*refs):
    later = len(LATER)
    solution_hbm, stiffness_hbm, star_hbm, send_hbm = refs[0:4]
    later_hbm, refs = refs[4 : 4 + later], refs[4 + later :]
    early_out, late_out, send_0, send_1, send_2, send_3 = refs[0:6]
    packed_ref, coef_ref, derive_ref, stiffness_ref, early_rows = refs[6:11]
    later_out, refs = refs[11 : 11 + later], refs[11 + later :]
    work_ref, late_rows, solution_ref, block_ref, star_ref, send_ref, sems = refs

    sources = (star_hbm, stiffness_hbm, solution_hbm, send_hbm, *later_hbm)
    targets = (star_ref, stiffness_ref, solution_ref, send_ref, *later_out)
    copies = [
        pltpu.make_async_copy(source, target, sems.at[number])
        for number, (source, target) in enumerate(zip(sources, targets))
    ]
    for copy in copies:
        copy.start()
    fields, kinds = star_ref.shape[0], star_ref.shape[2]
    pairs = (fields + 1) // 2
    for copy in copies[0:3]:
        copy.wait()
    derive_ref[...] = stack_right(stiffness_blocks(stiffness_ref, block_ref, True))
    star_coefficients(star_ref, work_ref, coef_ref)
    pack(solution_ref, packed_ref)
    start = packed_ref[...].reshape(fields * ROWS, LANES)

    def step(degree, carry):
        current, early, late = carry
        current = star_mix(product(stack_left(current), derive_ref[...]), coef_ref, fields, kinds)
        early = early + weight_at(0.0, 0.5, degree) * current
        late = late + weight_at(0.5, 1.0, degree) * current
        return current, early, late

    _, early, late = lax.fori_loop(
        1, DERIVS, step, (start, taylor_weight(0.0, 0.5, 0) * start, taylor_weight(0.5, 1.0, 0) * start),
        unroll=True,
    )
    early_out[...] = early.reshape(fields, ROWS, LANES)
    late_out[...] = late.reshape(fields, ROWS, LANES)
    rows_by_pair(early, early_rows, fields)
    rows_by_pair(late, late_rows, fields)
    copies[3].wait()
    sends = send_ref.shape[2]
    fast = sends // 2
    for side, out in enumerate((send_0, send_1, send_2, send_3)):
        out[...] = jnp.zeros(out.shape, F32)
        for place in range(sends):
            element = send_ref[0, message_side(side), place]
            for pair in range(pairs):
                row = pair * sends + place
                out[row : row + 1, :] = early_rows[pair, pl.ds(element, 1), :]
            if place >= fast:
                for pair in range(pairs):
                    row = pairs * sends + pair * fast + place - fast
                    out[row : row + 1, :] = late_rows[pair, pl.ds(element, 1), :]
    for copy in copies[4:]:
        copy.wait()


def rows_by_pair(packed, out_ref, fields):
    lower = lower_half((ROWS, LANES))
    for pair in range((fields + 1) // 2):
        even = packed[2 * pair * ROWS : (2 * pair + 1) * ROWS]
        odd = jnp.zeros_like(even)
        if 2 * pair + 1 < fields:
            odd = packed[(2 * pair + 1) * ROWS : (2 * pair + 2) * ROWS]
        out_ref[pair, 0:ROWS, :] = jnp.where(lower, even, swap_halves(odd))
        out_ref[pair, ROWS : 2 * ROWS, :] = jnp.where(lower, swap_halves(even), odd)


def flux_local_coefficients(flux_ref, stage_ref, out_ref):
    fields, faces, elements = flux_ref.shape[0], flux_ref.shape[2], flux_ref.shape[3]
    rows = 2 * ROWS
    filled = lane_index((rows, LANES)) < elements
    lanes, sublanes = lane_index((ROWS, LANES)), row_index((ROWS, LANES))
    picks = [one_where(lanes % elements == half * ROWS + sublanes) for half in range(2)]
    square = (LANES, LANES)
    right = one_where(row_index(square) // (2 * elements) == lane_index(square) % faces).astype(BF16)
    for row in range(fields):
        values = None
        for face in range(faces):
            stage_ref[row, face * rows : face * rows + fields, 0:elements] = flux_ref[row, :, face, :]
            part = jnp.where(filled, stage_ref[row, face * rows : (face + 1) * rows, :], 0.0)
            values = part if values is None else values + pltpu.roll(part, face * 2 * elements, 1)
        stage_ref[row, 0:rows, :] = high_and_low(values, elements)
        left = [stage_ref[row, col : col + 1, :] * pick for col in range(fields) for pick in picks]
        spread = product(jnp.concatenate(left, axis=0).astype(BF16), right)
        out_ref[row * fields : (row + 1) * fields] = spread.reshape(fields, 2, ROWS, LANES)


def flux_remote_coefficients(flux_ref, stage_ref, out_ref):
    fields, faces, elements = flux_ref.shape[0], flux_ref.shape[2], flux_ref.shape[3]
    pairs = (fields + 1) // 2
    rows = stage_ref.shape[1] // 2
    filled = lane_index((rows, LANES)) < elements
    lanes, sublanes = lane_index((elements, LANES)), row_index((elements, LANES))
    pick = one_where((lanes % elements == sublanes) & (lanes < 4 * elements))
    square = (LANES, LANES)
    from_lane = row_index(square)
    same_parity = (from_lane // elements) % 2 == lane_index(square) // HALF
    right = one_where(same_parity & (from_lane < 4 * elements)).astype(BF16)
    for pair in range(pairs):
        values = None
        for row in range(2 * pair, min(2 * pair + 2, fields)):
            start = (row % 2) * rows
            for col in range(fields):
                at = start + col * faces
                stage_ref[pair, at : at + faces, 0:elements] = flux_ref[row, col]
            part = jnp.where(filled, stage_ref[pair, start : start + rows, :], 0.0)
            values = part if values is None else values + pltpu.roll(part, elements, 1)
        stage_ref[pair, 0:rows, :] = high_and_low(values, 2 * elements)
        for face in range(faces):
            left = []
            for col in range(fields):
                at = col * faces + face
                left.append(stage_ref[pair, at : at + 1, :] * pick)
            spread = product(jnp.concatenate(left, axis=0).astype(BF16), right)
            at = (face * pairs + pair) * fields
            out_ref[at : at + fields] = spread.reshape(fields, elements, LANES)


def local_terms(packed, star_ref, flux_ref, volume_ref, trace_ref, lift_ref, fields, kinds):
    left = stack_left(packed)
    volume = star_mix(product(left, volume_ref[...]), star_ref, fields, kinds)
    traces = product(left, trace_ref[...])
    sums = []
    for col in range(fields):
        halves = []
        for half in range(2):
            total = None
            for row in range(fields):
                part = traces[row * ROWS : (row + 1) * ROWS, half * LANES : (half + 1) * LANES]
                term = flux_ref[row * fields + col, half] * part
                total = term if total is None else total + term
            halves.append(total)
        sums.append(jnp.concatenate(halves, axis=1))
    return volume + product(stack_left(jnp.concatenate(sums, axis=0)), lift_ref[...])


def combo_code(lanes, turns, face_modes):
    in_face = lanes % HALF
    code = jnp.where(in_face < turns * face_modes, (lanes // HALF) * turns + in_face // face_modes, -1)
    return code.astype(F32)


def ghost_terms(
    flux_ref, stage_ref, code_ref, composed, lift_sides, lane_code, flux_out, operator_out, scatter_out, sends, fields
):
    faces, elements = flux_ref.shape[2], flux_ref.shape[3]
    rows = 2 * ROWS
    shape = (rows, LANES)
    lanes = lane_index(shape)

    def along_lanes(start):
        row = code_ref[start : start + 1, :]
        for face in range(1, faces):
            row = row + pltpu.roll(code_ref[start + face : start + face + 1, :], face * elements, 1)
        return row + swap_halves(row)

    slots, codes = along_lanes(0), along_lanes(faces)
    ghosts = elements + row_index(shape)
    found = one_where(jnp.broadcast_to(slots, shape) == ghosts.astype(F32))
    first = jnp.where(lanes < HALF, found, 0.0)
    code = jnp.sum(first * codes, axis=1, keepdims=True)
    face_of = jnp.sum(first * (lanes // elements).astype(F32), axis=1, keepdims=True)
    element_of = jnp.sum(first * (lanes % elements).astype(F32), axis=1, keepdims=True)
    numbers = [slot * sends + place for slot in range(4) for place in range(sends // 2)]

    filled = lanes < elements
    values = []
    for field in range(fields):
        total = None
        for face in range(faces):
            stage_ref[field, face * rows : face * rows + fields, 0:elements] = flux_ref[field, :, face, :]
            part = jnp.where(filled, stage_ref[field, face * rows : (face + 1) * rows, :], 0.0)
            total = part if total is None else total + pltpu.roll(part, face * elements, 1)
        total = jnp.where(row_index(shape) < fields, total, 0.0)
        values.append(high_and_low(total, HALF))
    picked = jnp.concatenate([jnp.broadcast_to(found[number : number + 1], (HALF, LANES)) for number in numbers], axis=0)
    flux_out[...] = lax.dot_general(
        jnp.concatenate(values, axis=0).astype(BF16), picked.astype(BF16), (((1,), (1,)), ((), ())),
        preferred_element_type=F32,
    )

    left = []
    for number in numbers:
        chosen = composed * one_where(lane_code == code[number : number + 1])
        both = chosen[:, 0:LANES] + chosen[:, LANES : 2 * LANES]
        high, low = split(both + swap_halves(both))
        left.append(jnp.concatenate([jnp.where(lower_half(high.shape), high, low), high], axis=1))
    high, low = split(lift_sides)
    lifts = product(jnp.concatenate(left, axis=0), jnp.concatenate([high, high, low, jnp.zeros_like(low)], axis=0))
    side_lane = (lane_index((1, faces * HALF)) // HALF).astype(F32)
    place_of = jnp.zeros((1, LANES), F32)
    for at, number in enumerate(numbers):
        chosen = lifts[at * HALF : (at + 1) * HALF] * one_where(side_lane == face_of[number : number + 1])
        both = chosen[:, 0:LANES] + chosen[:, LANES : 2 * LANES]
        high, low = split(both + swap_halves(both))
        operator_out[at] = jnp.concatenate([high, high, low, jnp.zeros_like(low)], axis=0)
        place_of = jnp.where(lane_index((1, LANES)) // rows == at, element_of[number : number + 1], place_of)
    square = (fields * elements, LANES)
    here = (row_index(square) // elements == lane_index(square) % rows) & (
        (row_index(square) % elements).astype(F32) == place_of
    )
    one = one_where(here).astype(BF16)
    scatter_out[...] = jnp.concatenate([one, one], axis=1)


def prepare_kernel(
    packed_ref, early_ref, stiffness_ref, star_ref, flux_local_ref, flux_remote_ref, restrict_ref, lift_ref, orient_ref,
    slot_ref, face_ref, turn_ref, rate_ref,
    base_out, local_out, remote_out, volume_out, trace_out, local_lift_out, compose_out,
    remote_lift_out, choose_out, mask_out, code_ref, composed_out, sides_ref, fast_out,
    local_work_ref, remote_work_ref, block_ref, wide_ref, face_work_ref, orient_work_ref, code_work_ref,
):
    fields, kinds = packed_ref.shape[0], stiffness_ref.shape[0]
    face_modes, faces, modes = restrict_ref.shape
    turns = orient_ref.shape[0]
    flux_local_coefficients(flux_local_ref, local_work_ref, local_out)
    flux_remote_coefficients(flux_remote_ref, remote_work_ref, remote_out)

    volume_out[...] = stack_right(stiffness_blocks(stiffness_ref, block_ref, False))

    wide_ref[...] = jnp.zeros(wide_ref.shape, F32)
    for mode in range(face_modes):
        at = mode * faces
        wide_ref[at : at + faces, 0:modes] = restrict_ref[mode]
        wide_ref[LANES + at : LANES + at + faces, HALF : HALF + modes] = restrict_ref[mode]
    trace_out[...] = stack_right(wide_ref[...].T)
    for mode in range(face_modes):
        at = mode * faces
        wide_ref[at : at + faces, 0:modes] = -lift_ref[mode]
        wide_ref[LANES + at : LANES + at + faces, HALF : HALF + modes] = -lift_ref[mode]
    local_lift_out[...] = stack_right(wide_ref[...])

    face_work_ref[...] = jnp.zeros(face_work_ref.shape, F32)
    orient_work_ref[...] = jnp.zeros(orient_work_ref.shape, F32)
    for turn in range(turns):
        orient_work_ref[turn * face_modes : (turn + 1) * face_modes, 0:face_modes] = orient_ref[turn]
    for face in range(faces):
        face_work_ref[0:face_modes, face * LANES : face * LANES + modes] = restrict_ref[:, face, :]
        face_work_ref[0:face_modes, face * LANES + HALF : face * LANES + HALF + modes] = restrict_ref[:, face, :]
    composed = jnp.dot(
        orient_work_ref[...], face_work_ref[...], precision=lax.Precision.HIGHEST, preferred_element_type=F32
    )
    stacked = jnp.concatenate([composed[:, face * LANES : (face + 1) * LANES] for face in range(faces)], axis=0)
    high, low = split(stacked.T[0:HALF])
    compose_out[...] = jnp.concatenate([high, high, low, jnp.zeros_like(low)], axis=0)
    wide_ref[...] = jnp.zeros(wide_ref.shape, F32)
    for face in range(faces):
        for turn in range(turns):
            rows = slice(face * HALF + turn * face_modes, face * HALF + (turn + 1) * face_modes)
            wide_ref[rows, 0:modes] = -lift_ref[:, face, :]
            wide_ref[rows, HALF : HALF + modes] = -lift_ref[:, face, :]
    remote_lift_out[...] = stack_right(wide_ref[...])

    elements = slot_ref.shape[1]
    code_work_ref[...] = jnp.zeros(code_work_ref.shape, F32)
    slots = slot_ref[...]
    sends = (choose_out.shape[1] // 2 - elements) // 4
    group = (slots - elements) // sends
    moved = slots
    for side in range(4):
        moved = jnp.where(group == side, slots + (ghost_slot(side) - side) * sends, moved)
    code_work_ref[0:faces, 0:elements] = jnp.where(slots < elements, slots, moved).astype(F32)
    code_work_ref[faces : 2 * faces, 0:elements] = (face_ref[...] * turns + turn_ref[...]).astype(F32)
    code_work_ref[2 * faces : 2 * faces + 1, 0:elements] = rate_ref[...].astype(F32)
    code_ref[...] = code_work_ref[0 : 2 * faces, :]
    codes = code_work_ref[...].T[0:elements, :]
    rates = codes[:, 2 * faces : 2 * faces + 1]
    fast_out[...] = jnp.where(lower_half((ROWS, LANES)), rates[0:ROWS], rates[ROWS : 2 * ROWS])
    sources = choose_out.shape[1] // 2
    source_lane = (lane_index((elements, 2 * sources)) % sources).astype(F32)
    lanes = lane_index((elements, mask_out.shape[1]))
    lane_code = combo_code(lanes, turns, face_modes)
    picks, masks = [], []
    for face in range(faces):
        picks.append(jnp.where(codes[:, face : face + 1] == source_lane, 1.0, 0.0))
        masks.append(jnp.where(codes[:, faces + face : faces + face + 1] == lane_code, 1.0, 0.0))
    choose_out[...] = jnp.concatenate(picks, axis=0).astype(BF16)
    mask_out[...] = jnp.concatenate(masks, axis=0)

    sides_ref[...] = jnp.zeros(sides_ref.shape, F32)
    for face in range(faces):
        for turn in range(turns):
            rows = slice(turn * face_modes, (turn + 1) * face_modes)
            sides_ref[rows, face * HALF : face * HALF + modes] = -lift_ref[:, face, :]
    composed_out[...] = stacked.T[0:HALF]

    early = early_ref[...].reshape(fields * ROWS, LANES)
    terms = local_terms(early, star_ref, local_out, volume_out, trace_out, local_lift_out, fields, kinds)
    base_out[...] = packed_ref[...] + terms.reshape(fields, ROWS, LANES)


def remote_terms(rows, remote_ref, compose_ref, lift_ref, choose_ref, mask_ref, fields):
    pairs = len(rows)
    faces = lift_ref.shape[0] // (3 * HALF)
    elements = choose_ref.shape[0] // faces
    sources = jnp.concatenate(rows, axis=1)
    gathered = product(choose_ref[...], jnp.concatenate(split(sources), axis=0))
    folded = []
    for face in range(faces):
        sums = []
        for col in range(fields):
            total = None
            for pair in range(pairs):
                part = gathered[face * elements : (face + 1) * elements, pair * LANES : (pair + 1) * LANES]
                term = remote_ref[(face * pairs + pair) * fields + col] * part
                total = term if total is None else total + term
            sums.append(total)
        mixed = jnp.concatenate(sums, axis=0)
        high, low = split(mixed + swap_halves(mixed))
        first = jnp.where(lower_half(high.shape), high, low)
        turned = product(jnp.concatenate([first, high], axis=1), compose_ref[...])
        mask = mask_ref[face * elements : (face + 1) * elements, :]
        chosen = (turned.reshape(fields, elements, turned.shape[1]) * mask[None]).reshape(turned.shape)
        both = chosen[:, 0:LANES] + chosen[:, LANES : 2 * LANES]
        folded.append(both + swap_halves(both))
    lower = lower_half(folded[0].shape)
    left = [jnp.where(lower, folded[face], folded[face + 1]) for face in range(0, faces, 2)]
    result = product(stack_left(jnp.concatenate(left, axis=1)), lift_ref[...])
    result = result.reshape(fields, 2, ROWS, LANES)
    return jnp.where(lower_half((ROWS, LANES))[None], result[:, 0], result[:, 1])


def middle_kernel(
    base_ref, early_rows, late_ref, star_ref, remote_ref, derive_ref, compose_ref, lift_ref, choose_ref, mask_ref,
    fast_ref, send_hbm, from_0, from_1, from_2, from_3,
    middle_out, late_out, send_0, send_1, send_2, send_3,
    rows_ref, late_rows, send_ref, sem,
):
    copy = pltpu.make_async_copy(send_hbm, send_ref, sem)
    copy.start()
    fields = base_ref.shape[0]
    kinds = star_ref.shape[0] // (fields * fields)
    pairs = rows_ref.shape[0]
    sends = send_ref.shape[2]
    fast = sends // 2
    for side, arrived in enumerate((from_0, from_1, from_2, from_3)):
        for pair in range(pairs):
            rows_ref[pair, side * sends : (side + 1) * sends, :] = arrived[pair * sends : (pair + 1) * sends, :]
    rows = [jnp.concatenate([early_rows[pair], rows_ref[pair]], axis=0) for pair in range(pairs)]
    middle = base_ref[...] + remote_terms(rows, remote_ref, compose_ref, lift_ref, choose_ref, mask_ref, fields)
    middle_out[...] = middle
    start = middle.reshape(fields * ROWS, LANES)

    def step(degree, carry):
        current, early = carry
        current = star_mix(product(stack_left(current), derive_ref[...]), star_ref, fields, kinds)
        return current, early + weight_at(0.0, 0.5, degree) * current

    _, restart = lax.fori_loop(1, DERIVS, step, (start, taylor_weight(0.0, 0.5, 0) * start), unroll=True)
    copy.wait()
    is_fast = fast_ref[...]
    late = jnp.where((is_fast == 2)[None], restart.reshape(fields, ROWS, LANES), late_ref[...])
    late_out[...] = late
    both = late.reshape(fields * ROWS, LANES)
    swapped = swap_halves(both)
    wide = lower_half(both.shape)
    late_rows[:, 0:ROWS, :] = jnp.where(wide, both, swapped).reshape(late.shape)
    late_rows[:, ROWS : 2 * ROWS, :] = jnp.where(wide, swapped, both).reshape(late.shape)
    first_half = lower_half((1, LANES))
    for slot, out in enumerate((send_0, send_1, send_2, send_3)):
        out[...] = jnp.zeros(out.shape, F32)
        side = message_side(slot)
        places = [send_ref[0, side, place] for place in range(fast)]
        for field in range(fields):
            halves = [late_rows[field, pl.ds(element, 1), :] for element in places]
            out[field : field + 1, :] = jnp.where(first_half, *halves)


def local_kernel(
    middle_ref, late_ref, star_ref, flux_ref, volume_ref, trace_ref, lift_ref,
    remote_ref, compose_ref, remote_lift_ref, choose_ref, mask_ref, flux_remote_ref, code_ref, composed_ref, sides_ref,
    orient_ref, first_0, first_1, first_2, first_3,
    base_out, ghost_flux_out, ghost_operator_out, scatter_out, rows_ref, stage_ref,
):
    fields = middle_ref.shape[0]
    kinds = star_ref.shape[0] // (fields * fields)
    pairs = rows_ref.shape[0]
    elements = 2 * ROWS
    sends = (rows_ref.shape[1] - elements) // 4
    fast = sends // 2
    late = late_ref[...].reshape(fields * ROWS, LANES)
    rows_by_pair(late, rows_ref, fields)
    for slot, first in enumerate((first_0, first_1, first_2, first_3)):
        at = elements + slot * sends
        for pair in range(pairs):
            rows_ref[pair, at : at + fast, :] = jnp.zeros((fast, LANES), F32)
            row = pairs * sends + pair * fast
            rows_ref[pair, at + fast : at + sends, :] = first[row : row + fast, :]
    terms = local_terms(late, star_ref, flux_ref, volume_ref, trace_ref, lift_ref, fields, kinds)
    rows = [rows_ref[pair] for pair in range(pairs)]
    remote = remote_terms(rows, remote_ref, compose_ref, remote_lift_ref, choose_ref, mask_ref, fields)
    base_out[...] = middle_ref[...] + terms.reshape(fields, ROWS, LANES) + remote
    lane_code = combo_code(lane_index((1, composed_ref.shape[1])), orient_ref.shape[0], orient_ref.shape[1])
    ghost_terms(
        flux_remote_ref, stage_ref, code_ref, composed_ref[...], sides_ref[...], lane_code,
        ghost_flux_out, ghost_operator_out, scatter_out, sends, fields,
    )


def final_kernel(
    base_ref, ghost_flux_ref, ghost_operator_ref, scatter_ref, second_0, second_1, second_2, second_3, result_out,
):
    fields = base_ref.shape[0]
    modes = result_out.shape[2]
    rows = second_0.shape[0]
    lower = lower_half((rows, LANES))
    added = []
    for slot, second in enumerate((second_0, second_1, second_2, second_3)):
        mixed = None
        for field in range(fields):
            coefficient = ghost_flux_ref[field * rows : (field + 1) * rows, slot * LANES : (slot + 1) * LANES]
            term = coefficient * second[field : field + 1, :]
            mixed = term if mixed is None else mixed + term
        high, low = split(mixed)
        high_swapped, low_swapped = split(swap_halves(mixed))
        for place, parts in enumerate(((high, low_swapped, high), (high_swapped, low, high_swapped))):
            left = jnp.concatenate([jnp.where(lower, parts[0], parts[1]), parts[2]], axis=1)
            added.append(product(left, ghost_operator_ref[2 * slot + place]))
    right = jnp.concatenate(split(jnp.concatenate(added, axis=0)), axis=0)
    scattered = product(scatter_ref[...], right).reshape(fields, 2, ROWS, LANES)
    result = base_ref[...] + jnp.where(lower_half((ROWS, LANES))[None], scattered[:, 0], scattered[:, 1])
    result_out[:, 0:ROWS, :] = result[:, :, 0:modes]
    result_out[:, ROWS : 2 * ROWS, :] = result[:, :, HALF : HALF + modes]


VMEM = pl.BlockSpec(memory_space=pltpu.VMEM)
HBM = pl.BlockSpec(memory_space=pltpu.HBM)


def call(kernel, ins, outs, scratch, args, name, flops):
    shapes = [jax.ShapeDtypeStruct(shape, dtype) for shape, dtype in outs]
    args = [
        pltpu.with_memory_space_constraint(arg, pltpu.HBM) if spec is HBM else arg for spec, arg in zip(ins, args)
    ]
    return pl.pallas_call(
        kernel,
        out_shape=shapes,
        in_specs=ins,
        out_specs=[VMEM] * len(outs),
        scratch_shapes=[pltpu.VMEM(*one) if isinstance(one, tuple) else one for one in scratch],
        compiler_params=pltpu.CompilerParams(vmem_limit_bytes=16 * 1024 * 1024),
        cost_estimate=pl.CostEstimate(flops=flops, bytes_accessed=4_000_000, transcendentals=0),
        name=name,
    )(*args)


def exchange(outgoing):
    arrived = []
    for (axis, far), message in zip(SWAPS, outgoing):
        size = lax.axis_size(axis)
        assert size % 2 == 0
        pairs = []
        for first in range(1 if far else 0, size, 2):
            second = (first + 1) % size
            pairs += [(first, second), (second, first)]
        arrived.append(lax.ppermute(message, axis, pairs))
    return arrived


def up_to(count, multiple):
    return -(-count // multiple) * multiple


def local(
    solution, stiffness, star_matrices, face_restrict, face_lift, orient_maps, flux_local, flux_remote,
    cluster_rate, send_list, neighbour_slot, neighbour_face, neighbour_turn,
):
    fields, elements = solution.shape[1], solution.shape[2]
    kinds = stiffness.shape[0]
    faces = face_restrict.shape[0]
    sides, sends = send_list.shape[1], send_list.shape[2]
    fast = sends // 2
    pairs = (fields + 1) // 2
    assert elements == 2 * ROWS and solution.shape[0] <= HALF and fast == 2
    values = jnp.transpose(solution, (1, 2, 0))
    star = jnp.transpose(star_matrices, (1, 2, 0, 3))
    local_part = jnp.transpose(flux_local, (1, 2, 0, 3))
    remote_part = jnp.transpose(flux_remote, (1, 2, 0, 3))
    restrict = jnp.transpose(face_restrict, (1, 0, 2))
    lift = jnp.transpose(face_lift, (2, 0, 1))

    packed = (fields, ROWS, LANES)
    first_shape = (up_to(pairs * (sends + fast), ROWS), LANES)
    second_shape = (up_to(fields, 2 * ROWS), LANES)
    star_shape = (fields * fields * kinds, ROWS, LANES)
    combos = faces * HALF
    sources = elements + sides * sends

    waiting = (
        local_part, remote_part, restrict, lift, orient_maps, neighbour_slot, neighbour_face, neighbour_turn,
        cluster_rate.reshape(1, elements),
    )
    made = call(
        predict_kernel,
        [HBM] * (4 + len(LATER)),
        [(packed, F32)] * 2 + [(first_shape, F32)] * sides + [
            (packed, F32), (star_shape, F32), ((3 * LANES, kinds * LANES), BF16), (stiffness.shape, F32),
            ((pairs, elements, LANES), F32),
        ] + [(array.shape, array.dtype) for array in waiting],
        [
            ((fields, up_to(4 * fields, ROWS), LANES), F32),
            ((pairs, elements, LANES), F32),
            (values.shape, F32), ((kinds, LANES, LANES), F32), (star.shape, F32),
            pltpu.SMEM(send_list.shape, jnp.int32), pltpu.SemaphoreType.DMA((4 + len(LATER),)),
        ],
        (values, stiffness, star, send_list, *waiting),
        "predict", 100_000_000,
    )
    early, late, outgoing = made[0], made[1], made[2 : 2 + sides]
    start, star_coef, derive_op, stiffness_kept, early_rows = made[2 + sides : 7 + sides]
    waiting = made[7 + sides :]
    first = exchange(outgoing)
    (
        base, local_coef, remote_coef, volume_op, trace_op, local_lift, compose_op, remote_lift, choose, mask,
        codes, composed, lift_sides, fast_mask,
    ) = call(
        prepare_kernel,
        [VMEM] * 13,
        [
            (packed, F32), ((fields * fields, 2, ROWS, LANES), F32),
            ((faces * pairs * fields, elements, LANES), F32),
            ((3 * LANES, kinds * LANES), BF16), ((3 * LANES, 2 * LANES), BF16),
            ((6 * LANES, LANES), BF16), ((2 * LANES, combos), BF16), ((3 * faces * HALF, LANES), BF16),
            ((faces * elements, 2 * sources), BF16), ((faces * elements, combos), F32),
            ((2 * faces, LANES), F32), ((HALF, combos), F32), ((HALF, faces * HALF), F32),
            ((ROWS, LANES), F32),
        ],
        [
            ((fields, 2 * ROWS * faces, LANES), F32), ((pairs, 2 * up_to(4 * fields, ROWS), LANES), F32),
            ((kinds, LANES, LANES), F32), ((2 * LANES, LANES), F32),
            ((LANES, faces * LANES), F32), ((HALF, LANES), F32), ((LANES, LANES), F32),
        ],
        (start, early, stiffness_kept, star_coef, *waiting),
        "prepare", 200_000_000,
    )
    middle, late_value, *outgoing = call(
        middle_kernel,
        [VMEM] * 11 + [HBM] + [VMEM] * 4,
        [(packed, F32)] * 2 + [(second_shape, F32)] * sides,
        [
            ((pairs, sides * sends, LANES), F32), ((fields, elements, LANES), F32),
            pltpu.SMEM(send_list.shape, jnp.int32), pltpu.SemaphoreType.DMA,
        ],
        (
            base, early_rows, late, star_coef, remote_coef, derive_op, compose_op, remote_lift, choose, mask,
            fast_mask, send_list, *first,
        ),
        "middle", 200_000_000,
    )
    second = exchange(outgoing)
    base, ghost_flux, ghost_op, scatter = call(
        local_kernel,
        [VMEM] * (17 + len(first)),
        [
            (packed, F32), ((fields * second_shape[0], sides * LANES), F32),
            ((sides * fast, 2 * LANES, LANES), BF16), ((fields * elements, 2 * LANES), BF16),
        ],
        [((pairs, sources, LANES), F32), ((fields, 2 * ROWS * faces, LANES), F32)],
        (
            middle, late_value, star_coef, local_coef, volume_op, trace_op, local_lift,
            remote_coef, compose_op, remote_lift, choose, mask, waiting[1], codes, composed, lift_sides, waiting[4],
            *first,
        ),
        "local_late", 200_000_000,
    )
    (result,) = call(
        final_kernel,
        [VMEM] * 8,
        [(values.shape, F32)],
        [],
        (base, ghost_flux, ghost_op, scatter, *second),
        "final", 200_000_000,
    )
    return jnp.transpose(result, (2, 0, 1))


def solution(mesh):
    placed = (
        P(None, None, ("dom", "sub")),
        P(),
        P(None, None, None, ("dom", "sub")),
        P(),
        P(),
        P(),
        P(None, None, None, ("dom", "sub")),
        P(None, None, None, ("dom", "sub")),
        P(("dom", "sub")),
        P(("dom", "sub"), None, None),
        P(None, ("dom", "sub")),
        P(None, ("dom", "sub")),
        P(None, ("dom", "sub")),
    )
    return jax.shard_map(
        local, mesh=mesh, in_specs=placed, out_specs=P(None, None, ("dom", "sub")), check_vma=False
    )
```

```python
import math

import jax
import jax.numpy as jnp
from jax import lax
from jax.experimental import pallas as pl
from jax.experimental.pallas import tpu as pltpu
from jax.sharding import PartitionSpec as P

DERIVS = 6
LANES = 128
HALF = 64
ROWS = 8
F32 = jnp.float32
BF16 = jnp.bfloat16
LATER = ("flux_local", "flux_remote", "face_restrict", "face_lift", "orient_maps", "slot", "face", "turn", "rate")
AXES = ("dom", "sub")
SWAPS = (("dom", True), ("dom", False), ("sub", True), ("sub", False))


def taylor_weight(lower, upper, degree):
    return (upper ** (degree + 1) - lower ** (degree + 1)) / math.factorial(degree + 1)


def weight_at(lower, upper, degree):
    result = jnp.float32(taylor_weight(lower, upper, 1))
    for option in range(2, DERIVS):
        result = jnp.where(degree == option, jnp.float32(taylor_weight(lower, upper, option)), result)
    return result


def split(values):
    high = values.astype(BF16)
    low = (values - high.astype(F32)).astype(BF16)
    return high, low


def stack_left(values):
    high, low = split(values)
    return jnp.concatenate([high, low, high], axis=1)


def stack_right(values):
    high, low = split(values)
    return jnp.concatenate([high, high, low], axis=0)


def product(left, right):
    return jnp.dot(left, right, preferred_element_type=F32)


def odd_place(axis):
    return lax.rem(lax.axis_index(axis), 2)


def message_side(slot):
    axis, far = SWAPS[slot]
    odd = odd_place(axis)
    return 2 * AXES.index(axis) + (odd if far else 1 - odd)


def ghost_slot(side):
    axis = AXES[side // 2]
    even_far = side % 2 == 0
    return jnp.where(odd_place(axis) == 0, SWAPS.index((axis, even_far)), SWAPS.index((axis, not even_far)))


def lane_index(shape):
    return lax.broadcasted_iota(jnp.int32, shape, len(shape) - 1)


def lower_half(shape):
    return lane_index(shape) < HALF


def swap_halves(values):
    return pltpu.roll(values, HALF, values.ndim - 1)


def pack(values_ref, packed_ref):
    modes = values_ref.shape[2]
    packed_ref[...] = jnp.zeros(packed_ref.shape, F32)
    packed_ref[:, :, 0:modes] = values_ref[:, 0:ROWS, :]
    packed_ref[:, :, HALF : HALF + modes] = values_ref[:, ROWS : 2 * ROWS, :]


def high_and_low(values, shift):
    high = values.astype(BF16).astype(F32)
    return high + pltpu.roll(values - high, shift, 1)


def row_index(shape):
    return lax.broadcasted_iota(jnp.int32, shape, len(shape) - 2)


def one_where(condition):
    return jnp.where(condition, 1.0, 0.0)


def star_coefficients(star_ref, stage_ref, star_out):
    fields, kinds, elements = star_ref.shape[0], star_ref.shape[2], star_ref.shape[3]
    lanes = lane_index((ROWS, LANES))
    pick = one_where((lanes % ROWS == row_index((ROWS, LANES))) & (lanes < 2 * elements))
    from_lane = row_index((LANES, LANES))
    same_half = (from_lane % elements) // ROWS == lane_index((LANES, LANES)) // HALF
    right = one_where(same_half & (from_lane < 2 * elements)).astype(BF16)
    filled = lane_index(stage_ref.shape[1:]) < elements
    for row in range(fields):
        for col in range(fields):
            stage_ref[row, col * 4 : col * 4 + kinds, 0:elements] = star_ref[row, col]
        values = jnp.where(filled, stage_ref[row], 0.0)
        stage_ref[row] = high_and_low(values, elements)
        spreads = []
        for kind in range(kinds):
            for col in range(fields):
                at = col * 4 + kind
                spreads.append(stage_ref[row, at : at + 1, :] * pick)
        spread_out = product(jnp.concatenate(spreads, axis=0).astype(BF16), right)
        count = kinds * fields
        star_out[row * count : (row + 1) * count] = spread_out.reshape(count, ROWS, LANES)


def star_mix(columns, star_ref, fields, kinds):
    sums = []
    for col in range(fields):
        parts = []
        for kind in range(kinds):
            total = None
            for row in range(fields):
                part = columns[row * ROWS : (row + 1) * ROWS, kind * LANES : (kind + 1) * LANES]
                term = star_ref[(row * kinds + kind) * fields + col] * part
                total = term if total is None else total + term
            parts.append(total)
        sums.append(sum(parts[1:], parts[0]))
    return jnp.concatenate(sums, axis=0)


def stiffness_blocks(stiffness_ref, block_ref, turned):
    kinds, modes = stiffness_ref.shape[0], stiffness_ref.shape[1]
    block_ref[...] = jnp.zeros(block_ref.shape, F32)
    for kind in range(kinds):
        matrix = -stiffness_ref[kind].T if turned else stiffness_ref[kind]
        block_ref[kind, 0:modes, 0:modes] = matrix
        block_ref[kind, HALF : HALF + modes, HALF : HALF + modes] = matrix
    return jnp.concatenate([block_ref[kind] for kind in range(kinds)], axis=1)


def predict_kernel(*refs):
    later = len(LATER)
    solution_hbm, stiffness_hbm, star_hbm, send_hbm = refs[0:4]
    later_hbm, refs = refs[4 : 4 + later], refs[4 + later :]
    early_out, late_out, send_0, send_1, send_2, send_3 = refs[0:6]
    packed_ref, coef_ref, derive_ref, stiffness_ref, early_rows = refs[6:11]
    later_out, refs = refs[11 : 11 + later], refs[11 + later :]
    work_ref, late_rows, solution_ref, block_ref, star_ref, send_ref, sems = refs

    sources = (star_hbm, stiffness_hbm, solution_hbm, send_hbm, *later_hbm)
    targets = (star_ref, stiffness_ref, solution_ref, send_ref, *later_out)
    copies = [
        pltpu.make_async_copy(source, target, sems.at[number])
        for number, (source, target) in enumerate(zip(sources, targets))
    ]
    for copy in copies:
        copy.start()
    fields, kinds = star_ref.shape[0], star_ref.shape[2]
    pairs = (fields + 1) // 2
    for copy in copies[0:3]:
        copy.wait()
    derive_ref[...] = stack_right(stiffness_blocks(stiffness_ref, block_ref, True))
    star_coefficients(star_ref, work_ref, coef_ref)
    pack(solution_ref, packed_ref)
    start = packed_ref[...].reshape(fields * ROWS, LANES)

    def step(degree, carry):
        current, early, late = carry
        current = star_mix(product(stack_left(current), derive_ref[...]), coef_ref, fields, kinds)
        early = early + weight_at(0.0, 0.5, degree) * current
        late = late + weight_at(0.5, 1.0, degree) * current
        return current, early, late

    _, early, late = lax.fori_loop(
        1, DERIVS, step, (start, taylor_weight(0.0, 0.5, 0) * start, taylor_weight(0.5, 1.0, 0) * start),
        unroll=True,
    )
    early_out[...] = early.reshape(fields, ROWS, LANES)
    late_out[...] = late.reshape(fields, ROWS, LANES)
    rows_by_pair(early, early_rows, fields)
    rows_by_pair(late, late_rows, fields)
    copies[3].wait()
    sends = send_ref.shape[2]
    fast = sends // 2
    for side, out in enumerate((send_0, send_1, send_2, send_3)):
        out[...] = jnp.zeros(out.shape, F32)
        for place in range(sends):
            element = send_ref[0, message_side(side), place]
            for pair in range(pairs):
                row = pair * sends + place
                out[row : row + 1, :] = early_rows[pair, pl.ds(element, 1), :]
            if place >= fast:
                for pair in range(pairs):
                    row = pairs * sends + pair * fast + place - fast
                    out[row : row + 1, :] = late_rows[pair, pl.ds(element, 1), :]
    for copy in copies[4:]:
        copy.wait()


def rows_by_pair(packed, out_ref, fields):
    lower = lower_half((ROWS, LANES))
    for pair in range((fields + 1) // 2):
        even = packed[2 * pair * ROWS : (2 * pair + 1) * ROWS]
        odd = jnp.zeros_like(even)
        if 2 * pair + 1 < fields:
            odd = packed[(2 * pair + 1) * ROWS : (2 * pair + 2) * ROWS]
        out_ref[pair, 0:ROWS, :] = jnp.where(lower, even, swap_halves(odd))
        out_ref[pair, ROWS : 2 * ROWS, :] = jnp.where(lower, swap_halves(even), odd)


def flux_local_coefficients(flux_ref, stage_ref, out_ref):
    fields, faces, elements = flux_ref.shape[0], flux_ref.shape[2], flux_ref.shape[3]
    rows = 2 * ROWS
    filled = lane_index((rows, LANES)) < elements
    lanes, sublanes = lane_index((ROWS, LANES)), row_index((ROWS, LANES))
    picks = [one_where(lanes % elements == half * ROWS + sublanes) for half in range(2)]
    square = (LANES, LANES)
    right = one_where(row_index(square) // (2 * elements) == lane_index(square) % faces).astype(BF16)
    for row in range(fields):
        values = None
        for face in range(faces):
            stage_ref[row, face * rows : face * rows + fields, 0:elements] = flux_ref[row, :, face, :]
            part = jnp.where(filled, stage_ref[row, face * rows : (face + 1) * rows, :], 0.0)
            values = part if values is None else values + pltpu.roll(part, face * 2 * elements, 1)
        stage_ref[row, 0:rows, :] = high_and_low(values, elements)
        left = [stage_ref[row, col : col + 1, :] * pick for col in range(fields) for pick in picks]
        spread = product(jnp.concatenate(left, axis=0).astype(BF16), right)
        out_ref[row * fields : (row + 1) * fields] = spread.reshape(fields, 2, ROWS, LANES)


def flux_remote_coefficients(flux_ref, stage_ref, out_ref):
    fields, faces, elements = flux_ref.shape[0], flux_ref.shape[2], flux_ref.shape[3]
    pairs = (fields + 1) // 2
    rows = stage_ref.shape[1] // 2
    filled = lane_index((rows, LANES)) < elements
    lanes, sublanes = lane_index((elements, LANES)), row_index((elements, LANES))
    pick = one_where((lanes % elements == sublanes) & (lanes < 4 * elements))
    square = (LANES, LANES)
    from_lane = row_index(square)
    same_parity = (from_lane // elements) % 2 == lane_index(square) // HALF
    right = one_where(same_parity & (from_lane < 4 * elements)).astype(BF16)
    for pair in range(pairs):
        values = None
        for row in range(2 * pair, min(2 * pair + 2, fields)):
            start = (row % 2) * rows
            for col in range(fields):
                at = start + col * faces
                stage_ref[pair, at : at + faces, 0:elements] = flux_ref[row, col]
            part = jnp.where(filled, stage_ref[pair, start : start + rows, :], 0.0)
            values = part if values is None else values + pltpu.roll(part, elements, 1)
        stage_ref[pair, 0:rows, :] = high_and_low(values, 2 * elements)
        for face in range(faces):
            left = []
            for col in range(fields):
                at = col * faces + face
                left.append(stage_ref[pair, at : at + 1, :] * pick)
            spread = product(jnp.concatenate(left, axis=0).astype(BF16), right)
            at = (face * pairs + pair) * fields
            out_ref[at : at + fields] = spread.reshape(fields, elements, LANES)


def local_terms(packed, star_ref, flux_ref, volume_ref, trace_ref, lift_ref, fields, kinds):
    left = stack_left(packed)
    volume = star_mix(product(left, volume_ref[...]), star_ref, fields, kinds)
    traces = product(left, trace_ref[...])
    sums = []
    for col in range(fields):
        halves = []
        for half in range(2):
            total = None
            for row in range(fields):
                part = traces[row * ROWS : (row + 1) * ROWS, half * LANES : (half + 1) * LANES]
                term = flux_ref[row * fields + col, half] * part
                total = term if total is None else total + term
            halves.append(total)
        sums.append(jnp.concatenate(halves, axis=1))
    return volume + product(stack_left(jnp.concatenate(sums, axis=0)), lift_ref[...])


def combo_code(lanes, turns, face_modes):
    in_face = lanes % HALF
    code = jnp.where(in_face < turns * face_modes, (lanes // HALF) * turns + in_face // face_modes, -1)
    return code.astype(F32)


def ghost_terms(
    flux_ref, stage_ref, code_ref, composed, lift_sides, lane_code, flux_out, operator_out, scatter_out, sends, fields
):
    faces, elements = flux_ref.shape[2], flux_ref.shape[3]
    rows = 2 * ROWS
    shape = (rows, LANES)
    lanes = lane_index(shape)

    def along_lanes(start):
        row = code_ref[start : start + 1, :]
        for face in range(1, faces):
            row = row + pltpu.roll(code_ref[start + face : start + face + 1, :], face * elements, 1)
        return row + swap_halves(row)

    slots, codes = along_lanes(0), along_lanes(faces)
    ghosts = elements + row_index(shape)
    found = one_where(jnp.broadcast_to(slots, shape) == ghosts.astype(F32))
    first = jnp.where(lanes < HALF, found, 0.0)
    code = jnp.sum(first * codes, axis=1, keepdims=True)
    face_of = jnp.sum(first * (lanes // elements).astype(F32), axis=1, keepdims=True)
    element_of = jnp.sum(first * (lanes % elements).astype(F32), axis=1, keepdims=True)
    numbers = [slot * sends + place for slot in range(4) for place in range(sends // 2)]

    filled = lanes < elements
    values = []
    for field in range(fields):
        total = None
        for face in range(faces):
            stage_ref[field, face * rows : face * rows + fields, 0:elements] = flux_ref[field, :, face, :]
            part = jnp.where(filled, stage_ref[field, face * rows : (face + 1) * rows, :], 0.0)
            total = part if total is None else total + pltpu.roll(part, face * elements, 1)
        total = jnp.where(row_index(shape) < fields, total, 0.0)
        values.append(high_and_low(total, HALF))
    picked = jnp.concatenate([jnp.broadcast_to(found[number : number + 1], (HALF, LANES)) for number in numbers], axis=0)
    flux_out[...] = lax.dot_general(
        jnp.concatenate(values, axis=0).astype(BF16), picked.astype(BF16), (((1,), (1,)), ((), ())),
        preferred_element_type=F32,
    )

    left = []
    for number in numbers:
        chosen = composed * one_where(lane_code == code[number : number + 1])
        both = chosen[:, 0:LANES] + chosen[:, LANES : 2 * LANES]
        high, low = split(both + swap_halves(both))
        left.append(jnp.concatenate([jnp.where(lower_half(high.shape), high, low), high], axis=1))
    high, low = split(lift_sides)
    lifts = product(jnp.concatenate(left, axis=0), jnp.concatenate([high, high, low, jnp.zeros_like(low)], axis=0))
    side_lane = (lane_index((1, faces * HALF)) // HALF).astype(F32)
    place_of = jnp.zeros((1, LANES), F32)
    for at, number in enumerate(numbers):
        chosen = lifts[at * HALF : (at + 1) * HALF] * one_where(side_lane == face_of[number : number + 1])
        both = chosen[:, 0:LANES] + chosen[:, LANES : 2 * LANES]
        high, low = split(both + swap_halves(both))
        operator_out[at] = jnp.concatenate([high, high, low, jnp.zeros_like(low)], axis=0)
        place_of = jnp.where(lane_index((1, LANES)) // rows == at, element_of[number : number + 1], place_of)
    square = (fields * elements, LANES)
    here = (row_index(square) // elements == lane_index(square) % rows) & (
        (row_index(square) % elements).astype(F32) == place_of
    )
    one = one_where(here).astype(BF16)
    scatter_out[...] = jnp.concatenate([one, one], axis=1)


def prepare_kernel(
    packed_ref, early_ref, stiffness_ref, star_ref, flux_local_ref, flux_remote_ref, restrict_ref, lift_ref, orient_ref,
    slot_ref, face_ref, turn_ref, rate_ref,
    base_out, local_out, remote_out, volume_out, trace_out, local_lift_out, compose_out,
    remote_lift_out, choose_out, mask_out, code_ref, composed_out, sides_ref, fast_out,
    local_work_ref, remote_work_ref, block_ref, wide_ref, face_work_ref, orient_work_ref, code_work_ref,
):
    fields, kinds = packed_ref.shape[0], stiffness_ref.shape[0]
    face_modes, faces, modes = restrict_ref.shape
    turns = orient_ref.shape[0]
    flux_local_coefficients(flux_local_ref, local_work_ref, local_out)
    flux_remote_coefficients(flux_remote_ref, remote_work_ref, remote_out)

    volume_out[...] = stack_right(stiffness_blocks(stiffness_ref, block_ref, False))

    wide_ref[...] = jnp.zeros(wide_ref.shape, F32)
    for mode in range(face_modes):
        at = mode * faces
        wide_ref[at : at + faces, 0:modes] = restrict_ref[mode]
        wide_ref[LANES + at : LANES + at + faces, HALF : HALF + modes] = restrict_ref[mode]
    trace_out[...] = stack_right(wide_ref[...].T)
    for mode in range(face_modes):
        at = mode * faces
        wide_ref[at : at + faces, 0:modes] = -lift_ref[mode]
        wide_ref[LANES + at : LANES + at + faces, HALF : HALF + modes] = -lift_ref[mode]
    local_lift_out[...] = stack_right(wide_ref[...])

    face_work_ref[...] = jnp.zeros(face_work_ref.shape, F32)
    orient_work_ref[...] = jnp.zeros(orient_work_ref.shape, F32)
    for turn in range(turns):
        orient_work_ref[turn * face_modes : (turn + 1) * face_modes, 0:face_modes] = orient_ref[turn]
    for face in range(faces):
        face_work_ref[0:face_modes, face * LANES : face * LANES + modes] = restrict_ref[:, face, :]
        face_work_ref[0:face_modes, face * LANES + HALF : face * LANES + HALF + modes] = restrict_ref[:, face, :]
    composed = jnp.dot(
        orient_work_ref[...], face_work_ref[...], precision=lax.Precision.HIGHEST, preferred_element_type=F32
    )
    stacked = jnp.concatenate([composed[:, face * LANES : (face + 1) * LANES] for face in range(faces)], axis=0)
    high, low = split(stacked.T[0:HALF])
    compose_out[...] = jnp.concatenate([high, high, low, jnp.zeros_like(low)], axis=0)
    wide_ref[...] = jnp.zeros(wide_ref.shape, F32)
    for face in range(faces):
        for turn in range(turns):
            rows = slice(face * HALF + turn * face_modes, face * HALF + (turn + 1) * face_modes)
            wide_ref[rows, 0:modes] = -lift_ref[:, face, :]
            wide_ref[rows, HALF : HALF + modes] = -lift_ref[:, face, :]
    remote_lift_out[...] = stack_right(wide_ref[...])

    elements = slot_ref.shape[1]
    code_work_ref[...] = jnp.zeros(code_work_ref.shape, F32)
    slots = slot_ref[...]
    sends = (choose_out.shape[1] // 2 - elements) // 4
    group = (slots - elements) // sends
    moved = slots
    for side in range(4):
        moved = jnp.where(group == side, slots + (ghost_slot(side) - side) * sends, moved)
    code_work_ref[0:faces, 0:elements] = jnp.where(slots < elements, slots, moved).astype(F32)
    code_work_ref[faces : 2 * faces, 0:elements] = (face_ref[...] * turns + turn_ref[...]).astype(F32)
    code_work_ref[2 * faces : 2 * faces + 1, 0:elements] = rate_ref[...].astype(F32)
    code_ref[...] = code_work_ref[0 : 2 * faces, :]
    codes = code_work_ref[...].T[0:elements, :]
    rates = codes[:, 2 * faces : 2 * faces + 1]
    fast_out[...] = jnp.where(lower_half((ROWS, LANES)), rates[0:ROWS], rates[ROWS : 2 * ROWS])
    sources = choose_out.shape[1] // 2
    source_lane = (lane_index((elements, 2 * sources)) % sources).astype(F32)
    lanes = lane_index((elements, mask_out.shape[1]))
    lane_code = combo_code(lanes, turns, face_modes)
    picks, masks = [], []
    for face in range(faces):
        picks.append(jnp.where(codes[:, face : face + 1] == source_lane, 1.0, 0.0))
        masks.append(jnp.where(codes[:, faces + face : faces + face + 1] == lane_code, 1.0, 0.0))
    choose_out[...] = jnp.concatenate(picks, axis=0).astype(BF16)
    mask_out[...] = jnp.concatenate(masks, axis=0)

    sides_ref[...] = jnp.zeros(sides_ref.shape, F32)
    for face in range(faces):
        for turn in range(turns):
            rows = slice(turn * face_modes, (turn + 1) * face_modes)
            sides_ref[rows, face * HALF : face * HALF + modes] = -lift_ref[:, face, :]
    composed_out[...] = stacked.T[0:HALF]

    early = early_ref[...].reshape(fields * ROWS, LANES)
    terms = local_terms(early, star_ref, local_out, volume_out, trace_out, local_lift_out, fields, kinds)
    base_out[...] = packed_ref[...] + terms.reshape(fields, ROWS, LANES)


def remote_terms(rows, remote_ref, compose_ref, lift_ref, choose_ref, mask_ref, fields):
    pairs = len(rows)
    faces = lift_ref.shape[0] // (3 * HALF)
    elements = choose_ref.shape[0] // faces
    sources = jnp.concatenate(rows, axis=1)
    gathered = product(choose_ref[...], jnp.concatenate(split(sources), axis=0))
    folded = []
    for face in range(faces):
        sums = []
        for col in range(fields):
            total = None
            for pair in range(pairs):
                part = gathered[face * elements : (face + 1) * elements, pair * LANES : (pair + 1) * LANES]
                term = remote_ref[(face * pairs + pair) * fields + col] * part
                total = term if total is None else total + term
            sums.append(total)
        mixed = jnp.concatenate(sums, axis=0)
        high, low = split(mixed + swap_halves(mixed))
        first = jnp.where(lower_half(high.shape), high, low)
        turned = product(jnp.concatenate([first, high], axis=1), compose_ref[...])
        mask = mask_ref[face * elements : (face + 1) * elements, :]
        chosen = (turned.reshape(fields, elements, turned.shape[1]) * mask[None]).reshape(turned.shape)
        both = chosen[:, 0:LANES] + chosen[:, LANES : 2 * LANES]
        folded.append(both + swap_halves(both))
    lower = lower_half(folded[0].shape)
    left = [jnp.where(lower, folded[face], folded[face + 1]) for face in range(0, faces, 2)]
    result = product(stack_left(jnp.concatenate(left, axis=1)), lift_ref[...])
    result = result.reshape(fields, 2, ROWS, LANES)
    return jnp.where(lower_half((ROWS, LANES))[None], result[:, 0], result[:, 1])


def middle_kernel(
    base_ref, early_rows, late_ref, star_ref, remote_ref, derive_ref, compose_ref, lift_ref, choose_ref, mask_ref,
    fast_ref, send_hbm, from_0, from_1, from_2, from_3,
    middle_out, late_out, send_0, send_1, send_2, send_3,
    rows_ref, late_rows, send_ref, sem,
):
    copy = pltpu.make_async_copy(send_hbm, send_ref, sem)
    copy.start()
    fields = base_ref.shape[0]
    kinds = star_ref.shape[0] // (fields * fields)
    pairs = rows_ref.shape[0]
    sends = send_ref.shape[2]
    fast = sends // 2
    for side, arrived in enumerate((from_0, from_1, from_2, from_3)):
        for pair in range(pairs):
            rows_ref[pair, side * sends : (side + 1) * sends, :] = arrived[pair * sends : (pair + 1) * sends, :]
    rows = [jnp.concatenate([early_rows[pair], rows_ref[pair]], axis=0) for pair in range(pairs)]
    middle = base_ref[...] + remote_terms(rows, remote_ref, compose_ref, lift_ref, choose_ref, mask_ref, fields)
    middle_out[...] = middle
    start = middle.reshape(fields * ROWS, LANES)

    def step(degree, carry):
        current, early = carry
        current = star_mix(product(stack_left(current), derive_ref[...]), star_ref, fields, kinds)
        return current, early + weight_at(0.0, 0.5, degree) * current

    _, restart = lax.fori_loop(1, DERIVS, step, (start, taylor_weight(0.0, 0.5, 0) * start))
    copy.wait()
    is_fast = fast_ref[...]
    late = jnp.where((is_fast == 2)[None], restart.reshape(fields, ROWS, LANES), late_ref[...])
    late_out[...] = late
    both = late.reshape(fields * ROWS, LANES)
    swapped = swap_halves(both)
    wide = lower_half(both.shape)
    late_rows[:, 0:ROWS, :] = jnp.where(wide, both, swapped).reshape(late.shape)
    late_rows[:, ROWS : 2 * ROWS, :] = jnp.where(wide, swapped, both).reshape(late.shape)
    first_half = lower_half((1, LANES))
    for slot, out in enumerate((send_0, send_1, send_2, send_3)):
        out[...] = jnp.zeros(out.shape, F32)
        side = message_side(slot)
        places = [send_ref[0, side, place] for place in range(fast)]
        for field in range(fields):
            halves = [late_rows[field, pl.ds(element, 1), :] for element in places]
            out[field : field + 1, :] = jnp.where(first_half, *halves)


def local_kernel(
    middle_ref, late_ref, star_ref, flux_ref, volume_ref, trace_ref, lift_ref,
    remote_ref, compose_ref, remote_lift_ref, choose_ref, mask_ref, flux_remote_ref, code_ref, composed_ref, sides_ref,
    orient_ref, first_0, first_1, first_2, first_3,
    base_out, ghost_flux_out, ghost_operator_out, scatter_out, rows_ref, stage_ref,
):
    fields = middle_ref.shape[0]
    kinds = star_ref.shape[0] // (fields * fields)
    pairs = rows_ref.shape[0]
    elements = 2 * ROWS
    sends = (rows_ref.shape[1] - elements) // 4
    fast = sends // 2
    late = late_ref[...].reshape(fields * ROWS, LANES)
    rows_by_pair(late, rows_ref, fields)
    for slot, first in enumerate((first_0, first_1, first_2, first_3)):
        at = elements + slot * sends
        for pair in range(pairs):
            rows_ref[pair, at : at + fast, :] = jnp.zeros((fast, LANES), F32)
            row = pairs * sends + pair * fast
            rows_ref[pair, at + fast : at + sends, :] = first[row : row + fast, :]
    terms = local_terms(late, star_ref, flux_ref, volume_ref, trace_ref, lift_ref, fields, kinds)
    rows = [rows_ref[pair] for pair in range(pairs)]
    remote = remote_terms(rows, remote_ref, compose_ref, remote_lift_ref, choose_ref, mask_ref, fields)
    base_out[...] = middle_ref[...] + terms.reshape(fields, ROWS, LANES) + remote
    lane_code = combo_code(lane_index((1, composed_ref.shape[1])), orient_ref.shape[0], orient_ref.shape[1])
    ghost_terms(
        flux_remote_ref, stage_ref, code_ref, composed_ref[...], sides_ref[...], lane_code,
        ghost_flux_out, ghost_operator_out, scatter_out, sends, fields,
    )


def final_kernel(
    base_ref, ghost_flux_ref, ghost_operator_ref, scatter_ref, second_0, second_1, second_2, second_3, result_out,
):
    fields = base_ref.shape[0]
    modes = result_out.shape[2]
    rows = second_0.shape[0]
    lower = lower_half((rows, LANES))
    added = []
    for slot, second in enumerate((second_0, second_1, second_2, second_3)):
        mixed = None
        for field in range(fields):
            coefficient = ghost_flux_ref[field * rows : (field + 1) * rows, slot * LANES : (slot + 1) * LANES]
            term = coefficient * second[field : field + 1, :]
            mixed = term if mixed is None else mixed + term
        high, low = split(mixed)
        high_swapped, low_swapped = split(swap_halves(mixed))
        for place, parts in enumerate(((high, low_swapped, high), (high_swapped, low, high_swapped))):
            left = jnp.concatenate([jnp.where(lower, parts[0], parts[1]), parts[2]], axis=1)
            added.append(product(left, ghost_operator_ref[2 * slot + place]))
    right = jnp.concatenate(split(jnp.concatenate(added, axis=0)), axis=0)
    scattered = product(scatter_ref[...], right).reshape(fields, 2, ROWS, LANES)
    result = base_ref[...] + jnp.where(lower_half((ROWS, LANES))[None], scattered[:, 0], scattered[:, 1])
    result_out[:, 0:ROWS, :] = result[:, :, 0:modes]
    result_out[:, ROWS : 2 * ROWS, :] = result[:, :, HALF : HALF + modes]


VMEM = pl.BlockSpec(memory_space=pltpu.VMEM)
HBM = pl.BlockSpec(memory_space=pltpu.HBM)


def call(kernel, ins, outs, scratch, args, name, flops):
    shapes = [jax.ShapeDtypeStruct(shape, dtype) for shape, dtype in outs]
    args = [
        pltpu.with_memory_space_constraint(arg, pltpu.HBM) if spec is HBM else arg for spec, arg in zip(ins, args)
    ]
    return pl.pallas_call(
        kernel,
        out_shape=shapes,
        in_specs=ins,
        out_specs=[VMEM] * len(outs),
        scratch_shapes=[pltpu.VMEM(*one) if isinstance(one, tuple) else one for one in scratch],
        compiler_params=pltpu.CompilerParams(vmem_limit_bytes=16 * 1024 * 1024),
        cost_estimate=pl.CostEstimate(flops=flops, bytes_accessed=4_000_000, transcendentals=0),
        name=name,
    )(*args)


def exchange(outgoing):
    arrived = []
    for (axis, far), message in zip(SWAPS, outgoing):
        size = lax.axis_size(axis)
        assert size % 2 == 0
        pairs = []
        for first in range(1 if far else 0, size, 2):
            second = (first + 1) % size
            pairs += [(first, second), (second, first)]
        arrived.append(lax.ppermute(message, axis, pairs))
    return arrived


def up_to(count, multiple):
    return -(-count // multiple) * multiple


def local(
    solution, stiffness, star_matrices, face_restrict, face_lift, orient_maps, flux_local, flux_remote,
    cluster_rate, send_list, neighbour_slot, neighbour_face, neighbour_turn,
):
    fields, elements = solution.shape[1], solution.shape[2]
    kinds = stiffness.shape[0]
    faces = face_restrict.shape[0]
    sides, sends = send_list.shape[1], send_list.shape[2]
    fast = sends // 2
    pairs = (fields + 1) // 2
    assert elements == 2 * ROWS and solution.shape[0] <= HALF and fast == 2
    values = jnp.transpose(solution, (1, 2, 0))
    star = jnp.transpose(star_matrices, (1, 2, 0, 3))
    local_part = jnp.transpose(flux_local, (1, 2, 0, 3))
    remote_part = jnp.transpose(flux_remote, (1, 2, 0, 3))
    restrict = jnp.transpose(face_restrict, (1, 0, 2))
    lift = jnp.transpose(face_lift, (2, 0, 1))

    packed = (fields, ROWS, LANES)
    first_shape = (up_to(pairs * (sends + fast), ROWS), LANES)
    second_shape = (up_to(fields, 2 * ROWS), LANES)
    star_shape = (fields * fields * kinds, ROWS, LANES)
    combos = faces * HALF
    sources = elements + sides * sends

    waiting = (
        local_part, remote_part, restrict, lift, orient_maps, neighbour_slot, neighbour_face, neighbour_turn,
        cluster_rate.reshape(1, elements),
    )
    made = call(
        predict_kernel,
        [HBM] * (4 + len(LATER)),
        [(packed, F32)] * 2 + [(first_shape, F32)] * sides + [
            (packed, F32), (star_shape, F32), ((3 * LANES, kinds * LANES), BF16), (stiffness.shape, F32),
            ((pairs, elements, LANES), F32),
        ] + [(array.shape, array.dtype) for array in waiting],
        [
            ((fields, up_to(4 * fields, ROWS), LANES), F32),
            ((pairs, elements, LANES), F32),
            (values.shape, F32), ((kinds, LANES, LANES), F32), (star.shape, F32),
            pltpu.SMEM(send_list.shape, jnp.int32), pltpu.SemaphoreType.DMA((4 + len(LATER),)),
        ],
        (values, stiffness, star, send_list, *waiting),
        "predict", 100_000_000,
    )
    early, late, outgoing = made[0], made[1], made[2 : 2 + sides]
    start, star_coef, derive_op, stiffness_kept, early_rows = made[2 + sides : 7 + sides]
    waiting = made[7 + sides :]
    first = exchange(outgoing)
    (
        base, local_coef, remote_coef, volume_op, trace_op, local_lift, compose_op, remote_lift, choose, mask,
        codes, composed, lift_sides, fast_mask,
    ) = call(
        prepare_kernel,
        [VMEM] * 13,
        [
            (packed, F32), ((fields * fields, 2, ROWS, LANES), F32),
            ((faces * pairs * fields, elements, LANES), F32),
            ((3 * LANES, kinds * LANES), BF16), ((3 * LANES, 2 * LANES), BF16),
            ((6 * LANES, LANES), BF16), ((2 * LANES, combos), BF16), ((3 * faces * HALF, LANES), BF16),
            ((faces * elements, 2 * sources), BF16), ((faces * elements, combos), F32),
            ((2 * faces, LANES), F32), ((HALF, combos), F32), ((HALF, faces * HALF), F32),
            ((ROWS, LANES), F32),
        ],
        [
            ((fields, 2 * ROWS * faces, LANES), F32), ((pairs, 2 * up_to(4 * fields, ROWS), LANES), F32),
            ((kinds, LANES, LANES), F32), ((2 * LANES, LANES), F32),
            ((LANES, faces * LANES), F32), ((HALF, LANES), F32), ((LANES, LANES), F32),
        ],
        (start, early, stiffness_kept, star_coef, *waiting),
        "prepare", 200_000_000,
    )
    middle, late_value, *outgoing = call(
        middle_kernel,
        [VMEM] * 11 + [HBM] + [VMEM] * 4,
        [(packed, F32)] * 2 + [(second_shape, F32)] * sides,
        [
            ((pairs, sides * sends, LANES), F32), ((fields, elements, LANES), F32),
            pltpu.SMEM(send_list.shape, jnp.int32), pltpu.SemaphoreType.DMA,
        ],
        (
            base, early_rows, late, star_coef, remote_coef, derive_op, compose_op, remote_lift, choose, mask,
            fast_mask, send_list, *first,
        ),
        "middle", 200_000_000,
    )
    second = exchange(outgoing)
    base, ghost_flux, ghost_op, scatter = call(
        local_kernel,
        [VMEM] * (17 + len(first)),
        [
            (packed, F32), ((fields * second_shape[0], sides * LANES), F32),
            ((sides * fast, 2 * LANES, LANES), BF16), ((fields * elements, 2 * LANES), BF16),
        ],
        [((pairs, sources, LANES), F32), ((fields, 2 * ROWS * faces, LANES), F32)],
        (
            middle, late_value, star_coef, local_coef, volume_op, trace_op, local_lift,
            remote_coef, compose_op, remote_lift, choose, mask, waiting[1], codes, composed, lift_sides, waiting[4],
            *first,
        ),
        "local_late", 200_000_000,
    )
    (result,) = call(
        final_kernel,
        [VMEM] * 8,
        [(values.shape, F32)],
        [],
        (base, ghost_flux, ghost_op, scatter, *second),
        "final", 200_000_000,
    )
    return jnp.transpose(result, (2, 0, 1))


def solution(mesh):
    placed = (
        P(None, None, ("dom", "sub")),
        P(),
        P(None, None, None, ("dom", "sub")),
        P(),
        P(),
        P(),
        P(None, None, None, ("dom", "sub")),
        P(None, None, None, ("dom", "sub")),
        P(("dom", "sub")),
        P(("dom", "sub"), None, None),
        P(None, ("dom", "sub")),
        P(None, ("dom", "sub")),
        P(None, ("dom", "sub")),
    )
    return jax.shard_map(
        local, mesh=mesh, in_specs=placed, out_specs=P(None, None, ("dom", "sub")), check_vma=False
    )
```

```python
import math

import jax
import jax.numpy as jnp
from jax import lax
from jax.experimental import pallas as pl
from jax.experimental.pallas import tpu as pltpu
from jax.sharding import PartitionSpec as P

DERIVS = 6
LANES = 128
HALF = 64
ROWS = 8
F32 = jnp.float32
BF16 = jnp.bfloat16
LATER = ("flux_local", "flux_remote", "face_restrict", "face_lift", "orient_maps", "slot", "face", "turn", "rate")
AXES = ("dom", "sub")
SWAPS = (("dom", True), ("dom", False), ("sub", True), ("sub", False))


def taylor_weight(lower, upper, degree):
    return (upper ** (degree + 1) - lower ** (degree + 1)) / math.factorial(degree + 1)


def weight_at(lower, upper, degree):
    result = jnp.float32(taylor_weight(lower, upper, 1))
    for option in range(2, DERIVS):
        result = jnp.where(degree == option, jnp.float32(taylor_weight(lower, upper, option)), result)
    return result


def split(values):
    high = values.astype(BF16)
    low = (values - high.astype(F32)).astype(BF16)
    return high, low


def stack_left(values):
    high, low = split(values)
    return jnp.concatenate([high, low, high], axis=1)


def stack_right(values):
    high, low = split(values)
    return jnp.concatenate([high, high, low], axis=0)


def product(left, right):
    return jnp.dot(left, right, preferred_element_type=F32)


def odd_place(axis):
    return lax.rem(lax.axis_index(axis), 2)


def message_side(slot):
    axis, far = SWAPS[slot]
    odd = odd_place(axis)
    return 2 * AXES.index(axis) + (odd if far else 1 - odd)


def ghost_slot(side):
    axis = AXES[side // 2]
    even_far = side % 2 == 0
    return jnp.where(odd_place(axis) == 0, SWAPS.index((axis, even_far)), SWAPS.index((axis, not even_far)))


def lane_index(shape):
    return lax.broadcasted_iota(jnp.int32, shape, len(shape) - 1)


def lower_half(shape):
    return lane_index(shape) < HALF


def swap_halves(values):
    return pltpu.roll(values, HALF, values.ndim - 1)


def pack(values_ref, packed_ref):
    modes = values_ref.shape[2]
    packed_ref[:, :, 0:modes] = values_ref[:, 0:ROWS, :]
    packed_ref[:, :, HALF : HALF + modes] = values_ref[:, ROWS : 2 * ROWS, :]


def high_and_low(values, shift):
    high = values.astype(BF16).astype(F32)
    return high + pltpu.roll(values - high, shift, 1)


def row_index(shape):
    return lax.broadcasted_iota(jnp.int32, shape, len(shape) - 2)


def one_where(condition):
    return jnp.where(condition, 1.0, 0.0)


def star_coefficients(star_ref, stage_ref, star_out):
    fields, kinds, elements = star_ref.shape[0], star_ref.shape[2], star_ref.shape[3]
    lanes = lane_index((ROWS, LANES))
    pick = one_where((lanes % ROWS == row_index((ROWS, LANES))) & (lanes < 2 * elements))
    from_lane = row_index((LANES, LANES))
    same_half = (from_lane % elements) // ROWS == lane_index((LANES, LANES)) // HALF
    right = one_where(same_half & (from_lane < 2 * elements)).astype(BF16)
    filled = lane_index(stage_ref.shape[1:]) < elements
    for row in range(fields):
        for col in range(fields):
            stage_ref[row, col * 4 : col * 4 + kinds, 0:elements] = star_ref[row, col]
        values = jnp.where(filled, stage_ref[row], 0.0)
        stage_ref[row] = high_and_low(values, elements)
        spreads = []
        for kind in range(kinds):
            for col in range(fields):
                at = col * 4 + kind
                spreads.append(stage_ref[row, at : at + 1, :] * pick)
        spread_out = product(jnp.concatenate(spreads, axis=0).astype(BF16), right)
        count = kinds * fields
        star_out[row * count : (row + 1) * count] = spread_out.reshape(count, ROWS, LANES)


def star_mix(columns, star_ref, fields, kinds):
    sums = []
    for col in range(fields):
        parts = []
        for kind in range(kinds):
            total = None
            for row in range(fields):
                part = columns[row * ROWS : (row + 1) * ROWS, kind * LANES : (kind + 1) * LANES]
                term = star_ref[(row * kinds + kind) * fields + col] * part
                total = term if total is None else total + term
            parts.append(total)
        sums.append(sum(parts[1:], parts[0]))
    return jnp.concatenate(sums, axis=0)


def stiffness_blocks(stiffness_ref, block_ref, turned):
    kinds, modes = stiffness_ref.shape[0], stiffness_ref.shape[1]
    for kind in range(kinds):
        matrix = -stiffness_ref[kind].T if turned else stiffness_ref[kind]
        block_ref[kind, 0:modes, 0:modes] = matrix
        block_ref[kind, HALF : HALF + modes, HALF : HALF + modes] = matrix
    return jnp.concatenate([block_ref[kind] for kind in range(kinds)], axis=1)


def predict_kernel(*refs):
    later = len(LATER)
    solution_hbm, stiffness_hbm, star_hbm, send_hbm = refs[0:4]
    later_hbm, refs = refs[4 : 4 + later], refs[4 + later :]
    early_out, late_out, send_0, send_1, send_2, send_3 = refs[0:6]
    packed_ref, coef_ref, derive_ref, stiffness_ref, early_rows = refs[6:11]
    later_out, refs = refs[11 : 11 + later], refs[11 + later :]
    work_ref, late_rows, solution_ref, block_ref, star_ref, send_ref, sems = refs

    sources = (star_hbm, stiffness_hbm, solution_hbm, send_hbm, *later_hbm)
    targets = (star_ref, stiffness_ref, solution_ref, send_ref, *later_out)
    copies = [
        pltpu.make_async_copy(source, target, sems.at[number])
        for number, (source, target) in enumerate(zip(sources, targets))
    ]
    for copy in copies:
        copy.start()
    fields, kinds = star_ref.shape[0], star_ref.shape[2]
    pairs = (fields + 1) // 2
    for cleared in (packed_ref, block_ref, send_0, send_1, send_2, send_3):
        cleared[...] = jnp.zeros(cleared.shape, F32)
    for copy in copies[0:3]:
        copy.wait()
    derive_ref[...] = stack_right(stiffness_blocks(stiffness_ref, block_ref, True))
    star_coefficients(star_ref, work_ref, coef_ref)
    pack(solution_ref, packed_ref)
    start = packed_ref[...].reshape(fields * ROWS, LANES)

    def step(degree, carry):
        current, early, late = carry
        current = star_mix(product(stack_left(current), derive_ref[...]), coef_ref, fields, kinds)
        early = early + weight_at(0.0, 0.5, degree) * current
        late = late + weight_at(0.5, 1.0, degree) * current
        return current, early, late

    _, early, late = lax.fori_loop(
        1, DERIVS, step, (start, taylor_weight(0.0, 0.5, 0) * start, taylor_weight(0.5, 1.0, 0) * start),
        unroll=True,
    )
    early_out[...] = early.reshape(fields, ROWS, LANES)
    late_out[...] = late.reshape(fields, ROWS, LANES)
    rows_by_pair(early, early_rows, fields)
    rows_by_pair(late, late_rows, fields)
    copies[3].wait()
    sends = send_ref.shape[2]
    fast = sends // 2
    for side, out in enumerate((send_0, send_1, send_2, send_3)):
        for place in range(sends):
            element = send_ref[0, message_side(side), place]
            for pair in range(pairs):
                row = pair * sends + place
                out[row : row + 1, :] = early_rows[pair, pl.ds(element, 1), :]
            if place >= fast:
                for pair in range(pairs):
                    row = pairs * sends + pair * fast + place - fast
                    out[row : row + 1, :] = late_rows[pair, pl.ds(element, 1), :]
    for copy in copies[4:]:
        copy.wait()


def rows_by_pair(packed, out_ref, fields):
    lower = lower_half((ROWS, LANES))
    for pair in range((fields + 1) // 2):
        even = packed[2 * pair * ROWS : (2 * pair + 1) * ROWS]
        odd = jnp.zeros_like(even)
        if 2 * pair + 1 < fields:
            odd = packed[(2 * pair + 1) * ROWS : (2 * pair + 2) * ROWS]
        out_ref[pair, 0:ROWS, :] = jnp.where(lower, even, swap_halves(odd))
        out_ref[pair, ROWS : 2 * ROWS, :] = jnp.where(lower, swap_halves(even), odd)


def flux_local_coefficients(flux_ref, stage_ref, out_ref):
    fields, faces, elements = flux_ref.shape[0], flux_ref.shape[2], flux_ref.shape[3]
    rows = 2 * ROWS
    filled = lane_index((rows, LANES)) < elements
    lanes, sublanes = lane_index((ROWS, LANES)), row_index((ROWS, LANES))
    picks = [one_where(lanes % elements == half * ROWS + sublanes) for half in range(2)]
    square = (LANES, LANES)
    right = one_where(row_index(square) // (2 * elements) == lane_index(square) % faces).astype(BF16)
    for row in range(fields):
        values = None
        for face in range(faces):
            stage_ref[row, face * rows : face * rows + fields, 0:elements] = flux_ref[row, :, face, :]
            part = jnp.where(filled, stage_ref[row, face * rows : (face + 1) * rows, :], 0.0)
            values = part if values is None else values + pltpu.roll(part, face * 2 * elements, 1)
        stage_ref[row, 0:rows, :] = high_and_low(values, elements)
        left = [stage_ref[row, col : col + 1, :] * pick for col in range(fields) for pick in picks]
        spread = product(jnp.concatenate(left, axis=0).astype(BF16), right)
        out_ref[row * fields : (row + 1) * fields] = spread.reshape(fields, 2, ROWS, LANES)


def flux_remote_coefficients(flux_ref, stage_ref, out_ref):
    fields, faces, elements = flux_ref.shape[0], flux_ref.shape[2], flux_ref.shape[3]
    pairs = (fields + 1) // 2
    rows = stage_ref.shape[1] // 2
    filled = lane_index((rows, LANES)) < elements
    lanes, sublanes = lane_index((elements, LANES)), row_index((elements, LANES))
    pick = one_where((lanes % elements == sublanes) & (lanes < 4 * elements))
    square = (LANES, LANES)
    from_lane = row_index(square)
    same_parity = (from_lane // elements) % 2 == lane_index(square) // HALF
    right = one_where(same_parity & (from_lane < 4 * elements)).astype(BF16)
    for pair in range(pairs):
        values = None
        for row in range(2 * pair, min(2 * pair + 2, fields)):
            start = (row % 2) * rows
            for col in range(fields):
                at = start + col * faces
                stage_ref[pair, at : at + faces, 0:elements] = flux_ref[row, col]
            part = jnp.where(filled, stage_ref[pair, start : start + rows, :], 0.0)
            values = part if values is None else values + pltpu.roll(part, elements, 1)
        stage_ref[pair, 0:rows, :] = high_and_low(values, 2 * elements)
        for face in range(faces):
            left = []
            for col in range(fields):
                at = col * faces + face
                left.append(stage_ref[pair, at : at + 1, :] * pick)
            spread = product(jnp.concatenate(left, axis=0).astype(BF16), right)
            at = (face * pairs + pair) * fields
            out_ref[at : at + fields] = spread.reshape(fields, elements, LANES)


def local_terms(packed, star_ref, flux_ref, volume_ref, trace_ref, lift_ref, fields, kinds):
    left = stack_left(packed)
    volume = star_mix(product(left, volume_ref[...]), star_ref, fields, kinds)
    traces = product(left, trace_ref[...])
    sums = []
    for col in range(fields):
        halves = []
        for half in range(2):
            total = None
            for row in range(fields):
                part = traces[row * ROWS : (row + 1) * ROWS, half * LANES : (half + 1) * LANES]
                term = flux_ref[row * fields + col, half] * part
                total = term if total is None else total + term
            halves.append(total)
        sums.append(jnp.concatenate(halves, axis=1))
    return volume + product(stack_left(jnp.concatenate(sums, axis=0)), lift_ref[...])


def combo_code(lanes, turns, face_modes):
    in_face = lanes % HALF
    code = jnp.where(in_face < turns * face_modes, (lanes // HALF) * turns + in_face // face_modes, -1)
    return code.astype(F32)


def ghost_terms(
    flux_ref, stage_ref, code_ref, composed, lift_sides, lane_code, flux_out, operator_out, scatter_out, sends, fields
):
    faces, elements = flux_ref.shape[2], flux_ref.shape[3]
    rows = 2 * ROWS
    shape = (rows, LANES)
    lanes = lane_index(shape)

    def along_lanes(start):
        row = code_ref[start : start + 1, :]
        for face in range(1, faces):
            row = row + pltpu.roll(code_ref[start + face : start + face + 1, :], face * elements, 1)
        return row + swap_halves(row)

    slots, codes = along_lanes(0), along_lanes(faces)
    ghosts = elements + row_index(shape)
    found = one_where(jnp.broadcast_to(slots, shape) == ghosts.astype(F32))
    first = jnp.where(lanes < HALF, found, 0.0)
    code = jnp.sum(first * codes, axis=1, keepdims=True)
    face_of = jnp.sum(first * (lanes // elements).astype(F32), axis=1, keepdims=True)
    element_of = jnp.sum(first * (lanes % elements).astype(F32), axis=1, keepdims=True)
    numbers = [slot * sends + place for slot in range(4) for place in range(sends // 2)]

    filled = lanes < elements
    values = []
    for field in range(fields):
        total = None
        for face in range(faces):
            stage_ref[field, face * rows : face * rows + fields, 0:elements] = flux_ref[field, :, face, :]
            part = jnp.where(filled, stage_ref[field, face * rows : (face + 1) * rows, :], 0.0)
            total = part if total is None else total + pltpu.roll(part, face * elements, 1)
        total = jnp.where(row_index(shape) < fields, total, 0.0)
        values.append(high_and_low(total, HALF))
    picked = jnp.concatenate([jnp.broadcast_to(found[number : number + 1], (HALF, LANES)) for number in numbers], axis=0)
    flux_out[...] = lax.dot_general(
        jnp.concatenate(values, axis=0).astype(BF16), picked.astype(BF16), (((1,), (1,)), ((), ())),
        preferred_element_type=F32,
    )

    left = []
    for number in numbers:
        chosen = composed * one_where(lane_code == code[number : number + 1])
        both = chosen[:, 0:LANES] + chosen[:, LANES : 2 * LANES]
        high, low = split(both + swap_halves(both))
        left.append(jnp.concatenate([jnp.where(lower_half(high.shape), high, low), high], axis=1))
    high, low = split(lift_sides)
    lifts = product(jnp.concatenate(left, axis=0), jnp.concatenate([high, high, low, jnp.zeros_like(low)], axis=0))
    side_lane = (lane_index((1, faces * HALF)) // HALF).astype(F32)
    place_of = jnp.zeros((1, LANES), F32)
    columns = []
    for at, number in enumerate(numbers):
        chosen = lifts[at * HALF : (at + 1) * HALF] * one_where(side_lane == face_of[number : number + 1])
        both = chosen[:, 0:LANES] + chosen[:, LANES : 2 * LANES]
        high, low = split(both + swap_halves(both))
        none = jnp.zeros_like(low)
        order = [high, none, high, none, low, none] if at % 2 == 0 else [none, high, none, high, none, low]
        columns.append(jnp.concatenate(order, axis=0))
        if at % 2 == 1:
            operator_out[at // 2] = jnp.concatenate(columns[-2:], axis=1)
        place_of = jnp.where(lane_index((1, LANES)) // rows == at, element_of[number : number + 1], place_of)
    square = (fields * elements, LANES)
    here = (row_index(square) // elements == lane_index(square) % rows) & (
        (row_index(square) % elements).astype(F32) == place_of
    )
    one = one_where(here).astype(BF16)
    scatter_out[...] = jnp.concatenate([one, one], axis=1)


def prepare_kernel(
    packed_ref, early_ref, stiffness_ref, star_ref, flux_local_ref, flux_remote_ref, restrict_ref, lift_ref, orient_ref,
    slot_ref, face_ref, turn_ref, rate_ref,
    base_out, local_out, remote_out, volume_out, trace_out, local_lift_out, compose_out,
    remote_lift_out, choose_out, mask_out, code_ref, composed_out, sides_ref, fast_out,
    local_work_ref, remote_work_ref, block_ref, wide_ref, face_work_ref, orient_work_ref, code_work_ref,
):
    fields, kinds = packed_ref.shape[0], stiffness_ref.shape[0]
    face_modes, faces, modes = restrict_ref.shape
    turns = orient_ref.shape[0]
    flux_local_coefficients(flux_local_ref, local_work_ref, local_out)
    flux_remote_coefficients(flux_remote_ref, remote_work_ref, remote_out)

    block_ref[...] = jnp.zeros(block_ref.shape, F32)
    volume_out[...] = stack_right(stiffness_blocks(stiffness_ref, block_ref, False))

    wide_ref[...] = jnp.zeros(wide_ref.shape, F32)
    for mode in range(face_modes):
        at = mode * faces
        wide_ref[at : at + faces, 0:modes] = restrict_ref[mode]
        wide_ref[LANES + at : LANES + at + faces, HALF : HALF + modes] = restrict_ref[mode]
    trace_out[...] = stack_right(wide_ref[...].T)
    for mode in range(face_modes):
        at = mode * faces
        wide_ref[at : at + faces, 0:modes] = -lift_ref[mode]
        wide_ref[LANES + at : LANES + at + faces, HALF : HALF + modes] = -lift_ref[mode]
    local_lift_out[...] = stack_right(wide_ref[...])

    face_work_ref[...] = jnp.zeros(face_work_ref.shape, F32)
    orient_work_ref[...] = jnp.zeros(orient_work_ref.shape, F32)
    for turn in range(turns):
        orient_work_ref[turn * face_modes : (turn + 1) * face_modes, 0:face_modes] = orient_ref[turn]
    for face in range(faces):
        face_work_ref[0:face_modes, face * LANES : face * LANES + modes] = restrict_ref[:, face, :]
        face_work_ref[0:face_modes, face * LANES + HALF : face * LANES + HALF + modes] = restrict_ref[:, face, :]
    composed = jnp.dot(
        orient_work_ref[...], face_work_ref[...], precision=lax.Precision.HIGHEST, preferred_element_type=F32
    )
    stacked = jnp.concatenate([composed[:, face * LANES : (face + 1) * LANES] for face in range(faces)], axis=0)
    high, low = split(stacked.T[0:HALF])
    compose_out[...] = jnp.concatenate([high, high, low, jnp.zeros_like(low)], axis=0)
    wide_ref[...] = jnp.zeros(wide_ref.shape, F32)
    for face in range(faces):
        for turn in range(turns):
            rows = slice(face * HALF + turn * face_modes, face * HALF + (turn + 1) * face_modes)
            wide_ref[rows, 0:modes] = -lift_ref[:, face, :]
            wide_ref[rows, HALF : HALF + modes] = -lift_ref[:, face, :]
    remote_lift_out[...] = stack_right(wide_ref[...])

    elements = slot_ref.shape[1]
    code_work_ref[...] = jnp.zeros(code_work_ref.shape, F32)
    slots = slot_ref[...]
    sends = (choose_out.shape[1] // 2 - elements) // 4
    group = (slots - elements) // sends
    moved = slots
    for side in range(4):
        moved = jnp.where(group == side, slots + (ghost_slot(side) - side) * sends, moved)
    code_work_ref[0:faces, 0:elements] = jnp.where(slots < elements, slots, moved).astype(F32)
    code_work_ref[faces : 2 * faces, 0:elements] = (face_ref[...] * turns + turn_ref[...]).astype(F32)
    code_work_ref[2 * faces : 2 * faces + 1, 0:elements] = rate_ref[...].astype(F32)
    code_ref[...] = code_work_ref[0 : 2 * faces, :]
    codes = code_work_ref[...].T[0:elements, :]
    rates = codes[:, 2 * faces : 2 * faces + 1]
    fast_out[...] = jnp.where(lower_half((ROWS, LANES)), rates[0:ROWS], rates[ROWS : 2 * ROWS])
    sources = choose_out.shape[1] // 2
    source_lane = (lane_index((elements, 2 * sources)) % sources).astype(F32)
    lanes = lane_index((elements, mask_out.shape[1]))
    lane_code = combo_code(lanes, turns, face_modes)
    picks, masks = [], []
    for face in range(faces):
        picks.append(jnp.where(codes[:, face : face + 1] == source_lane, 1.0, 0.0))
        masks.append(jnp.where(codes[:, faces + face : faces + face + 1] == lane_code, 1.0, 0.0))
    choose_out[...] = jnp.concatenate(picks, axis=0).astype(BF16)
    mask_out[...] = jnp.concatenate(masks, axis=0)

    sides_ref[...] = jnp.zeros(sides_ref.shape, F32)
    for face in range(faces):
        for turn in range(turns):
            rows = slice(turn * face_modes, (turn + 1) * face_modes)
            sides_ref[rows, face * HALF : face * HALF + modes] = -lift_ref[:, face, :]
    composed_out[...] = stacked.T[0:HALF]

    early = early_ref[...].reshape(fields * ROWS, LANES)
    terms = local_terms(early, star_ref, local_out, volume_out, trace_out, local_lift_out, fields, kinds)
    base_out[...] = packed_ref[...] + terms.reshape(fields, ROWS, LANES)


def remote_terms(rows, remote_ref, compose_ref, lift_ref, choose_ref, mask_ref, fields):
    pairs = len(rows)
    faces = lift_ref.shape[0] // (3 * HALF)
    elements = choose_ref.shape[0] // faces
    sources = jnp.concatenate(rows, axis=1)
    gathered = product(choose_ref[...], jnp.concatenate(split(sources), axis=0))
    folded = []
    for face in range(faces):
        sums = []
        for col in range(fields):
            total = None
            for pair in range(pairs):
                part = gathered[face * elements : (face + 1) * elements, pair * LANES : (pair + 1) * LANES]
                term = remote_ref[(face * pairs + pair) * fields + col] * part
                total = term if total is None else total + term
            sums.append(total)
        mixed = jnp.concatenate(sums, axis=0)
        high, low = split(mixed + swap_halves(mixed))
        first = jnp.where(lower_half(high.shape), high, low)
        turned = product(jnp.concatenate([first, high], axis=1), compose_ref[...])
        mask = mask_ref[face * elements : (face + 1) * elements, :]
        chosen = (turned.reshape(fields, elements, turned.shape[1]) * mask[None]).reshape(turned.shape)
        both = chosen[:, 0:LANES] + chosen[:, LANES : 2 * LANES]
        folded.append(both + swap_halves(both))
    lower = lower_half(folded[0].shape)
    left = [jnp.where(lower, folded[face], folded[face + 1]) for face in range(0, faces, 2)]
    result = product(stack_left(jnp.concatenate(left, axis=1)), lift_ref[...])
    result = result.reshape(fields, 2, ROWS, LANES)
    return jnp.where(lower_half((ROWS, LANES))[None], result[:, 0], result[:, 1])


def middle_kernel(
    base_ref, early_rows, late_ref, star_ref, remote_ref, derive_ref, compose_ref, lift_ref, choose_ref, mask_ref,
    fast_ref, send_hbm, from_0, from_1, from_2, from_3,
    middle_out, late_out, send_0, send_1, send_2, send_3,
    rows_ref, late_rows, send_ref, sem,
):
    copy = pltpu.make_async_copy(send_hbm, send_ref, sem)
    copy.start()
    fields = base_ref.shape[0]
    kinds = star_ref.shape[0] // (fields * fields)
    pairs = rows_ref.shape[0]
    sends = send_ref.shape[2]
    fast = sends // 2
    for side, arrived in enumerate((from_0, from_1, from_2, from_3)):
        for pair in range(pairs):
            rows_ref[pair, side * sends : (side + 1) * sends, :] = arrived[pair * sends : (pair + 1) * sends, :]
    rows = [jnp.concatenate([early_rows[pair], rows_ref[pair]], axis=0) for pair in range(pairs)]
    middle = base_ref[...] + remote_terms(rows, remote_ref, compose_ref, lift_ref, choose_ref, mask_ref, fields)
    middle_out[...] = middle
    start = middle.reshape(fields * ROWS, LANES)

    def step(degree, carry):
        current, early = carry
        current = star_mix(product(stack_left(current), derive_ref[...]), star_ref, fields, kinds)
        return current, early + weight_at(0.0, 0.5, degree) * current

    _, restart = lax.fori_loop(1, DERIVS, step, (start, taylor_weight(0.0, 0.5, 0) * start))
    copy.wait()
    is_fast = fast_ref[...]
    late = jnp.where((is_fast == 2)[None], restart.reshape(fields, ROWS, LANES), late_ref[...])
    late_out[...] = late
    both = late.reshape(fields * ROWS, LANES)
    swapped = swap_halves(both)
    wide = lower_half(both.shape)
    late_rows[:, 0:ROWS, :] = jnp.where(wide, both, swapped).reshape(late.shape)
    late_rows[:, ROWS : 2 * ROWS, :] = jnp.where(wide, swapped, both).reshape(late.shape)
    first_half = lower_half((1, LANES))
    for slot, out in enumerate((send_0, send_1, send_2, send_3)):
        out[...] = jnp.zeros(out.shape, F32)
        side = message_side(slot)
        places = [send_ref[0, side, place] for place in range(fast)]
        for field in range(fields):
            halves = [late_rows[field, pl.ds(element, 1), :] for element in places]
            out[field : field + 1, :] = jnp.where(first_half, *halves)


def local_kernel(
    middle_ref, late_ref, star_ref, flux_ref, volume_ref, trace_ref, lift_ref,
    remote_ref, compose_ref, remote_lift_ref, choose_ref, mask_ref, flux_remote_ref, code_ref, composed_ref, sides_ref,
    orient_ref, first_0, first_1, first_2, first_3,
    base_out, ghost_flux_out, ghost_operator_out, scatter_out, rows_ref, stage_ref,
):
    fields = middle_ref.shape[0]
    kinds = star_ref.shape[0] // (fields * fields)
    pairs = rows_ref.shape[0]
    elements = 2 * ROWS
    sends = (rows_ref.shape[1] - elements) // 4
    fast = sends // 2
    late = late_ref[...].reshape(fields * ROWS, LANES)
    rows_by_pair(late, rows_ref, fields)
    for slot, first in enumerate((first_0, first_1, first_2, first_3)):
        at = elements + slot * sends
        for pair in range(pairs):
            rows_ref[pair, at : at + fast, :] = jnp.zeros((fast, LANES), F32)
            row = pairs * sends + pair * fast
            rows_ref[pair, at + fast : at + sends, :] = first[row : row + fast, :]
    terms = local_terms(late, star_ref, flux_ref, volume_ref, trace_ref, lift_ref, fields, kinds)
    rows = [rows_ref[pair] for pair in range(pairs)]
    remote = remote_terms(rows, remote_ref, compose_ref, remote_lift_ref, choose_ref, mask_ref, fields)
    base = middle_ref[...] + terms.reshape(fields, ROWS, LANES) + remote
    base_out[:, 0:ROWS, :] = base
    base_out[:, ROWS : 2 * ROWS, :] = swap_halves(base.reshape(fields * ROWS, LANES)).reshape(base.shape)
    lane_code = combo_code(lane_index((1, composed_ref.shape[1])), orient_ref.shape[0], orient_ref.shape[1])
    ghost_terms(
        flux_remote_ref, stage_ref, code_ref, composed_ref[...], sides_ref[...], lane_code,
        ghost_flux_out, ghost_operator_out, scatter_out, sends, fields,
    )


def final_kernel(
    base_ref, ghost_flux_ref, ghost_operator_ref, scatter_ref, second_0, second_1, second_2, second_3, result_out,
):
    fields = base_ref.shape[0]
    modes = result_out.shape[2]
    rows = second_0.shape[0]
    added = []
    for slot, second in enumerate((second_0, second_1, second_2, second_3)):
        sums = [None] * 3
        for field in range(fields):
            coefficient = ghost_flux_ref[field * rows : (field + 1) * rows, slot * LANES : (slot + 1) * LANES]
            term = coefficient * second[field : field + 1, :]
            sums[field % 3] = term if sums[field % 3] is None else sums[field % 3] + term
        both = product(stack_left(sums[0] + sums[1] + sums[2]), ghost_operator_ref[slot])
        added += [both[:, 0:LANES], both[:, LANES : 2 * LANES]]
    right = jnp.concatenate(split(jnp.concatenate(added, axis=0)), axis=0)
    result = base_ref[...] + product(scatter_ref[...], right).reshape(base_ref.shape)
    result_out[...] = result[:, :, 0:modes]


VMEM = pl.BlockSpec(memory_space=pltpu.VMEM)
HBM = pl.BlockSpec(memory_space=pltpu.HBM)


def call(kernel, ins, outs, scratch, args, name, flops):
    shapes = [jax.ShapeDtypeStruct(shape, dtype) for shape, dtype in outs]
    args = [
        pltpu.with_memory_space_constraint(arg, pltpu.HBM) if spec is HBM else arg for spec, arg in zip(ins, args)
    ]
    return pl.pallas_call(
        kernel,
        out_shape=shapes,
        in_specs=ins,
        out_specs=[VMEM] * len(outs),
        scratch_shapes=[pltpu.VMEM(*one) if isinstance(one, tuple) else one for one in scratch],
        compiler_params=pltpu.CompilerParams(vmem_limit_bytes=16 * 1024 * 1024),
        cost_estimate=pl.CostEstimate(flops=flops, bytes_accessed=4_000_000, transcendentals=0),
        name=name,
    )(*args)


def exchange(outgoing):
    arrived = []
    for (axis, far), message in zip(SWAPS, outgoing):
        size = lax.axis_size(axis)
        assert size % 2 == 0
        pairs = []
        for first in range(1 if far else 0, size, 2):
            second = (first + 1) % size
            pairs += [(first, second), (second, first)]
        arrived.append(lax.ppermute(message, axis, pairs))
    return arrived


def up_to(count, multiple):
    return -(-count // multiple) * multiple


def local(
    solution, stiffness, star_matrices, face_restrict, face_lift, orient_maps, flux_local, flux_remote,
    cluster_rate, send_list, neighbour_slot, neighbour_face, neighbour_turn,
):
    fields, elements = solution.shape[1], solution.shape[2]
    kinds = stiffness.shape[0]
    faces = face_restrict.shape[0]
    sides, sends = send_list.shape[1], send_list.shape[2]
    fast = sends // 2
    pairs = (fields + 1) // 2
    assert elements == 2 * ROWS and solution.shape[0] <= HALF and fast == 2
    values = jnp.transpose(solution, (1, 2, 0))
    star = jnp.transpose(star_matrices, (1, 2, 0, 3))
    local_part = jnp.transpose(flux_local, (1, 2, 0, 3))
    remote_part = jnp.transpose(flux_remote, (1, 2, 0, 3))
    restrict = jnp.transpose(face_restrict, (1, 0, 2))
    lift = jnp.transpose(face_lift, (2, 0, 1))

    packed = (fields, ROWS, LANES)
    first_shape = (up_to(pairs * (sends + fast), ROWS), LANES)
    second_shape = (up_to(fields, 2 * ROWS), LANES)
    star_shape = (fields * fields * kinds, ROWS, LANES)
    combos = faces * HALF
    sources = elements + sides * sends

    waiting = (
        local_part, remote_part, restrict, lift, orient_maps, neighbour_slot, neighbour_face, neighbour_turn,
        cluster_rate.reshape(1, elements),
    )
    made = call(
        predict_kernel,
        [HBM] * (4 + len(LATER)),
        [(packed, F32)] * 2 + [(first_shape, F32)] * sides + [
            (packed, F32), (star_shape, F32), ((3 * LANES, kinds * LANES), BF16), (stiffness.shape, F32),
            ((pairs, elements, LANES), F32),
        ] + [(array.shape, array.dtype) for array in waiting],
        [
            ((fields, up_to(4 * fields, ROWS), LANES), F32),
            ((pairs, elements, LANES), F32),
            (values.shape, F32), ((kinds, LANES, LANES), F32), (star.shape, F32),
            pltpu.SMEM(send_list.shape, jnp.int32), pltpu.SemaphoreType.DMA((4 + len(LATER),)),
        ],
        (values, stiffness, star, send_list, *waiting),
        "predict", 100_000_000,
    )
    early, late, outgoing = made[0], made[1], made[2 : 2 + sides]
    start, star_coef, derive_op, stiffness_kept, early_rows = made[2 + sides : 7 + sides]
    waiting = made[7 + sides :]
    first = exchange(outgoing)
    (
        base, local_coef, remote_coef, volume_op, trace_op, local_lift, compose_op, remote_lift, choose, mask,
        codes, composed, lift_sides, fast_mask,
    ) = call(
        prepare_kernel,
        [VMEM] * 13,
        [
            (packed, F32), ((fields * fields, 2, ROWS, LANES), F32),
            ((faces * pairs * fields, elements, LANES), F32),
            ((3 * LANES, kinds * LANES), BF16), ((3 * LANES, 2 * LANES), BF16),
            ((6 * LANES, LANES), BF16), ((2 * LANES, combos), BF16), ((3 * faces * HALF, LANES), BF16),
            ((faces * elements, 2 * sources), BF16), ((faces * elements, combos), F32),
            ((2 * faces, LANES), F32), ((HALF, combos), F32), ((HALF, faces * HALF), F32),
            ((ROWS, LANES), F32),
        ],
        [
            ((fields, 2 * ROWS * faces, LANES), F32), ((pairs, 2 * up_to(4 * fields, ROWS), LANES), F32),
            ((kinds, LANES, LANES), F32), ((2 * LANES, LANES), F32),
            ((LANES, faces * LANES), F32), ((HALF, LANES), F32), ((LANES, LANES), F32),
        ],
        (start, early, stiffness_kept, star_coef, *waiting),
        "prepare", 200_000_000,
    )
    middle, late_value, *outgoing = call(
        middle_kernel,
        [VMEM] * 11 + [HBM] + [VMEM] * 4,
        [(packed, F32)] * 2 + [(second_shape, F32)] * sides,
        [
            ((pairs, sides * sends, LANES), F32), ((fields, elements, LANES), F32),
            pltpu.SMEM(send_list.shape, jnp.int32), pltpu.SemaphoreType.DMA,
        ],
        (
            base, early_rows, late, star_coef, remote_coef, derive_op, compose_op, remote_lift, choose, mask,
            fast_mask, send_list, *first,
        ),
        "middle", 200_000_000,
    )
    second = exchange(outgoing)
    base, ghost_flux, ghost_op, scatter = call(
        local_kernel,
        [VMEM] * (17 + len(first)),
        [
            ((fields, elements, LANES), F32), ((fields * second_shape[0], sides * LANES), F32),
            ((sides, 3 * LANES, 2 * LANES), BF16), ((fields * elements, 2 * LANES), BF16),
        ],
        [((pairs, sources, LANES), F32), ((fields, 2 * ROWS * faces, LANES), F32)],
        (
            middle, late_value, star_coef, local_coef, volume_op, trace_op, local_lift,
            remote_coef, compose_op, remote_lift, choose, mask, waiting[1], codes, composed, lift_sides, waiting[4],
            *first,
        ),
        "local_late", 200_000_000,
    )
    (result,) = call(
        final_kernel,
        [VMEM] * 8,
        [(values.shape, F32)],
        [],
        (base, ghost_flux, ghost_op, scatter, *second),
        "final", 200_000_000,
    )
    return jnp.transpose(result, (2, 0, 1))


def solution(mesh):
    placed = (
        P(None, None, ("dom", "sub")),
        P(),
        P(None, None, None, ("dom", "sub")),
        P(),
        P(),
        P(),
        P(None, None, None, ("dom", "sub")),
        P(None, None, None, ("dom", "sub")),
        P(("dom", "sub")),
        P(("dom", "sub"), None, None),
        P(None, ("dom", "sub")),
        P(None, ("dom", "sub")),
        P(None, ("dom", "sub")),
    )
    return jax.shard_map(
        local, mesh=mesh, in_specs=placed, out_specs=P(None, None, ("dom", "sub")), check_vma=False
    )
```

```python
import functools
import math

import jax
import jax.numpy as jnp
from jax import lax
from jax.experimental import pallas as pl
from jax.experimental.pallas import tpu as pltpu
from jax.sharding import PartitionSpec as P

DERIVS = 6
LANES = 128
HALF = 64
ROWS = 8
F32 = jnp.float32
BF16 = jnp.bfloat16
LATER = ("flux_local", "flux_remote", "face_restrict", "face_lift", "orient_maps", "slot", "face", "turn", "rate")
AXES = ("dom", "sub")
SWAPS = (("dom", True), ("dom", False), ("sub", True), ("sub", False))


def taylor_weight(lower, upper, degree):
    return (upper ** (degree + 1) - lower ** (degree + 1)) / math.factorial(degree + 1)


def weight_at(lower, upper, degree):
    result = jnp.float32(taylor_weight(lower, upper, 1))
    for option in range(2, DERIVS):
        result = jnp.where(degree == option, jnp.float32(taylor_weight(lower, upper, option)), result)
    return result


def split(values):
    high = values.astype(BF16)
    low = (values - high.astype(F32)).astype(BF16)
    return high, low


def stack_left(values):
    high, low = split(values)
    return jnp.concatenate([high, low, high], axis=1)


def stack_right(values):
    high, low = split(values)
    return jnp.concatenate([high, high, low], axis=0)


def product(left, right):
    return jnp.dot(left, right, preferred_element_type=F32)


def odd_place(axis):
    return lax.rem(lax.axis_index(axis), 2)


def message_side(slot):
    axis, far = SWAPS[slot]
    odd = odd_place(axis)
    return 2 * AXES.index(axis) + (odd if far else 1 - odd)


def ghost_slot(side):
    axis = AXES[side // 2]
    even_far = side % 2 == 0
    return jnp.where(odd_place(axis) == 0, SWAPS.index((axis, even_far)), SWAPS.index((axis, not even_far)))


def lane_index(shape):
    return lax.broadcasted_iota(jnp.int32, shape, len(shape) - 1)


def lower_half(shape):
    return lane_index(shape) < HALF


def swap_halves(values):
    return pltpu.roll(values, HALF, values.ndim - 1)


def pack(values_ref, packed_ref):
    modes = values_ref.shape[2]
    packed_ref[:, :, 0:modes] = values_ref[:, 0:ROWS, :]
    packed_ref[:, :, HALF : HALF + modes] = values_ref[:, ROWS : 2 * ROWS, :]


def high_and_low(values, shift):
    high = values.astype(BF16).astype(F32)
    return high + pltpu.roll(values - high, shift, 1)


def row_index(shape):
    return lax.broadcasted_iota(jnp.int32, shape, len(shape) - 2)


def one_where(condition):
    return jnp.where(condition, 1.0, 0.0)


def star_coefficients(star_ref, stage_ref, star_out):
    fields, kinds, elements = star_ref.shape[0], star_ref.shape[2], star_ref.shape[3]
    lanes = lane_index((ROWS, LANES))
    pick = one_where((lanes % ROWS == row_index((ROWS, LANES))) & (lanes < 2 * elements))
    from_lane = row_index((LANES, LANES))
    same_half = (from_lane % elements) // ROWS == lane_index((LANES, LANES)) // HALF
    right = one_where(same_half & (from_lane < 2 * elements)).astype(BF16)
    filled = lane_index(stage_ref.shape[1:]) < elements
    for row in range(fields):
        for col in range(fields):
            stage_ref[row, col * 4 : col * 4 + kinds, 0:elements] = star_ref[row, col]
        values = jnp.where(filled, stage_ref[row], 0.0)
        stage_ref[row] = high_and_low(values, elements)
        spreads = []
        for kind in range(kinds):
            for col in range(fields):
                at = col * 4 + kind
                spreads.append(stage_ref[row, at : at + 1, :] * pick)
        spread_out = product(jnp.concatenate(spreads, axis=0).astype(BF16), right)
        count = kinds * fields
        star_out[row * count : (row + 1) * count] = spread_out.reshape(count, ROWS, LANES)


def star_mix(columns, star_ref, fields, kinds):
    sums = []
    for col in range(fields):
        parts = []
        for kind in range(kinds):
            total = None
            for row in range(fields):
                part = columns[row * ROWS : (row + 1) * ROWS, kind * LANES : (kind + 1) * LANES]
                term = star_ref[(row * kinds + kind) * fields + col] * part
                total = term if total is None else total + term
            parts.append(total)
        sums.append(sum(parts[1:], parts[0]))
    return jnp.concatenate(sums, axis=0)


def stiffness_blocks(stiffness_ref, block_ref, turned):
    kinds, modes = stiffness_ref.shape[0], stiffness_ref.shape[1]
    for kind in range(kinds):
        matrix = -stiffness_ref[kind].T if turned else stiffness_ref[kind]
        block_ref[kind, 0:modes, 0:modes] = matrix
        block_ref[kind, HALF : HALF + modes, HALF : HALF + modes] = matrix
    return jnp.concatenate([block_ref[kind] for kind in range(kinds)], axis=1)


def predict_kernel(*refs):
    later = len(LATER)
    solution_hbm, stiffness_hbm, star_hbm, send_hbm = refs[0:4]
    later_hbm, refs = refs[4 : 4 + later], refs[4 + later :]
    early_out, late_out, send_0, send_1, send_2, send_3 = refs[0:6]
    packed_ref, coef_ref, derive_ref, stiffness_ref, early_rows = refs[6:11]
    later_out, refs = refs[11 : 11 + later], refs[11 + later :]
    work_ref, late_rows, early_squeezed, late_squeezed, solution_ref, block_ref, star_ref, send_ref, sems = refs

    sources = (star_hbm, stiffness_hbm, solution_hbm, send_hbm, *later_hbm)
    targets = (star_ref, stiffness_ref, solution_ref, send_ref, *later_out)
    copies = [
        pltpu.make_async_copy(source, target, sems.at[number])
        for number, (source, target) in enumerate(zip(sources, targets))
    ]
    for copy in copies:
        copy.start()
    fields, kinds = star_ref.shape[0], star_ref.shape[2]
    pairs = (fields + 1) // 2
    for cleared in (packed_ref, block_ref):
        cleared[...] = jnp.zeros(cleared.shape, F32)
    for copy in copies[0:3]:
        copy.wait()
    derive_ref[...] = stack_right(stiffness_blocks(stiffness_ref, block_ref, True))
    star_coefficients(star_ref, work_ref, coef_ref)
    pack(solution_ref, packed_ref)
    start = packed_ref[...].reshape(fields * ROWS, LANES)

    def step(degree, carry):
        current, early, late = carry
        current = star_mix(product(stack_left(current), derive_ref[...]), coef_ref, fields, kinds)
        early = early + weight_at(0.0, 0.5, degree) * current
        late = late + weight_at(0.5, 1.0, degree) * current
        return current, early, late

    _, early, late = lax.fori_loop(
        1, DERIVS, step, (start, taylor_weight(0.0, 0.5, 0) * start, taylor_weight(0.5, 1.0, 0) * start),
        unroll=True,
    )
    early_out[...] = early.reshape(fields, ROWS, LANES)
    late_out[...] = late.reshape(fields, ROWS, LANES)
    rows_by_pair(early, early_rows, fields)
    rows_by_pair(late, late_rows, fields)
    modes = solution_ref.shape[2]
    squeeze(early_rows, early_squeezed, modes)
    squeeze(late_rows, late_squeezed, modes)
    copies[3].wait()
    sends = send_ref.shape[2]
    fast = sends // 2
    for side, out in enumerate((send_0, send_1, send_2, send_3)):
        for place in range(sends):
            element = send_ref[0, message_side(side), place]
            for pair in range(pairs - 1):
                row = pair * sends + place
                out[row : row + 1, :] = early_squeezed[pair, pl.ds(element, 1), :]
            if place >= fast:
                for pair in range(pairs - 1):
                    row = (pairs - 1) * sends + pair * fast + place - fast
                    out[row : row + 1, :] = late_squeezed[pair, pl.ds(element, 1), :]
    for copy in copies[4:]:
        copy.wait()


def rows_by_pair(packed, out_ref, fields):
    lower = lower_half((ROWS, LANES))
    for pair in range((fields + 1) // 2):
        even = packed[2 * pair * ROWS : (2 * pair + 1) * ROWS]
        odd = jnp.zeros_like(even)
        if 2 * pair + 1 < fields:
            odd = packed[(2 * pair + 1) * ROWS : (2 * pair + 2) * ROWS]
        out_ref[pair, 0:ROWS, :] = jnp.where(lower, even, swap_halves(odd))
        out_ref[pair, ROWS : 2 * ROWS, :] = jnp.where(lower, swap_halves(even), odd)


def last_pieces(pairs, modes):
    gap = HALF - modes
    pieces = []
    for pair in range(pairs - 1):
        for half in range(2):
            first = half * HALF + modes
            pieces.append((pair, first, first - (2 * pair + half) * gap))
    assert len(pieces) * gap >= modes
    return pieces


def squeeze(rows_ref, out_ref, modes):
    pairs = rows_ref.shape[0]
    lanes = lane_index(rows_ref.shape[1:])
    for pair in range(pairs - 1):
        out_ref[pair] = rows_ref[pair]
    for pair, first, shift in last_pieces(pairs, modes):
        here = (lanes >= first) & (lanes < first + HALF - modes)
        out_ref[pair] = jnp.where(here, pltpu.roll(rows_ref[pairs - 1], shift, 1), out_ref[pair])


def unsqueeze(rows, modes):
    lanes = lane_index(rows[0].shape)
    last = None
    for pair, first, shift in last_pieces(len(rows) + 1, modes):
        here = (lanes >= first) & (lanes < first + HALF - modes)
        piece = pltpu.roll(jnp.where(here, rows[pair], 0.0), LANES - shift, 1)
        last = piece if last is None else last + piece
    return last


def flux_local_coefficients(flux_ref, stage_ref, out_ref):
    fields, faces, elements = flux_ref.shape[0], flux_ref.shape[2], flux_ref.shape[3]
    rows = 2 * ROWS
    filled = lane_index((rows, LANES)) < elements
    lanes, sublanes = lane_index((ROWS, LANES)), row_index((ROWS, LANES))
    picks = [one_where(lanes % elements == half * ROWS + sublanes) for half in range(2)]
    square = (LANES, LANES)
    right = one_where(row_index(square) // (2 * elements) == lane_index(square) % faces).astype(BF16)
    for row in range(fields):
        values = None
        for face in range(faces):
            stage_ref[row, face * rows : face * rows + fields, 0:elements] = flux_ref[row, :, face, :]
            part = jnp.where(filled, stage_ref[row, face * rows : (face + 1) * rows, :], 0.0)
            values = part if values is None else values + pltpu.roll(part, face * 2 * elements, 1)
        stage_ref[row, 0:rows, :] = high_and_low(values, elements)
        left = [stage_ref[row, col : col + 1, :] * pick for col in range(fields) for pick in picks]
        spread = product(jnp.concatenate(left, axis=0).astype(BF16), right)
        out_ref[row * fields : (row + 1) * fields] = spread.reshape(fields, 2, ROWS, LANES)


def flux_remote_coefficients(flux_ref, stage_ref, out_ref):
    fields, faces, elements = flux_ref.shape[0], flux_ref.shape[2], flux_ref.shape[3]
    pairs = (fields + 1) // 2
    rows = stage_ref.shape[1] // 2
    filled = lane_index((rows, LANES)) < elements
    lanes, sublanes = lane_index((elements, LANES)), row_index((elements, LANES))
    pick = one_where((lanes % elements == sublanes) & (lanes < 4 * elements))
    square = (LANES, LANES)
    from_lane = row_index(square)
    same_parity = (from_lane // elements) % 2 == lane_index(square) // HALF
    right = one_where(same_parity & (from_lane < 4 * elements)).astype(BF16)
    for pair in range(pairs):
        values = None
        for row in range(2 * pair, min(2 * pair + 2, fields)):
            start = (row % 2) * rows
            for col in range(fields):
                at = start + col * faces
                stage_ref[pair, at : at + faces, 0:elements] = flux_ref[row, col]
            part = jnp.where(filled, stage_ref[pair, start : start + rows, :], 0.0)
            values = part if values is None else values + pltpu.roll(part, elements, 1)
        stage_ref[pair, 0:rows, :] = high_and_low(values, 2 * elements)
        for face in range(faces):
            left = []
            for col in range(fields):
                at = col * faces + face
                left.append(stage_ref[pair, at : at + 1, :] * pick)
            spread = product(jnp.concatenate(left, axis=0).astype(BF16), right)
            at = (face * pairs + pair) * fields
            out_ref[at : at + fields] = spread.reshape(fields, elements, LANES)


def local_terms(packed, star_ref, flux_ref, volume_ref, trace_ref, lift_ref, fields, kinds):
    left = stack_left(packed)
    volume = star_mix(product(left, volume_ref[...]), star_ref, fields, kinds)
    traces = product(left, trace_ref[...])
    sums = []
    for col in range(fields):
        halves = []
        for half in range(2):
            total = None
            for row in range(fields):
                part = traces[row * ROWS : (row + 1) * ROWS, half * LANES : (half + 1) * LANES]
                term = flux_ref[row * fields + col, half] * part
                total = term if total is None else total + term
            halves.append(total)
        sums.append(jnp.concatenate(halves, axis=1))
    return volume + product(stack_left(jnp.concatenate(sums, axis=0)), lift_ref[...])


def combo_code(lanes, turns, face_modes):
    in_face = lanes % HALF
    code = jnp.where(in_face < turns * face_modes, (lanes // HALF) * turns + in_face // face_modes, -1)
    return code.astype(F32)


def ghost_terms(
    flux_ref, stage_ref, code_ref, composed, lift_sides, lane_code, flux_out, operator_out, scatter_out, sends, fields
):
    faces, elements = flux_ref.shape[2], flux_ref.shape[3]
    rows = 2 * ROWS
    shape = (rows, LANES)
    lanes = lane_index(shape)

    def along_lanes(start):
        row = code_ref[start : start + 1, :]
        for face in range(1, faces):
            row = row + pltpu.roll(code_ref[start + face : start + face + 1, :], face * elements, 1)
        return row + swap_halves(row)

    slots, codes = along_lanes(0), along_lanes(faces)
    ghosts = elements + row_index(shape)
    found = one_where(jnp.broadcast_to(slots, shape) == ghosts.astype(F32))
    first = jnp.where(lanes < HALF, found, 0.0)
    code = jnp.sum(first * codes, axis=1, keepdims=True)
    face_of = jnp.sum(first * (lanes // elements).astype(F32), axis=1, keepdims=True)
    element_of = jnp.sum(first * (lanes % elements).astype(F32), axis=1, keepdims=True)
    numbers = [slot * sends + place for slot in range(4) for place in range(sends // 2)]

    filled = lanes < elements
    values = []
    for field in range(fields):
        total = None
        for face in range(faces):
            stage_ref[field, face * rows : face * rows + fields, 0:elements] = flux_ref[field, :, face, :]
            part = jnp.where(filled, stage_ref[field, face * rows : (face + 1) * rows, :], 0.0)
            total = part if total is None else total + pltpu.roll(part, face * elements, 1)
        total = jnp.where(row_index(shape) < fields, total, 0.0)
        values.append(high_and_low(total, HALF))
    picked = jnp.concatenate([jnp.broadcast_to(found[number : number + 1], (HALF, LANES)) for number in numbers], axis=0)
    flux_out[...] = lax.dot_general(
        jnp.concatenate(values, axis=0).astype(BF16), picked.astype(BF16), (((1,), (1,)), ((), ())),
        preferred_element_type=F32,
    )

    left = []
    for number in numbers:
        chosen = composed * one_where(lane_code == code[number : number + 1])
        both = chosen[:, 0:LANES] + chosen[:, LANES : 2 * LANES]
        high, low = split(both + swap_halves(both))
        left.append(jnp.concatenate([jnp.where(lower_half(high.shape), high, low), high], axis=1))
    high, low = split(lift_sides)
    lifts = product(jnp.concatenate(left, axis=0), jnp.concatenate([high, high, low, jnp.zeros_like(low)], axis=0))
    side_lane = (lane_index((1, faces * HALF)) // HALF).astype(F32)
    place_of = jnp.zeros((1, LANES), F32)
    columns = []
    for at, number in enumerate(numbers):
        chosen = lifts[at * HALF : (at + 1) * HALF] * one_where(side_lane == face_of[number : number + 1])
        both = chosen[:, 0:LANES] + chosen[:, LANES : 2 * LANES]
        high, low = split(both + swap_halves(both))
        none = jnp.zeros_like(low)
        order = [high, none, high, none, low, none] if at % 2 == 0 else [none, high, none, high, none, low]
        columns.append(jnp.concatenate(order, axis=0))
        if at % 2 == 1:
            operator_out[at // 2] = jnp.concatenate(columns[-2:], axis=1)
        place_of = jnp.where(lane_index((1, LANES)) // rows == at, element_of[number : number + 1], place_of)
    square = (fields * elements, LANES)
    here = (row_index(square) // elements == lane_index(square) % rows) & (
        (row_index(square) % elements).astype(F32) == place_of
    )
    one = one_where(here).astype(BF16)
    scatter_out[...] = jnp.concatenate([one, one], axis=1)


def prepare_kernel(
    packed_ref, early_ref, stiffness_ref, star_ref, flux_local_ref, flux_remote_ref, restrict_ref, lift_ref, orient_ref,
    slot_ref, face_ref, turn_ref, rate_ref,
    base_out, local_out, remote_out, volume_out, trace_out, local_lift_out, compose_out,
    remote_lift_out, choose_out, mask_out, code_ref, composed_out, sides_ref, fast_out,
    local_work_ref, remote_work_ref, block_ref, wide_ref, face_work_ref, orient_work_ref, code_work_ref,
):
    fields, kinds = packed_ref.shape[0], stiffness_ref.shape[0]
    face_modes, faces, modes = restrict_ref.shape
    turns = orient_ref.shape[0]
    flux_local_coefficients(flux_local_ref, local_work_ref, local_out)
    flux_remote_coefficients(flux_remote_ref, remote_work_ref, remote_out)

    block_ref[...] = jnp.zeros(block_ref.shape, F32)
    volume_out[...] = stack_right(stiffness_blocks(stiffness_ref, block_ref, False))

    wide_ref[...] = jnp.zeros(wide_ref.shape, F32)
    for mode in range(face_modes):
        at = mode * faces
        wide_ref[at : at + faces, 0:modes] = restrict_ref[mode]
        wide_ref[LANES + at : LANES + at + faces, HALF : HALF + modes] = restrict_ref[mode]
    trace_out[...] = stack_right(wide_ref[...].T)
    for mode in range(face_modes):
        at = mode * faces
        wide_ref[at : at + faces, 0:modes] = -lift_ref[mode]
        wide_ref[LANES + at : LANES + at + faces, HALF : HALF + modes] = -lift_ref[mode]
    local_lift_out[...] = stack_right(wide_ref[...])

    face_work_ref[...] = jnp.zeros(face_work_ref.shape, F32)
    orient_work_ref[...] = jnp.zeros(orient_work_ref.shape, F32)
    for turn in range(turns):
        orient_work_ref[turn * face_modes : (turn + 1) * face_modes, 0:face_modes] = orient_ref[turn]
    for face in range(faces):
        face_work_ref[0:face_modes, face * LANES : face * LANES + modes] = restrict_ref[:, face, :]
        face_work_ref[0:face_modes, face * LANES + HALF : face * LANES + HALF + modes] = restrict_ref[:, face, :]
    composed = jnp.dot(
        orient_work_ref[...], face_work_ref[...], precision=lax.Precision.HIGHEST, preferred_element_type=F32
    )
    stacked = jnp.concatenate([composed[:, face * LANES : (face + 1) * LANES] for face in range(faces)], axis=0)
    high, low = split(stacked.T[0:HALF])
    compose_out[...] = jnp.concatenate([high, high, low, jnp.zeros_like(low)], axis=0)
    wide_ref[...] = jnp.zeros(wide_ref.shape, F32)
    for face in range(faces):
        for turn in range(turns):
            rows = slice(face * HALF + turn * face_modes, face * HALF + (turn + 1) * face_modes)
            wide_ref[rows, 0:modes] = -lift_ref[:, face, :]
            wide_ref[rows, HALF : HALF + modes] = -lift_ref[:, face, :]
    remote_lift_out[...] = stack_right(wide_ref[...])

    elements = slot_ref.shape[1]
    code_work_ref[...] = jnp.zeros(code_work_ref.shape, F32)
    slots = slot_ref[...]
    sends = (choose_out.shape[1] // 2 - elements) // 4
    group = (slots - elements) // sends
    moved = slots
    for side in range(4):
        moved = jnp.where(group == side, slots + (ghost_slot(side) - side) * sends, moved)
    code_work_ref[0:faces, 0:elements] = jnp.where(slots < elements, slots, moved).astype(F32)
    code_work_ref[faces : 2 * faces, 0:elements] = (face_ref[...] * turns + turn_ref[...]).astype(F32)
    code_work_ref[2 * faces : 2 * faces + 1, 0:elements] = rate_ref[...].astype(F32)
    code_ref[...] = code_work_ref[0 : 2 * faces, :]
    codes = code_work_ref[...].T[0:elements, :]
    rates = codes[:, 2 * faces : 2 * faces + 1]
    fast_out[...] = jnp.where(lower_half((ROWS, LANES)), rates[0:ROWS], rates[ROWS : 2 * ROWS])
    sources = choose_out.shape[1] // 2
    source_lane = (lane_index((elements, 2 * sources)) % sources).astype(F32)
    lanes = lane_index((elements, mask_out.shape[1]))
    lane_code = combo_code(lanes, turns, face_modes)
    picks, masks = [], []
    for face in range(faces):
        picks.append(jnp.where(codes[:, face : face + 1] == source_lane, 1.0, 0.0))
        masks.append(jnp.where(codes[:, faces + face : faces + face + 1] == lane_code, 1.0, 0.0))
    choose_out[...] = jnp.concatenate(picks, axis=0).astype(BF16)
    mask_out[...] = jnp.concatenate(masks, axis=0)

    sides_ref[...] = jnp.zeros(sides_ref.shape, F32)
    for face in range(faces):
        for turn in range(turns):
            rows = slice(turn * face_modes, (turn + 1) * face_modes)
            sides_ref[rows, face * HALF : face * HALF + modes] = -lift_ref[:, face, :]
    composed_out[...] = stacked.T[0:HALF]

    early = early_ref[...].reshape(fields * ROWS, LANES)
    terms = local_terms(early, star_ref, local_out, volume_out, trace_out, local_lift_out, fields, kinds)
    base_out[...] = packed_ref[...] + terms.reshape(fields, ROWS, LANES)


def remote_terms(rows, remote_ref, compose_ref, lift_ref, choose_ref, mask_ref, fields):
    pairs = len(rows)
    faces = lift_ref.shape[0] // (3 * HALF)
    elements = choose_ref.shape[0] // faces
    sources = jnp.concatenate(rows, axis=1)
    gathered = product(choose_ref[...], jnp.concatenate(split(sources), axis=0))
    folded = []
    for face in range(faces):
        sums = []
        for col in range(fields):
            total = None
            for pair in range(pairs):
                part = gathered[face * elements : (face + 1) * elements, pair * LANES : (pair + 1) * LANES]
                term = remote_ref[(face * pairs + pair) * fields + col] * part
                total = term if total is None else total + term
            sums.append(total)
        mixed = jnp.concatenate(sums, axis=0)
        high, low = split(mixed + swap_halves(mixed))
        first = jnp.where(lower_half(high.shape), high, low)
        turned = product(jnp.concatenate([first, high], axis=1), compose_ref[...])
        mask = mask_ref[face * elements : (face + 1) * elements, :]
        chosen = (turned.reshape(fields, elements, turned.shape[1]) * mask[None]).reshape(turned.shape)
        both = chosen[:, 0:LANES] + chosen[:, LANES : 2 * LANES]
        folded.append(both + swap_halves(both))
    lower = lower_half(folded[0].shape)
    left = [jnp.where(lower, folded[face], folded[face + 1]) for face in range(0, faces, 2)]
    result = product(stack_left(jnp.concatenate(left, axis=1)), lift_ref[...])
    result = result.reshape(fields, 2, ROWS, LANES)
    return jnp.where(lower_half((ROWS, LANES))[None], result[:, 0], result[:, 1])


def middle_kernel(
    modes, base_ref, early_rows, late_ref, star_ref, remote_ref, derive_ref, compose_ref, lift_ref, choose_ref, mask_ref,
    fast_ref, send_hbm, from_0, from_1, from_2, from_3,
    middle_out, late_out, send_0, send_1, send_2, send_3,
    rows_ref, late_rows, send_ref, sem,
):
    copy = pltpu.make_async_copy(send_hbm, send_ref, sem)
    copy.start()
    fields = base_ref.shape[0]
    kinds = star_ref.shape[0] // (fields * fields)
    pairs = early_rows.shape[0]
    sends = send_ref.shape[2]
    fast = sends // 2
    for side, arrived in enumerate((from_0, from_1, from_2, from_3)):
        for pair in range(pairs - 1):
            rows_ref[pair, side * sends : (side + 1) * sends, :] = arrived[pair * sends : (pair + 1) * sends, :]
    ghosts = [rows_ref[pair] for pair in range(pairs - 1)]
    ghosts.append(unsqueeze(ghosts, modes))
    rows = [jnp.concatenate([early_rows[pair], ghosts[pair]], axis=0) for pair in range(pairs)]
    middle = base_ref[...] + remote_terms(rows, remote_ref, compose_ref, lift_ref, choose_ref, mask_ref, fields)
    middle_out[...] = middle
    start = middle.reshape(fields * ROWS, LANES)

    def step(degree, carry):
        current, early = carry
        current = star_mix(product(stack_left(current), derive_ref[...]), star_ref, fields, kinds)
        return current, early + weight_at(0.0, 0.5, degree) * current

    _, restart = lax.fori_loop(1, DERIVS, step, (start, taylor_weight(0.0, 0.5, 0) * start))
    copy.wait()
    is_fast = fast_ref[...]
    late = jnp.where((is_fast == 2)[None], restart.reshape(fields, ROWS, LANES), late_ref[...])
    late_out[...] = late
    both = late.reshape(fields * ROWS, LANES)
    swapped = swap_halves(both)
    wide = lower_half(both.shape)
    late_rows[:, 0:ROWS, :] = jnp.where(wide, both, swapped).reshape(late.shape)
    late_rows[:, ROWS : 2 * ROWS, :] = jnp.where(wide, swapped, both).reshape(late.shape)
    first_half = lower_half((1, LANES))
    for slot, out in enumerate((send_0, send_1, send_2, send_3)):
        out[...] = jnp.zeros(out.shape, F32)
        side = message_side(slot)
        places = [send_ref[0, side, place] for place in range(fast)]
        for field in range(fields):
            halves = [late_rows[field, pl.ds(element, 1), :] for element in places]
            out[field : field + 1, :] = jnp.where(first_half, *halves)


def local_kernel(
    modes, middle_ref, late_ref, star_ref, flux_ref, volume_ref, trace_ref, lift_ref,
    remote_ref, compose_ref, remote_lift_ref, choose_ref, mask_ref, flux_remote_ref, code_ref, composed_ref, sides_ref,
    orient_ref, first_0, first_1, first_2, first_3,
    base_out, ghost_flux_out, ghost_operator_out, scatter_out, rows_ref, stage_ref,
):
    fields = middle_ref.shape[0]
    kinds = star_ref.shape[0] // (fields * fields)
    pairs = rows_ref.shape[0]
    elements = 2 * ROWS
    sends = (rows_ref.shape[1] - elements) // 4
    fast = sends // 2
    late = late_ref[...].reshape(fields * ROWS, LANES)
    rows_by_pair(late, rows_ref, fields)
    for slot, first in enumerate((first_0, first_1, first_2, first_3)):
        at = elements + slot * sends
        for pair in range(pairs - 1):
            rows_ref[pair, at : at + fast, :] = jnp.zeros((fast, LANES), F32)
            row = (pairs - 1) * sends + pair * fast
            rows_ref[pair, at + fast : at + sends, :] = first[row : row + fast, :]
    ghosts = [rows_ref[pair, elements:, :] for pair in range(pairs - 1)]
    rows_ref[pairs - 1, elements:, :] = unsqueeze(ghosts, modes)
    terms = local_terms(late, star_ref, flux_ref, volume_ref, trace_ref, lift_ref, fields, kinds)
    rows = [rows_ref[pair] for pair in range(pairs)]
    remote = remote_terms(rows, remote_ref, compose_ref, remote_lift_ref, choose_ref, mask_ref, fields)
    base = middle_ref[...] + terms.reshape(fields, ROWS, LANES) + remote
    base_out[:, 0:ROWS, :] = base
    base_out[:, ROWS : 2 * ROWS, :] = swap_halves(base.reshape(fields * ROWS, LANES)).reshape(base.shape)
    lane_code = combo_code(lane_index((1, composed_ref.shape[1])), orient_ref.shape[0], orient_ref.shape[1])
    ghost_terms(
        flux_remote_ref, stage_ref, code_ref, composed_ref[...], sides_ref[...], lane_code,
        ghost_flux_out, ghost_operator_out, scatter_out, sends, fields,
    )


def final_kernel(
    base_ref, ghost_flux_ref, ghost_operator_ref, scatter_ref, second_0, second_1, second_2, second_3, result_out,
):
    fields = base_ref.shape[0]
    modes = result_out.shape[2]
    rows = second_0.shape[0]
    added = []
    for slot, second in enumerate((second_0, second_1, second_2, second_3)):
        sums = [None] * 3
        for field in range(fields):
            coefficient = ghost_flux_ref[field * rows : (field + 1) * rows, slot * LANES : (slot + 1) * LANES]
            term = coefficient * second[field : field + 1, :]
            sums[field % 3] = term if sums[field % 3] is None else sums[field % 3] + term
        both = product(stack_left(sums[0] + sums[1] + sums[2]), ghost_operator_ref[slot])
        added += [both[:, 0:LANES], both[:, LANES : 2 * LANES]]
    right = jnp.concatenate(split(jnp.concatenate(added, axis=0)), axis=0)
    result = base_ref[...] + product(scatter_ref[...], right).reshape(base_ref.shape)
    result_out[...] = result[:, :, 0:modes]


VMEM = pl.BlockSpec(memory_space=pltpu.VMEM)
HBM = pl.BlockSpec(memory_space=pltpu.HBM)


def call(kernel, ins, outs, scratch, args, name, flops):
    shapes = [jax.ShapeDtypeStruct(shape, dtype) for shape, dtype in outs]
    args = [
        pltpu.with_memory_space_constraint(arg, pltpu.HBM) if spec is HBM else arg for spec, arg in zip(ins, args)
    ]
    return pl.pallas_call(
        kernel,
        out_shape=shapes,
        in_specs=ins,
        out_specs=[VMEM] * len(outs),
        scratch_shapes=[pltpu.VMEM(*one) if isinstance(one, tuple) else one for one in scratch],
        compiler_params=pltpu.CompilerParams(vmem_limit_bytes=16 * 1024 * 1024),
        cost_estimate=pl.CostEstimate(flops=flops, bytes_accessed=4_000_000, transcendentals=0),
        name=name,
    )(*args)


def exchange(outgoing):
    arrived = []
    for (axis, far), message in zip(SWAPS, outgoing):
        size = lax.axis_size(axis)
        assert size % 2 == 0
        pairs = []
        for first in range(1 if far else 0, size, 2):
            second = (first + 1) % size
            pairs += [(first, second), (second, first)]
        arrived.append(lax.ppermute(message, axis, pairs))
    return arrived


def up_to(count, multiple):
    return -(-count // multiple) * multiple


def local(
    solution, stiffness, star_matrices, face_restrict, face_lift, orient_maps, flux_local, flux_remote,
    cluster_rate, send_list, neighbour_slot, neighbour_face, neighbour_turn,
):
    modes, fields, elements = solution.shape
    kinds = stiffness.shape[0]
    faces = face_restrict.shape[0]
    sides, sends = send_list.shape[1], send_list.shape[2]
    fast = sends // 2
    pairs = (fields + 1) // 2
    assert elements == 2 * ROWS and modes <= HALF and fast == 2 and fields % 2 == 1
    values = jnp.transpose(solution, (1, 2, 0))
    star = jnp.transpose(star_matrices, (1, 2, 0, 3))
    local_part = jnp.transpose(flux_local, (1, 2, 0, 3))
    remote_part = jnp.transpose(flux_remote, (1, 2, 0, 3))
    restrict = jnp.transpose(face_restrict, (1, 0, 2))
    lift = jnp.transpose(face_lift, (2, 0, 1))

    packed = (fields, ROWS, LANES)
    first_shape = (up_to((pairs - 1) * (sends + fast), ROWS), LANES)
    second_shape = (up_to(fields, 2 * ROWS), LANES)
    star_shape = (fields * fields * kinds, ROWS, LANES)
    combos = faces * HALF
    sources = elements + sides * sends

    waiting = (
        local_part, remote_part, restrict, lift, orient_maps, neighbour_slot, neighbour_face, neighbour_turn,
        cluster_rate.reshape(1, elements),
    )
    made = call(
        predict_kernel,
        [HBM] * (4 + len(LATER)),
        [(packed, F32)] * 2 + [(first_shape, F32)] * sides + [
            (packed, F32), (star_shape, F32), ((3 * LANES, kinds * LANES), BF16), (stiffness.shape, F32),
            ((pairs, elements, LANES), F32),
        ] + [(array.shape, array.dtype) for array in waiting],
        [
            ((fields, up_to(4 * fields, ROWS), LANES), F32),
            ((pairs, elements, LANES), F32),
            ((pairs - 1, elements, LANES), F32), ((pairs - 1, elements, LANES), F32),
            (values.shape, F32), ((kinds, LANES, LANES), F32), (star.shape, F32),
            pltpu.SMEM(send_list.shape, jnp.int32), pltpu.SemaphoreType.DMA((4 + len(LATER),)),
        ],
        (values, stiffness, star, send_list, *waiting),
        "predict", 100_000_000,
    )
    early, late, outgoing = made[0], made[1], made[2 : 2 + sides]
    start, star_coef, derive_op, stiffness_kept, early_rows = made[2 + sides : 7 + sides]
    waiting = made[7 + sides :]
    first = exchange(outgoing)
    (
        base, local_coef, remote_coef, volume_op, trace_op, local_lift, compose_op, remote_lift, choose, mask,
        codes, composed, lift_sides, fast_mask,
    ) = call(
        prepare_kernel,
        [VMEM] * 13,
        [
            (packed, F32), ((fields * fields, 2, ROWS, LANES), F32),
            ((faces * pairs * fields, elements, LANES), F32),
            ((3 * LANES, kinds * LANES), BF16), ((3 * LANES, 2 * LANES), BF16),
            ((6 * LANES, LANES), BF16), ((2 * LANES, combos), BF16), ((3 * faces * HALF, LANES), BF16),
            ((faces * elements, 2 * sources), BF16), ((faces * elements, combos), F32),
            ((2 * faces, LANES), F32), ((HALF, combos), F32), ((HALF, faces * HALF), F32),
            ((ROWS, LANES), F32),
        ],
        [
            ((fields, 2 * ROWS * faces, LANES), F32), ((pairs, 2 * up_to(4 * fields, ROWS), LANES), F32),
            ((kinds, LANES, LANES), F32), ((2 * LANES, LANES), F32),
            ((LANES, faces * LANES), F32), ((HALF, LANES), F32), ((LANES, LANES), F32),
        ],
        (start, early, stiffness_kept, star_coef, *waiting),
        "prepare", 200_000_000,
    )
    middle, late_value, *outgoing = call(
        functools.partial(middle_kernel, modes),
        [VMEM] * 11 + [HBM] + [VMEM] * 4,
        [(packed, F32)] * 2 + [(second_shape, F32)] * sides,
        [
            ((pairs, sides * sends, LANES), F32), ((fields, elements, LANES), F32),
            pltpu.SMEM(send_list.shape, jnp.int32), pltpu.SemaphoreType.DMA,
        ],
        (
            base, early_rows, late, star_coef, remote_coef, derive_op, compose_op, remote_lift, choose, mask,
            fast_mask, send_list, *first,
        ),
        "middle", 200_000_000,
    )
    second = exchange(outgoing)
    base, ghost_flux, ghost_op, scatter = call(
        functools.partial(local_kernel, modes),
        [VMEM] * (17 + len(first)),
        [
            ((fields, elements, LANES), F32), ((fields * second_shape[0], sides * LANES), F32),
            ((sides, 3 * LANES, 2 * LANES), BF16), ((fields * elements, 2 * LANES), BF16),
        ],
        [((pairs, sources, LANES), F32), ((fields, 2 * ROWS * faces, LANES), F32)],
        (
            middle, late_value, star_coef, local_coef, volume_op, trace_op, local_lift,
            remote_coef, compose_op, remote_lift, choose, mask, waiting[1], codes, composed, lift_sides, waiting[4],
            *first,
        ),
        "local_late", 200_000_000,
    )
    (result,) = call(
        final_kernel,
        [VMEM] * 8,
        [(values.shape, F32)],
        [],
        (base, ghost_flux, ghost_op, scatter, *second),
        "final", 200_000_000,
    )
    return jnp.transpose(result, (2, 0, 1))


def solution(mesh):
    placed = (
        P(None, None, ("dom", "sub")),
        P(),
        P(None, None, None, ("dom", "sub")),
        P(),
        P(),
        P(),
        P(None, None, None, ("dom", "sub")),
        P(None, None, None, ("dom", "sub")),
        P(("dom", "sub")),
        P(("dom", "sub"), None, None),
        P(None, ("dom", "sub")),
        P(None, ("dom", "sub")),
        P(None, ("dom", "sub")),
    )
    return jax.shard_map(
        local, mesh=mesh, in_specs=placed, out_specs=P(None, None, ("dom", "sub")), check_vma=False
    )
```

```python
import math

import jax
import jax.numpy as jnp
from jax import lax
from jax.experimental import pallas as pl
from jax.experimental.pallas import tpu as pltpu
from jax.sharding import PartitionSpec as P

DERIVS = 6
LANES = 128
HALF = 64
ROWS = 8
F32 = jnp.float32
BF16 = jnp.bfloat16
LATER = ("flux_local", "flux_remote", "face_restrict", "face_lift", "orient_maps", "slot", "face", "turn", "rate")
AXES = ("dom", "sub")
SWAPS = (("dom", True), ("dom", False), ("sub", True), ("sub", False))


def taylor_weight(lower, upper, degree):
    return (upper ** (degree + 1) - lower ** (degree + 1)) / math.factorial(degree + 1)


def weight_at(lower, upper, degree):
    result = jnp.float32(taylor_weight(lower, upper, 1))
    for option in range(2, DERIVS):
        result = jnp.where(degree == option, jnp.float32(taylor_weight(lower, upper, option)), result)
    return result


def split(values):
    high = values.astype(BF16)
    low = (values - high.astype(F32)).astype(BF16)
    return high, low


def stack_left(values):
    high, low = split(values)
    return jnp.concatenate([high, low, high], axis=1)


def stack_right(values):
    high, low = split(values)
    return jnp.concatenate([high, high, low], axis=0)


def product(left, right):
    return jnp.dot(left, right, preferred_element_type=F32)


def odd_place(axis):
    return lax.rem(lax.axis_index(axis), 2)


def message_side(slot):
    axis, far = SWAPS[slot]
    odd = odd_place(axis)
    return 2 * AXES.index(axis) + (odd if far else 1 - odd)


def ghost_slot(side):
    axis = AXES[side // 2]
    even_far = side % 2 == 0
    return jnp.where(odd_place(axis) == 0, SWAPS.index((axis, even_far)), SWAPS.index((axis, not even_far)))


def lane_index(shape):
    return lax.broadcasted_iota(jnp.int32, shape, len(shape) - 1)


def lower_half(shape):
    return lane_index(shape) < HALF


def swap_halves(values):
    return pltpu.roll(values, HALF, values.ndim - 1)


def pack(values_ref, packed_ref):
    modes = values_ref.shape[2]
    packed_ref[:, :, 0:modes] = values_ref[:, 0:ROWS, :]
    packed_ref[:, :, HALF : HALF + modes] = values_ref[:, ROWS : 2 * ROWS, :]


def high_and_low(values, shift):
    high = values.astype(BF16).astype(F32)
    return high + pltpu.roll(values - high, shift, 1)


def row_index(shape):
    return lax.broadcasted_iota(jnp.int32, shape, len(shape) - 2)


def one_where(condition):
    return jnp.where(condition, 1.0, 0.0)


def star_coefficients(star_ref, stage_ref, star_out):
    fields, kinds, elements = star_ref.shape[0], star_ref.shape[2], star_ref.shape[3]
    lanes = lane_index((ROWS, LANES))
    pick = one_where((lanes % ROWS == row_index((ROWS, LANES))) & (lanes < 2 * elements))
    from_lane = row_index((LANES, LANES))
    same_half = (from_lane % elements) // ROWS == lane_index((LANES, LANES)) // HALF
    right = one_where(same_half & (from_lane < 2 * elements)).astype(BF16)
    filled = lane_index(stage_ref.shape[1:]) < elements
    for row in range(fields):
        for col in range(fields):
            stage_ref[row, col * 4 : col * 4 + kinds, 0:elements] = star_ref[row, col]
        values = jnp.where(filled, stage_ref[row], 0.0)
        stage_ref[row] = high_and_low(values, elements)
        spreads = []
        for kind in range(kinds):
            for col in range(fields):
                at = col * 4 + kind
                spreads.append(stage_ref[row, at : at + 1, :] * pick)
        spread_out = product(jnp.concatenate(spreads, axis=0).astype(BF16), right)
        count = kinds * fields
        star_out[row * count : (row + 1) * count] = spread_out.reshape(count, ROWS, LANES)


def star_mix(columns, star_ref, fields, kinds):
    sums = []
    for col in range(fields):
        parts = []
        for kind in range(kinds):
            total = None
            for row in range(fields):
                part = columns[row * ROWS : (row + 1) * ROWS, kind * LANES : (kind + 1) * LANES]
                term = star_ref[(row * kinds + kind) * fields + col] * part
                total = term if total is None else total + term
            parts.append(total)
        sums.append(sum(parts[1:], parts[0]))
    return jnp.concatenate(sums, axis=0)


def stiffness_blocks(stiffness_ref, block_ref, turned):
    kinds, modes = stiffness_ref.shape[0], stiffness_ref.shape[1]
    for kind in range(kinds):
        matrix = -stiffness_ref[kind].T if turned else stiffness_ref[kind]
        block_ref[kind, 0:modes, 0:modes] = matrix
        block_ref[kind, HALF : HALF + modes, HALF : HALF + modes] = matrix
    return jnp.concatenate([block_ref[kind] for kind in range(kinds)], axis=1)


def predict_kernel(*refs):
    later = len(LATER)
    solution_hbm, stiffness_hbm, star_hbm, send_hbm = refs[0:4]
    later_hbm, refs = refs[4 : 4 + later], refs[4 + later :]
    early_out, late_out, send_0, send_1, send_2, send_3 = refs[0:6]
    packed_ref, coef_ref, derive_ref, stiffness_ref, early_rows = refs[6:11]
    later_out, refs = refs[11 : 11 + later], refs[11 + later :]
    work_ref, late_rows, solution_ref, block_ref, star_ref, send_ref, sems = refs

    pieces = []
    for source, target in ((star_hbm, star_ref), (stiffness_hbm, stiffness_ref), (solution_hbm, solution_ref)):
        step = source.shape[0] // 3
        pieces += [(source.at[pl.ds(at, step)], target.at[pl.ds(at, step)]) for at in range(0, source.shape[0], step)]
    first = len(pieces)
    pieces += zip((send_hbm, *later_hbm), (send_ref, *later_out))
    copies = [
        pltpu.make_async_copy(source, target, sems.at[number]) for number, (source, target) in enumerate(pieces)
    ]
    for copy in copies:
        copy.start()
    fields, kinds = star_ref.shape[0], star_ref.shape[2]
    pairs = (fields + 1) // 2
    for cleared in (packed_ref, block_ref, send_0, send_1, send_2, send_3):
        cleared[...] = jnp.zeros(cleared.shape, F32)
    for copy in copies[0:first]:
        copy.wait()
    derive_ref[...] = stack_right(stiffness_blocks(stiffness_ref, block_ref, True))
    star_coefficients(star_ref, work_ref, coef_ref)
    pack(solution_ref, packed_ref)
    start = packed_ref[...].reshape(fields * ROWS, LANES)

    def step(degree, carry):
        current, early, late = carry
        current = star_mix(product(stack_left(current), derive_ref[...]), coef_ref, fields, kinds)
        early = early + weight_at(0.0, 0.5, degree) * current
        late = late + weight_at(0.5, 1.0, degree) * current
        return current, early, late

    _, early, late = lax.fori_loop(
        1, DERIVS, step, (start, taylor_weight(0.0, 0.5, 0) * start, taylor_weight(0.5, 1.0, 0) * start),
        unroll=True,
    )
    early_out[...] = early.reshape(fields, ROWS, LANES)
    late_out[...] = late.reshape(fields, ROWS, LANES)
    rows_by_pair(early, early_rows, fields)
    rows_by_pair(late, late_rows, fields)
    copies[first].wait()
    sends = send_ref.shape[2]
    fast = sends // 2
    for side, out in enumerate((send_0, send_1, send_2, send_3)):
        for place in range(sends):
            element = send_ref[0, message_side(side), place]
            for pair in range(pairs):
                row = pair * sends + place
                out[row : row + 1, :] = early_rows[pair, pl.ds(element, 1), :]
            if place >= fast:
                for pair in range(pairs):
                    row = pairs * sends + pair * fast + place - fast
                    out[row : row + 1, :] = late_rows[pair, pl.ds(element, 1), :]
    for copy in copies[first + 1 :]:
        copy.wait()


def rows_by_pair(packed, out_ref, fields):
    lower = lower_half((ROWS, LANES))
    for pair in range((fields + 1) // 2):
        even = packed[2 * pair * ROWS : (2 * pair + 1) * ROWS]
        odd = jnp.zeros_like(even)
        if 2 * pair + 1 < fields:
            odd = packed[(2 * pair + 1) * ROWS : (2 * pair + 2) * ROWS]
        out_ref[pair, 0:ROWS, :] = jnp.where(lower, even, swap_halves(odd))
        out_ref[pair, ROWS : 2 * ROWS, :] = jnp.where(lower, swap_halves(even), odd)


def flux_local_coefficients(flux_ref, stage_ref, out_ref):
    fields, faces, elements = flux_ref.shape[0], flux_ref.shape[2], flux_ref.shape[3]
    rows = 2 * ROWS
    filled = lane_index((rows, LANES)) < elements
    lanes, sublanes = lane_index((ROWS, LANES)), row_index((ROWS, LANES))
    picks = [one_where(lanes % elements == half * ROWS + sublanes) for half in range(2)]
    square = (LANES, LANES)
    right = one_where(row_index(square) // (2 * elements) == lane_index(square) % faces).astype(BF16)
    for row in range(fields):
        values = None
        for face in range(faces):
            stage_ref[row, face * rows : face * rows + fields, 0:elements] = flux_ref[row, :, face, :]
            part = jnp.where(filled, stage_ref[row, face * rows : (face + 1) * rows, :], 0.0)
            values = part if values is None else values + pltpu.roll(part, face * 2 * elements, 1)
        stage_ref[row, 0:rows, :] = high_and_low(values, elements)
        left = [stage_ref[row, col : col + 1, :] * pick for col in range(fields) for pick in picks]
        spread = product(jnp.concatenate(left, axis=0).astype(BF16), right)
        out_ref[row * fields : (row + 1) * fields] = spread.reshape(fields, 2, ROWS, LANES)


def flux_remote_coefficients(flux_ref, stage_ref, out_ref):
    fields, faces, elements = flux_ref.shape[0], flux_ref.shape[2], flux_ref.shape[3]
    pairs = (fields + 1) // 2
    rows = stage_ref.shape[1] // 2
    filled = lane_index((rows, LANES)) < elements
    lanes, sublanes = lane_index((elements, LANES)), row_index((elements, LANES))
    pick = one_where((lanes % elements == sublanes) & (lanes < 4 * elements))
    square = (LANES, LANES)
    from_lane = row_index(square)
    same_parity = (from_lane // elements) % 2 == lane_index(square) // HALF
    right = one_where(same_parity & (from_lane < 4 * elements)).astype(BF16)
    for pair in range(pairs):
        values = None
        for row in range(2 * pair, min(2 * pair + 2, fields)):
            start = (row % 2) * rows
            for col in range(fields):
                at = start + col * faces
                stage_ref[pair, at : at + faces, 0:elements] = flux_ref[row, col]
            part = jnp.where(filled, stage_ref[pair, start : start + rows, :], 0.0)
            values = part if values is None else values + pltpu.roll(part, elements, 1)
        stage_ref[pair, 0:rows, :] = high_and_low(values, 2 * elements)
        for face in range(faces):
            left = []
            for col in range(fields):
                at = col * faces + face
                left.append(stage_ref[pair, at : at + 1, :] * pick)
            spread = product(jnp.concatenate(left, axis=0).astype(BF16), right)
            at = (face * pairs + pair) * fields
            out_ref[at : at + fields] = spread.reshape(fields, elements, LANES)


def local_terms(packed, star_ref, flux_ref, volume_ref, trace_ref, lift_ref, fields, kinds):
    left = stack_left(packed)
    volume = star_mix(product(left, volume_ref[...]), star_ref, fields, kinds)
    traces = product(left, trace_ref[...])
    sums = []
    for col in range(fields):
        halves = []
        for half in range(2):
            total = None
            for row in range(fields):
                part = traces[row * ROWS : (row + 1) * ROWS, half * LANES : (half + 1) * LANES]
                term = flux_ref[row * fields + col, half] * part
                total = term if total is None else total + term
            halves.append(total)
        sums.append(jnp.concatenate(halves, axis=1))
    return volume + product(stack_left(jnp.concatenate(sums, axis=0)), lift_ref[...])


def combo_code(lanes, turns, face_modes):
    in_face = lanes % HALF
    code = jnp.where(in_face < turns * face_modes, (lanes // HALF) * turns + in_face // face_modes, -1)
    return code.astype(F32)


def ghost_terms(
    flux_ref, stage_ref, code_ref, composed, lift_sides, lane_code, flux_out, operator_out, scatter_out, sends, fields
):
    faces, elements = flux_ref.shape[2], flux_ref.shape[3]
    rows = 2 * ROWS
    shape = (rows, LANES)
    lanes = lane_index(shape)

    def along_lanes(start):
        row = code_ref[start : start + 1, :]
        for face in range(1, faces):
            row = row + pltpu.roll(code_ref[start + face : start + face + 1, :], face * elements, 1)
        return row + swap_halves(row)

    slots, codes = along_lanes(0), along_lanes(faces)
    ghosts = elements + row_index(shape)
    found = one_where(jnp.broadcast_to(slots, shape) == ghosts.astype(F32))
    first = jnp.where(lanes < HALF, found, 0.0)
    code = jnp.sum(first * codes, axis=1, keepdims=True)
    face_of = jnp.sum(first * (lanes // elements).astype(F32), axis=1, keepdims=True)
    element_of = jnp.sum(first * (lanes % elements).astype(F32), axis=1, keepdims=True)
    numbers = [slot * sends + place for slot in range(4) for place in range(sends // 2)]

    filled = lanes < elements
    values = []
    for field in range(fields):
        total = None
        for face in range(faces):
            stage_ref[field, face * rows : face * rows + fields, 0:elements] = flux_ref[field, :, face, :]
            part = jnp.where(filled, stage_ref[field, face * rows : (face + 1) * rows, :], 0.0)
            total = part if total is None else total + pltpu.roll(part, face * elements, 1)
        total = jnp.where(row_index(shape) < fields, total, 0.0)
        values.append(high_and_low(total, HALF))
    picked = jnp.concatenate([jnp.broadcast_to(found[number : number + 1], (HALF, LANES)) for number in numbers], axis=0)
    flux_out[...] = lax.dot_general(
        jnp.concatenate(values, axis=0).astype(BF16), picked.astype(BF16), (((1,), (1,)), ((), ())),
        preferred_element_type=F32,
    )

    left = []
    for number in numbers:
        chosen = composed * one_where(lane_code == code[number : number + 1])
        both = chosen[:, 0:LANES] + chosen[:, LANES : 2 * LANES]
        high, low = split(both + swap_halves(both))
        left.append(jnp.concatenate([jnp.where(lower_half(high.shape), high, low), high], axis=1))
    high, low = split(lift_sides)
    lifts = product(jnp.concatenate(left, axis=0), jnp.concatenate([high, high, low, jnp.zeros_like(low)], axis=0))
    side_lane = (lane_index((1, faces * HALF)) // HALF).astype(F32)
    place_of = jnp.zeros((1, LANES), F32)
    columns = []
    for at, number in enumerate(numbers):
        chosen = lifts[at * HALF : (at + 1) * HALF] * one_where(side_lane == face_of[number : number + 1])
        both = chosen[:, 0:LANES] + chosen[:, LANES : 2 * LANES]
        high, low = split(both + swap_halves(both))
        none = jnp.zeros_like(low)
        order = [high, none, high, none, low, none] if at % 2 == 0 else [none, high, none, high, none, low]
        columns.append(jnp.concatenate(order, axis=0))
        if at % 2 == 1:
            operator_out[at // 2] = jnp.concatenate(columns[-2:], axis=1)
        place_of = jnp.where(lane_index((1, LANES)) // rows == at, element_of[number : number + 1], place_of)
    square = (fields * elements, LANES)
    here = (row_index(square) // elements == lane_index(square) % rows) & (
        (row_index(square) % elements).astype(F32) == place_of
    )
    one = one_where(here).astype(BF16)
    scatter_out[...] = jnp.concatenate([one, one], axis=1)


def prepare_kernel(
    packed_ref, early_ref, stiffness_ref, star_ref, flux_local_ref, flux_remote_ref, restrict_ref, lift_ref, orient_ref,
    slot_ref, face_ref, turn_ref, rate_ref,
    base_out, local_out, remote_out, volume_out, trace_out, local_lift_out, compose_out,
    remote_lift_out, choose_out, mask_out, code_ref, composed_out, sides_ref, fast_out,
    local_work_ref, remote_work_ref, block_ref, wide_ref, face_work_ref, orient_work_ref, code_work_ref,
):
    fields, kinds = packed_ref.shape[0], stiffness_ref.shape[0]
    face_modes, faces, modes = restrict_ref.shape
    turns = orient_ref.shape[0]
    flux_local_coefficients(flux_local_ref, local_work_ref, local_out)
    flux_remote_coefficients(flux_remote_ref, remote_work_ref, remote_out)

    block_ref[...] = jnp.zeros(block_ref.shape, F32)
    volume_out[...] = stack_right(stiffness_blocks(stiffness_ref, block_ref, False))

    wide_ref[...] = jnp.zeros(wide_ref.shape, F32)
    for mode in range(face_modes):
        at = mode * faces
        wide_ref[at : at + faces, 0:modes] = restrict_ref[mode]
        wide_ref[LANES + at : LANES + at + faces, HALF : HALF + modes] = restrict_ref[mode]
    trace_out[...] = stack_right(wide_ref[...].T)
    for mode in range(face_modes):
        at = mode * faces
        wide_ref[at : at + faces, 0:modes] = -lift_ref[mode]
        wide_ref[LANES + at : LANES + at + faces, HALF : HALF + modes] = -lift_ref[mode]
    local_lift_out[...] = stack_right(wide_ref[...])

    face_work_ref[...] = jnp.zeros(face_work_ref.shape, F32)
    orient_work_ref[...] = jnp.zeros(orient_work_ref.shape, F32)
    for turn in range(turns):
        orient_work_ref[turn * face_modes : (turn + 1) * face_modes, 0:face_modes] = orient_ref[turn]
    for face in range(faces):
        face_work_ref[0:face_modes, face * LANES : face * LANES + modes] = restrict_ref[:, face, :]
        face_work_ref[0:face_modes, face * LANES + HALF : face * LANES + HALF + modes] = restrict_ref[:, face, :]
    composed = jnp.dot(
        orient_work_ref[...], face_work_ref[...], precision=lax.Precision.HIGHEST, preferred_element_type=F32
    )
    stacked = jnp.concatenate([composed[:, face * LANES : (face + 1) * LANES] for face in range(faces)], axis=0)
    high, low = split(stacked.T[0:HALF])
    compose_out[...] = jnp.concatenate([high, high, low, jnp.zeros_like(low)], axis=0)
    wide_ref[...] = jnp.zeros(wide_ref.shape, F32)
    for face in range(faces):
        for turn in range(turns):
            rows = slice(face * HALF + turn * face_modes, face * HALF + (turn + 1) * face_modes)
            wide_ref[rows, 0:modes] = -lift_ref[:, face, :]
            wide_ref[rows, HALF : HALF + modes] = -lift_ref[:, face, :]
    remote_lift_out[...] = stack_right(wide_ref[...])

    elements = slot_ref.shape[1]
    code_work_ref[...] = jnp.zeros(code_work_ref.shape, F32)
    slots = slot_ref[...]
    sends = (choose_out.shape[1] // 2 - elements) // 4
    group = (slots - elements) // sends
    moved = slots
    for side in range(4):
        moved = jnp.where(group == side, slots + (ghost_slot(side) - side) * sends, moved)
    code_work_ref[0:faces, 0:elements] = jnp.where(slots < elements, slots, moved).astype(F32)
    code_work_ref[faces : 2 * faces, 0:elements] = (face_ref[...] * turns + turn_ref[...]).astype(F32)
    code_work_ref[2 * faces : 2 * faces + 1, 0:elements] = rate_ref[...].astype(F32)
    code_ref[...] = code_work_ref[0 : 2 * faces, :]
    codes = code_work_ref[...].T[0:elements, :]
    rates = codes[:, 2 * faces : 2 * faces + 1]
    fast_out[...] = jnp.where(lower_half((ROWS, LANES)), rates[0:ROWS], rates[ROWS : 2 * ROWS])
    sources = choose_out.shape[1] // 2
    source_lane = (lane_index((elements, 2 * sources)) % sources).astype(F32)
    lanes = lane_index((elements, mask_out.shape[1]))
    lane_code = combo_code(lanes, turns, face_modes)
    picks, masks = [], []
    for face in range(faces):
        picks.append(jnp.where(codes[:, face : face + 1] == source_lane, 1.0, 0.0))
        masks.append(jnp.where(codes[:, faces + face : faces + face + 1] == lane_code, 1.0, 0.0))
    choose_out[...] = jnp.concatenate(picks, axis=0).astype(BF16)
    mask_out[...] = jnp.concatenate(masks, axis=0)

    sides_ref[...] = jnp.zeros(sides_ref.shape, F32)
    for face in range(faces):
        for turn in range(turns):
            rows = slice(turn * face_modes, (turn + 1) * face_modes)
            sides_ref[rows, face * HALF : face * HALF + modes] = -lift_ref[:, face, :]
    composed_out[...] = stacked.T[0:HALF]

    early = early_ref[...].reshape(fields * ROWS, LANES)
    terms = local_terms(early, star_ref, local_out, volume_out, trace_out, local_lift_out, fields, kinds)
    base_out[...] = packed_ref[...] + terms.reshape(fields, ROWS, LANES)


def remote_terms(rows, remote_ref, compose_ref, lift_ref, choose_ref, mask_ref, fields):
    pairs = len(rows)
    faces = lift_ref.shape[0] // (3 * HALF)
    elements = choose_ref.shape[0] // faces
    sources = jnp.concatenate(rows, axis=1)
    gathered = product(choose_ref[...], jnp.concatenate(split(sources), axis=0))
    folded = []
    for face in range(faces):
        sums = []
        for col in range(fields):
            total = None
            for pair in range(pairs):
                part = gathered[face * elements : (face + 1) * elements, pair * LANES : (pair + 1) * LANES]
                term = remote_ref[(face * pairs + pair) * fields + col] * part
                total = term if total is None else total + term
            sums.append(total)
        mixed = jnp.concatenate(sums, axis=0)
        high, low = split(mixed + swap_halves(mixed))
        first = jnp.where(lower_half(high.shape), high, low)
        turned = product(jnp.concatenate([first, high], axis=1), compose_ref[...])
        mask = mask_ref[face * elements : (face + 1) * elements, :]
        chosen = (turned.reshape(fields, elements, turned.shape[1]) * mask[None]).reshape(turned.shape)
        both = chosen[:, 0:LANES] + chosen[:, LANES : 2 * LANES]
        folded.append(both + swap_halves(both))
    lower = lower_half(folded[0].shape)
    left = [jnp.where(lower, folded[face], folded[face + 1]) for face in range(0, faces, 2)]
    result = product(stack_left(jnp.concatenate(left, axis=1)), lift_ref[...])
    result = result.reshape(fields, 2, ROWS, LANES)
    return jnp.where(lower_half((ROWS, LANES))[None], result[:, 0], result[:, 1])


def middle_kernel(
    base_ref, early_rows, late_ref, star_ref, remote_ref, derive_ref, compose_ref, lift_ref, choose_ref, mask_ref,
    fast_ref, send_hbm, from_0, from_1, from_2, from_3,
    middle_out, late_out, send_0, send_1, send_2, send_3,
    rows_ref, late_rows, send_ref, sem,
):
    copy = pltpu.make_async_copy(send_hbm, send_ref, sem)
    copy.start()
    fields = base_ref.shape[0]
    kinds = star_ref.shape[0] // (fields * fields)
    pairs = rows_ref.shape[0]
    sends = send_ref.shape[2]
    fast = sends // 2
    for side, arrived in enumerate((from_0, from_1, from_2, from_3)):
        for pair in range(pairs):
            rows_ref[pair, side * sends : (side + 1) * sends, :] = arrived[pair * sends : (pair + 1) * sends, :]
    rows = [jnp.concatenate([early_rows[pair], rows_ref[pair]], axis=0) for pair in range(pairs)]
    middle = base_ref[...] + remote_terms(rows, remote_ref, compose_ref, lift_ref, choose_ref, mask_ref, fields)
    middle_out[...] = middle
    start = middle.reshape(fields * ROWS, LANES)

    def step(degree, carry):
        current, early = carry
        current = star_mix(product(stack_left(current), derive_ref[...]), star_ref, fields, kinds)
        return current, early + weight_at(0.0, 0.5, degree) * current

    _, restart = lax.fori_loop(1, DERIVS, step, (start, taylor_weight(0.0, 0.5, 0) * start))
    copy.wait()
    is_fast = fast_ref[...]
    late = jnp.where((is_fast == 2)[None], restart.reshape(fields, ROWS, LANES), late_ref[...])
    late_out[...] = late
    both = late.reshape(fields * ROWS, LANES)
    swapped = swap_halves(both)
    wide = lower_half(both.shape)
    late_rows[:, 0:ROWS, :] = jnp.where(wide, both, swapped).reshape(late.shape)
    late_rows[:, ROWS : 2 * ROWS, :] = jnp.where(wide, swapped, both).reshape(late.shape)
    first_half = lower_half((1, LANES))
    for slot, out in enumerate((send_0, send_1, send_2, send_3)):
        out[...] = jnp.zeros(out.shape, F32)
        side = message_side(slot)
        places = [send_ref[0, side, place] for place in range(fast)]
        for field in range(fields):
            halves = [late_rows[field, pl.ds(element, 1), :] for element in places]
            out[field : field + 1, :] = jnp.where(first_half, *halves)


def local_kernel(
    middle_ref, late_ref, star_ref, flux_ref, volume_ref, trace_ref, lift_ref,
    remote_ref, compose_ref, remote_lift_ref, choose_ref, mask_ref, flux_remote_ref, code_ref, composed_ref, sides_ref,
    orient_ref, first_0, first_1, first_2, first_3,
    base_out, ghost_flux_out, ghost_operator_out, scatter_out, rows_ref, stage_ref,
):
    fields = middle_ref.shape[0]
    kinds = star_ref.shape[0] // (fields * fields)
    pairs = rows_ref.shape[0]
    elements = 2 * ROWS
    sends = (rows_ref.shape[1] - elements) // 4
    fast = sends // 2
    late = late_ref[...].reshape(fields * ROWS, LANES)
    rows_by_pair(late, rows_ref, fields)
    for slot, first in enumerate((first_0, first_1, first_2, first_3)):
        at = elements + slot * sends
        for pair in range(pairs):
            rows_ref[pair, at : at + fast, :] = jnp.zeros((fast, LANES), F32)
            row = pairs * sends + pair * fast
            rows_ref[pair, at + fast : at + sends, :] = first[row : row + fast, :]
    terms = local_terms(late, star_ref, flux_ref, volume_ref, trace_ref, lift_ref, fields, kinds)
    rows = [rows_ref[pair] for pair in range(pairs)]
    remote = remote_terms(rows, remote_ref, compose_ref, remote_lift_ref, choose_ref, mask_ref, fields)
    base = middle_ref[...] + terms.reshape(fields, ROWS, LANES) + remote
    base_out[:, 0:ROWS, :] = base
    base_out[:, ROWS : 2 * ROWS, :] = swap_halves(base.reshape(fields * ROWS, LANES)).reshape(base.shape)
    lane_code = combo_code(lane_index((1, composed_ref.shape[1])), orient_ref.shape[0], orient_ref.shape[1])
    ghost_terms(
        flux_remote_ref, stage_ref, code_ref, composed_ref[...], sides_ref[...], lane_code,
        ghost_flux_out, ghost_operator_out, scatter_out, sends, fields,
    )


def final_kernel(
    base_ref, ghost_flux_ref, ghost_operator_ref, scatter_ref, second_0, second_1, second_2, second_3, result_hbm,
    result_ref, sems,
):
    fields = base_ref.shape[0]
    modes = result_ref.shape[2]
    rows = second_0.shape[0]
    added = []
    for slot, second in enumerate((second_0, second_1, second_2, second_3)):
        sums = [None] * 3
        for field in range(fields):
            coefficient = ghost_flux_ref[field * rows : (field + 1) * rows, slot * LANES : (slot + 1) * LANES]
            term = coefficient * second[field : field + 1, :]
            sums[field % 3] = term if sums[field % 3] is None else sums[field % 3] + term
        both = product(stack_left(sums[0] + sums[1] + sums[2]), ghost_operator_ref[slot])
        added += [both[:, 0:LANES], both[:, LANES : 2 * LANES]]
    right = jnp.concatenate(split(jnp.concatenate(added, axis=0)), axis=0)
    result = base_ref[...] + product(scatter_ref[...], right).reshape(base_ref.shape)
    copies = []
    for field in range(fields):
        result_ref[field] = result[field, :, 0:modes]
        copies.append(pltpu.make_async_copy(result_ref.at[field], result_hbm.at[field], sems.at[field]))
        copies[-1].start()
    for copy in copies:
        copy.wait()


VMEM = pl.BlockSpec(memory_space=pltpu.VMEM)
HBM = pl.BlockSpec(memory_space=pltpu.HBM)


def call(kernel, ins, outs, scratch, args, name, flops, out_spec=VMEM):
    shapes = [jax.ShapeDtypeStruct(shape, dtype) for shape, dtype in outs]
    args = [
        pltpu.with_memory_space_constraint(arg, pltpu.HBM) if spec is HBM else arg for spec, arg in zip(ins, args)
    ]
    return pl.pallas_call(
        kernel,
        out_shape=shapes,
        in_specs=ins,
        out_specs=[out_spec] * len(outs),
        scratch_shapes=[pltpu.VMEM(*one) if isinstance(one, tuple) else one for one in scratch],
        compiler_params=pltpu.CompilerParams(vmem_limit_bytes=16 * 1024 * 1024),
        cost_estimate=pl.CostEstimate(flops=flops, bytes_accessed=4_000_000, transcendentals=0),
        name=name,
    )(*args)


def exchange(outgoing):
    arrived = []
    for (axis, far), message in zip(SWAPS, outgoing):
        size = lax.axis_size(axis)
        assert size % 2 == 0
        pairs = []
        for first in range(1 if far else 0, size, 2):
            second = (first + 1) % size
            pairs += [(first, second), (second, first)]
        arrived.append(lax.ppermute(message, axis, pairs))
    return arrived


def up_to(count, multiple):
    return -(-count // multiple) * multiple


def local(
    solution, stiffness, star_matrices, face_restrict, face_lift, orient_maps, flux_local, flux_remote,
    cluster_rate, send_list, neighbour_slot, neighbour_face, neighbour_turn,
):
    fields, elements = solution.shape[1], solution.shape[2]
    kinds = stiffness.shape[0]
    faces = face_restrict.shape[0]
    sides, sends = send_list.shape[1], send_list.shape[2]
    fast = sends // 2
    pairs = (fields + 1) // 2
    assert elements == 2 * ROWS and solution.shape[0] <= HALF and fast == 2
    values = jnp.transpose(solution, (1, 2, 0))
    star = jnp.transpose(star_matrices, (1, 2, 0, 3))
    local_part = jnp.transpose(flux_local, (1, 2, 0, 3))
    remote_part = jnp.transpose(flux_remote, (1, 2, 0, 3))
    restrict = jnp.transpose(face_restrict, (1, 0, 2))
    lift = jnp.transpose(face_lift, (2, 0, 1))

    packed = (fields, ROWS, LANES)
    first_shape = (up_to(pairs * (sends + fast), ROWS), LANES)
    second_shape = (up_to(fields, 2 * ROWS), LANES)
    star_shape = (fields * fields * kinds, ROWS, LANES)
    combos = faces * HALF
    sources = elements + sides * sends

    waiting = (
        local_part, remote_part, restrict, lift, orient_maps, neighbour_slot, neighbour_face, neighbour_turn,
        cluster_rate.reshape(1, elements),
    )
    made = call(
        predict_kernel,
        [HBM] * (4 + len(LATER)),
        [(packed, F32)] * 2 + [(first_shape, F32)] * sides + [
            (packed, F32), (star_shape, F32), ((3 * LANES, kinds * LANES), BF16), (stiffness.shape, F32),
            ((pairs, elements, LANES), F32),
        ] + [(array.shape, array.dtype) for array in waiting],
        [
            ((fields, up_to(4 * fields, ROWS), LANES), F32),
            ((pairs, elements, LANES), F32),
            (values.shape, F32), ((kinds, LANES, LANES), F32), (star.shape, F32),
            pltpu.SMEM(send_list.shape, jnp.int32), pltpu.SemaphoreType.DMA((10 + len(LATER),)),
        ],
        (values, stiffness, star, send_list, *waiting),
        "predict", 100_000_000,
    )
    early, late, outgoing = made[0], made[1], made[2 : 2 + sides]
    start, star_coef, derive_op, stiffness_kept, early_rows = made[2 + sides : 7 + sides]
    waiting = made[7 + sides :]
    first = exchange(outgoing)
    (
        base, local_coef, remote_coef, volume_op, trace_op, local_lift, compose_op, remote_lift, choose, mask,
        codes, composed, lift_sides, fast_mask,
    ) = call(
        prepare_kernel,
        [VMEM] * 13,
        [
            (packed, F32), ((fields * fields, 2, ROWS, LANES), F32),
            ((faces * pairs * fields, elements, LANES), F32),
            ((3 * LANES, kinds * LANES), BF16), ((3 * LANES, 2 * LANES), BF16),
            ((6 * LANES, LANES), BF16), ((2 * LANES, combos), BF16), ((3 * faces * HALF, LANES), BF16),
            ((faces * elements, 2 * sources), BF16), ((faces * elements, combos), F32),
            ((2 * faces, LANES), F32), ((HALF, combos), F32), ((HALF, faces * HALF), F32),
            ((ROWS, LANES), F32),
        ],
        [
            ((fields, 2 * ROWS * faces, LANES), F32), ((pairs, 2 * up_to(4 * fields, ROWS), LANES), F32),
            ((kinds, LANES, LANES), F32), ((2 * LANES, LANES), F32),
            ((LANES, faces * LANES), F32), ((HALF, LANES), F32), ((LANES, LANES), F32),
        ],
        (start, early, stiffness_kept, star_coef, *waiting),
        "prepare", 200_000_000,
    )
    middle, late_value, *outgoing = call(
        middle_kernel,
        [VMEM] * 11 + [HBM] + [VMEM] * 4,
        [(packed, F32)] * 2 + [(second_shape, F32)] * sides,
        [
            ((pairs, sides * sends, LANES), F32), ((fields, elements, LANES), F32),
            pltpu.SMEM(send_list.shape, jnp.int32), pltpu.SemaphoreType.DMA,
        ],
        (
            base, early_rows, late, star_coef, remote_coef, derive_op, compose_op, remote_lift, choose, mask,
            fast_mask, send_list, *first,
        ),
        "middle", 200_000_000,
    )
    second = exchange(outgoing)
    base, ghost_flux, ghost_op, scatter = call(
        local_kernel,
        [VMEM] * (17 + len(first)),
        [
            ((fields, elements, LANES), F32), ((fields * second_shape[0], sides * LANES), F32),
            ((sides, 3 * LANES, 2 * LANES), BF16), ((fields * elements, 2 * LANES), BF16),
        ],
        [((pairs, sources, LANES), F32), ((fields, 2 * ROWS * faces, LANES), F32)],
        (
            middle, late_value, star_coef, local_coef, volume_op, trace_op, local_lift,
            remote_coef, compose_op, remote_lift, choose, mask, waiting[1], codes, composed, lift_sides, waiting[4],
            *first,
        ),
        "local_late", 200_000_000,
    )
    (result,) = call(
        final_kernel,
        [VMEM] * 8,
        [(values.shape, F32)],
        [(values.shape, F32), pltpu.SemaphoreType.DMA((fields,))],
        (base, ghost_flux, ghost_op, scatter, *second),
        "final", 200_000_000, HBM,
    )
    return jnp.transpose(result, (2, 0, 1))


def solution(mesh):
    placed = (
        P(None, None, ("dom", "sub")),
        P(),
        P(None, None, None, ("dom", "sub")),
        P(),
        P(),
        P(),
        P(None, None, None, ("dom", "sub")),
        P(None, None, None, ("dom", "sub")),
        P(("dom", "sub")),
        P(("dom", "sub"), None, None),
        P(None, ("dom", "sub")),
        P(None, ("dom", "sub")),
        P(None, ("dom", "sub")),
    )
    return jax.shard_map(
        local, mesh=mesh, in_specs=placed, out_specs=P(None, None, ("dom", "sub")), check_vma=False
    )
```

```python
import math

import jax
import jax.numpy as jnp
from jax import lax
from jax.experimental import pallas as pl
from jax.experimental.pallas import tpu as pltpu
from jax.sharding import PartitionSpec as P

DERIVS = 6
LANES = 128
HALF = 64
ROWS = 8
F32 = jnp.float32
BF16 = jnp.bfloat16
LATER = ("flux_local", "flux_remote", "face_restrict", "face_lift", "orient_maps", "slot", "face", "turn", "rate")
AXES = ("dom", "sub")
SWAPS = (("dom", True), ("dom", False), ("sub", True), ("sub", False))


def taylor_weight(lower, upper, degree):
    return (upper ** (degree + 1) - lower ** (degree + 1)) / math.factorial(degree + 1)


def weight_at(lower, upper, degree):
    result = jnp.float32(taylor_weight(lower, upper, 1))
    for option in range(2, DERIVS):
        result = jnp.where(degree == option, jnp.float32(taylor_weight(lower, upper, option)), result)
    return result


def split(values):
    high = values.astype(BF16)
    low = (values - high.astype(F32)).astype(BF16)
    return high, low


def stack_left(values):
    high, low = split(values)
    return jnp.concatenate([high, low, high], axis=1)


def stack_right(values):
    high, low = split(values)
    return jnp.concatenate([high, high, low], axis=0)


def product(left, right):
    return jnp.dot(left, right, preferred_element_type=F32)


def odd_place(axis):
    return lax.rem(lax.axis_index(axis), 2)


def message_side(slot):
    axis, far = SWAPS[slot]
    odd = odd_place(axis)
    return 2 * AXES.index(axis) + (odd if far else 1 - odd)


def ghost_slot(side):
    axis = AXES[side // 2]
    even_far = side % 2 == 0
    return jnp.where(odd_place(axis) == 0, SWAPS.index((axis, even_far)), SWAPS.index((axis, not even_far)))


def lane_index(shape):
    return lax.broadcasted_iota(jnp.int32, shape, len(shape) - 1)


def lower_half(shape):
    return lane_index(shape) < HALF


def swap_halves(values):
    return pltpu.roll(values, HALF, values.ndim - 1)


def pack(values_ref, packed_ref):
    modes = values_ref.shape[2]
    packed_ref[:, :, 0:modes] = values_ref[:, 0:ROWS, :]
    packed_ref[:, :, HALF : HALF + modes] = values_ref[:, ROWS : 2 * ROWS, :]


def high_and_low(values, shift):
    high = values.astype(BF16).astype(F32)
    return high + pltpu.roll(values - high, shift, 1)


def row_index(shape):
    return lax.broadcasted_iota(jnp.int32, shape, len(shape) - 2)


def one_where(condition):
    return jnp.where(condition, 1.0, 0.0)


def star_coefficients(star_ref, stage_ref, star_out):
    fields, kinds, elements = star_ref.shape[0], star_ref.shape[2], star_ref.shape[3]
    lanes = lane_index((ROWS, LANES))
    pick = one_where((lanes % ROWS == row_index((ROWS, LANES))) & (lanes < 2 * elements))
    from_lane = row_index((LANES, LANES))
    same_half = (from_lane % elements) // ROWS == lane_index((LANES, LANES)) // HALF
    right = one_where(same_half & (from_lane < 2 * elements)).astype(BF16)
    filled = lane_index(stage_ref.shape[1:]) < elements
    spreads = []
    for row in range(fields):
        for col in range(fields):
            stage_ref[row, col * 4 : col * 4 + kinds, 0:elements] = star_ref[row, col]
        values = jnp.where(filled, stage_ref[row], 0.0)
        stage_ref[row] = high_and_low(values, elements)
        for kind in range(kinds):
            for col in range(fields):
                at = col * 4 + kind
                spreads.append(stage_ref[row, at : at + 1, :] * pick)
    star_out[...] = product(jnp.concatenate(spreads, axis=0).astype(BF16), right).reshape(star_out.shape)


def star_mix(columns, star_ref, fields, kinds):
    sums = []
    for col in range(fields):
        parts = []
        for kind in range(kinds):
            total = None
            for row in range(fields):
                part = columns[row * ROWS : (row + 1) * ROWS, kind * LANES : (kind + 1) * LANES]
                term = star_ref[(row * kinds + kind) * fields + col] * part
                total = term if total is None else total + term
            parts.append(total)
        sums.append(sum(parts[1:], parts[0]))
    return jnp.concatenate(sums, axis=0)


def stiffness_blocks(stiffness_ref, block_ref, turned):
    kinds, modes = stiffness_ref.shape[0], stiffness_ref.shape[1]
    for kind in range(kinds):
        matrix = -stiffness_ref[kind].T if turned else stiffness_ref[kind]
        block_ref[kind, 0:modes, 0:modes] = matrix
        block_ref[kind, HALF : HALF + modes, HALF : HALF + modes] = matrix
    return jnp.concatenate([block_ref[kind] for kind in range(kinds)], axis=1)


def predict_kernel(*refs):
    later = len(LATER)
    solution_hbm, stiffness_hbm, star_hbm, send_hbm = refs[0:4]
    later_hbm, refs = refs[4 : 4 + later], refs[4 + later :]
    early_out, late_out, send_0, send_1, send_2, send_3 = refs[0:6]
    packed_ref, coef_ref, derive_ref, stiffness_ref, early_rows = refs[6:11]
    later_out, refs = refs[11 : 11 + later], refs[11 + later :]
    work_ref, late_rows, solution_ref, block_ref, star_ref, send_ref, sems = refs

    pieces = []
    for source, target in ((star_hbm, star_ref), (stiffness_hbm, stiffness_ref), (solution_hbm, solution_ref)):
        step = source.shape[0] // 3
        pieces += [(source.at[pl.ds(at, step)], target.at[pl.ds(at, step)]) for at in range(0, source.shape[0], step)]
    first = len(pieces)
    pieces += zip((send_hbm, *later_hbm), (send_ref, *later_out))
    copies = [
        pltpu.make_async_copy(source, target, sems.at[number]) for number, (source, target) in enumerate(pieces)
    ]
    for copy in copies:
        copy.start()
    fields, kinds = star_ref.shape[0], star_ref.shape[2]
    pairs = (fields + 1) // 2
    for cleared in (packed_ref, block_ref, send_0, send_1, send_2, send_3):
        cleared[...] = jnp.zeros(cleared.shape, F32)
    for copy in copies[0:first]:
        copy.wait()
    derive_ref[...] = stack_right(stiffness_blocks(stiffness_ref, block_ref, True))
    star_coefficients(star_ref, work_ref, coef_ref)
    pack(solution_ref, packed_ref)
    start = packed_ref[...].reshape(fields * ROWS, LANES)

    def step(degree, carry):
        current, early, late = carry
        current = star_mix(product(stack_left(current), derive_ref[...]), coef_ref, fields, kinds)
        early = early + weight_at(0.0, 0.5, degree) * current
        late = late + weight_at(0.5, 1.0, degree) * current
        return current, early, late

    _, early, late = lax.fori_loop(
        1, DERIVS, step, (start, taylor_weight(0.0, 0.5, 0) * start, taylor_weight(0.5, 1.0, 0) * start),
        unroll=True,
    )
    early_out[...] = early.reshape(fields, ROWS, LANES)
    late_out[...] = late.reshape(fields, ROWS, LANES)
    rows_by_pair(early, early_rows, fields)
    rows_by_pair(late, late_rows, fields)
    copies[first].wait()
    sends = send_ref.shape[2]
    fast = sends // 2
    for side, out in enumerate((send_0, send_1, send_2, send_3)):
        for place in range(sends):
            element = send_ref[0, message_side(side), place]
            for pair in range(pairs):
                row = pair * sends + place
                out[row : row + 1, :] = early_rows[pair, pl.ds(element, 1), :]
            if place >= fast:
                for pair in range(pairs):
                    row = pairs * sends + pair * fast + place - fast
                    out[row : row + 1, :] = late_rows[pair, pl.ds(element, 1), :]
    for copy in copies[first + 1 :]:
        copy.wait()


def rows_by_pair(packed, out_ref, fields):
    lower = lower_half((ROWS, LANES))
    for pair in range((fields + 1) // 2):
        even = packed[2 * pair * ROWS : (2 * pair + 1) * ROWS]
        odd = jnp.zeros_like(even)
        if 2 * pair + 1 < fields:
            odd = packed[(2 * pair + 1) * ROWS : (2 * pair + 2) * ROWS]
        out_ref[pair, 0:ROWS, :] = jnp.where(lower, even, swap_halves(odd))
        out_ref[pair, ROWS : 2 * ROWS, :] = jnp.where(lower, swap_halves(even), odd)


def flux_local_coefficients(flux_ref, stage_ref, out_ref):
    fields, faces, elements = flux_ref.shape[0], flux_ref.shape[2], flux_ref.shape[3]
    rows = 2 * ROWS
    filled = lane_index((rows, LANES)) < elements
    lanes, sublanes = lane_index((ROWS, LANES)), row_index((ROWS, LANES))
    picks = [one_where(lanes % elements == half * ROWS + sublanes) for half in range(2)]
    square = (LANES, LANES)
    right = one_where(row_index(square) // (2 * elements) == lane_index(square) % faces).astype(BF16)
    for row in range(fields):
        values = None
        for face in range(faces):
            stage_ref[row, face * rows : face * rows + fields, 0:elements] = flux_ref[row, :, face, :]
            part = jnp.where(filled, stage_ref[row, face * rows : (face + 1) * rows, :], 0.0)
            values = part if values is None else values + pltpu.roll(part, face * 2 * elements, 1)
        stage_ref[row, 0:rows, :] = high_and_low(values, elements)
        left = [stage_ref[row, col : col + 1, :] * pick for col in range(fields) for pick in picks]
        spread = product(jnp.concatenate(left, axis=0).astype(BF16), right)
        out_ref[row * fields : (row + 1) * fields] = spread.reshape(fields, 2, ROWS, LANES)


def flux_remote_coefficients(flux_ref, stage_ref, out_ref):
    fields, faces, elements = flux_ref.shape[0], flux_ref.shape[2], flux_ref.shape[3]
    pairs = (fields + 1) // 2
    rows = stage_ref.shape[1] // 2
    filled = lane_index((rows, LANES)) < elements
    lanes, sublanes = lane_index((elements, LANES)), row_index((elements, LANES))
    pick = one_where((lanes % elements == sublanes) & (lanes < 4 * elements))
    square = (LANES, LANES)
    from_lane = row_index(square)
    same_parity = (from_lane // elements) % 2 == lane_index(square) // HALF
    right = one_where(same_parity & (from_lane < 4 * elements)).astype(BF16)
    for pair in range(pairs):
        values = None
        for row in range(2 * pair, min(2 * pair + 2, fields)):
            start = (row % 2) * rows
            for col in range(fields):
                at = start + col * faces
                stage_ref[pair, at : at + faces, 0:elements] = flux_ref[row, col]
            part = jnp.where(filled, stage_ref[pair, start : start + rows, :], 0.0)
            values = part if values is None else values + pltpu.roll(part, elements, 1)
        stage_ref[pair, 0:rows, :] = high_and_low(values, 2 * elements)
        for face in range(faces):
            left = []
            for col in range(fields):
                at = col * faces + face
                left.append(stage_ref[pair, at : at + 1, :] * pick)
            spread = product(jnp.concatenate(left, axis=0).astype(BF16), right)
            at = (face * pairs + pair) * fields
            out_ref[at : at + fields] = spread.reshape(fields, elements, LANES)


def local_terms(packed, star_ref, flux_ref, volume_ref, trace_ref, lift_ref, fields, kinds):
    left = stack_left(packed)
    volume = star_mix(product(left, volume_ref[...]), star_ref, fields, kinds)
    traces = product(left, trace_ref[...])
    sums = []
    for col in range(fields):
        halves = []
        for half in range(2):
            total = None
            for row in range(fields):
                part = traces[row * ROWS : (row + 1) * ROWS, half * LANES : (half + 1) * LANES]
                term = flux_ref[row * fields + col, half] * part
                total = term if total is None else total + term
            halves.append(total)
        sums.append(jnp.concatenate(halves, axis=1))
    return volume + product(stack_left(jnp.concatenate(sums, axis=0)), lift_ref[...])


def combo_code(lanes, turns, face_modes):
    in_face = lanes % HALF
    code = jnp.where(in_face < turns * face_modes, (lanes // HALF) * turns + in_face // face_modes, -1)
    return code.astype(F32)


def ghost_terms(
    flux_ref, stage_ref, code_ref, composed, lift_sides, lane_code, flux_out, operator_out, scatter_out, sends, fields
):
    faces, elements = flux_ref.shape[2], flux_ref.shape[3]
    rows = 2 * ROWS
    shape = (rows, LANES)
    lanes = lane_index(shape)

    def along_lanes(start):
        row = code_ref[start : start + 1, :]
        for face in range(1, faces):
            row = row + pltpu.roll(code_ref[start + face : start + face + 1, :], face * elements, 1)
        return row + swap_halves(row)

    slots, codes = along_lanes(0), along_lanes(faces)
    ghosts = elements + row_index(shape)
    found = one_where(jnp.broadcast_to(slots, shape) == ghosts.astype(F32))
    first = jnp.where(lanes < HALF, found, 0.0)
    code = jnp.sum(first * codes, axis=1, keepdims=True)
    face_of = jnp.sum(first * (lanes // elements).astype(F32), axis=1, keepdims=True)
    element_of = jnp.sum(first * (lanes % elements).astype(F32), axis=1, keepdims=True)
    numbers = [slot * sends + place for slot in range(4) for place in range(sends // 2)]

    filled = lanes < elements
    values = []
    for field in range(fields):
        total = None
        for face in range(faces):
            stage_ref[field, face * rows : face * rows + fields, 0:elements] = flux_ref[field, :, face, :]
            part = jnp.where(filled, stage_ref[field, face * rows : (face + 1) * rows, :], 0.0)
            total = part if total is None else total + pltpu.roll(part, face * elements, 1)
        total = jnp.where(row_index(shape) < fields, total, 0.0)
        values.append(high_and_low(total, HALF))
    picked = jnp.concatenate([jnp.broadcast_to(found[number : number + 1], (HALF, LANES)) for number in numbers], axis=0)
    flux_out[...] = lax.dot_general(
        jnp.concatenate(values, axis=0).astype(BF16), picked.astype(BF16), (((1,), (1,)), ((), ())),
        preferred_element_type=F32,
    )

    left = []
    for number in numbers:
        chosen = composed * one_where(lane_code == code[number : number + 1])
        both = chosen[:, 0:LANES] + chosen[:, LANES : 2 * LANES]
        high, low = split(both + swap_halves(both))
        left.append(jnp.concatenate([jnp.where(lower_half(high.shape), high, low), high], axis=1))
    high, low = split(lift_sides)
    lifts = product(jnp.concatenate(left, axis=0), jnp.concatenate([high, high, low, jnp.zeros_like(low)], axis=0))
    side_lane = (lane_index((1, faces * HALF)) // HALF).astype(F32)
    place_of = jnp.zeros((1, LANES), F32)
    columns = []
    for at, number in enumerate(numbers):
        chosen = lifts[at * HALF : (at + 1) * HALF] * one_where(side_lane == face_of[number : number + 1])
        both = chosen[:, 0:LANES] + chosen[:, LANES : 2 * LANES]
        high, low = split(both + swap_halves(both))
        none = jnp.zeros_like(low)
        order = [high, none, high, none, low, none] if at % 2 == 0 else [none, high, none, high, none, low]
        columns.append(jnp.concatenate(order, axis=0))
        if at % 2 == 1:
            operator_out[at // 2] = jnp.concatenate(columns[-2:], axis=1)
        place_of = jnp.where(lane_index((1, LANES)) // rows == at, element_of[number : number + 1], place_of)
    square = (fields * elements, LANES)
    here = (row_index(square) // elements == lane_index(square) % rows) & (
        (row_index(square) % elements).astype(F32) == place_of
    )
    one = one_where(here).astype(BF16)
    scatter_out[...] = jnp.concatenate([one, one], axis=1)


def prepare_kernel(
    packed_ref, early_ref, stiffness_ref, star_ref, flux_local_ref, flux_remote_ref, restrict_ref, lift_ref, orient_ref,
    slot_ref, face_ref, turn_ref, rate_ref,
    base_out, local_out, remote_out, volume_out, trace_out, local_lift_out, compose_out,
    remote_lift_out, choose_out, mask_out, code_ref, composed_out, sides_ref, fast_out,
    local_work_ref, remote_work_ref, block_ref, wide_ref, face_work_ref, orient_work_ref, code_work_ref,
):
    fields, kinds = packed_ref.shape[0], stiffness_ref.shape[0]
    face_modes, faces, modes = restrict_ref.shape
    turns = orient_ref.shape[0]
    flux_local_coefficients(flux_local_ref, local_work_ref, local_out)
    flux_remote_coefficients(flux_remote_ref, remote_work_ref, remote_out)

    block_ref[...] = jnp.zeros(block_ref.shape, F32)
    volume_out[...] = stack_right(stiffness_blocks(stiffness_ref, block_ref, False))

    wide_ref[...] = jnp.zeros(wide_ref.shape, F32)
    for mode in range(face_modes):
        at = mode * faces
        wide_ref[at : at + faces, 0:modes] = restrict_ref[mode]
        wide_ref[LANES + at : LANES + at + faces, HALF : HALF + modes] = restrict_ref[mode]
    trace_out[...] = stack_right(wide_ref[...].T)
    for mode in range(face_modes):
        at = mode * faces
        wide_ref[at : at + faces, 0:modes] = -lift_ref[mode]
        wide_ref[LANES + at : LANES + at + faces, HALF : HALF + modes] = -lift_ref[mode]
    local_lift_out[...] = stack_right(wide_ref[...])

    face_work_ref[...] = jnp.zeros(face_work_ref.shape, F32)
    orient_work_ref[...] = jnp.zeros(orient_work_ref.shape, F32)
    for turn in range(turns):
        orient_work_ref[turn * face_modes : (turn + 1) * face_modes, 0:face_modes] = orient_ref[turn]
    for face in range(faces):
        face_work_ref[0:face_modes, face * LANES : face * LANES + modes] = restrict_ref[:, face, :]
        face_work_ref[0:face_modes, face * LANES + HALF : face * LANES + HALF + modes] = restrict_ref[:, face, :]
    composed = jnp.dot(
        orient_work_ref[...], face_work_ref[...], precision=lax.Precision.HIGHEST, preferred_element_type=F32
    )
    stacked = jnp.concatenate([composed[:, face * LANES : (face + 1) * LANES] for face in range(faces)], axis=0)
    high, low = split(stacked.T[0:HALF])
    compose_out[...] = jnp.concatenate([high, high, low, jnp.zeros_like(low)], axis=0)
    wide_ref[...] = jnp.zeros(wide_ref.shape, F32)
    for face in range(faces):
        for turn in range(turns):
            rows = slice(face * HALF + turn * face_modes, face * HALF + (turn + 1) * face_modes)
            wide_ref[rows, 0:modes] = -lift_ref[:, face, :]
            wide_ref[rows, HALF : HALF + modes] = -lift_ref[:, face, :]
    remote_lift_out[...] = stack_right(wide_ref[...])

    elements = slot_ref.shape[1]
    code_work_ref[...] = jnp.zeros(code_work_ref.shape, F32)
    slots = slot_ref[...]
    sends = (choose_out.shape[1] // 2 - elements) // 4
    group = (slots - elements) // sends
    moved = slots
    for side in range(4):
        moved = jnp.where(group == side, slots + (ghost_slot(side) - side) * sends, moved)
    code_work_ref[0:faces, 0:elements] = jnp.where(slots < elements, slots, moved).astype(F32)
    code_work_ref[faces : 2 * faces, 0:elements] = (face_ref[...] * turns + turn_ref[...]).astype(F32)
    code_work_ref[2 * faces : 2 * faces + 1, 0:elements] = rate_ref[...].astype(F32)
    code_ref[...] = code_work_ref[0 : 2 * faces, :]
    codes = code_work_ref[...].T[0:elements, :]
    rates = codes[:, 2 * faces : 2 * faces + 1]
    fast_out[...] = jnp.where(lower_half((ROWS, LANES)), rates[0:ROWS], rates[ROWS : 2 * ROWS])
    sources = choose_out.shape[1] // 2
    source_lane = (lane_index((elements, 2 * sources)) % sources).astype(F32)
    lanes = lane_index((elements, mask_out.shape[1]))
    lane_code = combo_code(lanes, turns, face_modes)
    picks, masks = [], []
    for face in range(faces):
        picks.append(jnp.where(codes[:, face : face + 1] == source_lane, 1.0, 0.0))
        masks.append(jnp.where(codes[:, faces + face : faces + face + 1] == lane_code, 1.0, 0.0))
    choose_out[...] = jnp.concatenate(picks, axis=0).astype(BF16)
    mask_out[...] = jnp.concatenate(masks, axis=0)

    sides_ref[...] = jnp.zeros(sides_ref.shape, F32)
    for face in range(faces):
        for turn in range(turns):
            rows = slice(turn * face_modes, (turn + 1) * face_modes)
            sides_ref[rows, face * HALF : face * HALF + modes] = -lift_ref[:, face, :]
    composed_out[...] = stacked.T[0:HALF]

    early = early_ref[...].reshape(fields * ROWS, LANES)
    terms = local_terms(early, star_ref, local_out, volume_out, trace_out, local_lift_out, fields, kinds)
    base_out[...] = packed_ref[...] + terms.reshape(fields, ROWS, LANES)


def remote_terms(rows, remote_ref, compose_ref, lift_ref, choose_ref, mask_ref, fields):
    pairs = len(rows)
    faces = lift_ref.shape[0] // (3 * HALF)
    elements = choose_ref.shape[0] // faces
    sources = jnp.concatenate(rows, axis=1)
    gathered = product(choose_ref[...], jnp.concatenate(split(sources), axis=0))
    folded = []
    for face in range(faces):
        sums = []
        for col in range(fields):
            total = None
            for pair in range(pairs):
                part = gathered[face * elements : (face + 1) * elements, pair * LANES : (pair + 1) * LANES]
                term = remote_ref[(face * pairs + pair) * fields + col] * part
                total = term if total is None else total + term
            sums.append(total)
        mixed = jnp.concatenate(sums, axis=0)
        high, low = split(mixed + swap_halves(mixed))
        first = jnp.where(lower_half(high.shape), high, low)
        turned = product(jnp.concatenate([first, high], axis=1), compose_ref[...])
        mask = mask_ref[face * elements : (face + 1) * elements, :]
        chosen = (turned.reshape(fields, elements, turned.shape[1]) * mask[None]).reshape(turned.shape)
        both = chosen[:, 0:LANES] + chosen[:, LANES : 2 * LANES]
        folded.append(both + swap_halves(both))
    lower = lower_half(folded[0].shape)
    left = [jnp.where(lower, folded[face], folded[face + 1]) for face in range(0, faces, 2)]
    result = product(stack_left(jnp.concatenate(left, axis=1)), lift_ref[...])
    result = result.reshape(fields, 2, ROWS, LANES)
    return jnp.where(lower_half((ROWS, LANES))[None], result[:, 0], result[:, 1])


def middle_kernel(
    base_ref, early_rows, late_ref, star_ref, remote_ref, derive_ref, compose_ref, lift_ref, choose_ref, mask_ref,
    fast_ref, send_hbm, from_0, from_1, from_2, from_3,
    middle_out, late_out, send_0, send_1, send_2, send_3,
    rows_ref, late_rows, send_ref, sem,
):
    copy = pltpu.make_async_copy(send_hbm, send_ref, sem)
    copy.start()
    fields = base_ref.shape[0]
    kinds = star_ref.shape[0] // (fields * fields)
    pairs = rows_ref.shape[0]
    sends = send_ref.shape[2]
    fast = sends // 2
    for side, arrived in enumerate((from_0, from_1, from_2, from_3)):
        for pair in range(pairs):
            rows_ref[pair, side * sends : (side + 1) * sends, :] = arrived[pair * sends : (pair + 1) * sends, :]
    rows = [jnp.concatenate([early_rows[pair], rows_ref[pair]], axis=0) for pair in range(pairs)]
    middle = base_ref[...] + remote_terms(rows, remote_ref, compose_ref, lift_ref, choose_ref, mask_ref, fields)
    middle_out[...] = middle
    start = middle.reshape(fields * ROWS, LANES)

    def step(degree, carry):
        current, early = carry
        current = star_mix(product(stack_left(current), derive_ref[...]), star_ref, fields, kinds)
        return current, early + weight_at(0.0, 0.5, degree) * current

    _, restart = lax.fori_loop(1, DERIVS, step, (start, taylor_weight(0.0, 0.5, 0) * start))
    copy.wait()
    is_fast = fast_ref[...]
    late = jnp.where((is_fast == 2)[None], restart.reshape(fields, ROWS, LANES), late_ref[...])
    late_out[...] = late
    both = late.reshape(fields * ROWS, LANES)
    swapped = swap_halves(both)
    wide = lower_half(both.shape)
    late_rows[:, 0:ROWS, :] = jnp.where(wide, both, swapped).reshape(late.shape)
    late_rows[:, ROWS : 2 * ROWS, :] = jnp.where(wide, swapped, both).reshape(late.shape)
    first_half = lower_half((1, LANES))
    for slot, out in enumerate((send_0, send_1, send_2, send_3)):
        out[...] = jnp.zeros(out.shape, F32)
        side = message_side(slot)
        places = [send_ref[0, side, place] for place in range(fast)]
        for field in range(fields):
            halves = [late_rows[field, pl.ds(element, 1), :] for element in places]
            out[field : field + 1, :] = jnp.where(first_half, *halves)


def local_kernel(
    middle_ref, late_ref, star_ref, flux_ref, volume_ref, trace_ref, lift_ref,
    remote_ref, compose_ref, remote_lift_ref, choose_ref, mask_ref, flux_remote_ref, code_ref, composed_ref, sides_ref,
    orient_ref, first_0, first_1, first_2, first_3,
    base_out, ghost_flux_out, ghost_operator_out, scatter_out, rows_ref, stage_ref,
):
    fields = middle_ref.shape[0]
    kinds = star_ref.shape[0] // (fields * fields)
    pairs = rows_ref.shape[0]
    elements = 2 * ROWS
    sends = (rows_ref.shape[1] - elements) // 4
    fast = sends // 2
    late = late_ref[...].reshape(fields * ROWS, LANES)
    rows_by_pair(late, rows_ref, fields)
    for slot, first in enumerate((first_0, first_1, first_2, first_3)):
        at = elements + slot * sends
        for pair in range(pairs):
            rows_ref[pair, at : at + fast, :] = jnp.zeros((fast, LANES), F32)
            row = pairs * sends + pair * fast
            rows_ref[pair, at + fast : at + sends, :] = first[row : row + fast, :]
    terms = local_terms(late, star_ref, flux_ref, volume_ref, trace_ref, lift_ref, fields, kinds)
    rows = [rows_ref[pair] for pair in range(pairs)]
    remote = remote_terms(rows, remote_ref, compose_ref, remote_lift_ref, choose_ref, mask_ref, fields)
    base = middle_ref[...] + terms.reshape(fields, ROWS, LANES) + remote
    base_out[:, 0:ROWS, :] = base
    base_out[:, ROWS : 2 * ROWS, :] = swap_halves(base.reshape(fields * ROWS, LANES)).reshape(base.shape)
    lane_code = combo_code(lane_index((1, composed_ref.shape[1])), orient_ref.shape[0], orient_ref.shape[1])
    ghost_terms(
        flux_remote_ref, stage_ref, code_ref, composed_ref[...], sides_ref[...], lane_code,
        ghost_flux_out, ghost_operator_out, scatter_out, sends, fields,
    )


def final_kernel(
    base_ref, ghost_flux_ref, ghost_operator_ref, scatter_ref, second_0, second_1, second_2, second_3, result_out,
):
    fields = base_ref.shape[0]
    modes = result_out.shape[2]
    rows = second_0.shape[0]
    added = []
    for slot, second in enumerate((second_0, second_1, second_2, second_3)):
        sums = [None] * 3
        for field in range(fields):
            coefficient = ghost_flux_ref[field * rows : (field + 1) * rows, slot * LANES : (slot + 1) * LANES]
            term = coefficient * second[field : field + 1, :]
            sums[field % 3] = term if sums[field % 3] is None else sums[field % 3] + term
        both = product(stack_left(sums[0] + sums[1] + sums[2]), ghost_operator_ref[slot])
        added += [both[:, 0:LANES], both[:, LANES : 2 * LANES]]
    right = jnp.concatenate(split(jnp.concatenate(added, axis=0)), axis=0)
    result = base_ref[...] + product(scatter_ref[...], right).reshape(base_ref.shape)
    result_out[...] = result[:, :, 0:modes]


VMEM = pl.BlockSpec(memory_space=pltpu.VMEM)
HBM = pl.BlockSpec(memory_space=pltpu.HBM)


def call(kernel, ins, outs, scratch, args, name, flops):
    shapes = [jax.ShapeDtypeStruct(shape, dtype) for shape, dtype in outs]
    args = [
        pltpu.with_memory_space_constraint(arg, pltpu.HBM) if spec is HBM else arg for spec, arg in zip(ins, args)
    ]
    return pl.pallas_call(
        kernel,
        out_shape=shapes,
        in_specs=ins,
        out_specs=[VMEM] * len(outs),
        scratch_shapes=[pltpu.VMEM(*one) if isinstance(one, tuple) else one for one in scratch],
        compiler_params=pltpu.CompilerParams(vmem_limit_bytes=16 * 1024 * 1024),
        cost_estimate=pl.CostEstimate(flops=flops, bytes_accessed=4_000_000, transcendentals=0),
        name=name,
    )(*args)


def exchange(outgoing):
    arrived = []
    for (axis, far), message in zip(SWAPS, outgoing):
        size = lax.axis_size(axis)
        assert size % 2 == 0
        pairs = []
        for first in range(1 if far else 0, size, 2):
            second = (first + 1) % size
            pairs += [(first, second), (second, first)]
        arrived.append(lax.ppermute(message, axis, pairs))
    return arrived


def up_to(count, multiple):
    return -(-count // multiple) * multiple


def local(
    solution, stiffness, star_matrices, face_restrict, face_lift, orient_maps, flux_local, flux_remote,
    cluster_rate, send_list, neighbour_slot, neighbour_face, neighbour_turn,
):
    fields, elements = solution.shape[1], solution.shape[2]
    kinds = stiffness.shape[0]
    faces = face_restrict.shape[0]
    sides, sends = send_list.shape[1], send_list.shape[2]
    fast = sends // 2
    pairs = (fields + 1) // 2
    assert elements == 2 * ROWS and solution.shape[0] <= HALF and fast == 2
    values = jnp.transpose(solution, (1, 2, 0))
    star = jnp.transpose(star_matrices, (1, 2, 0, 3))
    local_part = jnp.transpose(flux_local, (1, 2, 0, 3))
    remote_part = jnp.transpose(flux_remote, (1, 2, 0, 3))
    restrict = jnp.transpose(face_restrict, (1, 0, 2))
    lift = jnp.transpose(face_lift, (2, 0, 1))

    packed = (fields, ROWS, LANES)
    first_shape = (up_to(pairs * (sends + fast), ROWS), LANES)
    second_shape = (up_to(fields, 2 * ROWS), LANES)
    star_shape = (fields * fields * kinds, ROWS, LANES)
    combos = faces * HALF
    sources = elements + sides * sends

    waiting = (
        local_part, remote_part, restrict, lift, orient_maps, neighbour_slot, neighbour_face, neighbour_turn,
        cluster_rate.reshape(1, elements),
    )
    made = call(
        predict_kernel,
        [HBM] * (4 + len(LATER)),
        [(packed, F32)] * 2 + [(first_shape, F32)] * sides + [
            (packed, F32), (star_shape, F32), ((3 * LANES, kinds * LANES), BF16), (stiffness.shape, F32),
            ((pairs, elements, LANES), F32),
        ] + [(array.shape, array.dtype) for array in waiting],
        [
            ((fields, up_to(4 * fields, ROWS), LANES), F32),
            ((pairs, elements, LANES), F32),
            (values.shape, F32), ((kinds, LANES, LANES), F32), (star.shape, F32),
            pltpu.SMEM(send_list.shape, jnp.int32), pltpu.SemaphoreType.DMA((10 + len(LATER),)),
        ],
        (values, stiffness, star, send_list, *waiting),
        "predict", 100_000_000,
    )
    early, late, outgoing = made[0], made[1], made[2 : 2 + sides]
    start, star_coef, derive_op, stiffness_kept, early_rows = made[2 + sides : 7 + sides]
    waiting = made[7 + sides :]
    first = exchange(outgoing)
    (
        base, local_coef, remote_coef, volume_op, trace_op, local_lift, compose_op, remote_lift, choose, mask,
        codes, composed, lift_sides, fast_mask,
    ) = call(
        prepare_kernel,
        [VMEM] * 13,
        [
            (packed, F32), ((fields * fields, 2, ROWS, LANES), F32),
            ((faces * pairs * fields, elements, LANES), F32),
            ((3 * LANES, kinds * LANES), BF16), ((3 * LANES, 2 * LANES), BF16),
            ((6 * LANES, LANES), BF16), ((2 * LANES, combos), BF16), ((3 * faces * HALF, LANES), BF16),
            ((faces * elements, 2 * sources), BF16), ((faces * elements, combos), F32),
            ((2 * faces, LANES), F32), ((HALF, combos), F32), ((HALF, faces * HALF), F32),
            ((ROWS, LANES), F32),
        ],
        [
            ((fields, 2 * ROWS * faces, LANES), F32), ((pairs, 2 * up_to(4 * fields, ROWS), LANES), F32),
            ((kinds, LANES, LANES), F32), ((2 * LANES, LANES), F32),
            ((LANES, faces * LANES), F32), ((HALF, LANES), F32), ((LANES, LANES), F32),
        ],
        (start, early, stiffness_kept, star_coef, *waiting),
        "prepare", 200_000_000,
    )
    middle, late_value, *outgoing = call(
        middle_kernel,
        [VMEM] * 11 + [HBM] + [VMEM] * 4,
        [(packed, F32)] * 2 + [(second_shape, F32)] * sides,
        [
            ((pairs, sides * sends, LANES), F32), ((fields, elements, LANES), F32),
            pltpu.SMEM(send_list.shape, jnp.int32), pltpu.SemaphoreType.DMA,
        ],
        (
            base, early_rows, late, star_coef, remote_coef, derive_op, compose_op, remote_lift, choose, mask,
            fast_mask, send_list, *first,
        ),
        "middle", 200_000_000,
    )
    second = exchange(outgoing)
    base, ghost_flux, ghost_op, scatter = call(
        local_kernel,
        [VMEM] * (17 + len(first)),
        [
            ((fields, elements, LANES), F32), ((fields * second_shape[0], sides * LANES), F32),
            ((sides, 3 * LANES, 2 * LANES), BF16), ((fields * elements, 2 * LANES), BF16),
        ],
        [((pairs, sources, LANES), F32), ((fields, 2 * ROWS * faces, LANES), F32)],
        (
            middle, late_value, star_coef, local_coef, volume_op, trace_op, local_lift,
            remote_coef, compose_op, remote_lift, choose, mask, waiting[1], codes, composed, lift_sides, waiting[4],
            *first,
        ),
        "local_late", 200_000_000,
    )
    (result,) = call(
        final_kernel,
        [VMEM] * 8,
        [(values.shape, F32)],
        [],
        (base, ghost_flux, ghost_op, scatter, *second),
        "final", 200_000_000,
    )
    return jnp.transpose(result, (2, 0, 1))


def solution(mesh):
    placed = (
        P(None, None, ("dom", "sub")),
        P(),
        P(None, None, None, ("dom", "sub")),
        P(),
        P(),
        P(),
        P(None, None, None, ("dom", "sub")),
        P(None, None, None, ("dom", "sub")),
        P(("dom", "sub")),
        P(("dom", "sub"), None, None),
        P(None, ("dom", "sub")),
        P(None, ("dom", "sub")),
        P(None, ("dom", "sub")),
    )
    return jax.shard_map(
        local, mesh=mesh, in_specs=placed, out_specs=P(None, None, ("dom", "sub")), check_vma=False
    )
```

```python
import math

import jax
import jax.numpy as jnp
from jax import lax
from jax.experimental import pallas as pl
from jax.experimental.pallas import tpu as pltpu
from jax.sharding import PartitionSpec as P

DERIVS = 6
LANES = 128
HALF = 64
ROWS = 8
F32 = jnp.float32
BF16 = jnp.bfloat16
LATER = ("flux_local", "flux_remote", "face_restrict", "face_lift", "orient_maps", "slot", "face", "turn", "rate")
AXES = ("dom", "sub")
SWAPS = (("dom", True), ("dom", False), ("sub", True), ("sub", False))


def taylor_weight(lower, upper, degree):
    return (upper ** (degree + 1) - lower ** (degree + 1)) / math.factorial(degree + 1)


def weight_at(lower, upper, degree):
    result = jnp.float32(taylor_weight(lower, upper, 1))
    for option in range(2, DERIVS):
        result = jnp.where(degree == option, jnp.float32(taylor_weight(lower, upper, option)), result)
    return result


def split(values):
    high = values.astype(BF16)
    low = (values - high.astype(F32)).astype(BF16)
    return high, low


def stack_left(values):
    high, low = split(values)
    return jnp.concatenate([high, low, high], axis=1)


def stack_right(values):
    high, low = split(values)
    return jnp.concatenate([high, high, low], axis=0)


def product(left, right):
    return jnp.dot(left, right, preferred_element_type=F32)


def odd_place(axis):
    return lax.rem(lax.axis_index(axis), 2)


def message_side(slot):
    axis, far = SWAPS[slot]
    odd = odd_place(axis)
    return 2 * AXES.index(axis) + (odd if far else 1 - odd)


def ghost_slot(side):
    axis = AXES[side // 2]
    even_far = side % 2 == 0
    return jnp.where(odd_place(axis) == 0, SWAPS.index((axis, even_far)), SWAPS.index((axis, not even_far)))


def lane_index(shape):
    return lax.broadcasted_iota(jnp.int32, shape, len(shape) - 1)


def lower_half(shape):
    return lane_index(shape) < HALF


def swap_halves(values):
    return pltpu.roll(values, HALF, values.ndim - 1)


def pack(values_ref, packed_ref):
    modes = values_ref.shape[2]
    packed_ref[:, :, 0:modes] = values_ref[:, 0:ROWS, :]
    packed_ref[:, :, HALF : HALF + modes] = values_ref[:, ROWS : 2 * ROWS, :]


def high_and_low(values, shift):
    high = values.astype(BF16).astype(F32)
    return high + pltpu.roll(values - high, shift, 1)


def row_index(shape):
    return lax.broadcasted_iota(jnp.int32, shape, len(shape) - 2)


def one_where(condition):
    return jnp.where(condition, 1.0, 0.0)


def star_coefficients(star_ref, stage_ref, star_out):
    fields, kinds, elements = star_ref.shape[0], star_ref.shape[2], star_ref.shape[3]
    lanes = lane_index((ROWS, LANES))
    pick = one_where((lanes % ROWS == row_index((ROWS, LANES))) & (lanes < 2 * elements))
    from_lane = row_index((LANES, LANES))
    same_half = (from_lane % elements) // ROWS == lane_index((LANES, LANES)) // HALF
    right = one_where(same_half & (from_lane < 2 * elements)).astype(BF16)
    filled = lane_index(stage_ref.shape[1:]) < elements
    for row in range(fields):
        for col in range(fields):
            stage_ref[row, col * 4 : col * 4 + kinds, 0:elements] = star_ref[row, col]
        values = jnp.where(filled, stage_ref[row], 0.0)
        stage_ref[row] = high_and_low(values, elements)
        spreads = []
        for kind in range(kinds):
            for col in range(fields):
                at = col * 4 + kind
                spreads.append(stage_ref[row, at : at + 1, :] * pick)
        spread_out = product(jnp.concatenate(spreads, axis=0).astype(BF16), right)
        count = kinds * fields
        star_out[row * count : (row + 1) * count] = spread_out.reshape(count, ROWS, LANES)


def star_mix(columns, star_ref, fields, kinds):
    sums = []
    for col in range(fields):
        parts = []
        for kind in range(kinds):
            total = None
            for row in range(fields):
                part = columns[row * ROWS : (row + 1) * ROWS, kind * LANES : (kind + 1) * LANES]
                term = star_ref[(row * kinds + kind) * fields + col] * part
                total = term if total is None else total + term
            parts.append(total)
        sums.append(sum(parts[1:], parts[0]))
    return jnp.concatenate(sums, axis=0)


def stiffness_blocks(stiffness_ref, block_ref, turned):
    kinds, modes = stiffness_ref.shape[0], stiffness_ref.shape[1]
    for kind in range(kinds):
        matrix = -stiffness_ref[kind].T if turned else stiffness_ref[kind]
        block_ref[kind, 0:modes, 0:modes] = matrix
        block_ref[kind, HALF : HALF + modes, HALF : HALF + modes] = matrix
    return jnp.concatenate([block_ref[kind] for kind in range(kinds)], axis=1)


def predict_kernel(*refs):
    later = len(LATER)
    solution_hbm, stiffness_hbm, star_hbm, send_hbm = refs[0:4]
    later_hbm, refs = refs[4 : 4 + later], refs[4 + later :]
    early_out, late_out, send_0, send_1, send_2, send_3 = refs[0:6]
    packed_ref, coef_ref, derive_ref, stiffness_ref, early_rows = refs[6:11]
    later_out, refs = refs[11 : 11 + later], refs[11 + later :]
    work_ref, late_rows, solution_ref, block_ref, star_ref, send_ref, sems = refs

    pieces = []
    for source, target in ((star_hbm, star_ref), (stiffness_hbm, stiffness_ref), (solution_hbm, solution_ref)):
        step = source.shape[0] // 3
        pieces += [(source.at[pl.ds(at, step)], target.at[pl.ds(at, step)]) for at in range(0, source.shape[0], step)]
    first = len(pieces)
    pieces += zip((send_hbm, *later_hbm), (send_ref, *later_out))
    copies = [
        pltpu.make_async_copy(source, target, sems.at[number]) for number, (source, target) in enumerate(pieces)
    ]
    for copy in copies:
        copy.start()
    fields, kinds = star_ref.shape[0], star_ref.shape[2]
    pairs = (fields + 1) // 2
    for cleared in (packed_ref, block_ref, send_0, send_1, send_2, send_3):
        cleared[...] = jnp.zeros(cleared.shape, F32)
    for copy in copies[0:first]:
        copy.wait()
    derive_ref[...] = stack_right(stiffness_blocks(stiffness_ref, block_ref, True))
    star_coefficients(star_ref, work_ref, coef_ref)
    pack(solution_ref, packed_ref)
    start = packed_ref[...].reshape(fields * ROWS, LANES)

    def step(degree, carry):
        current, early, late = carry
        current = star_mix(product(stack_left(current), derive_ref[...]), coef_ref, fields, kinds)
        early = early + weight_at(0.0, 0.5, degree) * current
        late = late + weight_at(0.5, 1.0, degree) * current
        return current, early, late

    _, early, late = lax.fori_loop(
        1, DERIVS, step, (start, taylor_weight(0.0, 0.5, 0) * start, taylor_weight(0.5, 1.0, 0) * start),
        unroll=True,
    )
    early_out[...] = early.reshape(fields, ROWS, LANES)
    late_out[...] = late.reshape(fields, ROWS, LANES)
    rows_by_pair(early, early_rows, fields)
    rows_by_pair(late, late_rows, fields)
    copies[first].wait()
    sends = send_ref.shape[2]
    fast = sends // 2
    for side, out in enumerate((send_0, send_1, send_2, send_3)):
        for place in range(sends):
            element = send_ref[0, message_side(side), place]
            for pair in range(pairs):
                row = pair * sends + place
                out[row : row + 1, :] = early_rows[pair, pl.ds(element, 1), :]
            if place >= fast:
                for pair in range(pairs):
                    row = pairs * sends + pair * fast + place - fast
                    out[row : row + 1, :] = late_rows[pair, pl.ds(element, 1), :]
    for copy in copies[first + 1 :]:
        copy.wait()


def rows_by_pair(packed, out_ref, fields):
    lower = lower_half((ROWS, LANES))
    for pair in range((fields + 1) // 2):
        even = packed[2 * pair * ROWS : (2 * pair + 1) * ROWS]
        odd = jnp.zeros_like(even)
        if 2 * pair + 1 < fields:
            odd = packed[(2 * pair + 1) * ROWS : (2 * pair + 2) * ROWS]
        out_ref[pair, 0:ROWS, :] = jnp.where(lower, even, swap_halves(odd))
        out_ref[pair, ROWS : 2 * ROWS, :] = jnp.where(lower, swap_halves(even), odd)


def flux_local_coefficients(flux_ref, stage_ref, out_ref):
    fields, faces, elements = flux_ref.shape[0], flux_ref.shape[2], flux_ref.shape[3]
    rows = 2 * ROWS
    filled = lane_index((rows, LANES)) < elements
    lanes, sublanes = lane_index((ROWS, LANES)), row_index((ROWS, LANES))
    picks = [one_where(lanes % elements == half * ROWS + sublanes) for half in range(2)]
    square = (LANES, LANES)
    right = one_where(row_index(square) // (2 * elements) == lane_index(square) % faces).astype(BF16)
    for row in range(fields):
        values = None
        for face in range(faces):
            stage_ref[row, face * rows : face * rows + fields, 0:elements] = flux_ref[row, :, face, :]
            part = jnp.where(filled, stage_ref[row, face * rows : (face + 1) * rows, :], 0.0)
            values = part if values is None else values + pltpu.roll(part, face * 2 * elements, 1)
        stage_ref[row, 0:rows, :] = high_and_low(values, elements)
        left = [stage_ref[row, col : col + 1, :] * pick for col in range(fields) for pick in picks]
        spread = product(jnp.concatenate(left, axis=0).astype(BF16), right)
        out_ref[row * fields : (row + 1) * fields] = spread.reshape(fields, 2, ROWS, LANES)


def flux_remote_coefficients(flux_ref, stage_ref, out_ref):
    fields, faces, elements = flux_ref.shape[0], flux_ref.shape[2], flux_ref.shape[3]
    pairs = (fields + 1) // 2
    rows = stage_ref.shape[1] // 2
    filled = lane_index((rows, LANES)) < elements
    lanes, sublanes = lane_index((elements, LANES)), row_index((elements, LANES))
    pick = one_where((lanes % elements == sublanes) & (lanes < 4 * elements))
    square = (LANES, LANES)
    from_lane = row_index(square)
    same_parity = (from_lane // elements) % 2 == lane_index(square) // HALF
    right = one_where(same_parity & (from_lane < 4 * elements)).astype(BF16)
    for pair in range(pairs):
        values = None
        for row in range(2 * pair, min(2 * pair + 2, fields)):
            start = (row % 2) * rows
            for col in range(fields):
                at = start + col * faces
                stage_ref[pair, at : at + faces, 0:elements] = flux_ref[row, col]
            part = jnp.where(filled, stage_ref[pair, start : start + rows, :], 0.0)
            values = part if values is None else values + pltpu.roll(part, elements, 1)
        stage_ref[pair, 0:rows, :] = high_and_low(values, 2 * elements)
        for face in range(faces):
            left = []
            for col in range(fields):
                at = col * faces + face
                left.append(stage_ref[pair, at : at + 1, :] * pick)
            spread = product(jnp.concatenate(left, axis=0).astype(BF16), right)
            at = (face * pairs + pair) * fields
            out_ref[at : at + fields] = spread.reshape(fields, elements, LANES)


def local_terms(packed, star_ref, flux_ref, volume_ref, trace_ref, lift_ref, fields, kinds):
    left = stack_left(packed)
    volume = star_mix(product(left, volume_ref[...]), star_ref, fields, kinds)
    traces = product(left, trace_ref[...])
    sums = []
    for col in range(fields):
        halves = []
        for half in range(2):
            total = None
            for row in range(fields):
                part = traces[row * ROWS : (row + 1) * ROWS, half * LANES : (half + 1) * LANES]
                term = flux_ref[row * fields + col, half] * part
                total = term if total is None else total + term
            halves.append(total)
        sums.append(jnp.concatenate(halves, axis=1))
    return volume + product(stack_left(jnp.concatenate(sums, axis=0)), lift_ref[...])


def combo_code(lanes, turns, face_modes):
    in_face = lanes % HALF
    code = jnp.where(in_face < turns * face_modes, (lanes // HALF) * turns + in_face // face_modes, -1)
    return code.astype(F32)


def ghost_terms(
    flux_ref, stage_ref, code_ref, composed, lift_sides, lane_code, flux_out, operator_out, scatter_out, sends, fields
):
    faces, elements = flux_ref.shape[2], flux_ref.shape[3]
    rows = 2 * ROWS
    shape = (rows, LANES)
    lanes = lane_index(shape)

    def along_lanes(start):
        row = code_ref[start : start + 1, :]
        for face in range(1, faces):
            row = row + pltpu.roll(code_ref[start + face : start + face + 1, :], face * elements, 1)
        return row + swap_halves(row)

    slots, codes = along_lanes(0), along_lanes(faces)
    ghosts = elements + row_index(shape)
    found = one_where(jnp.broadcast_to(slots, shape) == ghosts.astype(F32))
    first = jnp.where(lanes < HALF, found, 0.0)
    code = jnp.sum(first * codes, axis=1, keepdims=True)
    face_of = jnp.sum(first * (lanes // elements).astype(F32), axis=1, keepdims=True)
    element_of = jnp.sum(first * (lanes % elements).astype(F32), axis=1, keepdims=True)
    numbers = [slot * sends + place for slot in range(4) for place in range(sends // 2)]

    filled = lanes < elements
    values = []
    for field in range(fields):
        total = None
        for face in range(faces):
            stage_ref[field, face * rows : face * rows + fields, 0:elements] = flux_ref[field, :, face, :]
            part = jnp.where(filled, stage_ref[field, face * rows : (face + 1) * rows, :], 0.0)
            total = part if total is None else total + pltpu.roll(part, face * elements, 1)
        total = jnp.where(row_index(shape) < fields, total, 0.0)
        values.append(high_and_low(total, HALF))
    picked = jnp.concatenate([jnp.broadcast_to(found[number : number + 1], (HALF, LANES)) for number in numbers], axis=0)
    flux_out[...] = lax.dot_general(
        jnp.concatenate(values, axis=0).astype(BF16), picked.astype(BF16), (((1,), (1,)), ((), ())),
        preferred_element_type=F32,
    )

    left = []
    for number in numbers:
        chosen = composed * one_where(lane_code == code[number : number + 1])
        both = chosen[:, 0:LANES] + chosen[:, LANES : 2 * LANES]
        high, low = split(both + swap_halves(both))
        left.append(jnp.concatenate([jnp.where(lower_half(high.shape), high, low), high], axis=1))
    high, low = split(lift_sides)
    lifts = product(jnp.concatenate(left, axis=0), jnp.concatenate([high, high, low, jnp.zeros_like(low)], axis=0))
    side_lane = (lane_index((1, faces * HALF)) // HALF).astype(F32)
    place_of = jnp.zeros((1, LANES), F32)
    columns = []
    for at, number in enumerate(numbers):
        chosen = lifts[at * HALF : (at + 1) * HALF] * one_where(side_lane == face_of[number : number + 1])
        both = chosen[:, 0:LANES] + chosen[:, LANES : 2 * LANES]
        high, low = split(both + swap_halves(both))
        none = jnp.zeros_like(low)
        order = [high, none, high, none, low, none] if at % 2 == 0 else [none, high, none, high, none, low]
        columns.append(jnp.concatenate(order, axis=0))
        if at % 2 == 1:
            operator_out[at // 2] = jnp.concatenate(columns[-2:], axis=1)
        place_of = jnp.where(lane_index((1, LANES)) // rows == at, element_of[number : number + 1], place_of)
    square = (fields * elements, LANES)
    here = (row_index(square) // elements == lane_index(square) % rows) & (
        (row_index(square) % elements).astype(F32) == place_of
    )
    one = one_where(here).astype(BF16)
    scatter_out[...] = jnp.concatenate([one, one], axis=1)


def prepare_kernel(
    packed_ref, early_ref, stiffness_ref, star_ref, flux_local_ref, flux_remote_ref, restrict_ref, lift_ref, orient_ref,
    slot_ref, face_ref, turn_ref, rate_ref,
    base_out, local_out, remote_out, volume_out, trace_out, local_lift_out, compose_out,
    remote_lift_out, choose_out, mask_out, code_ref, composed_out, sides_ref, fast_out,
    local_work_ref, remote_work_ref, block_ref, wide_ref, face_work_ref, orient_work_ref, code_work_ref,
):
    fields, kinds = packed_ref.shape[0], stiffness_ref.shape[0]
    face_modes, faces, modes = restrict_ref.shape
    turns = orient_ref.shape[0]
    flux_local_coefficients(flux_local_ref, local_work_ref, local_out)
    flux_remote_coefficients(flux_remote_ref, remote_work_ref, remote_out)

    block_ref[...] = jnp.zeros(block_ref.shape, F32)
    volume_out[...] = stack_right(stiffness_blocks(stiffness_ref, block_ref, False))

    wide_ref[...] = jnp.zeros(wide_ref.shape, F32)
    for mode in range(face_modes):
        at = mode * faces
        wide_ref[at : at + faces, 0:modes] = restrict_ref[mode]
        wide_ref[LANES + at : LANES + at + faces, HALF : HALF + modes] = restrict_ref[mode]
    trace_out[...] = stack_right(wide_ref[...].T)
    for mode in range(face_modes):
        at = mode * faces
        wide_ref[at : at + faces, 0:modes] = -lift_ref[mode]
        wide_ref[LANES + at : LANES + at + faces, HALF : HALF + modes] = -lift_ref[mode]
    local_lift_out[...] = stack_right(wide_ref[...])

    face_work_ref[...] = jnp.zeros(face_work_ref.shape, F32)
    orient_work_ref[...] = jnp.zeros(orient_work_ref.shape, F32)
    for turn in range(turns):
        orient_work_ref[turn * face_modes : (turn + 1) * face_modes, 0:face_modes] = orient_ref[turn]
    for face in range(faces):
        face_work_ref[0:face_modes, face * LANES : face * LANES + modes] = restrict_ref[:, face, :]
        face_work_ref[0:face_modes, face * LANES + HALF : face * LANES + HALF + modes] = restrict_ref[:, face, :]
    composed = jnp.dot(
        orient_work_ref[...], face_work_ref[...], precision=lax.Precision.HIGHEST, preferred_element_type=F32
    )
    stacked = jnp.concatenate([composed[:, face * LANES : (face + 1) * LANES] for face in range(faces)], axis=0)
    high, low = split(stacked.T[0:HALF])
    compose_out[...] = jnp.concatenate([high, high, low, jnp.zeros_like(low)], axis=0)
    wide_ref[...] = jnp.zeros(wide_ref.shape, F32)
    for face in range(faces):
        for turn in range(turns):
            rows = slice(face * HALF + turn * face_modes, face * HALF + (turn + 1) * face_modes)
            wide_ref[rows, 0:modes] = -lift_ref[:, face, :]
            wide_ref[rows, HALF : HALF + modes] = -lift_ref[:, face, :]
    remote_lift_out[...] = stack_right(wide_ref[...])

    elements = slot_ref.shape[1]
    code_work_ref[...] = jnp.zeros(code_work_ref.shape, F32)
    slots = slot_ref[...]
    sends = (choose_out.shape[1] // 2 - elements) // 4
    group = (slots - elements) // sends
    moved = slots
    for side in range(4):
        moved = jnp.where(group == side, slots + (ghost_slot(side) - side) * sends, moved)
    code_work_ref[0:faces, 0:elements] = jnp.where(slots < elements, slots, moved).astype(F32)
    code_work_ref[faces : 2 * faces, 0:elements] = (face_ref[...] * turns + turn_ref[...]).astype(F32)
    code_work_ref[2 * faces : 2 * faces + 1, 0:elements] = rate_ref[...].astype(F32)
    code_ref[...] = code_work_ref[0 : 2 * faces, :]
    codes = code_work_ref[...].T[0:elements, :]
    rates = codes[:, 2 * faces : 2 * faces + 1]
    fast_out[...] = jnp.where(lower_half((ROWS, LANES)), rates[0:ROWS], rates[ROWS : 2 * ROWS])
    sources = choose_out.shape[1] // 2
    source_lane = (lane_index((elements, 2 * sources)) % sources).astype(F32)
    lanes = lane_index((elements, mask_out.shape[1]))
    lane_code = combo_code(lanes, turns, face_modes)
    picks, masks = [], []
    for face in range(faces):
        picks.append(jnp.where(codes[:, face : face + 1] == source_lane, 1.0, 0.0))
        masks.append(jnp.where(codes[:, faces + face : faces + face + 1] == lane_code, 1.0, 0.0))
    choose_out[...] = jnp.concatenate(picks, axis=0).astype(BF16)
    mask_out[...] = jnp.concatenate(masks, axis=0)

    sides_ref[...] = jnp.zeros(sides_ref.shape, F32)
    for face in range(faces):
        for turn in range(turns):
            rows = slice(turn * face_modes, (turn + 1) * face_modes)
            sides_ref[rows, face * HALF : face * HALF + modes] = -lift_ref[:, face, :]
    composed_out[...] = stacked.T[0:HALF]

    early = early_ref[...].reshape(fields * ROWS, LANES)
    terms = local_terms(early, star_ref, local_out, volume_out, trace_out, local_lift_out, fields, kinds)
    base_out[...] = packed_ref[...] + terms.reshape(fields, ROWS, LANES)


def remote_terms(rows, remote_ref, compose_ref, lift_ref, choose_ref, mask_ref, fields):
    pairs = len(rows)
    faces = lift_ref.shape[0] // (3 * HALF)
    elements = choose_ref.shape[0] // faces
    sources = jnp.concatenate(rows, axis=1)
    gathered = product(choose_ref[...], jnp.concatenate(split(sources), axis=0))
    folded = []
    for face in range(faces):
        sums = []
        for col in range(fields):
            total = None
            for pair in range(pairs):
                part = gathered[face * elements : (face + 1) * elements, pair * LANES : (pair + 1) * LANES]
                term = remote_ref[(face * pairs + pair) * fields + col] * part
                total = term if total is None else total + term
            sums.append(total)
        mixed = jnp.concatenate(sums, axis=0)
        high, low = split(mixed + swap_halves(mixed))
        first = jnp.where(lower_half(high.shape), high, low)
        turned = product(jnp.concatenate([first, high], axis=1), compose_ref[...])
        mask = mask_ref[face * elements : (face + 1) * elements, :]
        chosen = (turned.reshape(fields, elements, turned.shape[1]) * mask[None]).reshape(turned.shape)
        both = chosen[:, 0:LANES] + chosen[:, LANES : 2 * LANES]
        folded.append(both + swap_halves(both))
    lower = lower_half(folded[0].shape)
    left = [jnp.where(lower, folded[face], folded[face + 1]) for face in range(0, faces, 2)]
    result = product(stack_left(jnp.concatenate(left, axis=1)), lift_ref[...])
    result = result.reshape(fields, 2, ROWS, LANES)
    return jnp.where(lower_half((ROWS, LANES))[None], result[:, 0], result[:, 1])


def middle_kernel(
    base_ref, early_rows, late_ref, star_ref, remote_ref, derive_ref, compose_ref, lift_ref, choose_ref, mask_ref,
    fast_ref, send_hbm, from_0, from_1, from_2, from_3,
    middle_out, late_out, send_0, send_1, send_2, send_3,
    rows_ref, late_rows, send_ref, sem,
):
    copy = pltpu.make_async_copy(send_hbm, send_ref, sem)
    copy.start()
    for cleared in (send_0, send_1, send_2, send_3):
        cleared[...] = jnp.zeros(cleared.shape, F32)
    fields = base_ref.shape[0]
    kinds = star_ref.shape[0] // (fields * fields)
    pairs = rows_ref.shape[0]
    sends = send_ref.shape[2]
    fast = sends // 2
    for side, arrived in enumerate((from_0, from_1, from_2, from_3)):
        for pair in range(pairs):
            rows_ref[pair, side * sends : (side + 1) * sends, :] = arrived[pair * sends : (pair + 1) * sends, :]
    rows = [jnp.concatenate([early_rows[pair], rows_ref[pair]], axis=0) for pair in range(pairs)]
    middle = base_ref[...] + remote_terms(rows, remote_ref, compose_ref, lift_ref, choose_ref, mask_ref, fields)
    middle_out[...] = middle
    start = middle.reshape(fields * ROWS, LANES)

    def step(degree, carry):
        current, early = carry
        current = star_mix(product(stack_left(current), derive_ref[...]), star_ref, fields, kinds)
        return current, early + weight_at(0.0, 0.5, degree) * current

    _, restart = lax.fori_loop(1, DERIVS, step, (start, taylor_weight(0.0, 0.5, 0) * start))
    copy.wait()
    is_fast = fast_ref[...]
    late = jnp.where((is_fast == 2)[None], restart.reshape(fields, ROWS, LANES), late_ref[...])
    late_out[...] = late
    both = late.reshape(fields * ROWS, LANES)
    swapped = swap_halves(both)
    wide = lower_half(both.shape)
    late_rows[:, 0:ROWS, :] = jnp.where(wide, both, swapped).reshape(late.shape)
    late_rows[:, ROWS : 2 * ROWS, :] = jnp.where(wide, swapped, both).reshape(late.shape)
    first_half = lower_half((1, LANES))
    for slot, out in enumerate((send_0, send_1, send_2, send_3)):
        side = message_side(slot)
        places = [send_ref[0, side, place] for place in range(fast)]
        for field in range(fields):
            halves = [late_rows[field, pl.ds(element, 1), :] for element in places]
            out[field : field + 1, :] = jnp.where(first_half, *halves)


def local_kernel(
    middle_ref, late_ref, star_ref, flux_ref, volume_ref, trace_ref, lift_ref,
    remote_ref, compose_ref, remote_lift_ref, choose_ref, mask_ref, flux_remote_ref, code_ref, composed_ref, sides_ref,
    orient_ref, first_0, first_1, first_2, first_3,
    base_out, ghost_flux_out, ghost_operator_out, scatter_out, rows_ref, stage_ref,
):
    fields = middle_ref.shape[0]
    kinds = star_ref.shape[0] // (fields * fields)
    pairs = rows_ref.shape[0]
    elements = 2 * ROWS
    sends = (rows_ref.shape[1] - elements) // 4
    fast = sends // 2
    late = late_ref[...].reshape(fields * ROWS, LANES)
    rows_by_pair(late, rows_ref, fields)
    for slot, first in enumerate((first_0, first_1, first_2, first_3)):
        at = elements + slot * sends
        for pair in range(pairs):
            rows_ref[pair, at : at + fast, :] = jnp.zeros((fast, LANES), F32)
            row = pairs * sends + pair * fast
            rows_ref[pair, at + fast : at + sends, :] = first[row : row + fast, :]
    terms = local_terms(late, star_ref, flux_ref, volume_ref, trace_ref, lift_ref, fields, kinds)
    rows = [rows_ref[pair] for pair in range(pairs)]
    remote = remote_terms(rows, remote_ref, compose_ref, remote_lift_ref, choose_ref, mask_ref, fields)
    base = middle_ref[...] + terms.reshape(fields, ROWS, LANES) + remote
    base_out[:, 0:ROWS, :] = base
    base_out[:, ROWS : 2 * ROWS, :] = swap_halves(base.reshape(fields * ROWS, LANES)).reshape(base.shape)
    lane_code = combo_code(lane_index((1, composed_ref.shape[1])), orient_ref.shape[0], orient_ref.shape[1])
    ghost_terms(
        flux_remote_ref, stage_ref, code_ref, composed_ref[...], sides_ref[...], lane_code,
        ghost_flux_out, ghost_operator_out, scatter_out, sends, fields,
    )


def final_kernel(
    base_ref, ghost_flux_ref, ghost_operator_ref, scatter_ref, second_0, second_1, second_2, second_3, result_out,
):
    fields = base_ref.shape[0]
    modes = result_out.shape[2]
    rows = second_0.shape[0]
    added = []
    for slot, second in enumerate((second_0, second_1, second_2, second_3)):
        sums = [None] * 3
        for field in range(fields):
            coefficient = ghost_flux_ref[field * rows : (field + 1) * rows, slot * LANES : (slot + 1) * LANES]
            term = coefficient * second[field : field + 1, :]
            sums[field % 3] = term if sums[field % 3] is None else sums[field % 3] + term
        both = product(stack_left(sums[0] + sums[1] + sums[2]), ghost_operator_ref[slot])
        added += [both[:, 0:LANES], both[:, LANES : 2 * LANES]]
    right = jnp.concatenate(split(jnp.concatenate(added, axis=0)), axis=0)
    result = base_ref[...] + product(scatter_ref[...], right).reshape(base_ref.shape)
    result_out[...] = result[:, :, 0:modes]


VMEM = pl.BlockSpec(memory_space=pltpu.VMEM)
HBM = pl.BlockSpec(memory_space=pltpu.HBM)


def call(kernel, ins, outs, scratch, args, name, flops):
    shapes = [jax.ShapeDtypeStruct(shape, dtype) for shape, dtype in outs]
    args = [
        pltpu.with_memory_space_constraint(arg, pltpu.HBM) if spec is HBM else arg for spec, arg in zip(ins, args)
    ]
    return pl.pallas_call(
        kernel,
        out_shape=shapes,
        in_specs=ins,
        out_specs=[VMEM] * len(outs),
        scratch_shapes=[pltpu.VMEM(*one) if isinstance(one, tuple) else one for one in scratch],
        compiler_params=pltpu.CompilerParams(vmem_limit_bytes=16 * 1024 * 1024),
        cost_estimate=pl.CostEstimate(flops=flops, bytes_accessed=4_000_000, transcendentals=0),
        name=name,
    )(*args)


def exchange(outgoing):
    arrived = []
    for (axis, far), message in zip(SWAPS, outgoing):
        size = lax.axis_size(axis)
        assert size % 2 == 0
        pairs = []
        for first in range(1 if far else 0, size, 2):
            second = (first + 1) % size
            pairs += [(first, second), (second, first)]
        arrived.append(lax.ppermute(message, axis, pairs))
    return arrived


def up_to(count, multiple):
    return -(-count // multiple) * multiple


def local(
    solution, stiffness, star_matrices, face_restrict, face_lift, orient_maps, flux_local, flux_remote,
    cluster_rate, send_list, neighbour_slot, neighbour_face, neighbour_turn,
):
    fields, elements = solution.shape[1], solution.shape[2]
    kinds = stiffness.shape[0]
    faces = face_restrict.shape[0]
    sides, sends = send_list.shape[1], send_list.shape[2]
    fast = sends // 2
    pairs = (fields + 1) // 2
    assert elements == 2 * ROWS and solution.shape[0] <= HALF and fast == 2
    values = jnp.transpose(solution, (1, 2, 0))
    star = jnp.transpose(star_matrices, (1, 2, 0, 3))
    local_part = jnp.transpose(flux_local, (1, 2, 0, 3))
    remote_part = jnp.transpose(flux_remote, (1, 2, 0, 3))
    restrict = jnp.transpose(face_restrict, (1, 0, 2))
    lift = jnp.transpose(face_lift, (2, 0, 1))

    packed = (fields, ROWS, LANES)
    first_shape = (up_to(pairs * (sends + fast), ROWS), LANES)
    second_shape = (up_to(fields, 2 * ROWS), LANES)
    star_shape = (fields * fields * kinds, ROWS, LANES)
    combos = faces * HALF
    sources = elements + sides * sends

    waiting = (
        local_part, remote_part, restrict, lift, orient_maps, neighbour_slot, neighbour_face, neighbour_turn,
        cluster_rate.reshape(1, elements),
    )
    made = call(
        predict_kernel,
        [HBM] * (4 + len(LATER)),
        [(packed, F32)] * 2 + [(first_shape, F32)] * sides + [
            (packed, F32), (star_shape, F32), ((3 * LANES, kinds * LANES), BF16), (stiffness.shape, F32),
            ((pairs, elements, LANES), F32),
        ] + [(array.shape, array.dtype) for array in waiting],
        [
            ((fields, up_to(4 * fields, ROWS), LANES), F32),
            ((pairs, elements, LANES), F32),
            (values.shape, F32), ((kinds, LANES, LANES), F32), (star.shape, F32),
            pltpu.SMEM(send_list.shape, jnp.int32), pltpu.SemaphoreType.DMA((10 + len(LATER),)),
        ],
        (values, stiffness, star, send_list, *waiting),
        "predict", 100_000_000,
    )
    early, late, outgoing = made[0], made[1], made[2 : 2 + sides]
    start, star_coef, derive_op, stiffness_kept, early_rows = made[2 + sides : 7 + sides]
    waiting = made[7 + sides :]
    first = exchange(outgoing)
    (
        base, local_coef, remote_coef, volume_op, trace_op, local_lift, compose_op, remote_lift, choose, mask,
        codes, composed, lift_sides, fast_mask,
    ) = call(
        prepare_kernel,
        [VMEM] * 13,
        [
            (packed, F32), ((fields * fields, 2, ROWS, LANES), F32),
            ((faces * pairs * fields, elements, LANES), F32),
            ((3 * LANES, kinds * LANES), BF16), ((3 * LANES, 2 * LANES), BF16),
            ((6 * LANES, LANES), BF16), ((2 * LANES, combos), BF16), ((3 * faces * HALF, LANES), BF16),
            ((faces * elements, 2 * sources), BF16), ((faces * elements, combos), F32),
            ((2 * faces, LANES), F32), ((HALF, combos), F32), ((HALF, faces * HALF), F32),
            ((ROWS, LANES), F32),
        ],
        [
            ((fields, 2 * ROWS * faces, LANES), F32), ((pairs, 2 * up_to(4 * fields, ROWS), LANES), F32),
            ((kinds, LANES, LANES), F32), ((2 * LANES, LANES), F32),
            ((LANES, faces * LANES), F32), ((HALF, LANES), F32), ((LANES, LANES), F32),
        ],
        (start, early, stiffness_kept, star_coef, *waiting),
        "prepare", 200_000_000,
    )
    middle, late_value, *outgoing = call(
        middle_kernel,
        [VMEM] * 11 + [HBM] + [VMEM] * 4,
        [(packed, F32)] * 2 + [(second_shape, F32)] * sides,
        [
            ((pairs, sides * sends, LANES), F32), ((fields, elements, LANES), F32),
            pltpu.SMEM(send_list.shape, jnp.int32), pltpu.SemaphoreType.DMA,
        ],
        (
            base, early_rows, late, star_coef, remote_coef, derive_op, compose_op, remote_lift, choose, mask,
            fast_mask, send_list, *first,
        ),
        "middle", 200_000_000,
    )
    second = exchange(outgoing)
    base, ghost_flux, ghost_op, scatter = call(
        local_kernel,
        [VMEM] * (17 + len(first)),
        [
            ((fields, elements, LANES), F32), ((fields * second_shape[0], sides * LANES), F32),
            ((sides, 3 * LANES, 2 * LANES), BF16), ((fields * elements, 2 * LANES), BF16),
        ],
        [((pairs, sources, LANES), F32), ((fields, 2 * ROWS * faces, LANES), F32)],
        (
            middle, late_value, star_coef, local_coef, volume_op, trace_op, local_lift,
            remote_coef, compose_op, remote_lift, choose, mask, waiting[1], codes, composed, lift_sides, waiting[4],
            *first,
        ),
        "local_late", 200_000_000,
    )
    (result,) = call(
        final_kernel,
        [VMEM] * 8,
        [(values.shape, F32)],
        [],
        (base, ghost_flux, ghost_op, scatter, *second),
        "final", 200_000_000,
    )
    return jnp.transpose(result, (2, 0, 1))


def solution(mesh):
    placed = (
        P(None, None, ("dom", "sub")),
        P(),
        P(None, None, None, ("dom", "sub")),
        P(),
        P(),
        P(),
        P(None, None, None, ("dom", "sub")),
        P(None, None, None, ("dom", "sub")),
        P(("dom", "sub")),
        P(("dom", "sub"), None, None),
        P(None, ("dom", "sub")),
        P(None, ("dom", "sub")),
        P(None, ("dom", "sub")),
    )
    return jax.shard_map(
        local, mesh=mesh, in_specs=placed, out_specs=P(None, None, ("dom", "sub")), check_vma=False
    )
```
